32 devices in a mesh: groups: 2 (over y), dp: 4 (over z), query: 4 (over x, core).
Axes of the slice: x: 2, y: 2, z: 4, core: 2. Of those that a mesh axis runs over, the one named last changes fastest.
Arguments:
- activations: bfloat16 [2048, 4096], P(('groups', 'dp'), 'query'), parts along dimension 0, may hold values from -6 to 6
- out_grads: bfloat16 [2048, 14336], P(('groups', 'dp'), 'query'), parts along dimension 0, may hold values from -6 to 6
- proj_in: bfloat16 [4096, 64], P('query'), may hold values from -0.09375 to 0.09375
- proj_out: bfloat16 [14336, 64], P('query')
- queries: bfloat16 [8192, 1024], P(('groups', 'dp'), 'query'), parts along dimension 0, may hold values from -2 to 2
- lengths: int32 [16], P(('groups', 'dp')), parts along dimension 0, may hold values from 32 to 128
- credit: int32 [16], P(('groups', 'dp')), parts along dimension 0, may hold values from 1 to 10
Outputs:
- hessian: float32 [8192, 4096], P(('groups', 'dp')), parts along dimension 0
- scores: bfloat16 [2048, 1024], P(('groups', 'dp'), 'query'), parts along dimension 0
The draws below stay inside these ranges and needn't reach their ends.
There are 2 independent parts, one for each index of `groups`. The reference program is written for one: setup_inputs(seed, part) draws one part's arguments, and reference() takes and returns one part's arrays. A program takes and returns all parts, laid end to end along the dimension named above; an argument that names none is the same for every part. Nothing has to cross between parts.
All inputs are finite; a program needn't handle non-finite values.
Results may differ from the reference program's by a relative error of at most 0.008.
Values may be sent and summed in bfloat16 or wider, within the bound.
No kernel may reach another device: no remote copies, remote signals or barrier semaphores. Data moves between devices by JAX's collectives and lax.ppermute only.
A program may use at most 128 MiB of HBM per device.

```python
import math
import jax
import jax.numpy as jnp
from jax import lax

D = 4096
FF = 14336
R = 64
F = 4096
NQ = 1024
SEQ = 128
TOKENS = 1024
NSEQ = 8


def draw_proj_out(key, part):
    key = jax.random.fold_in(key, 7)
    base_key, scale_key = jax.random.split(key)
    base = jnp.clip(jax.random.normal(base_key, (FF, R), jnp.float32), -5.0, 5.0)
    top = jnp.log(4.0)
    scales = jnp.exp(jax.random.uniform(scale_key, (R,), jnp.float32, 0.0, top))
    return (base * FF ** (-0.5) * scales[None, :]).astype(jnp.bfloat16)


def set_ends(array, key, smallest, largest):
    longest = array.shape.index(max(array.shape))
    spots = []
    for shift in (0, 1):
        where = [jax.random.randint(jax.random.fold_in(key, axis), (), 0, length) for axis, length in enumerate(array.shape)]
        where[longest] = (where[longest] + shift) % array.shape[longest]
        spots.append(tuple(where))
    return array.at[spots[0]].set(smallest).at[spots[1]].set(largest)


def block_levels(rng, extent, shards, low, top_value):
    factor_of = 1.0
    for dim, blocks in shards:
        heights = jax.random.uniform(jax.random.fold_in(jax.random.fold_in(rng, 6), dim), (blocks,), jnp.float32, low / len(shards), top_value / len(shards))
        factor_of = factor_of * jnp.repeat(jnp.exp(heights), extent[dim] // blocks).reshape((-1,) + (1,) * (len(extent) - 1 - dim))
    return factor_of


def centred(stream_key, dims, deviation, reach, cuts=(), kind=jnp.bfloat16):
    values = jax.random.normal(stream_key, dims, jnp.float32) * deviation
    if len(cuts) > 0:
        values = block_levels(stream_key, dims, cuts, -0.22, 0.18) * values
    return jnp.clip(values, min=-reach, max=reach).astype(kind)


def setup_inputs(seed: int = 0, part: int = 0) -> dict:
    keys = jax.random.split(jax.random.key(seed), 8)
    own_keys = jax.random.split(jax.random.fold_in(keys[7], part), 8)
    activations = centred(own_keys[0], (TOKENS, D), 1.0, 6.0, ((0, 4), (1, 4)))
    out_grads = centred(own_keys[1], (TOKENS, FF), 1.0, 6.0, ((0, 4), (1, 4)))
    proj_in = centred(keys[2], (D, R), D ** -0.5, 0.09375, ((0, 4),))
    proj_out = draw_proj_out(jax.random.fold_in(keys[7], 71), part)
    queries = centred(own_keys[4], (F, NQ), 0.25, 2.0, ((0, 4), (1, 4)))
    lengths = set_ends(jax.random.randint(own_keys[5], (NSEQ,), SEQ // 4, SEQ + 1), jax.random.fold_in(own_keys[5], 1), SEQ // 4, SEQ).astype(jnp.int32)
    credit = set_ends(jax.random.randint(own_keys[6], (NSEQ,), 1, 11), jax.random.fold_in(own_keys[6], 1), 1, 10).astype(jnp.int32)
    return dict(activations=activations, out_grads=out_grads, proj_in=proj_in, proj_out=proj_out, queries=queries, lengths=lengths, credit=credit)


def kron_rows(grad_rows, act_rows):
    count = grad_rows.shape[0]
    outer = grad_rows.astype(jnp.float32)[:, :, None] * act_rows.astype(jnp.float32)[:, None, :]
    return outer.reshape(count, R * R).astype(jnp.bfloat16)


def reference(activations, out_grads, proj_in, proj_out, queries, lengths, credit):
    act_proj = jnp.dot(activations, proj_in, preferred_element_type=jnp.float32).astype(jnp.bfloat16)
    grad_proj = jnp.dot(out_grads, proj_out, preferred_element_type=jnp.float32).astype(jnp.bfloat16)
    live = jnp.arange(SEQ, dtype=jnp.int32)[None, :] < lengths[:, None]
    weight = (credit[:, None].astype(jnp.float32) * live.astype(jnp.float32)).reshape(-1)
    mask = live.astype(jnp.float32).reshape(-1)
    block = math.gcd(TOKENS, 1024)
    count = TOKENS // block

    def accumulate(total, index):
        start = (index * block).astype(jnp.int32)
        grad_rows = lax.dynamic_slice_in_dim(grad_proj, start, block, 0)
        act_rows = lax.dynamic_slice_in_dim(act_proj, start, block, 0)
        weight_rows = lax.dynamic_slice_in_dim(weight, start, block, 0)
        features = kron_rows(grad_rows, act_rows)
        weighted = (weight_rows[:, None] * features.astype(jnp.float32)).astype(jnp.bfloat16)
        term = lax.dot_general(weighted, features, (((0,), (0,)), ((), ())), preferred_element_type=jnp.float32)
        return total + term, None

    hessian, _ = lax.scan(accumulate, jnp.zeros((R * R, R * R), jnp.float32), jnp.arange(count, dtype=jnp.int32))
    hessian = hessian / TOKENS
    level = jnp.trace(hessian) / (R * R)
    step = 1.1 * level
    query_f = queries.astype(jnp.float32)
    image = jnp.dot(hessian, query_f, precision=lax.Precision.HIGHEST)
    precond = ((2.0 * query_f - (image + 0.1 * level * query_f) / step) / step).astype(jnp.bfloat16)

    def scoring(carry, index):
        start = (index * block).astype(jnp.int32)
        grad_rows = lax.dynamic_slice_in_dim(grad_proj, start, block, 0)
        act_rows = lax.dynamic_slice_in_dim(act_proj, start, block, 0)
        features = kron_rows(grad_rows, act_rows)
        return carry, jnp.dot(features, precond, preferred_element_type=jnp.float32)

    _, blocks = lax.scan(scoring, jnp.float32(0.0), jnp.arange(count, dtype=jnp.int32))
    scores = (blocks.reshape(TOKENS, NQ) * mask[:, None]).astype(jnp.bfloat16)
    return hessian, scores
```

```python
import functools
import jax
import jax.numpy as jnp
from jax import lax
from jax.experimental import pallas as pl
from jax.experimental.pallas import tpu as pltpu
from jax.sharding import PartitionSpec as P


def kron_columns(grad_rows, act_rows, start, count):
    rank = grad_rows.shape[1]
    tokens_here = grad_rows.shape[0]
    grad_cols = lax.dynamic_slice_in_dim(grad_rows, start // rank, count // rank, 1)
    outer = grad_cols.astype(jnp.float32)[:, :, None] * act_rows.astype(jnp.float32)[:, None, :]
    return outer.reshape(tokens_here, count).astype(jnp.bfloat16)


def hessian_block(total, pieces, row_start, rows_own, col_start, col_count):
    grad_rows, act_rows, weights = pieces
    left = kron_columns(grad_rows, act_rows, row_start, rows_own)
    weighted = (weights.astype(jnp.float32)[:, None] * left.astype(jnp.float32)).astype(
        jnp.bfloat16
    )
    right = kron_columns(grad_rows, act_rows, col_start, col_count)
    return total + lax.dot_general(
        weighted, right, (((0,), (0,)), ((), ())), preferred_element_type=jnp.float32
    )


def fold_blocks(total, pieces, step_fn):
    count = pieces[0].shape[0]
    shaped = tuple((p.reshape((count // 512, 512) + p.shape[1:]) for p in pieces))

    def inner(carry, block):
        return (step_fn(carry, block), None)

    return lax.scan(inner, total, shaped)[0]


def split_parts(matrix):
    high_part = matrix.astype(jnp.bfloat16)
    first_rest = matrix - high_part.astype(jnp.float32)
    middle_part = first_rest.astype(jnp.bfloat16)
    low_part = (first_rest - middle_part.astype(jnp.float32)).astype(jnp.bfloat16)
    return (high_part, middle_part, low_part)


def many_tokens(activations, out_grads, proj_in, proj_out, queries, lengths, credit):
    tok_rows = activations.shape[0]
    seq_len = tok_rows // lengths.shape[0]
    dp_count = lax.axis_size("dp")
    query_count = lax.axis_size("query")
    dp_index = lax.axis_index("dp")
    query_index = lax.axis_index("query")
    part_act = jnp.dot(activations, proj_in, preferred_element_type=jnp.float32)
    part_grad = jnp.dot(out_grads, proj_out, preferred_element_type=jnp.float32)
    sum_act, sum_grad = lax.psum((part_act, part_grad), "query")
    act_proj = sum_act.astype(jnp.bfloat16)
    grad_proj = sum_grad.astype(jnp.bfloat16)
    rank = act_proj.shape[1]
    feat = rank * rank
    live = jnp.arange(seq_len, dtype=jnp.int32)[None, :] < lengths[:, None]
    weight = (credit[:, None].astype(jnp.float32) * live.astype(jnp.float32)).reshape(-1)
    mask = live.astype(jnp.float32).reshape(-1)
    weight_wire = weight.astype(jnp.bfloat16)
    rows_own = feat // dp_count
    row_start = dp_index * rows_own
    all_tokens = tok_rows * dp_count
    col_count = feat // query_count
    col_start = query_index * col_count
    owned = fold_blocks(
        jnp.zeros((rows_own, col_count), jnp.float32),
        (
            lax.all_gather(grad_proj, "dp", axis=0, tiled=True),
            lax.all_gather(act_proj, "dp", axis=0, tiled=True),
            lax.all_gather(weight_wire, "dp", axis=0, tiled=True),
        ),
        lambda carry, block: hessian_block(carry, block, row_start, rows_own, col_start, col_count),
    )
    hessian = lax.all_gather(owned, "query", axis=1, tiled=True) / all_tokens
    diagonal_block = lax.dynamic_slice_in_dim(hessian, row_start, rows_own, 1)
    level = lax.psum(jnp.trace(diagonal_block), "dp") / feat
    step = 1.1 * level
    high_part, middle_part, low_part = split_parts(hessian)
    piece = lax.all_gather(queries, "dp", axis=0, tiled=True)
    result = jnp.zeros(queries.shape, jnp.float32)
    for part_matrix in (low_part, middle_part, high_part):
        columns = part_matrix
        result = result + jnp.dot(columns, piece, preferred_element_type=jnp.float32)
    query_f = queries.astype(jnp.float32)
    precond = ((2.0 * query_f - (result + 0.1 * level * query_f) / step) / step).astype(
        jnp.bfloat16
    )
    local_features = kron_columns(grad_proj, act_proj, 0, feat)
    piece = lax.all_gather(precond, "dp", axis=0, tiled=True)
    columns = lax.slice_in_dim(local_features, 0, piece.shape[0], axis=1)
    scores = jnp.zeros((tok_rows, precond.shape[1]), jnp.float32) + jnp.dot(
        columns, piece, preferred_element_type=jnp.float32
    )
    return (hessian, (scores * mask[:, None]).astype(jnp.bfloat16))


MEM = pltpu.CompilerParams(vmem_limit_bytes=48 * 1024 * 1024)
NT = (((1,), (1,)), ((), ()))


def project_kernel(act_ref, grad_ref, pin_ref, pout_ref, out_ref):
    @pl.when(pl.program_id(0) == 0)
    def _():
        out_ref[...] = jnp.zeros_like(out_ref)

    part_act = jnp.dot(act_ref[...], pin_ref[...], preferred_element_type=jnp.float32)
    part_grad = jnp.dot(grad_ref[...], pout_ref[...], preferred_element_type=jnp.float32)
    out_ref[...] += jnp.concatenate([part_act, part_grad], axis=1)


def project(activations, out_grads, proj_in, proj_out, steps=4):
    tok, d_here = activations.shape
    f_here = out_grads.shape[1]
    rank = proj_in.shape[1]
    return pl.pallas_call(
        project_kernel,
        grid=(steps,),
        in_specs=[
            pl.BlockSpec((tok, d_here // steps), lambda s: (0, s)),
            pl.BlockSpec((tok, f_here // steps), lambda s: (0, s)),
            pl.BlockSpec((d_here // steps, rank), lambda s: (s, 0)),
            pl.BlockSpec((f_here // steps, rank), lambda s: (s, 0)),
        ],
        out_specs=pl.BlockSpec((tok, 2 * rank), lambda s: (0, 0)),
        out_shape=jax.ShapeDtypeStruct((tok, 2 * rank), jnp.float32),
        compiler_params=MEM,
    )(activations, out_grads, proj_in, proj_out)


def total_kernel(*refs):
    out_ref = refs[-1]
    total = refs[0][...]
    for ref in refs[1:-1]:
        total = total + ref[...]
    out_ref[...] = total.T.astype(out_ref.dtype)


def add_projections(parts):
    tok, width = parts[0].shape
    return pl.pallas_call(
        total_kernel,
        out_shape=jax.ShapeDtypeStruct((width, tok), jnp.bfloat16),
        compiler_params=MEM,
    )(*parts)


def lay_out_factors(factor_refs, weight_refs, factors, weights):
    tok = factor_refs[0].shape[1]
    for k, (factor_ref, weight_ref) in enumerate(zip(factor_refs, weight_refs)):
        factors[:, k * tok : (k + 1) * tok] = factor_ref[...].astype(jnp.float32)
        weights[:, k * tok : (k + 1) * tok] = weight_ref[...]


def range_scale(values):
    top = jnp.max(jnp.abs(values), keepdims=True)
    scale = jnp.ones_like(top)
    for low in (16, 48, 80, 112):
        scale = jnp.where(top > 2.0**low, 2.0 ** -min(low + 16, 126), scale)
        scale = jnp.where(top < 2.0**-low, 2.0 ** min(low + 16, 126), scale)
    return scale


def share_kernel(blocks, row_count, *refs):
    factor_refs, weight_refs = refs[:blocks], refs[blocks : 2 * blocks]
    query_ref = refs[2 * blocks]
    out_refs = refs[2 * blocks + 1 : 3 * blocks + 1]
    factors, weights, features = refs[3 * blocks + 1 :]
    lay_out_factors(factor_refs, weight_refs, factors, weights)
    rank = factors.shape[0] // 2
    tokens = factors.shape[1]
    tok = tokens // blocks
    first = rank + lax.axis_index("dp") * row_count
    act = factors[:rank, :]
    for i in range(row_count):
        row = factors[pl.ds(first + i, 1), :]
        features[i * rank : (i + 1) * rank, :] = (row * act).astype(jnp.bfloat16)
    plain = jnp.dot(query_ref[...], features[...], preferred_element_type=jnp.float32)
    weight = weights[...]
    live = weight > 0.0
    act = jnp.where(live, act, 0.0)
    grad = jnp.where(live, factors[rank:, :], 0.0)
    act_scale, grad_scale = range_scale(act), range_scale(grad)
    act, grad = act * act_scale, grad * grad_scale
    norms = jnp.sum(act * act, axis=0, keepdims=True) * jnp.sum(grad * grad, axis=0, keepdims=True)
    level = jnp.sum(weight * norms, axis=1, keepdims=True) / (tokens * rank * rank)
    step = 1.1 * level
    act_b, grad_b = act.astype(jnp.bfloat16), grad.astype(jnp.bfloat16)
    gram = jnp.dot(act.T.astype(jnp.bfloat16), act_b, preferred_element_type=jnp.float32) * jnp.dot(
        grad.T.astype(jnp.bfloat16), grad_b, preferred_element_type=jnp.float32
    )
    gram = (gram * (1.0 / (tokens * step))).astype(jnp.bfloat16)
    image = jnp.dot((plain * weight).astype(jnp.bfloat16), gram, preferred_element_type=jnp.float32)
    scale = act_scale * grad_scale
    share = ((2.0 - 0.1 / 1.1) * plain - image) * scale * (scale / step)
    for k, out_ref in enumerate(out_refs):
        out_ref[...] = share[:, k * tok : (k + 1) * tok].astype(jnp.bfloat16)


def score_shares(factors, weights, queries_t, row_count):
    blocks = len(factors)
    width, tok = factors[0].shape
    rows = queries_t.shape[1]
    out = jax.ShapeDtypeStruct((queries_t.shape[0], tok), jnp.bfloat16)
    return pl.pallas_call(
        functools.partial(share_kernel, blocks, row_count),
        out_shape=[out] * blocks,
        scratch_shapes=[
            pltpu.VMEM((width, tok * blocks), jnp.float32),
            pltpu.VMEM((1, tok * blocks), jnp.float32),
            pltpu.VMEM((rows, tok * blocks), jnp.bfloat16),
        ],
        compiler_params=MEM,
    )(*factors, *weights, queries_t)


def hessian_kernel(blocks, row_count, col_count, *refs):
    factor_refs, weight_refs = refs[:blocks], refs[blocks : 2 * blocks]
    out_ref, factors, weights, weighted, right = refs[2 * blocks :]
    rank = factors.shape[0] // 2
    tokens = factors.shape[1]

    @pl.when(pl.program_id(0) == 0)
    def _():
        lay_out_factors(factor_refs, weight_refs, factors, weights)
        first = rank + lax.axis_index("dp") * row_count
        act, weight = factors[:rank, :], weights[...]
        for i in range(row_count):
            left = (factors[pl.ds(first + i, 1), :] * act).astype(jnp.bfloat16)
            left = (weight * left.astype(jnp.float32)).astype(jnp.bfloat16)
            weighted[i * rank : (i + 1) * rank, :] = left

    act = factors[:rank, :]
    first = rank + pl.program_id(0) * col_count
    for i in range(col_count):
        row = factors[pl.ds(first + i, 1), :]
        right[i * rank : (i + 1) * rank, :] = (row * act).astype(jnp.bfloat16)
    block = lax.dot_general(weighted[...], right[...], NT, preferred_element_type=jnp.float32)
    out_ref[...] = block / tokens


def hessian_rows(factors, weights, row_count, col_count=8):
    blocks = len(factors)
    width, tok = factors[0].shape
    rank = width // 2
    feat = rank * rank
    rows, cols = row_count * rank, col_count * rank
    return pl.pallas_call(
        functools.partial(hessian_kernel, blocks, row_count, col_count),
        grid=(feat // cols,),
        in_specs=[pl.BlockSpec((width, tok), lambda s: (0, 0))] * blocks
        + [pl.BlockSpec((1, tok), lambda s: (0, 0))] * blocks,
        out_specs=pl.BlockSpec((rows, cols), lambda s: (0, s)),
        out_shape=jax.ShapeDtypeStruct((rows, feat), jnp.float32),
        scratch_shapes=[
            pltpu.VMEM((width, tok * blocks), jnp.float32),
            pltpu.VMEM((1, tok * blocks), jnp.float32),
            pltpu.VMEM((rows, tok * blocks), jnp.bfloat16),
            pltpu.VMEM((cols, tok * blocks), jnp.bfloat16),
        ],
        compiler_params=MEM,
    )(*factors, *weights)


def finish_kernel(*refs):
    weight_ref, out_ref = refs[-2], refs[-1]
    total = refs[0][...].astype(jnp.float32)
    for ref in refs[1:-2]:
        total = total + ref[...].astype(jnp.float32)
    total = jnp.where(weight_ref[...] > 0.0, total, 0.0)
    out_ref[...] = total.T.astype(out_ref.dtype)


def finish_scores(shares, weight):
    count, tok = shares[0].shape
    return pl.pallas_call(
        finish_kernel,
        out_shape=jax.ShapeDtypeStruct((tok, count), jnp.bfloat16),
        compiler_params=MEM,
    )(*shares, weight)


def shifted(array, axis, by):
    count = lax.axis_size(axis)
    return lax.ppermute(array, axis, [(i, (i + by) % count) for i in range(count)])


def from_all(array, axis):
    return [array] + [shifted(array, axis, k) for k in range(1, lax.axis_size(axis))]


def few_tokens(activations, out_grads, proj_in, proj_out, queries, lengths, credit):
    tok_rows = activations.shape[0]
    seq_len = tok_rows // lengths.shape[0]
    dp_count = lax.axis_size("dp")
    rank = proj_in.shape[1]
    row_count = rank // dp_count
    live = jnp.arange(seq_len, dtype=jnp.int32)[None, :] < lengths[:, None]
    weight = (credit[:, None].astype(jnp.float32) * live.astype(jnp.float32)).reshape(1, -1)
    weights = from_all(weight, "dp")
    part = project(activations, out_grads, proj_in, proj_out)
    factors = from_all(add_projections(from_all(part, "query")), "dp")
    shares = score_shares(factors, weights, queries.T, row_count)
    arrived = [shares[0]] + [shifted(shares[k], "dp", -k) for k in range(1, dp_count)]
    hessian = hessian_rows(factors, weights, row_count)
    return hessian, finish_scores(arrived, weight)


def per_device(activations, *others):
    rank = others[1].shape[1]
    if activations.shape[0] * lax.axis_size("dp") > rank * rank:
        return many_tokens(activations, *others)
    return few_tokens(activations, *others)


def solution(mesh):
    placed = (
        P(("groups", "dp"), "query"),
        P(("groups", "dp"), "query"),
        P("query", None),
        P("query", None),
        P(("groups", "dp"), "query"),
        P(("groups", "dp")),
        P(("groups", "dp")),
    )
    return jax.shard_map(
        per_device,
        mesh=mesh,
        in_specs=placed,
        out_specs=(P(("groups", "dp"), None), P(("groups", "dp"), "query")),
        check_vma=False,
    )
```

```python
import functools
import jax
import jax.numpy as jnp
from jax import lax
from jax.experimental import pallas as pl
from jax.experimental.pallas import tpu as pltpu
from jax.sharding import PartitionSpec as P


def kron_columns(grad_rows, act_rows, start, count):
    rank = grad_rows.shape[1]
    tokens_here = grad_rows.shape[0]
    grad_cols = lax.dynamic_slice_in_dim(grad_rows, start // rank, count // rank, 1)
    outer = grad_cols.astype(jnp.float32)[:, :, None] * act_rows.astype(jnp.float32)[:, None, :]
    return outer.reshape(tokens_here, count).astype(jnp.bfloat16)


def hessian_block(total, pieces, row_start, rows_own, col_start, col_count):
    grad_rows, act_rows, weights = pieces
    left = kron_columns(grad_rows, act_rows, row_start, rows_own)
    weighted = (weights.astype(jnp.float32)[:, None] * left.astype(jnp.float32)).astype(
        jnp.bfloat16
    )
    right = kron_columns(grad_rows, act_rows, col_start, col_count)
    return total + lax.dot_general(
        weighted, right, (((0,), (0,)), ((), ())), preferred_element_type=jnp.float32
    )


def fold_blocks(total, pieces, step_fn):
    count = pieces[0].shape[0]
    shaped = tuple((p.reshape((count // 512, 512) + p.shape[1:]) for p in pieces))

    def inner(carry, block):
        return (step_fn(carry, block), None)

    return lax.scan(inner, total, shaped)[0]


def split_parts(matrix):
    high_part = matrix.astype(jnp.bfloat16)
    first_rest = matrix - high_part.astype(jnp.float32)
    middle_part = first_rest.astype(jnp.bfloat16)
    low_part = (first_rest - middle_part.astype(jnp.float32)).astype(jnp.bfloat16)
    return (high_part, middle_part, low_part)


def many_tokens(activations, out_grads, proj_in, proj_out, queries, lengths, credit):
    tok_rows = activations.shape[0]
    seq_len = tok_rows // lengths.shape[0]
    dp_count = lax.axis_size("dp")
    query_count = lax.axis_size("query")
    dp_index = lax.axis_index("dp")
    query_index = lax.axis_index("query")
    part_act = jnp.dot(activations, proj_in, preferred_element_type=jnp.float32)
    part_grad = jnp.dot(out_grads, proj_out, preferred_element_type=jnp.float32)
    sum_act, sum_grad = lax.psum((part_act, part_grad), "query")
    act_proj = sum_act.astype(jnp.bfloat16)
    grad_proj = sum_grad.astype(jnp.bfloat16)
    rank = act_proj.shape[1]
    feat = rank * rank
    live = jnp.arange(seq_len, dtype=jnp.int32)[None, :] < lengths[:, None]
    weight = (credit[:, None].astype(jnp.float32) * live.astype(jnp.float32)).reshape(-1)
    mask = live.astype(jnp.float32).reshape(-1)
    weight_wire = weight.astype(jnp.bfloat16)
    rows_own = feat // dp_count
    row_start = dp_index * rows_own
    all_tokens = tok_rows * dp_count
    col_count = feat // query_count
    col_start = query_index * col_count
    owned = fold_blocks(
        jnp.zeros((rows_own, col_count), jnp.float32),
        (
            lax.all_gather(grad_proj, "dp", axis=0, tiled=True),
            lax.all_gather(act_proj, "dp", axis=0, tiled=True),
            lax.all_gather(weight_wire, "dp", axis=0, tiled=True),
        ),
        lambda carry, block: hessian_block(carry, block, row_start, rows_own, col_start, col_count),
    )
    hessian = lax.all_gather(owned, "query", axis=1, tiled=True) / all_tokens
    diagonal_block = lax.dynamic_slice_in_dim(hessian, row_start, rows_own, 1)
    level = lax.psum(jnp.trace(diagonal_block), "dp") / feat
    step = 1.1 * level
    high_part, middle_part, low_part = split_parts(hessian)
    piece = lax.all_gather(queries, "dp", axis=0, tiled=True)
    result = jnp.zeros(queries.shape, jnp.float32)
    for part_matrix in (low_part, middle_part, high_part):
        columns = part_matrix
        result = result + jnp.dot(columns, piece, preferred_element_type=jnp.float32)
    query_f = queries.astype(jnp.float32)
    precond = ((2.0 * query_f - (result + 0.1 * level * query_f) / step) / step).astype(
        jnp.bfloat16
    )
    local_features = kron_columns(grad_proj, act_proj, 0, feat)
    piece = lax.all_gather(precond, "dp", axis=0, tiled=True)
    columns = lax.slice_in_dim(local_features, 0, piece.shape[0], axis=1)
    scores = jnp.zeros((tok_rows, precond.shape[1]), jnp.float32) + jnp.dot(
        columns, piece, preferred_element_type=jnp.float32
    )
    return (hessian, (scores * mask[:, None]).astype(jnp.bfloat16))


MIB = 1024 * 1024
NT = (((1,), (1,)), ((), ()))
TN = (((0,), (0,)), ((), ()))


def params(mib):
    return pltpu.CompilerParams(vmem_limit_bytes=mib * MIB)


def project_kernel(act, grad, pin, pout, out_ref, act_v, grad_v, pin_v, pout_v, sems):
    chunk = act.shape[1] // 2
    copies, jobs = [], []
    for source, weight, source_v, weight_v, is_grad in (
        (grad, pout, grad_v, pout_v, 1),
        (act, pin, act_v, pin_v, 0),
    ):
        for c in range(source.shape[1] // chunk):
            span = pl.ds(c * chunk, chunk)
            n = len(copies)
            pair = [
                pltpu.make_async_copy(weight.at[:, span], weight_v.at[:, span], sems.at[n]),
                pltpu.make_async_copy(source.at[:, span], source_v.at[:, span], sems.at[n + 1]),
            ]
            for copy in pair:
                copy.start()
            copies += pair
            jobs.append((pair, weight_v, source_v, span, is_grad))
    rank = pin.shape[0]
    totals = [jnp.zeros((rank, act.shape[0]), jnp.float32) for _ in range(2)]
    for pair, weight_v, source_v, span, is_grad in jobs:
        for copy in pair:
            copy.wait()
        totals[is_grad] += lax.dot_general(
            weight_v[:, span], source_v[:, span], NT, preferred_element_type=jnp.float32
        )
    rows = out_ref.shape[1]
    for q in range(out_ref.shape[0]):
        total = totals[q * rows // rank]
        start = q * rows % rank
        out_ref[q] = total[start : start + rows]


def project(activations, out_grads, proj_in_t, proj_out_t, parts):
    tok, d_here = activations.shape
    f_here = out_grads.shape[1]
    rank = proj_in_t.shape[0]
    copies = 2 * (2 + 2 * f_here // d_here)
    return pl.pallas_call(
        project_kernel,
        in_specs=[pl.BlockSpec(memory_space=pl.ANY)] * 4,
        out_shape=jax.ShapeDtypeStruct((parts, 2 * rank // parts, tok), jnp.float32),
        scratch_shapes=[
            pltpu.VMEM((tok, d_here), jnp.bfloat16),
            pltpu.VMEM((tok, f_here), jnp.bfloat16),
            pltpu.VMEM((rank, d_here), jnp.bfloat16),
            pltpu.VMEM((rank, f_here), jnp.bfloat16),
            pltpu.SemaphoreType.DMA((copies,)),
        ],
        compiler_params=params(60),
    )(activations, out_grads, proj_in_t, proj_out_t)


def total_kernel(part_ref, weight_ref, out_ref):
    rows = part_ref.shape[1]
    total = part_ref[0]
    for q in range(1, part_ref.shape[0]):
        total = total + part_ref[q]
    weight = jnp.broadcast_to(weight_ref[...], (out_ref.shape[1] - rows, weight_ref.shape[1]))
    payload = jnp.concatenate([total, weight], axis=0).astype(out_ref.dtype)
    for k in range(out_ref.shape[0]):
        out_ref[k] = payload


def add_projections(parts, weight, copies):
    _, rows, tok = parts.shape
    return pl.pallas_call(
        total_kernel,
        out_shape=jax.ShapeDtypeStruct((copies, rows + 16, tok), jnp.bfloat16),
        compiler_params=params(48),
    )(parts, weight)


def lay_out_factors(gathered, blocks, factors, weights):
    per_block = gathered.shape[0] // blocks
    tok = gathered.shape[2]
    rows = factors.shape[0] // per_block
    for k in range(blocks):
        source = lax.rem(lax.axis_index("dp") + blocks - k, blocks) * per_block
        span = slice(k * tok, (k + 1) * tok)
        for q in range(per_block):
            part = gathered[source + q]
            factors[q * rows : (q + 1) * rows, span] = part[:rows].astype(jnp.float32)
            if q == 0:
                weights[:, span] = part[rows:].astype(jnp.float32)[:1]


def range_scale(values):
    top = jnp.max(jnp.abs(values), keepdims=True)
    scale = jnp.ones_like(top)
    for low in (16, 48, 80, 112):
        scale = jnp.where(top > 2.0**low, 2.0 ** -min(low + 16, 126), scale)
        scale = jnp.where(top < 2.0**-low, 2.0 ** min(low + 16, 126), scale)
    return scale


def share_kernel(blocks, row_count, gathered, query_ref, *refs):
    out_refs = refs[:blocks]
    factors, weights, features, query_v, sem = refs[blocks:]
    fetch = pltpu.make_async_copy(query_ref, query_v, sem)
    fetch.start()
    lay_out_factors(gathered, blocks, factors, weights)
    rank = factors.shape[0] // 2
    tokens = factors.shape[1]
    tok = tokens // blocks
    first = rank + lax.axis_index("dp") * row_count
    act = factors[:rank, :]
    for i in range(row_count):
        row = factors[pl.ds(first + i, 1), :]
        features[i * rank : (i + 1) * rank, :] = (row * act).astype(jnp.bfloat16)
    fetch.wait()
    plain = lax.dot_general(query_v[...], features[...], TN, preferred_element_type=jnp.float32)
    weight = weights[...]
    live = weight > 0.0
    act = jnp.where(live, act, 0.0)
    grad = jnp.where(live, factors[rank:, :], 0.0)
    act_scale, grad_scale = range_scale(act), range_scale(grad)
    act, grad = act * act_scale, grad * grad_scale
    norms = jnp.sum(act * act, axis=0, keepdims=True) * jnp.sum(grad * grad, axis=0, keepdims=True)
    level = jnp.sum(weight * norms, axis=1, keepdims=True) / (tokens * rank * rank)
    step = 1.1 * level
    act_b, grad_b = act.astype(jnp.bfloat16), grad.astype(jnp.bfloat16)
    gram = jnp.dot(act.T.astype(jnp.bfloat16), act_b, preferred_element_type=jnp.float32) * jnp.dot(
        grad.T.astype(jnp.bfloat16), grad_b, preferred_element_type=jnp.float32
    )
    gram = (gram * (1.0 / (tokens * step))).astype(jnp.bfloat16)
    image = jnp.dot((plain * weight).astype(jnp.bfloat16), gram, preferred_element_type=jnp.float32)
    scale = act_scale * grad_scale
    share = ((2.0 - 0.1 / 1.1) * plain - image) * scale * (scale / step)
    for k, out_ref in enumerate(out_refs):
        out_ref[...] = share[:, k * tok : (k + 1) * tok].astype(jnp.bfloat16)


def score_shares(gathered, queries, blocks, rank, row_count):
    tok = gathered.shape[2]
    rows, count = queries.shape
    out = jax.ShapeDtypeStruct((count, tok), jnp.bfloat16)
    return pl.pallas_call(
        functools.partial(share_kernel, blocks, row_count),
        in_specs=[pl.BlockSpec(memory_space=pltpu.VMEM), pl.BlockSpec(memory_space=pl.ANY)],
        out_shape=[out] * blocks,
        scratch_shapes=[
            pltpu.VMEM((2 * rank, tok * blocks), jnp.float32),
            pltpu.VMEM((1, tok * blocks), jnp.float32),
            pltpu.VMEM((rows, tok * blocks), jnp.bfloat16),
            pltpu.VMEM(queries.shape, queries.dtype),
            pltpu.SemaphoreType.DMA,
        ],
        compiler_params=params(60),
    )(gathered, queries)


def hessian_kernel(blocks, row_count, col_count, gathered, out_ref, factors, weights, weighted, right):
    rank = factors.shape[0] // 2
    tokens = factors.shape[1]

    @pl.when(pl.program_id(0) == 0)
    def _():
        lay_out_factors(gathered, blocks, factors, weights)
        first = rank + lax.axis_index("dp") * row_count
        act, weight = factors[:rank, :], weights[...]
        for i in range(row_count):
            left = (factors[pl.ds(first + i, 1), :] * act).astype(jnp.bfloat16)
            left = (weight * left.astype(jnp.float32)).astype(jnp.bfloat16)
            weighted[i * rank : (i + 1) * rank, :] = left

    act = factors[:rank, :]
    first = rank + pl.program_id(0) * col_count
    for i in range(col_count):
        row = factors[pl.ds(first + i, 1), :]
        right[i * rank : (i + 1) * rank, :] = (row * act).astype(jnp.bfloat16)
    block = lax.dot_general(weighted[...], right[...], NT, preferred_element_type=jnp.float32)
    out_ref[...] = block / tokens


def hessian_rows(gathered, blocks, rank, row_count, col_count=8):
    tok = gathered.shape[2]
    feat = rank * rank
    rows, cols = row_count * rank, col_count * rank
    return pl.pallas_call(
        functools.partial(hessian_kernel, blocks, row_count, col_count),
        grid=(feat // cols,),
        in_specs=[pl.BlockSpec(gathered.shape, lambda s: (0, 0, 0))],
        out_specs=pl.BlockSpec((rows, cols), lambda s: (0, s)),
        out_shape=jax.ShapeDtypeStruct((rows, feat), jnp.float32),
        scratch_shapes=[
            pltpu.VMEM((2 * rank, tok * blocks), jnp.float32),
            pltpu.VMEM((1, tok * blocks), jnp.float32),
            pltpu.VMEM((rows, tok * blocks), jnp.bfloat16),
            pltpu.VMEM((cols, tok * blocks), jnp.bfloat16),
        ],
        compiler_params=params(48),
    )(gathered)


def finish_kernel(*refs):
    weight_ref, out_ref = refs[-2], refs[-1]
    total = refs[0][...].astype(jnp.float32)
    for ref in refs[1:-2]:
        total = total + ref[...].astype(jnp.float32)
    total = jnp.where(weight_ref[...] > 0.0, total, 0.0)
    out_ref[...] = total.T.astype(out_ref.dtype)


def finish_scores(shares, weight):
    count, tok = shares[0].shape
    return pl.pallas_call(
        finish_kernel,
        out_shape=jax.ShapeDtypeStruct((tok, count), jnp.bfloat16),
        compiler_params=params(48),
    )(*shares, weight)


def shifted(array, axis, by):
    count = lax.axis_size(axis)
    return lax.ppermute(array, axis, [(i, (i + by) % count) for i in range(count)])


def few_tokens(activations, out_grads, proj_in, proj_out, queries, lengths, credit):
    tok_rows = activations.shape[0]
    seq_len = tok_rows // lengths.shape[0]
    dp_count = lax.axis_size("dp")
    query_count = lax.axis_size("query")
    rank = proj_in.shape[1]
    row_count = rank // dp_count
    live = jnp.arange(seq_len, dtype=jnp.int32)[None, :] < lengths[:, None]
    weight = (credit[:, None].astype(jnp.float32) * live.astype(jnp.float32)).reshape(1, -1)
    parts = project(activations, out_grads, proj_in.T, proj_out.T, query_count)
    parts = lax.all_to_all(parts, "query", 0, 0, tiled=True)
    payloads = add_projections(parts, weight, dp_count * query_count)
    gathered = lax.all_to_all(payloads, ("dp", "query"), 0, 0, tiled=True)
    shares = score_shares(gathered, queries, dp_count, rank, row_count)
    arrived = [shares[0]] + [shifted(shares[k], "dp", -k) for k in range(1, dp_count)]
    hessian = hessian_rows(gathered, dp_count, rank, row_count)
    return hessian, finish_scores(arrived, weight)


def per_device(activations, *others):
    rank = others[1].shape[1]
    if activations.shape[0] * lax.axis_size("dp") > rank * rank:
        return many_tokens(activations, *others)
    return few_tokens(activations, *others)


def solution(mesh):
    placed = (
        P(("groups", "dp"), "query"),
        P(("groups", "dp"), "query"),
        P("query", None),
        P("query", None),
        P(("groups", "dp"), "query"),
        P(("groups", "dp")),
        P(("groups", "dp")),
    )
    return jax.shard_map(
        per_device,
        mesh=mesh,
        in_specs=placed,
        out_specs=(P(("groups", "dp"), None), P(("groups", "dp"), "query")),
        check_vma=False,
    )
```

```python
import functools
import jax
import jax.numpy as jnp
from jax import lax
from jax.experimental import pallas as pl
from jax.experimental.pallas import tpu as pltpu
from jax.sharding import PartitionSpec as P


def kron_columns(grad_rows, act_rows, start, count):
    rank = grad_rows.shape[1]
    tokens_here = grad_rows.shape[0]
    grad_cols = lax.dynamic_slice_in_dim(grad_rows, start // rank, count // rank, 1)
    outer = grad_cols.astype(jnp.float32)[:, :, None] * act_rows.astype(jnp.float32)[:, None, :]
    return outer.reshape(tokens_here, count).astype(jnp.bfloat16)


def hessian_block(total, pieces, row_start, rows_own, col_start, col_count):
    grad_rows, act_rows, weights = pieces
    left = kron_columns(grad_rows, act_rows, row_start, rows_own)
    weighted = (weights.astype(jnp.float32)[:, None] * left.astype(jnp.float32)).astype(
        jnp.bfloat16
    )
    right = kron_columns(grad_rows, act_rows, col_start, col_count)
    return total + lax.dot_general(
        weighted, right, (((0,), (0,)), ((), ())), preferred_element_type=jnp.float32
    )


def fold_blocks(total, pieces, step_fn):
    count = pieces[0].shape[0]
    shaped = tuple((p.reshape((count // 512, 512) + p.shape[1:]) for p in pieces))

    def inner(carry, block):
        return (step_fn(carry, block), None)

    return lax.scan(inner, total, shaped)[0]


def split_parts(matrix):
    high_part = matrix.astype(jnp.bfloat16)
    first_rest = matrix - high_part.astype(jnp.float32)
    middle_part = first_rest.astype(jnp.bfloat16)
    low_part = (first_rest - middle_part.astype(jnp.float32)).astype(jnp.bfloat16)
    return (high_part, middle_part, low_part)


def many_tokens(activations, out_grads, proj_in, proj_out, queries, lengths, credit):
    tok_rows = activations.shape[0]
    seq_len = tok_rows // lengths.shape[0]
    dp_count = lax.axis_size("dp")
    query_count = lax.axis_size("query")
    dp_index = lax.axis_index("dp")
    query_index = lax.axis_index("query")
    part_act = jnp.dot(activations, proj_in, preferred_element_type=jnp.float32)
    part_grad = jnp.dot(out_grads, proj_out, preferred_element_type=jnp.float32)
    sum_act, sum_grad = lax.psum((part_act, part_grad), "query")
    act_proj = sum_act.astype(jnp.bfloat16)
    grad_proj = sum_grad.astype(jnp.bfloat16)
    rank = act_proj.shape[1]
    feat = rank * rank
    live = jnp.arange(seq_len, dtype=jnp.int32)[None, :] < lengths[:, None]
    weight = (credit[:, None].astype(jnp.float32) * live.astype(jnp.float32)).reshape(-1)
    mask = live.astype(jnp.float32).reshape(-1)
    weight_wire = weight.astype(jnp.bfloat16)
    rows_own = feat // dp_count
    row_start = dp_index * rows_own
    all_tokens = tok_rows * dp_count
    col_count = feat // query_count
    col_start = query_index * col_count
    owned = fold_blocks(
        jnp.zeros((rows_own, col_count), jnp.float32),
        (
            lax.all_gather(grad_proj, "dp", axis=0, tiled=True),
            lax.all_gather(act_proj, "dp", axis=0, tiled=True),
            lax.all_gather(weight_wire, "dp", axis=0, tiled=True),
        ),
        lambda carry, block: hessian_block(carry, block, row_start, rows_own, col_start, col_count),
    )
    hessian = lax.all_gather(owned, "query", axis=1, tiled=True) / all_tokens
    diagonal_block = lax.dynamic_slice_in_dim(hessian, row_start, rows_own, 1)
    level = lax.psum(jnp.trace(diagonal_block), "dp") / feat
    step = 1.1 * level
    high_part, middle_part, low_part = split_parts(hessian)
    piece = lax.all_gather(queries, "dp", axis=0, tiled=True)
    result = jnp.zeros(queries.shape, jnp.float32)
    for part_matrix in (low_part, middle_part, high_part):
        columns = part_matrix
        result = result + jnp.dot(columns, piece, preferred_element_type=jnp.float32)
    query_f = queries.astype(jnp.float32)
    precond = ((2.0 * query_f - (result + 0.1 * level * query_f) / step) / step).astype(
        jnp.bfloat16
    )
    local_features = kron_columns(grad_proj, act_proj, 0, feat)
    piece = lax.all_gather(precond, "dp", axis=0, tiled=True)
    columns = lax.slice_in_dim(local_features, 0, piece.shape[0], axis=1)
    scores = jnp.zeros((tok_rows, precond.shape[1]), jnp.float32) + jnp.dot(
        columns, piece, preferred_element_type=jnp.float32
    )
    return (hessian, (scores * mask[:, None]).astype(jnp.bfloat16))


MIB = 1024 * 1024
NT = (((1,), (1,)), ((), ()))


def params(mib):
    return pltpu.CompilerParams(vmem_limit_bytes=int(mib * MIB))


def project_kernel(act, grad, pin, pout, keep_ref, send_ref, act_v, grad_v, pin_v, pout_v, sems):
    chunk = act.shape[1]
    while grad.shape[1] % chunk:
        chunk //= 2
    spans = [pl.ds(c, chunk) for c in range(0, grad.shape[1], chunk)]
    copies = [pltpu.make_async_copy(s, d, sems.at[n]) for n, (s, d) in enumerate(((pin, pin_v), (act, act_v), (pout, pout_v)))]
    copies += [
        pltpu.make_async_copy(grad.at[:, span], grad_v.at[:, span], sems.at[3 + n])
        for n, span in enumerate(spans)
    ]
    for copy in copies:
        copy.start()
    copies[0].wait()
    copies[1].wait()
    part_act = lax.dot_general(pin_v[...], act_v[...], NT, preferred_element_type=jnp.float32)
    copies[2].wait()
    part_grad = jnp.zeros_like(part_act)
    for copy, span in zip(copies[3:], spans):
        copy.wait()
        part_grad += lax.dot_general(
            pout_v[:, span], grad_v[:, span], NT, preferred_element_type=jnp.float32
        )
    even = lax.rem(lax.axis_index("query"), 2) == 0
    keep_ref[...] = jnp.where(even, part_act, part_grad)
    send_ref[...] = jnp.where(even, part_grad, part_act)


def project(activations, out_grads, proj_in_t, proj_out_t):
    tok, d_here = activations.shape
    f_here = out_grads.shape[1]
    rank = proj_in_t.shape[0]
    out = jax.ShapeDtypeStruct((rank, tok), jnp.float32)
    return pl.pallas_call(
        project_kernel,
        in_specs=[pl.BlockSpec(memory_space=pl.ANY)] * 4,
        out_shape=[out, out],
        scratch_shapes=[
            pltpu.VMEM((tok, d_here), jnp.bfloat16),
            pltpu.VMEM((tok, f_here), jnp.bfloat16),
            pltpu.VMEM((rank, d_here), jnp.bfloat16),
            pltpu.VMEM((rank, f_here), jnp.bfloat16),
            pltpu.SemaphoreType.DMA((3 + f_here // 128,)),
        ],
        compiler_params=params(53.75),
    )(activations, out_grads, proj_in_t, proj_out_t)


def add_kernel(one_ref, other_ref, out_ref):
    out_ref[...] = one_ref[...] + other_ref[...]


def add(one, other):
    return pl.pallas_call(
        add_kernel,
        out_shape=jax.ShapeDtypeStruct(one.shape, one.dtype),
        compiler_params=params(40),
    )(one, other)


def payload_kernel(one_ref, other_ref, weight_ref, out_ref):
    total = one_ref[...] + other_ref[...]
    weight = jnp.broadcast_to(weight_ref[...], (16, weight_ref.shape[1]))
    out_ref[...] = jnp.concatenate([total, weight], axis=0).astype(out_ref.dtype)


def add_to_payload(one, other, weight):
    rows, tok = one.shape
    return pl.pallas_call(
        payload_kernel,
        out_shape=jax.ShapeDtypeStruct((rows + 16, tok), jnp.bfloat16),
        compiler_params=params(40),
    )(one, other, weight)


def stack_kernel(*refs):
    for k, ref in enumerate(refs[:-1]):
        refs[-1][k] = ref[...]


def stack(parts):
    return pl.pallas_call(
        stack_kernel,
        out_shape=jax.ShapeDtypeStruct((len(parts),) + parts[0].shape, parts[0].dtype),
        compiler_params=params(40),
    )(*parts)


def lay_out_factors(mine, other, factors, weights):
    blocks, _, tok = mine.shape
    rank = factors.shape[0] // 2
    here = pl.multiple_of(lax.rem(lax.axis_index("query"), 2) * rank, rank)
    there = pl.multiple_of(rank - here, rank)
    for k in range(blocks):
        span = slice(k * tok, (k + 1) * tok)
        factors[pl.ds(here, rank), span] = mine[k, :rank].astype(jnp.float32)
        factors[pl.ds(there, rank), span] = other[k, :rank].astype(jnp.float32)
        weights[:, span] = mine[k, rank:].astype(jnp.float32)[:1]


def range_scale(values):
    top = jnp.max(jnp.abs(values), keepdims=True)
    scale = jnp.ones_like(top)
    for low in (16, 48, 80, 112):
        scale = jnp.where(top > 2.0**low, 2.0 ** -min(low + 16, 126), scale)
        scale = jnp.where(top < 2.0**-low, 2.0 ** min(low + 16, 126), scale)
    return scale


def share_kernel(row_count, mine, other, query_ref, *refs):
    factors, weights, features = refs[-3:]
    out_refs = refs[:-3]
    lay_out_factors(mine, other, factors, weights)
    rank = factors.shape[0] // 2
    tokens = factors.shape[1]
    tok = tokens // len(out_refs)
    first = rank + lax.axis_index("dp") * row_count
    act = factors[:rank, :]
    for i in range(row_count):
        row = factors[pl.ds(first + i, 1), :]
        features[i * rank : (i + 1) * rank, :] = (row * act).astype(jnp.bfloat16)
    plain = jnp.dot(query_ref[...], features[...], preferred_element_type=jnp.float32)
    weight = weights[...]
    live = weight > 0.0
    act = jnp.where(live, act, 0.0)
    grad = jnp.where(live, factors[rank:, :], 0.0)
    act_scale, grad_scale = range_scale(act), range_scale(grad)
    act, grad = act * act_scale, grad * grad_scale
    norms = jnp.sum(act * act, axis=0, keepdims=True) * jnp.sum(grad * grad, axis=0, keepdims=True)
    level = jnp.sum(weight * norms, axis=1, keepdims=True) / (tokens * rank * rank)
    step = 1.1 * level
    act_b, grad_b = act.astype(jnp.bfloat16), grad.astype(jnp.bfloat16)
    gram = jnp.dot(act.T.astype(jnp.bfloat16), act_b, preferred_element_type=jnp.float32) * jnp.dot(
        grad.T.astype(jnp.bfloat16), grad_b, preferred_element_type=jnp.float32
    )
    gram = (gram * (1.0 / (tokens * step))).astype(jnp.bfloat16)
    image = jnp.dot((plain * weight).astype(jnp.bfloat16), gram, preferred_element_type=jnp.float32)
    scale = act_scale * grad_scale
    share = ((2.0 - 0.1 / 1.1) * plain - image) * scale * (scale / step)
    for k, out_ref in enumerate(out_refs):
        out_ref[...] = share[:, k * tok : (k + 1) * tok].astype(jnp.bfloat16)


def score_shares(mine, other, queries_t, rank, row_count):
    blocks, _, tok = mine.shape
    count, rows = queries_t.shape
    out = jax.ShapeDtypeStruct((count, tok), jnp.bfloat16)
    return pl.pallas_call(
        functools.partial(share_kernel, row_count),
        out_shape=[out] * blocks,
        scratch_shapes=[
            pltpu.VMEM((2 * rank, tok * blocks), jnp.float32),
            pltpu.VMEM((1, tok * blocks), jnp.float32),
            pltpu.VMEM((rows, tok * blocks), jnp.bfloat16),
        ],
        compiler_params=params(40),
    )(mine, other, queries_t)


def hessian_kernel(row_count, col_count, mine, other, out, factors, weights, weighted, *scratch):
    rights, results, sems = scratch[:2], scratch[2:4], scratch[4]
    rank = factors.shape[0] // 2
    tokens = factors.shape[1]
    cols = col_count * rank
    steps = rank // col_count
    lay_out_factors(mine, other, factors, weights)
    act, weight = factors[:rank, :], weights[...]
    first = rank + lax.axis_index("dp") * row_count
    for i in range(row_count):
        left = (factors[pl.ds(first + i, 1), :] * act).astype(jnp.bfloat16)
        left = (weight * left.astype(jnp.float32)).astype(jnp.bfloat16)
        weighted[i * rank : (i + 1) * rank, :] = left

    def build(step):
        for i in range(col_count):
            row = rank + step * col_count + i
            right = (factors[row : row + 1, :] * act).astype(jnp.bfloat16)
            rights[step % 2][i * rank : (i + 1) * rank, :] = right

    def store(step):
        return pltpu.make_async_copy(
            results[step % 2], out.at[:, pl.ds(step * cols, cols)], sems.at[step % 2]
        )

    build(0)
    for step in range(steps):
        if step + 1 < steps:
            build(step + 1)
        if step > 1:
            store(step - 2).wait()
        block = lax.dot_general(
            weighted[...], rights[step % 2][...], NT, preferred_element_type=jnp.float32
        )
        results[step % 2][...] = block * (1.0 / tokens)
        store(step).start()
    for step in range(max(steps - 2, 0), steps):
        store(step).wait()


def hessian_rows(mine, other, rank, row_count, col_count=8):
    blocks, _, tok = mine.shape
    feat = rank * rank
    rows, cols = row_count * rank, col_count * rank
    return pl.pallas_call(
        functools.partial(hessian_kernel, row_count, col_count),
        out_specs=pl.BlockSpec(memory_space=pl.ANY),
        out_shape=jax.ShapeDtypeStruct((rows, feat), jnp.float32),
        scratch_shapes=[
            pltpu.VMEM((2 * rank, tok * blocks), jnp.float32),
            pltpu.VMEM((1, tok * blocks), jnp.float32),
            pltpu.VMEM((rows, tok * blocks), jnp.bfloat16),
            pltpu.VMEM((cols, tok * blocks), jnp.bfloat16),
            pltpu.VMEM((cols, tok * blocks), jnp.bfloat16),
            pltpu.VMEM((rows, cols), jnp.float32),
            pltpu.VMEM((rows, cols), jnp.float32),
            pltpu.SemaphoreType.DMA((2,)),
        ],
        compiler_params=params(40),
    )(mine, other)


def finish_kernel(*refs):
    weight_ref, out_ref = refs[-2], refs[-1]
    total = refs[0][...].astype(jnp.float32)
    for ref in refs[1:-2]:
        total = total + ref[...].astype(jnp.float32)
    total = jnp.where(weight_ref[...] > 0.0, total, 0.0)
    out_ref[...] = total.T.astype(out_ref.dtype)


def finish_scores(shares, weight):
    count, tok = shares[0].shape
    return pl.pallas_call(
        finish_kernel,
        out_shape=jax.ShapeDtypeStruct((tok, count), jnp.bfloat16),
        compiler_params=params(40),
    )(*shares, weight)


def swapped(array, axis, distance):
    return lax.ppermute(array, axis, [(i, i ^ distance) for i in range(lax.axis_size(axis))])


def few_tokens(activations, out_grads, proj_in, proj_out, queries, lengths, credit):
    tok_rows = activations.shape[0]
    seq_len = tok_rows // lengths.shape[0]
    dp_count = lax.axis_size("dp")
    query_count = lax.axis_size("query")
    rank = proj_in.shape[1]
    row_count = rank // dp_count
    live = jnp.arange(seq_len, dtype=jnp.int32)[None, :] < lengths[:, None]
    weight = (credit[:, None].astype(jnp.float32) * live.astype(jnp.float32)).reshape(1, -1)
    keep, send = project(activations, out_grads, proj_in.T, proj_out.T)
    other = swapped(send, "query", 1)
    distance = 2
    while distance < query_count:
        keep = add(keep, other)
        other = swapped(keep, "query", distance)
        distance *= 2
    payload = add_to_payload(keep, other, weight)
    others = [swapped(payload, "dp", k) for k in reversed(range(1, dp_count))]
    mine = stack([payload] + others[::-1])
    other = swapped(mine, "query", 1)
    shares = score_shares(mine, other, queries.T, rank, row_count)
    arrived = [swapped(shares[k], "dp", k) for k in reversed(range(1, dp_count))]
    hessian = hessian_rows(mine, other, rank, row_count)
    return hessian, finish_scores([shares[0]] + arrived, weight)


def power_of_two(count):
    return count & (count - 1) == 0


def per_device(activations, *others):
    rank = others[1].shape[1]
    dp_count, query_count = lax.axis_size("dp"), lax.axis_size("query")
    pairs = query_count > 1 and power_of_two(query_count) and power_of_two(dp_count)
    if pairs and activations.shape[0] * dp_count <= rank * rank:
        return few_tokens(activations, *others)
    return many_tokens(activations, *others)


def solution(mesh):
    placed = (
        P(("groups", "dp"), "query"),
        P(("groups", "dp"), "query"),
        P("query", None),
        P("query", None),
        P(("groups", "dp"), "query"),
        P(("groups", "dp")),
        P(("groups", "dp")),
    )
    return jax.shard_map(
        per_device,
        mesh=mesh,
        in_specs=placed,
        out_specs=(P(("groups", "dp"), None), P(("groups", "dp"), "query")),
        check_vma=False,
    )
```

```python
import functools
import jax
import jax.numpy as jnp
from jax import lax
from jax.experimental import pallas as pl
from jax.experimental.pallas import tpu as pltpu
from jax.sharding import PartitionSpec as P


def kron_columns(grad_rows, act_rows, start, count):
    rank = grad_rows.shape[1]
    tokens_here = grad_rows.shape[0]
    grad_cols = lax.dynamic_slice_in_dim(grad_rows, start // rank, count // rank, 1)
    outer = grad_cols.astype(jnp.float32)[:, :, None] * act_rows.astype(jnp.float32)[:, None, :]
    return outer.reshape(tokens_here, count).astype(jnp.bfloat16)


def hessian_block(total, pieces, row_start, rows_own, col_start, col_count):
    grad_rows, act_rows, weights = pieces
    left = kron_columns(grad_rows, act_rows, row_start, rows_own)
    weighted = (weights.astype(jnp.float32)[:, None] * left.astype(jnp.float32)).astype(
        jnp.bfloat16
    )
    right = kron_columns(grad_rows, act_rows, col_start, col_count)
    return total + lax.dot_general(
        weighted, right, (((0,), (0,)), ((), ())), preferred_element_type=jnp.float32
    )


def fold_blocks(total, pieces, step_fn):
    count = pieces[0].shape[0]
    shaped = tuple((p.reshape((count // 512, 512) + p.shape[1:]) for p in pieces))

    def inner(carry, block):
        return (step_fn(carry, block), None)

    return lax.scan(inner, total, shaped)[0]


def split_parts(matrix):
    high_part = matrix.astype(jnp.bfloat16)
    first_rest = matrix - high_part.astype(jnp.float32)
    middle_part = first_rest.astype(jnp.bfloat16)
    low_part = (first_rest - middle_part.astype(jnp.float32)).astype(jnp.bfloat16)
    return (high_part, middle_part, low_part)


def many_tokens(activations, out_grads, proj_in, proj_out, queries, lengths, credit):
    tok_rows = activations.shape[0]
    seq_len = tok_rows // lengths.shape[0]
    dp_count = lax.axis_size("dp")
    query_count = lax.axis_size("query")
    dp_index = lax.axis_index("dp")
    query_index = lax.axis_index("query")
    part_act = jnp.dot(activations, proj_in, preferred_element_type=jnp.float32)
    part_grad = jnp.dot(out_grads, proj_out, preferred_element_type=jnp.float32)
    sum_act, sum_grad = lax.psum((part_act, part_grad), "query")
    act_proj = sum_act.astype(jnp.bfloat16)
    grad_proj = sum_grad.astype(jnp.bfloat16)
    rank = act_proj.shape[1]
    feat = rank * rank
    live = jnp.arange(seq_len, dtype=jnp.int32)[None, :] < lengths[:, None]
    weight = (credit[:, None].astype(jnp.float32) * live.astype(jnp.float32)).reshape(-1)
    mask = live.astype(jnp.float32).reshape(-1)
    weight_wire = weight.astype(jnp.bfloat16)
    rows_own = feat // dp_count
    row_start = dp_index * rows_own
    all_tokens = tok_rows * dp_count
    col_count = feat // query_count
    col_start = query_index * col_count
    owned = fold_blocks(
        jnp.zeros((rows_own, col_count), jnp.float32),
        (
            lax.all_gather(grad_proj, "dp", axis=0, tiled=True),
            lax.all_gather(act_proj, "dp", axis=0, tiled=True),
            lax.all_gather(weight_wire, "dp", axis=0, tiled=True),
        ),
        lambda carry, block: hessian_block(carry, block, row_start, rows_own, col_start, col_count),
    )
    hessian = lax.all_gather(owned, "query", axis=1, tiled=True) / all_tokens
    diagonal_block = lax.dynamic_slice_in_dim(hessian, row_start, rows_own, 1)
    level = lax.psum(jnp.trace(diagonal_block), "dp") / feat
    step = 1.1 * level
    high_part, middle_part, low_part = split_parts(hessian)
    piece = lax.all_gather(queries, "dp", axis=0, tiled=True)
    result = jnp.zeros(queries.shape, jnp.float32)
    for part_matrix in (low_part, middle_part, high_part):
        columns = part_matrix
        result = result + jnp.dot(columns, piece, preferred_element_type=jnp.float32)
    query_f = queries.astype(jnp.float32)
    precond = ((2.0 * query_f - (result + 0.1 * level * query_f) / step) / step).astype(
        jnp.bfloat16
    )
    local_features = kron_columns(grad_proj, act_proj, 0, feat)
    piece = lax.all_gather(precond, "dp", axis=0, tiled=True)
    columns = lax.slice_in_dim(local_features, 0, piece.shape[0], axis=1)
    scores = jnp.zeros((tok_rows, precond.shape[1]), jnp.float32) + jnp.dot(
        columns, piece, preferred_element_type=jnp.float32
    )
    return (hessian, (scores * mask[:, None]).astype(jnp.bfloat16))


MIB = 1024 * 1024
NT = (((1,), (1,)), ((), ()))


def params(mib):
    return pltpu.CompilerParams(vmem_limit_bytes=int(mib * MIB))


def project_kernel(act, grad, pin, pout, keep_ref, send_ref, act_v, grad_v, pin_v, pout_v, sems):
    chunk = act.shape[1]
    while grad.shape[1] % chunk:
        chunk //= 2
    spans = [pl.ds(c, chunk) for c in range(0, grad.shape[1], chunk)]
    copies = [pltpu.make_async_copy(s, d, sems.at[n]) for n, (s, d) in enumerate(((pin, pin_v), (act, act_v), (pout, pout_v)))]
    copies += [
        pltpu.make_async_copy(grad.at[:, span], grad_v.at[:, span], sems.at[3 + n])
        for n, span in enumerate(spans)
    ]
    for copy in copies:
        copy.start()
    copies[0].wait()
    copies[1].wait()
    part_act = lax.dot_general(pin_v[...], act_v[...], NT, preferred_element_type=jnp.float32)
    copies[2].wait()
    part_grad = jnp.zeros_like(part_act)
    for copy, span in zip(copies[3:], spans):
        copy.wait()
        part_grad += lax.dot_general(
            pout_v[:, span], grad_v[:, span], NT, preferred_element_type=jnp.float32
        )
    even = lax.rem(lax.axis_index("query"), 2) == 0
    keep_ref[...] = jnp.where(even, part_act, part_grad)
    send_ref[...] = jnp.where(even, part_grad, part_act)


def project(activations, out_grads, proj_in_t, proj_out_t):
    tok, d_here = activations.shape
    f_here = out_grads.shape[1]
    rank = proj_in_t.shape[0]
    out = jax.ShapeDtypeStruct((rank, tok), jnp.float32)
    return pl.pallas_call(
        project_kernel,
        in_specs=[pl.BlockSpec(memory_space=pl.ANY)] * 4,
        out_shape=[out, out],
        scratch_shapes=[
            pltpu.VMEM((tok, d_here), jnp.bfloat16),
            pltpu.VMEM((tok, f_here), jnp.bfloat16),
            pltpu.VMEM((rank, d_here), jnp.bfloat16),
            pltpu.VMEM((rank, f_here), jnp.bfloat16),
            pltpu.SemaphoreType.DMA((3 + f_here // 128,)),
        ],
        compiler_params=params(53.75),
    )(activations, out_grads, proj_in_t, proj_out_t)


def add_kernel(one_ref, other_ref, out_ref):
    out_ref[...] = one_ref[...] + other_ref[...]


def add(one, other):
    return pl.pallas_call(
        add_kernel,
        out_shape=jax.ShapeDtypeStruct(one.shape, one.dtype),
        compiler_params=params(40),
    )(one, other)


def payload_kernel(one_ref, other_ref, weight_ref, out_ref):
    total = one_ref[...] + other_ref[...]
    weight = jnp.broadcast_to(weight_ref[...], (16, weight_ref.shape[1]))
    out_ref[...] = jnp.concatenate([total, weight], axis=0).astype(out_ref.dtype)


def add_to_payload(one, other, weight):
    rows, tok = one.shape
    return pl.pallas_call(
        payload_kernel,
        out_shape=jax.ShapeDtypeStruct((rows + 16, tok), jnp.bfloat16),
        compiler_params=params(40),
    )(one, other, weight)


def stack_kernel(*refs):
    for k, ref in enumerate(refs[:-1]):
        refs[-1][k] = ref[...]


def stack(parts):
    return pl.pallas_call(
        stack_kernel,
        out_shape=jax.ShapeDtypeStruct((len(parts),) + parts[0].shape, parts[0].dtype),
        compiler_params=params(40),
    )(*parts)


def lay_out_factors(mine, other, factors, weights):
    blocks, _, tok = mine.shape
    rank = factors.shape[0] // 2
    here = pl.multiple_of(lax.rem(lax.axis_index("query"), 2) * rank, rank)
    there = pl.multiple_of(rank - here, rank)
    for k in range(blocks):
        span = slice(k * tok, (k + 1) * tok)
        factors[pl.ds(here, rank), span] = mine[k, :rank].astype(jnp.float32)
        factors[pl.ds(there, rank), span] = other[k, :rank].astype(jnp.float32)
        weights[:, span] = mine[k, rank:].astype(jnp.float32)[:1]


def range_scale(values):
    top = jnp.max(jnp.abs(values), keepdims=True)
    scale = jnp.ones_like(top)
    for low in (16, 48, 80, 112):
        scale = jnp.where(top > 2.0**low, 2.0 ** -min(low + 16, 126), scale)
        scale = jnp.where(top < 2.0**-low, 2.0 ** min(low + 16, 126), scale)
    return scale


def share_kernel(row_count, mine, other, query_ref, *refs):
    factors, weights, features = refs[-3:]
    out_refs = refs[:-3]
    lay_out_factors(mine, other, factors, weights)
    rank = factors.shape[0] // 2
    tokens = factors.shape[1]
    tok = tokens // len(out_refs)
    first = rank + lax.axis_index("dp") * row_count
    act = factors[:rank, :]
    for i in range(row_count):
        row = factors[pl.ds(first + i, 1), :]
        features[i * rank : (i + 1) * rank, :] = (row * act).astype(jnp.bfloat16)
    plain = jnp.dot(query_ref[...], features[...], preferred_element_type=jnp.float32)
    weight = weights[...]
    live = weight > 0.0
    act = jnp.where(live, act, 0.0)
    grad = jnp.where(live, factors[rank:, :], 0.0)
    act_scale, grad_scale = range_scale(act), range_scale(grad)
    act, grad = act * act_scale, grad * grad_scale
    norms = jnp.sum(act * act, axis=0, keepdims=True) * jnp.sum(grad * grad, axis=0, keepdims=True)
    level = jnp.sum(weight * norms, axis=1, keepdims=True) / (tokens * rank * rank)
    step = 1.1 * level
    act_b, grad_b = act.astype(jnp.bfloat16), grad.astype(jnp.bfloat16)
    gram = jnp.dot(act.T.astype(jnp.bfloat16), act_b, preferred_element_type=jnp.float32) * jnp.dot(
        grad.T.astype(jnp.bfloat16), grad_b, preferred_element_type=jnp.float32
    )
    gram = (gram * (1.0 / (tokens * step))).astype(jnp.bfloat16)
    image = jnp.dot((plain * weight).astype(jnp.bfloat16), gram, preferred_element_type=jnp.float32)
    scale = act_scale * grad_scale
    share = ((2.0 - 0.1 / 1.1) * plain - image) * scale * (scale / step)
    for k, out_ref in enumerate(out_refs):
        out_ref[...] = share[:, k * tok : (k + 1) * tok].astype(jnp.bfloat16)


def score_shares(mine, other, queries_t, rank, row_count):
    blocks, _, tok = mine.shape
    count, rows = queries_t.shape
    out = jax.ShapeDtypeStruct((count, tok), jnp.bfloat16)
    return pl.pallas_call(
        functools.partial(share_kernel, row_count),
        out_shape=[out] * blocks,
        scratch_shapes=[
            pltpu.VMEM((2 * rank, tok * blocks), jnp.float32),
            pltpu.VMEM((1, tok * blocks), jnp.float32),
            pltpu.VMEM((rows, tok * blocks), jnp.bfloat16),
        ],
        compiler_params=params(40),
    )(mine, other, queries_t)


def hessian_kernel(row_count, col_count, mine, other, out, factors, weights, weighted, *scratch):
    rights, results, sems = scratch[:2], scratch[2:4], scratch[4]
    rank = factors.shape[0] // 2
    tokens = factors.shape[1]
    cols = col_count * rank
    steps = rank // col_count
    lay_out_factors(mine, other, factors, weights)
    act, weight = factors[:rank, :], weights[...]
    first = rank + lax.axis_index("dp") * row_count
    for i in range(row_count):
        left = (factors[pl.ds(first + i, 1), :] * act).astype(jnp.bfloat16)
        left = (weight * left.astype(jnp.float32)).astype(jnp.bfloat16)
        weighted[i * rank : (i + 1) * rank, :] = left
    act_rows = jnp.concatenate([act, act], axis=0).T
    grad_rows = factors[rank:, :].T.astype(jnp.bfloat16)
    spread_row = lax.broadcasted_iota(jnp.int32, (rank, cols), 0)
    spread_col = lax.broadcasted_iota(jnp.int32, (rank, cols), 1) // rank

    def build(step):
        spread = jnp.where(spread_row == spread_col + step * col_count, 1.0, 0.0)
        grad = jnp.dot(grad_rows, spread.astype(jnp.bfloat16), preferred_element_type=jnp.float32)
        for i in range(0, cols, 2 * rank):
            span = slice(i, i + 2 * rank)
            rights[step % 2][:, span] = (grad[:, span] * act_rows).astype(jnp.bfloat16)

    def store(step):
        return pltpu.make_async_copy(
            results[step % 2], out.at[:, pl.ds(step * cols, cols)], sems.at[step % 2]
        )

    build(0)
    for step in range(steps):
        if step + 1 < steps:
            build(step + 1)
        if step > 1:
            store(step - 2).wait()
        block = jnp.dot(
            weighted[...], rights[step % 2][...], preferred_element_type=jnp.float32
        )
        results[step % 2][...] = block * (1.0 / tokens)
        store(step).start()
    for step in range(max(steps - 2, 0), steps):
        store(step).wait()


def hessian_rows(mine, other, rank, row_count, col_count=8):
    blocks, _, tok = mine.shape
    feat = rank * rank
    rows, cols = row_count * rank, col_count * rank
    return pl.pallas_call(
        functools.partial(hessian_kernel, row_count, col_count),
        out_specs=pl.BlockSpec(memory_space=pl.ANY),
        out_shape=jax.ShapeDtypeStruct((rows, feat), jnp.float32),
        scratch_shapes=[
            pltpu.VMEM((2 * rank, tok * blocks), jnp.float32),
            pltpu.VMEM((1, tok * blocks), jnp.float32),
            pltpu.VMEM((rows, tok * blocks), jnp.bfloat16),
            pltpu.VMEM((tok * blocks, cols), jnp.bfloat16),
            pltpu.VMEM((tok * blocks, cols), jnp.bfloat16),
            pltpu.VMEM((rows, cols), jnp.float32),
            pltpu.VMEM((rows, cols), jnp.float32),
            pltpu.SemaphoreType.DMA((2,)),
        ],
        compiler_params=params(40),
    )(mine, other)


def finish_kernel(*refs):
    weight_ref, out_ref = refs[-2], refs[-1]
    total = refs[0][...].astype(jnp.float32)
    for ref in refs[1:-2]:
        total = total + ref[...].astype(jnp.float32)
    total = jnp.where(weight_ref[...] > 0.0, total, 0.0)
    out_ref[...] = total.T.astype(out_ref.dtype)


def finish_scores(shares, weight):
    count, tok = shares[0].shape
    return pl.pallas_call(
        finish_kernel,
        out_shape=jax.ShapeDtypeStruct((tok, count), jnp.bfloat16),
        compiler_params=params(40),
    )(*shares, weight)


def swapped(array, axis, distance):
    return lax.ppermute(array, axis, [(i, i ^ distance) for i in range(lax.axis_size(axis))])


def few_tokens(activations, out_grads, proj_in, proj_out, queries, lengths, credit):
    tok_rows = activations.shape[0]
    seq_len = tok_rows // lengths.shape[0]
    dp_count = lax.axis_size("dp")
    query_count = lax.axis_size("query")
    rank = proj_in.shape[1]
    row_count = rank // dp_count
    live = jnp.arange(seq_len, dtype=jnp.int32)[None, :] < lengths[:, None]
    weight = (credit[:, None].astype(jnp.float32) * live.astype(jnp.float32)).reshape(1, -1)
    keep, send = project(activations, out_grads, proj_in.T, proj_out.T)
    other = swapped(send, "query", 1)
    distance = 2
    while distance < query_count:
        keep = add(keep, other)
        other = swapped(keep, "query", distance)
        distance *= 2
    payload = add_to_payload(keep, other, weight)
    others = [swapped(payload, "dp", k) for k in reversed(range(1, dp_count))]
    mine = stack([payload] + others[::-1])
    other = swapped(mine, "query", 1)
    shares = score_shares(mine, other, queries.T, rank, row_count)
    arrived = [swapped(shares[k], "dp", k) for k in reversed(range(1, dp_count))]
    hessian = hessian_rows(mine, other, rank, row_count)
    return hessian, finish_scores([shares[0]] + arrived, weight)


def power_of_two(count):
    return count & (count - 1) == 0


def per_device(activations, *others):
    rank = others[1].shape[1]
    dp_count, query_count = lax.axis_size("dp"), lax.axis_size("query")
    pairs = query_count > 1 and power_of_two(query_count) and power_of_two(dp_count)
    if pairs and activations.shape[0] * dp_count <= rank * rank:
        return few_tokens(activations, *others)
    return many_tokens(activations, *others)


def solution(mesh):
    placed = (
        P(("groups", "dp"), "query"),
        P(("groups", "dp"), "query"),
        P("query", None),
        P("query", None),
        P(("groups", "dp"), "query"),
        P(("groups", "dp")),
        P(("groups", "dp")),
    )
    return jax.shard_map(
        per_device,
        mesh=mesh,
        in_specs=placed,
        out_specs=(P(("groups", "dp"), None), P(("groups", "dp"), "query")),
        check_vma=False,
    )
```

```python
import functools
import jax
import jax.numpy as jnp
from jax import lax
from jax.experimental import pallas as pl
from jax.experimental.pallas import tpu as pltpu
from jax.sharding import PartitionSpec as P


def kron_columns(grad_rows, act_rows, start, count):
    rank = grad_rows.shape[1]
    tokens_here = grad_rows.shape[0]
    grad_cols = lax.dynamic_slice_in_dim(grad_rows, start // rank, count // rank, 1)
    outer = grad_cols.astype(jnp.float32)[:, :, None] * act_rows.astype(jnp.float32)[:, None, :]
    return outer.reshape(tokens_here, count).astype(jnp.bfloat16)


def hessian_block(total, pieces, row_start, rows_own, col_start, col_count):
    grad_rows, act_rows, weights = pieces
    left = kron_columns(grad_rows, act_rows, row_start, rows_own)
    weighted = (weights.astype(jnp.float32)[:, None] * left.astype(jnp.float32)).astype(
        jnp.bfloat16
    )
    right = kron_columns(grad_rows, act_rows, col_start, col_count)
    return total + lax.dot_general(
        weighted, right, (((0,), (0,)), ((), ())), preferred_element_type=jnp.float32
    )


def fold_blocks(total, pieces, step_fn):
    count = pieces[0].shape[0]
    shaped = tuple((p.reshape((count // 512, 512) + p.shape[1:]) for p in pieces))

    def inner(carry, block):
        return (step_fn(carry, block), None)

    return lax.scan(inner, total, shaped)[0]


def split_parts(matrix):
    high_part = matrix.astype(jnp.bfloat16)
    first_rest = matrix - high_part.astype(jnp.float32)
    middle_part = first_rest.astype(jnp.bfloat16)
    low_part = (first_rest - middle_part.astype(jnp.float32)).astype(jnp.bfloat16)
    return (high_part, middle_part, low_part)


def many_tokens(activations, out_grads, proj_in, proj_out, queries, lengths, credit):
    tok_rows = activations.shape[0]
    seq_len = tok_rows // lengths.shape[0]
    dp_count = lax.axis_size("dp")
    query_count = lax.axis_size("query")
    dp_index = lax.axis_index("dp")
    query_index = lax.axis_index("query")
    part_act = jnp.dot(activations, proj_in, preferred_element_type=jnp.float32)
    part_grad = jnp.dot(out_grads, proj_out, preferred_element_type=jnp.float32)
    sum_act, sum_grad = lax.psum((part_act, part_grad), "query")
    act_proj = sum_act.astype(jnp.bfloat16)
    grad_proj = sum_grad.astype(jnp.bfloat16)
    rank = act_proj.shape[1]
    feat = rank * rank
    live = jnp.arange(seq_len, dtype=jnp.int32)[None, :] < lengths[:, None]
    weight = (credit[:, None].astype(jnp.float32) * live.astype(jnp.float32)).reshape(-1)
    mask = live.astype(jnp.float32).reshape(-1)
    weight_wire = weight.astype(jnp.bfloat16)
    rows_own = feat // dp_count
    row_start = dp_index * rows_own
    all_tokens = tok_rows * dp_count
    col_count = feat // query_count
    col_start = query_index * col_count
    owned = fold_blocks(
        jnp.zeros((rows_own, col_count), jnp.float32),
        (
            lax.all_gather(grad_proj, "dp", axis=0, tiled=True),
            lax.all_gather(act_proj, "dp", axis=0, tiled=True),
            lax.all_gather(weight_wire, "dp", axis=0, tiled=True),
        ),
        lambda carry, block: hessian_block(carry, block, row_start, rows_own, col_start, col_count),
    )
    hessian = lax.all_gather(owned, "query", axis=1, tiled=True) / all_tokens
    diagonal_block = lax.dynamic_slice_in_dim(hessian, row_start, rows_own, 1)
    level = lax.psum(jnp.trace(diagonal_block), "dp") / feat
    step = 1.1 * level
    high_part, middle_part, low_part = split_parts(hessian)
    piece = lax.all_gather(queries, "dp", axis=0, tiled=True)
    result = jnp.zeros(queries.shape, jnp.float32)
    for part_matrix in (low_part, middle_part, high_part):
        columns = part_matrix
        result = result + jnp.dot(columns, piece, preferred_element_type=jnp.float32)
    query_f = queries.astype(jnp.float32)
    precond = ((2.0 * query_f - (result + 0.1 * level * query_f) / step) / step).astype(
        jnp.bfloat16
    )
    local_features = kron_columns(grad_proj, act_proj, 0, feat)
    piece = lax.all_gather(precond, "dp", axis=0, tiled=True)
    columns = lax.slice_in_dim(local_features, 0, piece.shape[0], axis=1)
    scores = jnp.zeros((tok_rows, precond.shape[1]), jnp.float32) + jnp.dot(
        columns, piece, preferred_element_type=jnp.float32
    )
    return (hessian, (scores * mask[:, None]).astype(jnp.bfloat16))


MIB = 1024 * 1024
TILE = 256
NT = (((1,), (1,)), ((), ()))


def params(mib):
    return pltpu.CompilerParams(vmem_limit_bytes=int(mib * MIB))


def project_kernel(act, grad, pin, pout, keep_ref, send_ref, act_v, grad_v, pin_v, pout_v, sems):
    chunk = act.shape[1]
    while grad.shape[1] % chunk:
        chunk //= 2
    spans = [pl.ds(c, chunk) for c in range(0, grad.shape[1], chunk)]
    copies = [pltpu.make_async_copy(s, d, sems.at[n]) for n, (s, d) in enumerate(((pin, pin_v), (act, act_v), (pout, pout_v)))]
    copies += [
        pltpu.make_async_copy(grad.at[:, span], grad_v.at[:, span], sems.at[3 + n])
        for n, span in enumerate(spans)
    ]
    for copy in copies:
        copy.start()
    copies[0].wait()
    copies[1].wait()
    part_act = lax.dot_general(pin_v[...], act_v[...], NT, preferred_element_type=jnp.float32)
    copies[2].wait()
    part_grad = jnp.zeros_like(part_act)
    for copy, span in zip(copies[3:], spans):
        copy.wait()
        part_grad += lax.dot_general(
            pout_v[:, span], grad_v[:, span], NT, preferred_element_type=jnp.float32
        )
    even = lax.rem(lax.axis_index("query"), 2) == 0
    keep_ref[...] = jnp.where(even, part_act, part_grad)
    send_ref[...] = jnp.where(even, part_grad, part_act)


def project(activations, out_grads, proj_in_t, proj_out_t):
    tok, d_here = activations.shape
    f_here = out_grads.shape[1]
    rank = proj_in_t.shape[0]
    out = jax.ShapeDtypeStruct((rank, tok), jnp.float32)
    return pl.pallas_call(
        project_kernel,
        in_specs=[pl.BlockSpec(memory_space=pl.ANY)] * 4,
        out_shape=[out, out],
        scratch_shapes=[
            pltpu.VMEM((tok, d_here), jnp.bfloat16),
            pltpu.VMEM((tok, f_here), jnp.bfloat16),
            pltpu.VMEM((rank, d_here), jnp.bfloat16),
            pltpu.VMEM((rank, f_here), jnp.bfloat16),
            pltpu.SemaphoreType.DMA((3 + f_here // 128,)),
        ],
        compiler_params=params(53.75),
    )(activations, out_grads, proj_in_t, proj_out_t)


def add_kernel(one_ref, other_ref, out_ref):
    out_ref[...] = one_ref[...] + other_ref[...]


def add(one, other):
    return pl.pallas_call(
        add_kernel,
        out_shape=jax.ShapeDtypeStruct(one.shape, one.dtype),
        compiler_params=params(40),
    )(one, other)


def payload_kernel(one_ref, other_ref, weight_ref, out_ref):
    total = one_ref[...] + other_ref[...]
    weight = jnp.broadcast_to(weight_ref[...], (16, weight_ref.shape[1]))
    out_ref[...] = jnp.concatenate([total, weight], axis=0).astype(out_ref.dtype)


def add_to_payload(one, other, weight):
    rows, tok = one.shape
    return pl.pallas_call(
        payload_kernel,
        out_shape=jax.ShapeDtypeStruct((rows + 16, tok), jnp.bfloat16),
        compiler_params=params(40),
    )(one, other, weight)


def stack_kernel(*refs):
    for k, ref in enumerate(refs[:-1]):
        refs[-1][k] = ref[...]


def stack(parts):
    return pl.pallas_call(
        stack_kernel,
        out_shape=jax.ShapeDtypeStruct((len(parts),) + parts[0].shape, parts[0].dtype),
        compiler_params=params(40),
    )(*parts)


def lay_out_factors(mine, other, factors, weights):
    blocks, _, tok = mine.shape
    rank = factors.shape[0] // 2
    here = pl.multiple_of(lax.rem(lax.axis_index("query"), 2) * rank, rank)
    there = pl.multiple_of(rank - here, rank)
    for k in range(blocks):
        span = slice(k * tok, (k + 1) * tok)
        factors[pl.ds(here, rank), span] = mine[k, :rank].astype(jnp.float32)
        factors[pl.ds(there, rank), span] = other[k, :rank].astype(jnp.float32)
        weights[:, span] = mine[k, rank:].astype(jnp.float32)[:1]


def range_scale(values):
    top = jnp.max(jnp.abs(values), keepdims=True)
    scale = jnp.ones_like(top)
    for low in (16, 48, 80, 112):
        scale = jnp.where(top > 2.0**low, 2.0 ** -min(low + 16, 126), scale)
        scale = jnp.where(top < 2.0**-low, 2.0 ** min(low + 16, 126), scale)
    return scale


def share_kernel(row_count, mine, other, query_ref, *refs):
    factors, weights, features = refs[-3:]
    out_refs = refs[:-3]
    lay_out_factors(mine, other, factors, weights)
    rank = factors.shape[0] // 2
    tokens = factors.shape[1]
    tok = tokens // len(out_refs)
    first = rank + lax.axis_index("dp") * row_count
    act = factors[:rank, :]
    for i in range(row_count):
        row = factors[pl.ds(first + i, 1), :]
        features[i * rank : (i + 1) * rank, :] = (row * act).astype(jnp.bfloat16)
    plain = jnp.dot(query_ref[...], features[...], preferred_element_type=jnp.float32)
    weight = weights[...]
    live = weight > 0.0
    act = jnp.where(live, act, 0.0)
    grad = jnp.where(live, factors[rank:, :], 0.0)
    act_scale, grad_scale = range_scale(act), range_scale(grad)
    act, grad = act * act_scale, grad * grad_scale
    norms = jnp.sum(act * act, axis=0, keepdims=True) * jnp.sum(grad * grad, axis=0, keepdims=True)
    level = jnp.sum(weight * norms, axis=1, keepdims=True) / (tokens * rank * rank)
    step = 1.1 * level
    act_b, grad_b = act.astype(jnp.bfloat16), grad.astype(jnp.bfloat16)
    gram = jnp.dot(act.T.astype(jnp.bfloat16), act_b, preferred_element_type=jnp.float32) * jnp.dot(
        grad.T.astype(jnp.bfloat16), grad_b, preferred_element_type=jnp.float32
    )
    gram = (gram * (1.0 / (tokens * step))).astype(jnp.bfloat16)
    image = jnp.dot((plain * weight).astype(jnp.bfloat16), gram, preferred_element_type=jnp.float32)
    scale = act_scale * grad_scale
    share = ((2.0 - 0.1 / 1.1) * plain - image) * scale * (scale / step)
    for k, out_ref in enumerate(out_refs):
        out_ref[...] = share[:, k * tok : (k + 1) * tok].astype(jnp.bfloat16)


def score_shares(mine, other, queries_t, rank, row_count):
    blocks, _, tok = mine.shape
    count, rows = queries_t.shape
    out = jax.ShapeDtypeStruct((count, tok), jnp.bfloat16)
    return pl.pallas_call(
        functools.partial(share_kernel, row_count),
        out_shape=[out] * blocks,
        scratch_shapes=[
            pltpu.VMEM((2 * rank, tok * blocks), jnp.float32),
            pltpu.VMEM((1, tok * blocks), jnp.float32),
            pltpu.VMEM((rows, tok * blocks), jnp.bfloat16),
        ],
        compiler_params=params(40),
    )(mine, other, queries_t)


def hessian_kernel(row_count, col_count, mine, other, out, factors, weights, weighted, *scratch):
    rights, results, sems = scratch[:2], scratch[2:4], scratch[4]
    rank = factors.shape[0] // 2
    tokens = factors.shape[1]
    rows, cols = row_count * rank, col_count * rank
    steps = rank // col_count
    lay_out_factors(mine, other, factors, weights)
    act, weight = factors[:rank, :], weights[...]
    first = rank + lax.axis_index("dp") * row_count
    for i in range(row_count):
        left = (factors[pl.ds(first + i, 1), :] * act).astype(jnp.bfloat16)
        left = (weight * left.astype(jnp.float32)).astype(jnp.bfloat16)
        weighted[i * rank : (i + 1) * rank, :] = left

    def build(step):
        for i in range(col_count):
            row = rank + step * col_count + i
            right = (factors[row : row + 1, :] * act).astype(jnp.bfloat16)
            rights[step % 2][i * rank : (i + 1) * rank, :] = right

    def store(step):
        return pltpu.make_async_copy(
            results[step % 2], out.at[:, pl.ds(step * cols, cols)], sems.at[step % 2]
        )

    build(0)
    for step in range(steps):
        if step + 1 < steps:
            build(step + 1)
        if step > 1:
            store(step - 2).wait()
        for col in range(0, cols, TILE):
            for row in range(0, rows, TILE):
                tile = lax.dot_general(
                    weighted[row : row + TILE, :],
                    rights[step % 2][col : col + TILE, :],
                    NT,
                    preferred_element_type=jnp.float32,
                )
                results[step % 2][row : row + TILE, col : col + TILE] = tile * (1.0 / tokens)
        store(step).start()
    for step in range(max(steps - 2, 0), steps):
        store(step).wait()


def hessian_rows(mine, other, rank, row_count, col_count=8):
    blocks, _, tok = mine.shape
    feat = rank * rank
    rows, cols = row_count * rank, col_count * rank
    return pl.pallas_call(
        functools.partial(hessian_kernel, row_count, col_count),
        out_specs=pl.BlockSpec(memory_space=pl.ANY),
        out_shape=jax.ShapeDtypeStruct((rows, feat), jnp.float32),
        scratch_shapes=[
            pltpu.VMEM((2 * rank, tok * blocks), jnp.float32),
            pltpu.VMEM((1, tok * blocks), jnp.float32),
            pltpu.VMEM((rows, tok * blocks), jnp.bfloat16),
            pltpu.VMEM((cols, tok * blocks), jnp.bfloat16),
            pltpu.VMEM((cols, tok * blocks), jnp.bfloat16),
            pltpu.VMEM((rows, cols), jnp.float32),
            pltpu.VMEM((rows, cols), jnp.float32),
            pltpu.SemaphoreType.DMA((2,)),
        ],
        compiler_params=params(40),
    )(mine, other)


def finish_kernel(*refs):
    weight_ref, out_ref = refs[-2], refs[-1]
    total = refs[0][...].astype(jnp.float32)
    for ref in refs[1:-2]:
        total = total + ref[...].astype(jnp.float32)
    total = jnp.where(weight_ref[...] > 0.0, total, 0.0)
    out_ref[...] = total.T.astype(out_ref.dtype)


def finish_scores(shares, weight):
    count, tok = shares[0].shape
    return pl.pallas_call(
        finish_kernel,
        out_shape=jax.ShapeDtypeStruct((tok, count), jnp.bfloat16),
        compiler_params=params(40),
    )(*shares, weight)


def swapped(array, axis, distance):
    return lax.ppermute(array, axis, [(i, i ^ distance) for i in range(lax.axis_size(axis))])


def few_tokens(activations, out_grads, proj_in, proj_out, queries, lengths, credit):
    tok_rows = activations.shape[0]
    seq_len = tok_rows // lengths.shape[0]
    dp_count = lax.axis_size("dp")
    query_count = lax.axis_size("query")
    rank = proj_in.shape[1]
    row_count = rank // dp_count
    live = jnp.arange(seq_len, dtype=jnp.int32)[None, :] < lengths[:, None]
    weight = (credit[:, None].astype(jnp.float32) * live.astype(jnp.float32)).reshape(1, -1)
    keep, send = project(activations, out_grads, proj_in.T, proj_out.T)
    other = swapped(send, "query", 1)
    distance = 2
    while distance < query_count:
        keep = add(keep, other)
        other = swapped(keep, "query", distance)
        distance *= 2
    payload = add_to_payload(keep, other, weight)
    others = [swapped(payload, "dp", k) for k in reversed(range(1, dp_count))]
    mine = stack([payload] + others[::-1])
    other = swapped(mine, "query", 1)
    shares = score_shares(mine, other, queries.T, rank, row_count)
    arrived = [swapped(shares[k], "dp", k) for k in reversed(range(1, dp_count))]
    hessian = hessian_rows(mine, other, rank, row_count)
    return hessian, finish_scores([shares[0]] + arrived, weight)


def power_of_two(count):
    return count & (count - 1) == 0


def per_device(activations, *others):
    rank = others[1].shape[1]
    dp_count, query_count = lax.axis_size("dp"), lax.axis_size("query")
    pairs = query_count > 1 and power_of_two(query_count) and power_of_two(dp_count)
    if pairs and activations.shape[0] * dp_count <= rank * rank:
        return few_tokens(activations, *others)
    return many_tokens(activations, *others)


def solution(mesh):
    placed = (
        P(("groups", "dp"), "query"),
        P(("groups", "dp"), "query"),
        P("query", None),
        P("query", None),
        P(("groups", "dp"), "query"),
        P(("groups", "dp")),
        P(("groups", "dp")),
    )
    return jax.shard_map(
        per_device,
        mesh=mesh,
        in_specs=placed,
        out_specs=(P(("groups", "dp"), None), P(("groups", "dp"), "query")),
        check_vma=False,
    )
```

```python
import functools
import jax
import jax.numpy as jnp
from jax import lax
from jax.experimental import pallas as pl
from jax.experimental.pallas import tpu as pltpu
from jax.sharding import PartitionSpec as P


def kron_columns(grad_rows, act_rows, start, count):
    rank = grad_rows.shape[1]
    tokens_here = grad_rows.shape[0]
    grad_cols = lax.dynamic_slice_in_dim(grad_rows, start // rank, count // rank, 1)
    outer = grad_cols.astype(jnp.float32)[:, :, None] * act_rows.astype(jnp.float32)[:, None, :]
    return outer.reshape(tokens_here, count).astype(jnp.bfloat16)


def hessian_block(total, pieces, row_start, rows_own, col_start, col_count):
    grad_rows, act_rows, weights = pieces
    left = kron_columns(grad_rows, act_rows, row_start, rows_own)
    weighted = (weights.astype(jnp.float32)[:, None] * left.astype(jnp.float32)).astype(
        jnp.bfloat16
    )
    right = kron_columns(grad_rows, act_rows, col_start, col_count)
    return total + lax.dot_general(
        weighted, right, (((0,), (0,)), ((), ())), preferred_element_type=jnp.float32
    )


def fold_blocks(total, pieces, step_fn):
    count = pieces[0].shape[0]
    shaped = tuple((p.reshape((count // 512, 512) + p.shape[1:]) for p in pieces))

    def inner(carry, block):
        return (step_fn(carry, block), None)

    return lax.scan(inner, total, shaped)[0]


def split_parts(matrix):
    high_part = matrix.astype(jnp.bfloat16)
    first_rest = matrix - high_part.astype(jnp.float32)
    middle_part = first_rest.astype(jnp.bfloat16)
    low_part = (first_rest - middle_part.astype(jnp.float32)).astype(jnp.bfloat16)
    return (high_part, middle_part, low_part)


def many_tokens(activations, out_grads, proj_in, proj_out, queries, lengths, credit):
    tok_rows = activations.shape[0]
    seq_len = tok_rows // lengths.shape[0]
    dp_count = lax.axis_size("dp")
    query_count = lax.axis_size("query")
    dp_index = lax.axis_index("dp")
    query_index = lax.axis_index("query")
    part_act = jnp.dot(activations, proj_in, preferred_element_type=jnp.float32)
    part_grad = jnp.dot(out_grads, proj_out, preferred_element_type=jnp.float32)
    sum_act, sum_grad = lax.psum((part_act, part_grad), "query")
    act_proj = sum_act.astype(jnp.bfloat16)
    grad_proj = sum_grad.astype(jnp.bfloat16)
    rank = act_proj.shape[1]
    feat = rank * rank
    live = jnp.arange(seq_len, dtype=jnp.int32)[None, :] < lengths[:, None]
    weight = (credit[:, None].astype(jnp.float32) * live.astype(jnp.float32)).reshape(-1)
    mask = live.astype(jnp.float32).reshape(-1)
    weight_wire = weight.astype(jnp.bfloat16)
    rows_own = feat // dp_count
    row_start = dp_index * rows_own
    all_tokens = tok_rows * dp_count
    col_count = feat // query_count
    col_start = query_index * col_count
    owned = fold_blocks(
        jnp.zeros((rows_own, col_count), jnp.float32),
        (
            lax.all_gather(grad_proj, "dp", axis=0, tiled=True),
            lax.all_gather(act_proj, "dp", axis=0, tiled=True),
            lax.all_gather(weight_wire, "dp", axis=0, tiled=True),
        ),
        lambda carry, block: hessian_block(carry, block, row_start, rows_own, col_start, col_count),
    )
    hessian = lax.all_gather(owned, "query", axis=1, tiled=True) / all_tokens
    diagonal_block = lax.dynamic_slice_in_dim(hessian, row_start, rows_own, 1)
    level = lax.psum(jnp.trace(diagonal_block), "dp") / feat
    step = 1.1 * level
    high_part, middle_part, low_part = split_parts(hessian)
    piece = lax.all_gather(queries, "dp", axis=0, tiled=True)
    result = jnp.zeros(queries.shape, jnp.float32)
    for part_matrix in (low_part, middle_part, high_part):
        columns = part_matrix
        result = result + jnp.dot(columns, piece, preferred_element_type=jnp.float32)
    query_f = queries.astype(jnp.float32)
    precond = ((2.0 * query_f - (result + 0.1 * level * query_f) / step) / step).astype(
        jnp.bfloat16
    )
    local_features = kron_columns(grad_proj, act_proj, 0, feat)
    piece = lax.all_gather(precond, "dp", axis=0, tiled=True)
    columns = lax.slice_in_dim(local_features, 0, piece.shape[0], axis=1)
    scores = jnp.zeros((tok_rows, precond.shape[1]), jnp.float32) + jnp.dot(
        columns, piece, preferred_element_type=jnp.float32
    )
    return (hessian, (scores * mask[:, None]).astype(jnp.bfloat16))


MIB = 1024 * 1024
TILE = 256
NT = (((1,), (1,)), ((), ()))


def params(mib):
    return pltpu.CompilerParams(vmem_limit_bytes=int(mib * MIB))


def project_kernel(act, grad, pin, pout, keep_ref, send_ref, act_v, grad_v, pin_v, pout_v, sems):
    chunk = act.shape[1]
    while grad.shape[1] % chunk:
        chunk //= 2
    spans = [pl.ds(c, chunk) for c in range(0, grad.shape[1], chunk)]
    copies = [pltpu.make_async_copy(s, d, sems.at[n]) for n, (s, d) in enumerate(((pin, pin_v), (act, act_v), (pout, pout_v)))]
    copies += [
        pltpu.make_async_copy(grad.at[:, span], grad_v.at[:, span], sems.at[3 + n])
        for n, span in enumerate(spans)
    ]
    for copy in copies:
        copy.start()
    copies[0].wait()
    copies[1].wait()
    part_act = lax.dot_general(pin_v[...], act_v[...], NT, preferred_element_type=jnp.float32)
    copies[2].wait()
    part_grad = jnp.zeros_like(part_act)
    for copy, span in zip(copies[3:], spans):
        copy.wait()
        part_grad += lax.dot_general(
            pout_v[:, span], grad_v[:, span], NT, preferred_element_type=jnp.float32
        )
    even = lax.rem(lax.axis_index("query"), 2) == 0
    keep_ref[...] = jnp.where(even, part_act, part_grad)
    send_ref[...] = jnp.where(even, part_grad, part_act)


def project(activations, out_grads, proj_in_t, proj_out_t):
    tok, d_here = activations.shape
    f_here = out_grads.shape[1]
    rank = proj_in_t.shape[0]
    out = jax.ShapeDtypeStruct((rank, tok), jnp.float32)
    return pl.pallas_call(
        project_kernel,
        in_specs=[pl.BlockSpec(memory_space=pl.ANY)] * 4,
        out_shape=[out, out],
        scratch_shapes=[
            pltpu.VMEM((tok, d_here), jnp.bfloat16),
            pltpu.VMEM((tok, f_here), jnp.bfloat16),
            pltpu.VMEM((rank, d_here), jnp.bfloat16),
            pltpu.VMEM((rank, f_here), jnp.bfloat16),
            pltpu.SemaphoreType.DMA((3 + f_here // 128,)),
        ],
        compiler_params=params(53.75),
    )(activations, out_grads, proj_in_t, proj_out_t)


def add_kernel(one_ref, other_ref, out_ref):
    out_ref[...] = one_ref[...] + other_ref[...]


def add(one, other):
    return pl.pallas_call(
        add_kernel,
        out_shape=jax.ShapeDtypeStruct(one.shape, one.dtype),
        compiler_params=params(40),
    )(one, other)


def payload_kernel(one_ref, other_ref, weight_ref, out_ref):
    total = one_ref[...] + other_ref[...]
    weight = jnp.broadcast_to(weight_ref[...], (16, weight_ref.shape[1]))
    out_ref[...] = jnp.concatenate([total, weight], axis=0).astype(out_ref.dtype)


def add_to_payload(one, other, weight):
    rows, tok = one.shape
    return pl.pallas_call(
        payload_kernel,
        out_shape=jax.ShapeDtypeStruct((rows + 16, tok), jnp.bfloat16),
        compiler_params=params(40),
    )(one, other, weight)


def stack_kernel(*refs):
    for k, ref in enumerate(refs[:-1]):
        refs[-1][k] = ref[...]


def stack(parts):
    return pl.pallas_call(
        stack_kernel,
        out_shape=jax.ShapeDtypeStruct((len(parts),) + parts[0].shape, parts[0].dtype),
        compiler_params=params(40),
    )(*parts)


def lay_out_factors(mine, other, factors, weights):
    blocks, _, tok = mine.shape
    rank = factors.shape[0] // 2
    here = pl.multiple_of(lax.rem(lax.axis_index("query"), 2) * rank, rank)
    there = pl.multiple_of(rank - here, rank)
    for k in range(blocks):
        span = slice(k * tok, (k + 1) * tok)
        factors[pl.ds(here, rank), span] = mine[k, :rank].astype(jnp.float32)
        factors[pl.ds(there, rank), span] = other[k, :rank].astype(jnp.float32)
        weights[:, span] = mine[k, rank:].astype(jnp.float32)[:1]


def range_scale(values):
    top = jnp.max(jnp.abs(values), keepdims=True)
    scale = jnp.ones_like(top)
    for low in (16, 48, 80, 112):
        scale = jnp.where(top > 2.0**low, 2.0 ** -min(low + 16, 126), scale)
        scale = jnp.where(top < 2.0**-low, 2.0 ** min(low + 16, 126), scale)
    return scale


def share_kernel(row_count, mine, other, query_ref, *refs):
    factors, weights, features = refs[-3:]
    out_refs = refs[:-3]
    lay_out_factors(mine, other, factors, weights)
    rank = factors.shape[0] // 2
    tokens = factors.shape[1]
    tok = tokens // len(out_refs)
    first = rank + lax.axis_index("dp") * row_count
    act = factors[:rank, :]
    for i in range(row_count):
        row = factors[pl.ds(first + i, 1), :]
        features[i * rank : (i + 1) * rank, :] = (row * act).astype(jnp.bfloat16)
    plain = jnp.dot(query_ref[...], features[...], preferred_element_type=jnp.float32)
    weight = weights[...]
    live = weight > 0.0
    act = jnp.where(live, act, 0.0)
    grad = jnp.where(live, factors[rank:, :], 0.0)
    act_scale, grad_scale = range_scale(act), range_scale(grad)
    act, grad = act * act_scale, grad * grad_scale
    norms = jnp.sum(act * act, axis=0, keepdims=True) * jnp.sum(grad * grad, axis=0, keepdims=True)
    level = jnp.sum(weight * norms, axis=1, keepdims=True) / (tokens * rank * rank)
    step = 1.1 * level
    act_b, grad_b = act.astype(jnp.bfloat16), grad.astype(jnp.bfloat16)
    gram = jnp.dot(act.T.astype(jnp.bfloat16), act_b, preferred_element_type=jnp.float32) * jnp.dot(
        grad.T.astype(jnp.bfloat16), grad_b, preferred_element_type=jnp.float32
    )
    gram = (gram * (1.0 / (tokens * step))).astype(jnp.bfloat16)
    image = jnp.dot((plain * weight).astype(jnp.bfloat16), gram, preferred_element_type=jnp.float32)
    scale = act_scale * grad_scale
    share = ((2.0 - 0.1 / 1.1) * plain - image) * scale * (scale / step)
    for k, out_ref in enumerate(out_refs):
        out_ref[...] = share[:, k * tok : (k + 1) * tok].astype(jnp.bfloat16)


def score_shares(mine, other, queries_t, rank, row_count):
    blocks, _, tok = mine.shape
    count, rows = queries_t.shape
    out = jax.ShapeDtypeStruct((count, tok), jnp.bfloat16)
    return pl.pallas_call(
        functools.partial(share_kernel, row_count),
        out_shape=[out] * blocks,
        scratch_shapes=[
            pltpu.VMEM((2 * rank, tok * blocks), jnp.float32),
            pltpu.VMEM((1, tok * blocks), jnp.float32),
            pltpu.VMEM((rows, tok * blocks), jnp.bfloat16),
        ],
        compiler_params=params(40),
    )(mine, other, queries_t)


def hessian_kernel(row_count, col_count, mine, other, out, factors, weights, weighted, *scratch):
    rights, result, sems = scratch[:2], scratch[2], scratch[3]
    rank = factors.shape[0] // 2
    tokens = factors.shape[1]
    rows, cols = row_count * rank, col_count * rank
    steps = rank // col_count
    lay_out_factors(mine, other, factors, weights)
    act, weight = factors[:rank, :], weights[...]
    first = rank + lax.axis_index("dp") * row_count
    for i in range(row_count):
        left = (factors[pl.ds(first + i, 1), :] * act).astype(jnp.bfloat16)
        left = (weight * left.astype(jnp.float32)).astype(jnp.bfloat16)
        weighted[i * rank : (i + 1) * rank, :] = left

    def build(step):
        for i in range(col_count):
            row = rank + step * col_count + i
            right = (factors[row : row + 1, :] * act).astype(jnp.bfloat16)
            rights[step % 2][i * rank : (i + 1) * rank, :] = right

    copies = []
    build(0)
    for step in range(steps):
        if step + 1 < steps:
            build(step + 1)
        for row in range(0, rows, TILE):
            here = pl.ds(row, TILE), pl.ds(step * cols, cols)
            tile = lax.dot_general(
                weighted[row : row + TILE, :],
                rights[step % 2][...],
                NT,
                preferred_element_type=jnp.float32,
            )
            result[here] = tile * (1.0 / tokens)
            copy = pltpu.make_async_copy(result.at[here], out.at[here], sems.at[len(copies)])
            copy.start()
            copies.append(copy)
    for copy in copies:
        copy.wait()


def hessian_rows(mine, other, rank, row_count, col_count=8):
    blocks, _, tok = mine.shape
    feat = rank * rank
    rows, cols = row_count * rank, col_count * rank
    return pl.pallas_call(
        functools.partial(hessian_kernel, row_count, col_count),
        out_specs=pl.BlockSpec(memory_space=pl.ANY),
        out_shape=jax.ShapeDtypeStruct((rows, feat), jnp.float32),
        scratch_shapes=[
            pltpu.VMEM((2 * rank, tok * blocks), jnp.float32),
            pltpu.VMEM((1, tok * blocks), jnp.float32),
            pltpu.VMEM((rows, tok * blocks), jnp.bfloat16),
            pltpu.VMEM((cols, tok * blocks), jnp.bfloat16),
            pltpu.VMEM((cols, tok * blocks), jnp.bfloat16),
            pltpu.VMEM((rows, feat), jnp.float32),
            pltpu.SemaphoreType.DMA((feat // cols * (rows // TILE),)),
        ],
        compiler_params=params(40),
    )(mine, other)


def finish_kernel(*refs):
    weight_ref, out_ref = refs[-2], refs[-1]
    total = refs[0][...].astype(jnp.float32)
    for ref in refs[1:-2]:
        total = total + ref[...].astype(jnp.float32)
    total = jnp.where(weight_ref[...] > 0.0, total, 0.0)
    out_ref[...] = total.T.astype(out_ref.dtype)


def finish_scores(shares, weight):
    count, tok = shares[0].shape
    return pl.pallas_call(
        finish_kernel,
        out_shape=jax.ShapeDtypeStruct((tok, count), jnp.bfloat16),
        compiler_params=params(40),
    )(*shares, weight)


def swapped(array, axis, distance):
    return lax.ppermute(array, axis, [(i, i ^ distance) for i in range(lax.axis_size(axis))])


def few_tokens(activations, out_grads, proj_in, proj_out, queries, lengths, credit):
    tok_rows = activations.shape[0]
    seq_len = tok_rows // lengths.shape[0]
    dp_count = lax.axis_size("dp")
    query_count = lax.axis_size("query")
    rank = proj_in.shape[1]
    row_count = rank // dp_count
    live = jnp.arange(seq_len, dtype=jnp.int32)[None, :] < lengths[:, None]
    weight = (credit[:, None].astype(jnp.float32) * live.astype(jnp.float32)).reshape(1, -1)
    keep, send = project(activations, out_grads, proj_in.T, proj_out.T)
    other = swapped(send, "query", 1)
    distance = 2
    while distance < query_count:
        keep = add(keep, other)
        other = swapped(keep, "query", distance)
        distance *= 2
    payload = add_to_payload(keep, other, weight)
    others = [swapped(payload, "dp", k) for k in reversed(range(1, dp_count))]
    mine = stack([payload] + others[::-1])
    other = swapped(mine, "query", 1)
    shares = score_shares(mine, other, queries.T, rank, row_count)
    arrived = [swapped(shares[k], "dp", k) for k in reversed(range(1, dp_count))]
    hessian = hessian_rows(mine, other, rank, row_count)
    return hessian, finish_scores([shares[0]] + arrived, weight)


def power_of_two(count):
    return count & (count - 1) == 0


def per_device(activations, *others):
    rank = others[1].shape[1]
    dp_count, query_count = lax.axis_size("dp"), lax.axis_size("query")
    pairs = query_count > 1 and power_of_two(query_count) and power_of_two(dp_count)
    if pairs and activations.shape[0] * dp_count <= rank * rank:
        return few_tokens(activations, *others)
    return many_tokens(activations, *others)


def solution(mesh):
    placed = (
        P(("groups", "dp"), "query"),
        P(("groups", "dp"), "query"),
        P("query", None),
        P("query", None),
        P(("groups", "dp"), "query"),
        P(("groups", "dp")),
        P(("groups", "dp")),
    )
    return jax.shard_map(
        per_device,
        mesh=mesh,
        in_specs=placed,
        out_specs=(P(("groups", "dp"), None), P(("groups", "dp"), "query")),
        check_vma=False,
    )
```

```python
import functools
import jax
import jax.numpy as jnp
from jax import lax
from jax.experimental import pallas as pl
from jax.experimental.pallas import tpu as pltpu
from jax.sharding import PartitionSpec as P


def kron_columns(grad_rows, act_rows, start, count):
    rank = grad_rows.shape[1]
    tokens_here = grad_rows.shape[0]
    grad_cols = lax.dynamic_slice_in_dim(grad_rows, start // rank, count // rank, 1)
    outer = grad_cols.astype(jnp.float32)[:, :, None] * act_rows.astype(jnp.float32)[:, None, :]
    return outer.reshape(tokens_here, count).astype(jnp.bfloat16)


def hessian_block(total, pieces, row_start, rows_own, col_start, col_count):
    grad_rows, act_rows, weights = pieces
    left = kron_columns(grad_rows, act_rows, row_start, rows_own)
    weighted = (weights.astype(jnp.float32)[:, None] * left.astype(jnp.float32)).astype(
        jnp.bfloat16
    )
    right = kron_columns(grad_rows, act_rows, col_start, col_count)
    return total + lax.dot_general(
        weighted, right, (((0,), (0,)), ((), ())), preferred_element_type=jnp.float32
    )


def fold_blocks(total, pieces, step_fn):
    count = pieces[0].shape[0]
    shaped = tuple((p.reshape((count // 512, 512) + p.shape[1:]) for p in pieces))

    def inner(carry, block):
        return (step_fn(carry, block), None)

    return lax.scan(inner, total, shaped)[0]


def split_parts(matrix):
    high_part = matrix.astype(jnp.bfloat16)
    first_rest = matrix - high_part.astype(jnp.float32)
    middle_part = first_rest.astype(jnp.bfloat16)
    low_part = (first_rest - middle_part.astype(jnp.float32)).astype(jnp.bfloat16)
    return (high_part, middle_part, low_part)


def many_tokens(activations, out_grads, proj_in, proj_out, queries, lengths, credit):
    tok_rows = activations.shape[0]
    seq_len = tok_rows // lengths.shape[0]
    dp_count = lax.axis_size("dp")
    query_count = lax.axis_size("query")
    dp_index = lax.axis_index("dp")
    query_index = lax.axis_index("query")
    part_act = jnp.dot(activations, proj_in, preferred_element_type=jnp.float32)
    part_grad = jnp.dot(out_grads, proj_out, preferred_element_type=jnp.float32)
    sum_act, sum_grad = lax.psum((part_act, part_grad), "query")
    act_proj = sum_act.astype(jnp.bfloat16)
    grad_proj = sum_grad.astype(jnp.bfloat16)
    rank = act_proj.shape[1]
    feat = rank * rank
    live = jnp.arange(seq_len, dtype=jnp.int32)[None, :] < lengths[:, None]
    weight = (credit[:, None].astype(jnp.float32) * live.astype(jnp.float32)).reshape(-1)
    mask = live.astype(jnp.float32).reshape(-1)
    weight_wire = weight.astype(jnp.bfloat16)
    rows_own = feat // dp_count
    row_start = dp_index * rows_own
    all_tokens = tok_rows * dp_count
    col_count = feat // query_count
    col_start = query_index * col_count
    owned = fold_blocks(
        jnp.zeros((rows_own, col_count), jnp.float32),
        (
            lax.all_gather(grad_proj, "dp", axis=0, tiled=True),
            lax.all_gather(act_proj, "dp", axis=0, tiled=True),
            lax.all_gather(weight_wire, "dp", axis=0, tiled=True),
        ),
        lambda carry, block: hessian_block(carry, block, row_start, rows_own, col_start, col_count),
    )
    hessian = lax.all_gather(owned, "query", axis=1, tiled=True) / all_tokens
    diagonal_block = lax.dynamic_slice_in_dim(hessian, row_start, rows_own, 1)
    level = lax.psum(jnp.trace(diagonal_block), "dp") / feat
    step = 1.1 * level
    high_part, middle_part, low_part = split_parts(hessian)
    piece = lax.all_gather(queries, "dp", axis=0, tiled=True)
    result = jnp.zeros(queries.shape, jnp.float32)
    for part_matrix in (low_part, middle_part, high_part):
        columns = part_matrix
        result = result + jnp.dot(columns, piece, preferred_element_type=jnp.float32)
    query_f = queries.astype(jnp.float32)
    precond = ((2.0 * query_f - (result + 0.1 * level * query_f) / step) / step).astype(
        jnp.bfloat16
    )
    local_features = kron_columns(grad_proj, act_proj, 0, feat)
    piece = lax.all_gather(precond, "dp", axis=0, tiled=True)
    columns = lax.slice_in_dim(local_features, 0, piece.shape[0], axis=1)
    scores = jnp.zeros((tok_rows, precond.shape[1]), jnp.float32) + jnp.dot(
        columns, piece, preferred_element_type=jnp.float32
    )
    return (hessian, (scores * mask[:, None]).astype(jnp.bfloat16))


MIB = 1024 * 1024
TILE = 256
NT = (((1,), (1,)), ((), ()))


def params(mib):
    return pltpu.CompilerParams(vmem_limit_bytes=int(mib * MIB))


def project_kernel(act, grad, pin, pout, keep_ref, send_ref, act_v, grad_v, pin_v, pout_v, sems):
    chunk = act.shape[1]
    while grad.shape[1] % chunk:
        chunk //= 2
    spans = [pl.ds(c, chunk) for c in range(0, grad.shape[1], chunk)]
    copies = [pltpu.make_async_copy(s, d, sems.at[n]) for n, (s, d) in enumerate(((pin, pin_v), (act, act_v), (pout, pout_v)))]
    copies += [
        pltpu.make_async_copy(grad.at[:, span], grad_v.at[:, span], sems.at[3 + n])
        for n, span in enumerate(spans)
    ]
    for copy in copies:
        copy.start()
    copies[0].wait()
    copies[1].wait()
    part_act = lax.dot_general(pin_v[...], act_v[...], NT, preferred_element_type=jnp.float32)
    copies[2].wait()
    part_grad = jnp.zeros_like(part_act)
    for copy, span in zip(copies[3:], spans):
        copy.wait()
        part_grad += lax.dot_general(
            pout_v[:, span], grad_v[:, span], NT, preferred_element_type=jnp.float32
        )
    even = lax.rem(lax.axis_index("query"), 2) == 0
    keep_ref[...] = jnp.where(even, part_act, part_grad)
    send_ref[...] = jnp.where(even, part_grad, part_act)


def project(activations, out_grads, proj_in_t, proj_out_t):
    tok, d_here = activations.shape
    f_here = out_grads.shape[1]
    rank = proj_in_t.shape[0]
    out = jax.ShapeDtypeStruct((rank, tok), jnp.float32)
    return pl.pallas_call(
        project_kernel,
        in_specs=[pl.BlockSpec(memory_space=pl.ANY)] * 4,
        out_shape=[out, out],
        scratch_shapes=[
            pltpu.VMEM((tok, d_here), jnp.bfloat16),
            pltpu.VMEM((tok, f_here), jnp.bfloat16),
            pltpu.VMEM((rank, d_here), jnp.bfloat16),
            pltpu.VMEM((rank, f_here), jnp.bfloat16),
            pltpu.SemaphoreType.DMA((3 + f_here // 128,)),
        ],
        compiler_params=params(53.75),
    )(activations, out_grads, proj_in_t, proj_out_t)


def add_kernel(one_ref, other_ref, out_ref):
    out_ref[...] = one_ref[...] + other_ref[...]


def add(one, other):
    return pl.pallas_call(
        add_kernel,
        out_shape=jax.ShapeDtypeStruct(one.shape, one.dtype),
        compiler_params=params(40),
    )(one, other)


def payload_kernel(one_ref, other_ref, weight_ref, out_ref):
    total = one_ref[...] + other_ref[...]
    weight = jnp.broadcast_to(weight_ref[...], (16, weight_ref.shape[1]))
    out_ref[...] = jnp.concatenate([total, weight], axis=0).astype(out_ref.dtype)


def add_to_payload(one, other, weight):
    rows, tok = one.shape
    return pl.pallas_call(
        payload_kernel,
        out_shape=jax.ShapeDtypeStruct((rows + 16, tok), jnp.bfloat16),
        compiler_params=params(40),
    )(one, other, weight)


def stack_kernel(*refs):
    for k, ref in enumerate(refs[:-1]):
        refs[-1][k] = ref[...]


def stack(parts):
    return pl.pallas_call(
        stack_kernel,
        out_shape=jax.ShapeDtypeStruct((len(parts),) + parts[0].shape, parts[0].dtype),
        compiler_params=params(40),
    )(*parts)


def lay_out_factors(mine, other, factors, weights):
    blocks, _, tok = mine.shape
    rank = factors.shape[0] // 2
    here = pl.multiple_of(lax.rem(lax.axis_index("query"), 2) * rank, rank)
    there = pl.multiple_of(rank - here, rank)
    for k in range(blocks):
        span = slice(k * tok, (k + 1) * tok)
        factors[pl.ds(here, rank), span] = mine[k, :rank].astype(jnp.float32)
        factors[pl.ds(there, rank), span] = other[k, :rank].astype(jnp.float32)
        weights[:, span] = mine[k, rank:].astype(jnp.float32)[:1]


def range_scale(values):
    top = jnp.max(jnp.abs(values), keepdims=True)
    scale = jnp.ones_like(top)
    for low in (16, 48, 80, 112):
        scale = jnp.where(top > 2.0**low, 2.0 ** -min(low + 16, 126), scale)
        scale = jnp.where(top < 2.0**-low, 2.0 ** min(low + 16, 126), scale)
    return scale


def share_kernel(row_count, mine, other, query_ref, out_ref, factors, weights, features):
    lay_out_factors(mine, other, factors, weights)
    rank = factors.shape[0] // 2
    tokens = factors.shape[1]
    tok = tokens // out_ref.shape[0]
    first = rank + lax.axis_index("dp") * row_count
    act = factors[:rank, :]
    for i in range(row_count):
        row = factors[pl.ds(first + i, 1), :]
        features[i * rank : (i + 1) * rank, :] = (row * act).astype(jnp.bfloat16)
    plain = jnp.dot(query_ref[...], features[...], preferred_element_type=jnp.float32)
    weight = weights[...]
    live = weight > 0.0
    act = jnp.where(live, act, 0.0)
    grad = jnp.where(live, factors[rank:, :], 0.0)
    act_scale, grad_scale = range_scale(act), range_scale(grad)
    act, grad = act * act_scale, grad * grad_scale
    norms = jnp.sum(act * act, axis=0, keepdims=True) * jnp.sum(grad * grad, axis=0, keepdims=True)
    level = jnp.sum(weight * norms, axis=1, keepdims=True) / (tokens * rank * rank)
    step = 1.1 * level
    act_b, grad_b = act.astype(jnp.bfloat16), grad.astype(jnp.bfloat16)
    gram = jnp.dot(act.T.astype(jnp.bfloat16), act_b, preferred_element_type=jnp.float32) * jnp.dot(
        grad.T.astype(jnp.bfloat16), grad_b, preferred_element_type=jnp.float32
    )
    gram = (gram * (1.0 / (tokens * step))).astype(jnp.bfloat16)
    image = jnp.dot((plain * weight).astype(jnp.bfloat16), gram, preferred_element_type=jnp.float32)
    scale = act_scale * grad_scale
    share = ((2.0 - 0.1 / 1.1) * plain - image) * scale * (scale / step)
    for k in range(out_ref.shape[0]):
        out_ref[lax.axis_index("dp") ^ k] = share[:, k * tok : (k + 1) * tok].astype(jnp.bfloat16)


def score_shares(mine, other, queries_t, rank, row_count):
    blocks, _, tok = mine.shape
    count, rows = queries_t.shape
    return pl.pallas_call(
        functools.partial(share_kernel, row_count),
        out_shape=jax.ShapeDtypeStruct((blocks, count, tok), jnp.bfloat16),
        scratch_shapes=[
            pltpu.VMEM((2 * rank, tok * blocks), jnp.float32),
            pltpu.VMEM((1, tok * blocks), jnp.float32),
            pltpu.VMEM((rows, tok * blocks), jnp.bfloat16),
        ],
        compiler_params=params(40),
    )(mine, other, queries_t)


def hessian_kernel(row_count, col_count, mine, other, out, factors, weights, weighted, *scratch):
    rights, result, sems = scratch[:2], scratch[2], scratch[3]
    rank = factors.shape[0] // 2
    tokens = factors.shape[1]
    rows, cols = row_count * rank, col_count * rank
    steps = rank // col_count
    lay_out_factors(mine, other, factors, weights)
    act, weight = factors[:rank, :], weights[...]
    first = rank + lax.axis_index("dp") * row_count
    for i in range(row_count):
        left = (factors[pl.ds(first + i, 1), :] * act).astype(jnp.bfloat16)
        left = (weight * left.astype(jnp.float32)).astype(jnp.bfloat16)
        weighted[i * rank : (i + 1) * rank, :] = left

    def build(step):
        for i in range(col_count):
            row = rank + step * col_count + i
            right = (factors[row : row + 1, :] * act).astype(jnp.bfloat16)
            rights[step % 2][i * rank : (i + 1) * rank, :] = right

    copies = []
    build(0)
    for step in range(steps):
        if step + 1 < steps:
            build(step + 1)
        for row in range(0, rows, TILE):
            here = pl.ds(row, TILE), pl.ds(step * cols, cols)
            tile = lax.dot_general(
                weighted[row : row + TILE, :],
                rights[step % 2][...],
                NT,
                preferred_element_type=jnp.float32,
            )
            result[here] = tile * (1.0 / tokens)
            copy = pltpu.make_async_copy(result.at[here], out.at[here], sems.at[len(copies)])
            copy.start()
            copies.append(copy)
    for copy in copies:
        copy.wait()


def hessian_rows(mine, other, rank, row_count, col_count=8):
    blocks, _, tok = mine.shape
    feat = rank * rank
    rows, cols = row_count * rank, col_count * rank
    return pl.pallas_call(
        functools.partial(hessian_kernel, row_count, col_count),
        out_specs=pl.BlockSpec(memory_space=pl.ANY),
        out_shape=jax.ShapeDtypeStruct((rows, feat), jnp.float32),
        scratch_shapes=[
            pltpu.VMEM((2 * rank, tok * blocks), jnp.float32),
            pltpu.VMEM((1, tok * blocks), jnp.float32),
            pltpu.VMEM((rows, tok * blocks), jnp.bfloat16),
            pltpu.VMEM((cols, tok * blocks), jnp.bfloat16),
            pltpu.VMEM((cols, tok * blocks), jnp.bfloat16),
            pltpu.VMEM((rows, feat), jnp.float32),
            pltpu.SemaphoreType.DMA((feat // cols * (rows // TILE),)),
        ],
        compiler_params=params(40),
    )(mine, other)


def finish_kernel(*refs):
    weight_ref, out_ref = refs[-2], refs[-1]
    total = refs[0][...].astype(jnp.float32)
    for ref in refs[1:-2]:
        total = total + ref[...].astype(jnp.float32)
    total = jnp.where(weight_ref[...] > 0.0, total, 0.0)
    out_ref[...] = total.T.astype(out_ref.dtype)


def finish_scores(shares, weight):
    count, tok = shares[0].shape
    return pl.pallas_call(
        finish_kernel,
        out_shape=jax.ShapeDtypeStruct((tok, count), jnp.bfloat16),
        compiler_params=params(40),
    )(*shares, weight)


def swapped(array, axis, distance):
    return lax.ppermute(array, axis, [(i, i ^ distance) for i in range(lax.axis_size(axis))])


def few_tokens(activations, out_grads, proj_in, proj_out, queries, lengths, credit):
    tok_rows = activations.shape[0]
    seq_len = tok_rows // lengths.shape[0]
    dp_count = lax.axis_size("dp")
    query_count = lax.axis_size("query")
    rank = proj_in.shape[1]
    row_count = rank // dp_count
    live = jnp.arange(seq_len, dtype=jnp.int32)[None, :] < lengths[:, None]
    weight = (credit[:, None].astype(jnp.float32) * live.astype(jnp.float32)).reshape(1, -1)
    keep, send = project(activations, out_grads, proj_in.T, proj_out.T)
    other = swapped(send, "query", 1)
    distance = 2
    while distance < query_count:
        keep = add(keep, other)
        other = swapped(keep, "query", distance)
        distance *= 2
    payload = add_to_payload(keep, other, weight)
    others = [swapped(payload, "dp", k) for k in reversed(range(1, dp_count))]
    mine = stack([payload] + others[::-1])
    other = swapped(mine, "query", 1)
    shares = score_shares(mine, other, queries.T, rank, row_count)
    arrived = lax.psum_scatter(shares, "dp", scatter_dimension=0)
    hessian = hessian_rows(mine, other, rank, row_count)
    return hessian, finish_scores([arrived], weight)


def power_of_two(count):
    return count & (count - 1) == 0


def per_device(activations, *others):
    rank = others[1].shape[1]
    dp_count, query_count = lax.axis_size("dp"), lax.axis_size("query")
    pairs = query_count > 1 and power_of_two(query_count) and power_of_two(dp_count)
    if pairs and activations.shape[0] * dp_count <= rank * rank:
        return few_tokens(activations, *others)
    return many_tokens(activations, *others)


def solution(mesh):
    placed = (
        P(("groups", "dp"), "query"),
        P(("groups", "dp"), "query"),
        P("query", None),
        P("query", None),
        P(("groups", "dp"), "query"),
        P(("groups", "dp")),
        P(("groups", "dp")),
    )
    return jax.shard_map(
        per_device,
        mesh=mesh,
        in_specs=placed,
        out_specs=(P(("groups", "dp"), None), P(("groups", "dp"), "query")),
        check_vma=False,
    )
```

```python
import functools
import jax
import jax.numpy as jnp
from jax import lax
from jax.experimental import pallas as pl
from jax.experimental.pallas import tpu as pltpu
from jax.sharding import PartitionSpec as P


def kron_columns(grad_rows, act_rows, start, count):
    rank = grad_rows.shape[1]
    tokens_here = grad_rows.shape[0]
    grad_cols = lax.dynamic_slice_in_dim(grad_rows, start // rank, count // rank, 1)
    outer = grad_cols.astype(jnp.float32)[:, :, None] * act_rows.astype(jnp.float32)[:, None, :]
    return outer.reshape(tokens_here, count).astype(jnp.bfloat16)


def hessian_block(total, pieces, row_start, rows_own, col_start, col_count):
    grad_rows, act_rows, weights = pieces
    left = kron_columns(grad_rows, act_rows, row_start, rows_own)
    weighted = (weights.astype(jnp.float32)[:, None] * left.astype(jnp.float32)).astype(
        jnp.bfloat16
    )
    right = kron_columns(grad_rows, act_rows, col_start, col_count)
    return total + lax.dot_general(
        weighted, right, (((0,), (0,)), ((), ())), preferred_element_type=jnp.float32
    )


def fold_blocks(total, pieces, step_fn):
    count = pieces[0].shape[0]
    shaped = tuple((p.reshape((count // 512, 512) + p.shape[1:]) for p in pieces))

    def inner(carry, block):
        return (step_fn(carry, block), None)

    return lax.scan(inner, total, shaped)[0]


def split_parts(matrix):
    high_part = matrix.astype(jnp.bfloat16)
    first_rest = matrix - high_part.astype(jnp.float32)
    middle_part = first_rest.astype(jnp.bfloat16)
    low_part = (first_rest - middle_part.astype(jnp.float32)).astype(jnp.bfloat16)
    return (high_part, middle_part, low_part)


def many_tokens(activations, out_grads, proj_in, proj_out, queries, lengths, credit):
    tok_rows = activations.shape[0]
    seq_len = tok_rows // lengths.shape[0]
    dp_count = lax.axis_size("dp")
    query_count = lax.axis_size("query")
    dp_index = lax.axis_index("dp")
    query_index = lax.axis_index("query")
    part_act = jnp.dot(activations, proj_in, preferred_element_type=jnp.float32)
    part_grad = jnp.dot(out_grads, proj_out, preferred_element_type=jnp.float32)
    sum_act, sum_grad = lax.psum((part_act, part_grad), "query")
    act_proj = sum_act.astype(jnp.bfloat16)
    grad_proj = sum_grad.astype(jnp.bfloat16)
    rank = act_proj.shape[1]
    feat = rank * rank
    live = jnp.arange(seq_len, dtype=jnp.int32)[None, :] < lengths[:, None]
    weight = (credit[:, None].astype(jnp.float32) * live.astype(jnp.float32)).reshape(-1)
    mask = live.astype(jnp.float32).reshape(-1)
    weight_wire = weight.astype(jnp.bfloat16)
    rows_own = feat // dp_count
    row_start = dp_index * rows_own
    all_tokens = tok_rows * dp_count
    col_count = feat // query_count
    col_start = query_index * col_count
    owned = fold_blocks(
        jnp.zeros((rows_own, col_count), jnp.float32),
        (
            lax.all_gather(grad_proj, "dp", axis=0, tiled=True),
            lax.all_gather(act_proj, "dp", axis=0, tiled=True),
            lax.all_gather(weight_wire, "dp", axis=0, tiled=True),
        ),
        lambda carry, block: hessian_block(carry, block, row_start, rows_own, col_start, col_count),
    )
    hessian = lax.all_gather(owned, "query", axis=1, tiled=True) / all_tokens
    diagonal_block = lax.dynamic_slice_in_dim(hessian, row_start, rows_own, 1)
    level = lax.psum(jnp.trace(diagonal_block), "dp") / feat
    step = 1.1 * level
    high_part, middle_part, low_part = split_parts(hessian)
    piece = lax.all_gather(queries, "dp", axis=0, tiled=True)
    result = jnp.zeros(queries.shape, jnp.float32)
    for part_matrix in (low_part, middle_part, high_part):
        columns = part_matrix
        result = result + jnp.dot(columns, piece, preferred_element_type=jnp.float32)
    query_f = queries.astype(jnp.float32)
    precond = ((2.0 * query_f - (result + 0.1 * level * query_f) / step) / step).astype(
        jnp.bfloat16
    )
    local_features = kron_columns(grad_proj, act_proj, 0, feat)
    piece = lax.all_gather(precond, "dp", axis=0, tiled=True)
    columns = lax.slice_in_dim(local_features, 0, piece.shape[0], axis=1)
    scores = jnp.zeros((tok_rows, precond.shape[1]), jnp.float32) + jnp.dot(
        columns, piece, preferred_element_type=jnp.float32
    )
    return (hessian, (scores * mask[:, None]).astype(jnp.bfloat16))


MIB = 1024 * 1024
TILE = 256
NT = (((1,), (1,)), ((), ()))


def params(mib):
    return pltpu.CompilerParams(vmem_limit_bytes=int(mib * MIB))


def project_kernel(
    act, grad, pin, pout, query, keep_ref, send_ref, keep_query_ref, send_query_ref, *scratch
):
    act_v, grad_v, pin_v, pout_v, query_v, sems = scratch
    chunk = act.shape[1]
    while grad.shape[1] % chunk:
        chunk //= 2
    spans = [pl.ds(c, chunk) for c in range(0, grad.shape[1], chunk)]
    pairs = [(pin, pin_v), (act, act_v), (query, query_v), (pout, pout_v)]
    pairs += [(grad.at[:, span], grad_v.at[:, span]) for span in spans]
    copies = [pltpu.make_async_copy(s, d, sems.at[n]) for n, (s, d) in enumerate(pairs)]
    for copy in copies:
        copy.start()
    copies[0].wait()
    copies[1].wait()
    part_act = lax.dot_general(pin_v[...], act_v[...], NT, preferred_element_type=jnp.float32)
    copies[2].wait()
    query_t = query_v[...].T
    half = query_t.shape[0] // 2
    even = lax.rem(lax.axis_index("dp"), 2) == 0
    keep_query_ref[...] = jnp.where(even, query_t[:half], query_t[half:])
    send_query_ref[...] = jnp.where(even, query_t[half:], query_t[:half])
    copies[3].wait()
    part_grad = jnp.zeros_like(part_act)
    for copy, span in zip(copies[4:], spans):
        copy.wait()
        part_grad += lax.dot_general(
            pout_v[:, span], grad_v[:, span], NT, preferred_element_type=jnp.float32
        )
    even = lax.rem(lax.axis_index("query"), 2) == 0
    keep_ref[...] = jnp.where(even, part_act, part_grad)
    send_ref[...] = jnp.where(even, part_grad, part_act)


def project(activations, out_grads, proj_in_t, proj_out_t, queries):
    tok, d_here = activations.shape
    f_here = out_grads.shape[1]
    rank = proj_in_t.shape[0]
    rows, count = queries.shape
    out = jax.ShapeDtypeStruct((rank, tok), jnp.float32)
    out_query = jax.ShapeDtypeStruct((count // 2, rows), queries.dtype)
    return pl.pallas_call(
        project_kernel,
        in_specs=[pl.BlockSpec(memory_space=pl.ANY)] * 5,
        out_shape=[out, out, out_query, out_query],
        scratch_shapes=[
            pltpu.VMEM((tok, d_here), jnp.bfloat16),
            pltpu.VMEM((tok, f_here), jnp.bfloat16),
            pltpu.VMEM((rank, d_here), jnp.bfloat16),
            pltpu.VMEM((rank, f_here), jnp.bfloat16),
            pltpu.VMEM((rows, count), queries.dtype),
            pltpu.SemaphoreType.DMA((4 + f_here // 128,)),
        ],
        compiler_params=params(53.75),
    )(activations, out_grads, proj_in_t, proj_out_t, queries)


def add_kernel(one_ref, other_ref, out_ref):
    out_ref[...] = one_ref[...] + other_ref[...]


def add(one, other):
    return pl.pallas_call(
        add_kernel,
        out_shape=jax.ShapeDtypeStruct(one.shape, one.dtype),
        compiler_params=params(40),
    )(one, other)


def payload_kernel(one_ref, other_ref, weight_ref, out_ref):
    total = one_ref[...] + other_ref[...]
    weight = jnp.broadcast_to(weight_ref[...], (16, weight_ref.shape[1]))
    out_ref[...] = jnp.concatenate([total, weight], axis=0).astype(out_ref.dtype)


def add_to_payload(one, other, weight):
    rows, tok = one.shape
    return pl.pallas_call(
        payload_kernel,
        out_shape=jax.ShapeDtypeStruct((rows + 16, tok), jnp.bfloat16),
        compiler_params=params(40),
    )(one, other, weight)


def stack_kernel(*refs):
    for k, ref in enumerate(refs[:-1]):
        refs[-1][k] = ref[...]


def stack(parts):
    return pl.pallas_call(
        stack_kernel,
        out_shape=jax.ShapeDtypeStruct((len(parts),) + parts[0].shape, parts[0].dtype),
        compiler_params=params(40),
    )(*parts)


def lay_out_factors(mine, other, factors, weights):
    blocks, _, tok = mine.shape
    rank = factors.shape[0] // 2
    here = pl.multiple_of(lax.rem(lax.axis_index("query"), 2) * rank, rank)
    there = pl.multiple_of(rank - here, rank)
    for k in range(blocks):
        span = slice(k * tok, (k + 1) * tok)
        factors[pl.ds(here, rank), span] = mine[k, :rank].astype(jnp.float32)
        factors[pl.ds(there, rank), span] = other[k, :rank].astype(jnp.float32)
        weights[:, span] = mine[k, rank:].astype(jnp.float32)[:1]


def range_scale(values):
    top = jnp.max(jnp.abs(values), keepdims=True)
    scale = jnp.ones_like(top)
    for low in (16, 48, 80, 112):
        scale = jnp.where(top > 2.0**low, 2.0 ** -min(low + 16, 126), scale)
        scale = jnp.where(top < 2.0**-low, 2.0 ** min(low + 16, 126), scale)
    return scale


def share_kernel(row_count, mine, other, query_ref, near_query_ref, *refs):
    factors, weights, features = refs[-3:]
    out_refs = refs[:-3]
    lay_out_factors(mine, other, factors, weights)
    rank = factors.shape[0] // 2
    tokens = factors.shape[1]
    tok = tokens // len(out_refs)
    act = factors[:rank, :]
    plain = 0.0
    for near, queries in ((0, query_ref), (1, near_query_ref)):
        first = rank + (lax.axis_index("dp") ^ near) * row_count
        for i in range(row_count):
            row = factors[pl.ds(first + i, 1), :]
            features[near, i * rank : (i + 1) * rank, :] = (row * act).astype(jnp.bfloat16)
        plain += jnp.dot(queries[...], features[near], preferred_element_type=jnp.float32)
    weight = weights[...]
    live = weight > 0.0
    act = jnp.where(live, act, 0.0)
    grad = jnp.where(live, factors[rank:, :], 0.0)
    act_scale, grad_scale = range_scale(act), range_scale(grad)
    act, grad = act * act_scale, grad * grad_scale
    norms = jnp.sum(act * act, axis=0, keepdims=True) * jnp.sum(grad * grad, axis=0, keepdims=True)
    level = jnp.sum(weight * norms, axis=1, keepdims=True) / (tokens * rank * rank)
    step = 1.1 * level
    act_b, grad_b = act.astype(jnp.bfloat16), grad.astype(jnp.bfloat16)
    gram = jnp.dot(act.T.astype(jnp.bfloat16), act_b, preferred_element_type=jnp.float32) * jnp.dot(
        grad.T.astype(jnp.bfloat16), grad_b, preferred_element_type=jnp.float32
    )
    gram = (gram * (1.0 / (tokens * step))).astype(jnp.bfloat16)
    image = jnp.dot((plain * weight).astype(jnp.bfloat16), gram, preferred_element_type=jnp.float32)
    scale = act_scale * grad_scale
    share = ((2.0 - 0.1 / 1.1) * plain - image) * scale * (scale / step)
    for k, out_ref in enumerate(out_refs):
        out_ref[...] = share[:, k * tok : (k + 1) * tok].astype(jnp.bfloat16)


def score_shares(mine, other, queries_t, near_queries_t, rank, row_count):
    blocks, _, tok = mine.shape
    count, rows = queries_t.shape
    out = jax.ShapeDtypeStruct((count, tok), jnp.bfloat16)
    return pl.pallas_call(
        functools.partial(share_kernel, row_count),
        out_shape=[out] * blocks,
        scratch_shapes=[
            pltpu.VMEM((2 * rank, tok * blocks), jnp.float32),
            pltpu.VMEM((1, tok * blocks), jnp.float32),
            pltpu.VMEM((2, rows, tok * blocks), jnp.bfloat16),
        ],
        compiler_params=params(40),
    )(mine, other, queries_t, near_queries_t)


def hessian_kernel(row_count, col_count, mine, other, out, factors, weights, weighted, *scratch):
    rights, result, sems = scratch[:2], scratch[2], scratch[3]
    rank = factors.shape[0] // 2
    tokens = factors.shape[1]
    rows, cols = row_count * rank, col_count * rank
    steps = rank // col_count
    lay_out_factors(mine, other, factors, weights)
    act, weight = factors[:rank, :], weights[...]
    first = rank + lax.axis_index("dp") * row_count
    for i in range(row_count):
        left = (factors[pl.ds(first + i, 1), :] * act).astype(jnp.bfloat16)
        left = (weight * left.astype(jnp.float32)).astype(jnp.bfloat16)
        weighted[i * rank : (i + 1) * rank, :] = left

    def build(step):
        for i in range(col_count):
            row = rank + step * col_count + i
            right = (factors[row : row + 1, :] * act).astype(jnp.bfloat16)
            rights[step % 2][i * rank : (i + 1) * rank, :] = right

    copies = []
    build(0)
    for step in range(steps):
        if step + 1 < steps:
            build(step + 1)
        for row in range(0, rows, TILE):
            here = pl.ds(row, TILE), pl.ds(step * cols, cols)
            tile = lax.dot_general(
                weighted[row : row + TILE, :],
                rights[step % 2][...],
                NT,
                preferred_element_type=jnp.float32,
            )
            result[here] = tile * (1.0 / tokens)
            copy = pltpu.make_async_copy(result.at[here], out.at[here], sems.at[len(copies)])
            copy.start()
            copies.append(copy)
    for copy in copies:
        copy.wait()


def hessian_rows(mine, other, rank, row_count, col_count=8):
    blocks, _, tok = mine.shape
    feat = rank * rank
    rows, cols = row_count * rank, col_count * rank
    return pl.pallas_call(
        functools.partial(hessian_kernel, row_count, col_count),
        out_specs=pl.BlockSpec(memory_space=pl.ANY),
        out_shape=jax.ShapeDtypeStruct((rows, feat), jnp.float32),
        scratch_shapes=[
            pltpu.VMEM((2 * rank, tok * blocks), jnp.float32),
            pltpu.VMEM((1, tok * blocks), jnp.float32),
            pltpu.VMEM((rows, tok * blocks), jnp.bfloat16),
            pltpu.VMEM((cols, tok * blocks), jnp.bfloat16),
            pltpu.VMEM((cols, tok * blocks), jnp.bfloat16),
            pltpu.VMEM((rows, feat), jnp.float32),
            pltpu.SemaphoreType.DMA((feat // cols * (rows // TILE),)),
        ],
        compiler_params=params(40),
    )(mine, other)


def finish_kernel(payload_ref, *refs):
    shares, out_ref = refs[:-1], refs[-1]
    weight = payload_ref[...].astype(jnp.float32)[-1:]
    totals = []
    for near in range(2):
        total = shares[near][...].astype(jnp.float32)
        for ref in shares[near + 2 :: 2]:
            total = total + ref[...].astype(jnp.float32)
        totals.append(jnp.where(weight > 0.0, total, 0.0).T.astype(out_ref.dtype))
    even = lax.rem(lax.axis_index("dp"), 2) == 0
    half = totals[0].shape[1]
    out_ref[:, :half] = jnp.where(even, totals[0], totals[1])
    out_ref[:, half:] = jnp.where(even, totals[1], totals[0])


def finish_scores(payload, shares):
    half, tok = shares[0].shape
    return pl.pallas_call(
        finish_kernel,
        out_shape=jax.ShapeDtypeStruct((tok, 2 * half), jnp.bfloat16),
        compiler_params=params(40),
    )(payload, *shares)


def swapped(array, axis, distance):
    return lax.ppermute(array, axis, [(i, i ^ distance) for i in range(lax.axis_size(axis))])


def few_tokens(activations, out_grads, proj_in, proj_out, queries, lengths, credit):
    dp_count = lax.axis_size("dp")
    query_count = lax.axis_size("query")
    rank = proj_in.shape[1]
    row_count = rank // dp_count
    seq_len = activations.shape[0] // lengths.shape[0]
    live = jnp.arange(seq_len, dtype=jnp.int32)[None, :] < lengths[:, None]
    weight = jnp.where(live, credit[:, None], 0).astype(jnp.float32).reshape(1, -1)
    keep, send, queries_t, send_queries = project(
        activations, out_grads, proj_in.T, proj_out.T, queries
    )
    other = swapped(send, "query", 1)
    near_queries_t = swapped(send_queries, "dp", 1)
    distance = 2
    while distance < query_count:
        keep = add(keep, other)
        other = swapped(keep, "query", distance)
        distance *= 2
    payload = add_to_payload(keep, other, weight)
    others = [swapped(payload, "dp", k) for k in reversed(range(1, dp_count))]
    mine = stack([payload] + others[::-1])
    other = swapped(mine, "query", 1)
    shares = score_shares(mine, other, queries_t, near_queries_t, rank, row_count)
    arrived = [swapped(shares[k], "dp", k) for k in reversed(range(1, dp_count))]
    hessian = hessian_rows(mine, other, rank, row_count)
    return hessian, finish_scores(payload, [shares[0]] + arrived[::-1])


def power_of_two(count):
    return count & (count - 1) == 0


def per_device(activations, *others):
    rank = others[1].shape[1]
    dp_count, query_count = lax.axis_size("dp"), lax.axis_size("query")
    pairs = min(dp_count, query_count) > 1 and power_of_two(dp_count) and power_of_two(query_count)
    if pairs and activations.shape[0] * dp_count <= rank * rank:
        return few_tokens(activations, *others)
    return many_tokens(activations, *others)


def solution(mesh):
    placed = (
        P(("groups", "dp"), "query"),
        P(("groups", "dp"), "query"),
        P("query", None),
        P("query", None),
        P(("groups", "dp"), "query"),
        P(("groups", "dp")),
        P(("groups", "dp")),
    )
    return jax.shard_map(
        per_device,
        mesh=mesh,
        in_specs=placed,
        out_specs=(P(("groups", "dp"), None), P(("groups", "dp"), "query")),
        check_vma=False,
    )
```

```python
import functools
import jax
import jax.numpy as jnp
from jax import lax
from jax.experimental import pallas as pl
from jax.experimental.pallas import tpu as pltpu
from jax.sharding import PartitionSpec as P


def kron_columns(grad_rows, act_rows, start, count):
    rank = grad_rows.shape[1]
    tokens_here = grad_rows.shape[0]
    grad_cols = lax.dynamic_slice_in_dim(grad_rows, start // rank, count // rank, 1)
    outer = grad_cols.astype(jnp.float32)[:, :, None] * act_rows.astype(jnp.float32)[:, None, :]
    return outer.reshape(tokens_here, count).astype(jnp.bfloat16)


def hessian_block(total, pieces, row_start, rows_own, col_start, col_count):
    grad_rows, act_rows, weights = pieces
    left = kron_columns(grad_rows, act_rows, row_start, rows_own)
    weighted = (weights.astype(jnp.float32)[:, None] * left.astype(jnp.float32)).astype(
        jnp.bfloat16
    )
    right = kron_columns(grad_rows, act_rows, col_start, col_count)
    return total + lax.dot_general(
        weighted, right, (((0,), (0,)), ((), ())), preferred_element_type=jnp.float32
    )


def fold_blocks(total, pieces, step_fn):
    count = pieces[0].shape[0]
    shaped = tuple((p.reshape((count // 512, 512) + p.shape[1:]) for p in pieces))

    def inner(carry, block):
        return (step_fn(carry, block), None)

    return lax.scan(inner, total, shaped)[0]


def split_parts(matrix):
    high_part = matrix.astype(jnp.bfloat16)
    first_rest = matrix - high_part.astype(jnp.float32)
    middle_part = first_rest.astype(jnp.bfloat16)
    low_part = (first_rest - middle_part.astype(jnp.float32)).astype(jnp.bfloat16)
    return (high_part, middle_part, low_part)


def many_tokens(activations, out_grads, proj_in, proj_out, queries, lengths, credit):
    tok_rows = activations.shape[0]
    seq_len = tok_rows // lengths.shape[0]
    dp_count = lax.axis_size("dp")
    query_count = lax.axis_size("query")
    dp_index = lax.axis_index("dp")
    query_index = lax.axis_index("query")
    part_act = jnp.dot(activations, proj_in, preferred_element_type=jnp.float32)
    part_grad = jnp.dot(out_grads, proj_out, preferred_element_type=jnp.float32)
    sum_act, sum_grad = lax.psum((part_act, part_grad), "query")
    act_proj = sum_act.astype(jnp.bfloat16)
    grad_proj = sum_grad.astype(jnp.bfloat16)
    rank = act_proj.shape[1]
    feat = rank * rank
    live = jnp.arange(seq_len, dtype=jnp.int32)[None, :] < lengths[:, None]
    weight = (credit[:, None].astype(jnp.float32) * live.astype(jnp.float32)).reshape(-1)
    mask = live.astype(jnp.float32).reshape(-1)
    weight_wire = weight.astype(jnp.bfloat16)
    rows_own = feat // dp_count
    row_start = dp_index * rows_own
    all_tokens = tok_rows * dp_count
    col_count = feat // query_count
    col_start = query_index * col_count
    owned = fold_blocks(
        jnp.zeros((rows_own, col_count), jnp.float32),
        (
            lax.all_gather(grad_proj, "dp", axis=0, tiled=True),
            lax.all_gather(act_proj, "dp", axis=0, tiled=True),
            lax.all_gather(weight_wire, "dp", axis=0, tiled=True),
        ),
        lambda carry, block: hessian_block(carry, block, row_start, rows_own, col_start, col_count),
    )
    hessian = lax.all_gather(owned, "query", axis=1, tiled=True) / all_tokens
    diagonal_block = lax.dynamic_slice_in_dim(hessian, row_start, rows_own, 1)
    level = lax.psum(jnp.trace(diagonal_block), "dp") / feat
    step = 1.1 * level
    high_part, middle_part, low_part = split_parts(hessian)
    piece = lax.all_gather(queries, "dp", axis=0, tiled=True)
    result = jnp.zeros(queries.shape, jnp.float32)
    for part_matrix in (low_part, middle_part, high_part):
        columns = part_matrix
        result = result + jnp.dot(columns, piece, preferred_element_type=jnp.float32)
    query_f = queries.astype(jnp.float32)
    precond = ((2.0 * query_f - (result + 0.1 * level * query_f) / step) / step).astype(
        jnp.bfloat16
    )
    local_features = kron_columns(grad_proj, act_proj, 0, feat)
    piece = lax.all_gather(precond, "dp", axis=0, tiled=True)
    columns = lax.slice_in_dim(local_features, 0, piece.shape[0], axis=1)
    scores = jnp.zeros((tok_rows, precond.shape[1]), jnp.float32) + jnp.dot(
        columns, piece, preferred_element_type=jnp.float32
    )
    return (hessian, (scores * mask[:, None]).astype(jnp.bfloat16))


MIB = 1024 * 1024
TILE = 256
NT = (((1,), (1,)), ((), ()))


def params(mib):
    return pltpu.CompilerParams(vmem_limit_bytes=int(mib * MIB))


def project_kernel(act, grad, pin, pout, keep_ref, send_ref, act_v, grad_v, pin_v, pout_v, sems):
    chunk = act.shape[1]
    while grad.shape[1] % chunk:
        chunk //= 2
    spans = [pl.ds(c, chunk) for c in range(0, grad.shape[1], chunk)]
    copies = [pltpu.make_async_copy(s, d, sems.at[n]) for n, (s, d) in enumerate(((pin, pin_v), (act, act_v), (pout, pout_v)))]
    copies += [
        pltpu.make_async_copy(grad.at[:, span], grad_v.at[:, span], sems.at[3 + n])
        for n, span in enumerate(spans)
    ]
    for copy in copies:
        copy.start()
    copies[0].wait()
    copies[1].wait()
    part_act = lax.dot_general(pin_v[...], act_v[...], NT, preferred_element_type=jnp.float32)
    copies[2].wait()
    part_grad = jnp.zeros_like(part_act)
    for copy, span in zip(copies[3:], spans):
        copy.wait()
        part_grad += lax.dot_general(
            pout_v[:, span], grad_v[:, span], NT, preferred_element_type=jnp.float32
        )
    even = lax.rem(lax.axis_index("query"), 2) == 0
    keep_ref[...] = jnp.where(even, part_act, part_grad)
    send_ref[...] = jnp.where(even, part_grad, part_act)


def project(activations, out_grads, proj_in_t, proj_out_t):
    tok, d_here = activations.shape
    f_here = out_grads.shape[1]
    rank = proj_in_t.shape[0]
    out = jax.ShapeDtypeStruct((rank, tok), jnp.float32)
    return pl.pallas_call(
        project_kernel,
        in_specs=[pl.BlockSpec(memory_space=pl.ANY)] * 4,
        out_shape=[out, out],
        scratch_shapes=[
            pltpu.VMEM((tok, d_here), jnp.bfloat16),
            pltpu.VMEM((tok, f_here), jnp.bfloat16),
            pltpu.VMEM((rank, d_here), jnp.bfloat16),
            pltpu.VMEM((rank, f_here), jnp.bfloat16),
            pltpu.SemaphoreType.DMA((3 + f_here // 128,)),
        ],
        compiler_params=params(53.75),
    )(activations, out_grads, proj_in_t, proj_out_t)


def split_kernel(query, _, keep_ref, send_ref, query_v, sem):
    fetch = pltpu.make_async_copy(query, query_v, sem)
    fetch.start()
    fetch.wait()
    query_t = query_v[...].T
    half = keep_ref.shape[0]
    even = lax.rem(lax.axis_index("dp"), 2) == 0
    keep_ref[...] = jnp.where(even, query_t[:half], query_t[half:])
    send_ref[...] = jnp.where(even, query_t[half:], query_t[:half])


def split_queries(queries, after):
    rows, count = queries.shape
    out = jax.ShapeDtypeStruct((count // 2, rows), queries.dtype)
    return pl.pallas_call(
        split_kernel,
        in_specs=[pl.BlockSpec(memory_space=pl.ANY)] * 2,
        out_shape=[out, out],
        scratch_shapes=[pltpu.VMEM(queries.shape, queries.dtype), pltpu.SemaphoreType.DMA],
        compiler_params=params(53),
    )(queries, after)


def add_kernel(one_ref, other_ref, out_ref):
    out_ref[...] = one_ref[...] + other_ref[...]


def add(one, other):
    return pl.pallas_call(
        add_kernel,
        out_shape=jax.ShapeDtypeStruct(one.shape, one.dtype),
        compiler_params=params(40),
    )(one, other)


def payload_kernel(one_ref, other_ref, weight_ref, out_ref):
    total = one_ref[...] + other_ref[...]
    weight = jnp.broadcast_to(weight_ref[...], (16, weight_ref.shape[1]))
    out_ref[...] = jnp.concatenate([total, weight], axis=0).astype(out_ref.dtype)


def add_to_payload(one, other, weight):
    rows, tok = one.shape
    return pl.pallas_call(
        payload_kernel,
        out_shape=jax.ShapeDtypeStruct((rows + 16, tok), jnp.bfloat16),
        compiler_params=params(40),
    )(one, other, weight)


def stack_kernel(_, *refs):
    for k, ref in enumerate(refs[:-1]):
        refs[-1][k] = ref[...]


def stack(parts, after):
    whole = pl.BlockSpec(memory_space=pltpu.VMEM)
    return pl.pallas_call(
        stack_kernel,
        in_specs=[pl.BlockSpec(memory_space=pl.ANY)] + [whole] * len(parts),
        out_shape=jax.ShapeDtypeStruct((len(parts),) + parts[0].shape, parts[0].dtype),
        compiler_params=params(30),
    )(after, *parts)


def lay_out_factors(blocks, factors, weights):
    rank = factors.shape[0] // 2
    here = pl.multiple_of(lax.rem(lax.axis_index("query"), 2) * rank, rank)
    there = pl.multiple_of(rank - here, rank)
    for k, (mine, other) in enumerate(blocks):
        span = slice(k * mine.shape[1], (k + 1) * mine.shape[1])
        factors[pl.ds(here, rank), span] = mine[:rank].astype(jnp.float32)
        factors[pl.ds(there, rank), span] = other[:rank].astype(jnp.float32)
        weights[:, span] = mine[rank:].astype(jnp.float32)[:1]


def block_pairs(mine, other):
    return [(mine.at[k], other.at[k]) for k in range(mine.shape[0])]


def weigh_rows(row_count, factors, weights, weighted):
    rank = factors.shape[0] // 2
    act, weight = factors[:rank, :], weights[...]
    first = rank + lax.axis_index("dp") * row_count
    for i in range(row_count):
        left = (factors[pl.ds(first + i, 1), :] * act).astype(jnp.bfloat16)
        left = (weight * left.astype(jnp.float32)).astype(jnp.bfloat16)
        weighted[i * rank : (i + 1) * rank, :] = left


def range_scale(values):
    top = jnp.max(jnp.abs(values), keepdims=True)
    scale = jnp.ones_like(top)
    for low in (16, 48, 80, 112):
        scale = jnp.where(top > 2.0**low, 2.0 ** -min(low + 16, 126), scale)
        scale = jnp.where(top < 2.0**-low, 2.0 ** min(low + 16, 126), scale)
    return scale


def share_kernel(row_count, own, own_other, mine, other, query_ref, near_query_ref, *refs):
    factors, weights, features = refs[-3:]
    out_refs = refs[:-3]
    lay_out_factors([(own, own_other)] + block_pairs(mine, other), factors, weights)
    rank = factors.shape[0] // 2
    tokens = factors.shape[1]
    tok = tokens // len(out_refs)
    act = factors[:rank, :]
    plain = 0.0
    for near, queries in ((0, query_ref), (1, near_query_ref)):
        first = rank + (lax.axis_index("dp") ^ near) * row_count
        for i in range(row_count):
            row = factors[pl.ds(first + i, 1), :]
            features[near, i * rank : (i + 1) * rank, :] = (row * act).astype(jnp.bfloat16)
        plain += jnp.dot(queries[...], features[near], preferred_element_type=jnp.float32)
    weight = weights[...]
    live = weight > 0.0
    act = jnp.where(live, act, 0.0)
    grad = jnp.where(live, factors[rank:, :], 0.0)
    act_scale, grad_scale = range_scale(act), range_scale(grad)
    act, grad = act * act_scale, grad * grad_scale
    norms = jnp.sum(act * act, axis=0, keepdims=True) * jnp.sum(grad * grad, axis=0, keepdims=True)
    level = jnp.sum(weight * norms, axis=1, keepdims=True) / (tokens * rank * rank)
    step = 1.1 * level
    act_b, grad_b = act.astype(jnp.bfloat16), grad.astype(jnp.bfloat16)
    gram = jnp.dot(act.T.astype(jnp.bfloat16), act_b, preferred_element_type=jnp.float32) * jnp.dot(
        grad.T.astype(jnp.bfloat16), grad_b, preferred_element_type=jnp.float32
    )
    gram = (gram * (1.0 / (tokens * step))).astype(jnp.bfloat16)
    image = jnp.dot((plain * weight).astype(jnp.bfloat16), gram, preferred_element_type=jnp.float32)
    scale = act_scale * grad_scale
    share = ((2.0 - 0.1 / 1.1) * plain - image) * scale * (scale / step)
    for k, out_ref in enumerate(out_refs):
        out_ref[...] = share[:, k * tok : (k + 1) * tok].astype(jnp.bfloat16)


def score_shares(own, own_other, mine, other, queries_t, near_queries_t, rank, row_count):
    blocks, tok = mine.shape[0] + 1, mine.shape[2]
    count, rows = queries_t.shape
    out = jax.ShapeDtypeStruct((count, tok), jnp.bfloat16)
    return pl.pallas_call(
        functools.partial(share_kernel, row_count),
        out_shape=[out] * blocks,
        scratch_shapes=[
            pltpu.VMEM((2 * rank, tok * blocks), jnp.float32),
            pltpu.VMEM((1, tok * blocks), jnp.float32),
            pltpu.VMEM((2, rows, tok * blocks), jnp.bfloat16),
        ],
        compiler_params=params(30),
    )(own, own_other, mine, other, queries_t, near_queries_t)


def build_columns(first, act, factors, right):
    rank = act.shape[0]
    for i in range(right.shape[0] // rank):
        row = rank + first + i
        right[i * rank : (i + 1) * rank, :] = (factors[row : row + 1, :] * act).astype(jnp.bfloat16)


def own_kernel(row_count, col_count, own, own_other, out, factors, weights, weighted, *rights):
    rank = factors.shape[0] // 2
    cols = col_count * rank
    lay_out_factors([(own, own_other)], factors, weights)
    weigh_rows(row_count, factors, weights, weighted)
    act = factors[:rank, :]
    build_columns(0, act, factors, rights[0])
    for step in range(rank // col_count):
        if (step + 1) * col_count < rank:
            build_columns((step + 1) * col_count, act, factors, rights[(step + 1) % 2])
        out[:, step * cols : (step + 1) * cols] = lax.dot_general(
            weighted[...], rights[step % 2][...], NT, preferred_element_type=jnp.float32
        )


def own_tokens_sum(own, own_other, rank, row_count, col_count=8):
    tok = own.shape[1]
    rows, cols = row_count * rank, col_count * rank
    return pl.pallas_call(
        functools.partial(own_kernel, row_count, col_count),
        out_shape=jax.ShapeDtypeStruct((rows, rank * rank), jnp.float32),
        scratch_shapes=[
            pltpu.VMEM((2 * rank, tok), jnp.float32),
            pltpu.VMEM((1, tok), jnp.float32),
            pltpu.VMEM((rows, tok), jnp.bfloat16),
            pltpu.VMEM((cols, tok), jnp.bfloat16),
            pltpu.VMEM((cols, tok), jnp.bfloat16),
        ],
        compiler_params=params(16),
    )(own, own_other)


def hessian_kernel(row_count, col_count, mine, other, own_sum, out, *scratch):
    factors, weights, weighted, rights = *scratch[:3], scratch[3:5]
    result, sems = scratch[5:]
    rank = factors.shape[0] // 2
    blocks = mine.shape[0]
    tokens = factors.shape[1] // blocks * (blocks + 1)
    rows, cols = row_count * rank, col_count * rank
    lay_out_factors(block_pairs(mine, other), factors, weights)
    weigh_rows(row_count, factors, weights, weighted)
    act = factors[:rank, :]
    copies = []
    build_columns(0, act, factors, rights[0])
    for step in range(rank // col_count):
        if (step + 1) * col_count < rank:
            build_columns((step + 1) * col_count, act, factors, rights[(step + 1) % 2])
        for row in range(0, rows, TILE):
            here = pl.ds(row, TILE), pl.ds(step * cols, cols)
            tile = lax.dot_general(
                weighted[row : row + TILE, :],
                rights[step % 2][...],
                NT,
                preferred_element_type=jnp.float32,
            )
            result[here] = (own_sum[here] + tile) * (1.0 / tokens)
            copy = pltpu.make_async_copy(result.at[here], out.at[here], sems.at[len(copies)])
            copy.start()
            copies.append(copy)
    for copy in copies:
        copy.wait()


def hessian_rows(mine, other, own_sum, rank, row_count, col_count=8):
    blocks, _, tok = mine.shape
    feat = rank * rank
    rows, cols = row_count * rank, col_count * rank
    return pl.pallas_call(
        functools.partial(hessian_kernel, row_count, col_count),
        out_specs=pl.BlockSpec(memory_space=pl.ANY),
        out_shape=jax.ShapeDtypeStruct((rows, feat), jnp.float32),
        scratch_shapes=[
            pltpu.VMEM((2 * rank, tok * blocks), jnp.float32),
            pltpu.VMEM((1, tok * blocks), jnp.float32),
            pltpu.VMEM((rows, tok * blocks), jnp.bfloat16),
            pltpu.VMEM((cols, tok * blocks), jnp.bfloat16),
            pltpu.VMEM((cols, tok * blocks), jnp.bfloat16),
            pltpu.VMEM((rows, feat), jnp.float32),
            pltpu.SemaphoreType.DMA((feat // cols * (rows // TILE),)),
        ],
        compiler_params=params(30),
    )(mine, other, own_sum)


def finish_kernel(payload_ref, *refs):
    shares, out_ref = refs[:-1], refs[-1]
    weight = payload_ref[...].astype(jnp.float32)[-1:]
    totals = []
    for near in range(2):
        total = shares[near][...].astype(jnp.float32)
        for ref in shares[near + 2 :: 2]:
            total = total + ref[...].astype(jnp.float32)
        totals.append(jnp.where(weight > 0.0, total, 0.0).T.astype(out_ref.dtype))
    even = lax.rem(lax.axis_index("dp"), 2) == 0
    half = totals[0].shape[1]
    out_ref[:, :half] = jnp.where(even, totals[0], totals[1])
    out_ref[:, half:] = jnp.where(even, totals[1], totals[0])


def finish_scores(payload, shares):
    half, tok = shares[0].shape
    return pl.pallas_call(
        finish_kernel,
        out_shape=jax.ShapeDtypeStruct((tok, 2 * half), jnp.bfloat16),
        compiler_params=params(40),
    )(payload, *shares)


def swapped(array, axis, distance):
    return lax.ppermute(array, axis, [(i, i ^ distance) for i in range(lax.axis_size(axis))])


def few_tokens(activations, out_grads, proj_in, proj_out, queries, lengths, credit):
    dp_count = lax.axis_size("dp")
    query_count = lax.axis_size("query")
    rank = proj_in.shape[1]
    row_count = rank // dp_count
    seq_len = activations.shape[0] // lengths.shape[0]
    live = jnp.arange(seq_len, dtype=jnp.int32)[None, :] < lengths[:, None]
    weight = jnp.where(live, credit[:, None], 0).astype(jnp.float32).reshape(1, -1)
    keep, send = project(activations, out_grads, proj_in.T, proj_out.T)
    other = swapped(send, "query", 1)
    distance = 2
    while distance < query_count:
        keep = add(keep, other)
        other = swapped(keep, "query", distance)
        distance *= 2
    queries_t, send_queries = split_queries(queries, keep)
    near_queries_t = swapped(send_queries, "dp", 1)
    own = add_to_payload(keep, other, weight)
    others = [swapped(own, "dp", k) for k in reversed(range(1, dp_count))]
    own_other = swapped(own, "query", 1)
    own_sum = own_tokens_sum(own, own_other, rank, row_count)
    mine = stack(others[::-1], own_sum)
    other = swapped(mine, "query", 1)
    shares = score_shares(
        own, own_other, mine, other, queries_t, near_queries_t, rank, row_count
    )
    arrived = [swapped(shares[k], "dp", k) for k in reversed(range(1, dp_count))]
    hessian = hessian_rows(mine, other, own_sum, rank, row_count)
    return hessian, finish_scores(own, [shares[0]] + arrived[::-1])


def power_of_two(count):
    return count & (count - 1) == 0


def per_device(activations, *others):
    rank = others[1].shape[1]
    dp_count, query_count = lax.axis_size("dp"), lax.axis_size("query")
    pairs = min(dp_count, query_count) > 1 and power_of_two(dp_count) and power_of_two(query_count)
    if pairs and activations.shape[0] * dp_count <= rank * rank:
        return few_tokens(activations, *others)
    return many_tokens(activations, *others)


def solution(mesh):
    placed = (
        P(("groups", "dp"), "query"),
        P(("groups", "dp"), "query"),
        P("query", None),
        P("query", None),
        P(("groups", "dp"), "query"),
        P(("groups", "dp")),
        P(("groups", "dp")),
    )
    return jax.shard_map(
        per_device,
        mesh=mesh,
        in_specs=placed,
        out_specs=(P(("groups", "dp"), None), P(("groups", "dp"), "query")),
        check_vma=False,
    )
```

```python
import functools
import jax
import jax.numpy as jnp
from jax import lax
from jax.experimental import pallas as pl
from jax.experimental.pallas import tpu as pltpu
from jax.sharding import PartitionSpec as P


def kron_columns(grad_rows, act_rows, start, count):
    rank = grad_rows.shape[1]
    tokens_here = grad_rows.shape[0]
    grad_cols = lax.dynamic_slice_in_dim(grad_rows, start // rank, count // rank, 1)
    outer = grad_cols.astype(jnp.float32)[:, :, None] * act_rows.astype(jnp.float32)[:, None, :]
    return outer.reshape(tokens_here, count).astype(jnp.bfloat16)


def hessian_block(total, pieces, row_start, rows_own, col_start, col_count):
    grad_rows, act_rows, weights = pieces
    left = kron_columns(grad_rows, act_rows, row_start, rows_own)
    weighted = (weights.astype(jnp.float32)[:, None] * left.astype(jnp.float32)).astype(
        jnp.bfloat16
    )
    right = kron_columns(grad_rows, act_rows, col_start, col_count)
    return total + lax.dot_general(
        weighted, right, (((0,), (0,)), ((), ())), preferred_element_type=jnp.float32
    )


def fold_blocks(total, pieces, step_fn):
    count = pieces[0].shape[0]
    shaped = tuple((p.reshape((count // 512, 512) + p.shape[1:]) for p in pieces))

    def inner(carry, block):
        return (step_fn(carry, block), None)

    return lax.scan(inner, total, shaped)[0]


def split_parts(matrix):
    high_part = matrix.astype(jnp.bfloat16)
    first_rest = matrix - high_part.astype(jnp.float32)
    middle_part = first_rest.astype(jnp.bfloat16)
    low_part = (first_rest - middle_part.astype(jnp.float32)).astype(jnp.bfloat16)
    return (high_part, middle_part, low_part)


def many_tokens(activations, out_grads, proj_in, proj_out, queries, lengths, credit):
    tok_rows = activations.shape[0]
    seq_len = tok_rows // lengths.shape[0]
    dp_count = lax.axis_size("dp")
    query_count = lax.axis_size("query")
    dp_index = lax.axis_index("dp")
    query_index = lax.axis_index("query")
    part_act = jnp.dot(activations, proj_in, preferred_element_type=jnp.float32)
    part_grad = jnp.dot(out_grads, proj_out, preferred_element_type=jnp.float32)
    sum_act, sum_grad = lax.psum((part_act, part_grad), "query")
    act_proj = sum_act.astype(jnp.bfloat16)
    grad_proj = sum_grad.astype(jnp.bfloat16)
    rank = act_proj.shape[1]
    feat = rank * rank
    live = jnp.arange(seq_len, dtype=jnp.int32)[None, :] < lengths[:, None]
    weight = (credit[:, None].astype(jnp.float32) * live.astype(jnp.float32)).reshape(-1)
    mask = live.astype(jnp.float32).reshape(-1)
    weight_wire = weight.astype(jnp.bfloat16)
    rows_own = feat // dp_count
    row_start = dp_index * rows_own
    all_tokens = tok_rows * dp_count
    col_count = feat // query_count
    col_start = query_index * col_count
    owned = fold_blocks(
        jnp.zeros((rows_own, col_count), jnp.float32),
        (
            lax.all_gather(grad_proj, "dp", axis=0, tiled=True),
            lax.all_gather(act_proj, "dp", axis=0, tiled=True),
            lax.all_gather(weight_wire, "dp", axis=0, tiled=True),
        ),
        lambda carry, block: hessian_block(carry, block, row_start, rows_own, col_start, col_count),
    )
    hessian = lax.all_gather(owned, "query", axis=1, tiled=True) / all_tokens
    diagonal_block = lax.dynamic_slice_in_dim(hessian, row_start, rows_own, 1)
    level = lax.psum(jnp.trace(diagonal_block), "dp") / feat
    step = 1.1 * level
    high_part, middle_part, low_part = split_parts(hessian)
    piece = lax.all_gather(queries, "dp", axis=0, tiled=True)
    result = jnp.zeros(queries.shape, jnp.float32)
    for part_matrix in (low_part, middle_part, high_part):
        columns = part_matrix
        result = result + jnp.dot(columns, piece, preferred_element_type=jnp.float32)
    query_f = queries.astype(jnp.float32)
    precond = ((2.0 * query_f - (result + 0.1 * level * query_f) / step) / step).astype(
        jnp.bfloat16
    )
    local_features = kron_columns(grad_proj, act_proj, 0, feat)
    piece = lax.all_gather(precond, "dp", axis=0, tiled=True)
    columns = lax.slice_in_dim(local_features, 0, piece.shape[0], axis=1)
    scores = jnp.zeros((tok_rows, precond.shape[1]), jnp.float32) + jnp.dot(
        columns, piece, preferred_element_type=jnp.float32
    )
    return (hessian, (scores * mask[:, None]).astype(jnp.bfloat16))


MIB = 1024 * 1024
TILE = 256
NT = (((1,), (1,)), ((), ()))


def params(mib):
    return pltpu.CompilerParams(vmem_limit_bytes=int(mib * MIB))


def project_kernel(
    act, grad, pin, pout, query, keep_ref, send_ref, send_query, act_v, grad_v, pin_v, pout_v, sems
):
    chunk = act.shape[1]
    while grad.shape[1] % chunk:
        chunk //= 2
    spans = [pl.ds(c, chunk) for c in range(0, grad.shape[1], chunk)]
    copies = [pltpu.make_async_copy(s, d, sems.at[n]) for n, (s, d) in enumerate(((pin, pin_v), (act, act_v), (pout, pout_v)))]
    copies += [
        pltpu.make_async_copy(grad.at[:, span], grad_v.at[:, span], sems.at[3 + n])
        for n, span in enumerate(spans)
    ]
    half = send_query.shape[1]
    even = lax.rem(lax.axis_index("dp"), 2) == 0
    span = pl.ds(pl.multiple_of(jnp.where(even, half, 0), half), half)
    copies.append(pltpu.make_async_copy(query.at[:, span], send_query, sems.at[len(copies)]))
    for copy in copies:
        copy.start()
    copies[0].wait()
    copies[1].wait()
    part_act = lax.dot_general(pin_v[...], act_v[...], NT, preferred_element_type=jnp.float32)
    copies[2].wait()
    part_grad = jnp.zeros_like(part_act)
    for copy, span in zip(copies[3:-1], spans):
        copy.wait()
        part_grad += lax.dot_general(
            pout_v[:, span], grad_v[:, span], NT, preferred_element_type=jnp.float32
        )
    even = lax.rem(lax.axis_index("query"), 2) == 0
    keep_ref[...] = jnp.where(even, part_act, part_grad)
    send_ref[...] = jnp.where(even, part_grad, part_act)
    copies[-1].wait()


def project(activations, out_grads, proj_in_t, proj_out_t, queries):
    tok, d_here = activations.shape
    f_here = out_grads.shape[1]
    rank = proj_in_t.shape[0]
    out = jax.ShapeDtypeStruct((rank, tok), jnp.float32)
    out_query = jax.ShapeDtypeStruct((queries.shape[0], queries.shape[1] // 2), queries.dtype)
    whole = pl.BlockSpec(memory_space=pltpu.VMEM)
    return pl.pallas_call(
        project_kernel,
        in_specs=[pl.BlockSpec(memory_space=pl.ANY)] * 5,
        out_specs=[whole, whole, pl.BlockSpec(memory_space=pl.ANY)],
        out_shape=[out, out, out_query],
        scratch_shapes=[
            pltpu.VMEM((tok, d_here), jnp.bfloat16),
            pltpu.VMEM((tok, f_here), jnp.bfloat16),
            pltpu.VMEM((rank, d_here), jnp.bfloat16),
            pltpu.VMEM((rank, f_here), jnp.bfloat16),
            pltpu.SemaphoreType.DMA((4 + f_here // 128,)),
        ],
        compiler_params=params(53.75),
    )(activations, out_grads, proj_in_t, proj_out_t, queries)


def turn_kernel(query, near_query, out_ref, near_out_ref, query_v, sem):
    half = query_v.shape[1]
    odd = lax.rem(lax.axis_index("dp"), 2)
    span = pl.ds(pl.multiple_of(odd * half, half), half)
    fetch = pltpu.make_async_copy(query.at[:, span], query_v, sem)
    fetch.start()
    near_out_ref[...] = near_query[...].T
    fetch.wait()
    out_ref[...] = query_v[...].T


def turn_queries(queries, near_queries):
    rows, half = near_queries.shape
    out = jax.ShapeDtypeStruct((half, rows), queries.dtype)
    return pl.pallas_call(
        turn_kernel,
        in_specs=[pl.BlockSpec(memory_space=pl.ANY), pl.BlockSpec(memory_space=pltpu.VMEM)],
        out_shape=[out, out],
        scratch_shapes=[pltpu.VMEM((rows, half), queries.dtype), pltpu.SemaphoreType.DMA],
        compiler_params=params(30),
    )(queries, near_queries)


def add_kernel(one_ref, other_ref, out_ref):
    out_ref[...] = one_ref[...] + other_ref[...]


def add(one, other):
    return pl.pallas_call(
        add_kernel,
        out_shape=jax.ShapeDtypeStruct(one.shape, one.dtype),
        compiler_params=params(40),
    )(one, other)


def payload_kernel(one_ref, other_ref, weight_ref, out_ref):
    total = one_ref[...] + other_ref[...]
    weight = jnp.broadcast_to(weight_ref[...], (16, weight_ref.shape[1]))
    out_ref[...] = jnp.concatenate([total, weight], axis=0).astype(out_ref.dtype)


def add_to_payload(one, other, weight):
    rows, tok = one.shape
    return pl.pallas_call(
        payload_kernel,
        out_shape=jax.ShapeDtypeStruct((rows + 16, tok), jnp.bfloat16),
        compiler_params=params(40),
    )(one, other, weight)


def stack_kernel(_, __, *refs):
    for k, ref in enumerate(refs[:-1]):
        refs[-1][k] = ref[...]


def stack(parts, after):
    whole = pl.BlockSpec(memory_space=pltpu.VMEM)
    return pl.pallas_call(
        stack_kernel,
        in_specs=[pl.BlockSpec(memory_space=pl.ANY)] * 2 + [whole] * len(parts),
        out_shape=jax.ShapeDtypeStruct((len(parts),) + parts[0].shape, parts[0].dtype),
        compiler_params=params(30),
    )(*after, *parts)


def lay_out_factors(blocks, factors, weights):
    rank = factors.shape[0] // 2
    here = pl.multiple_of(lax.rem(lax.axis_index("query"), 2) * rank, rank)
    there = pl.multiple_of(rank - here, rank)
    for k, (mine, other) in enumerate(blocks):
        span = slice(k * mine.shape[1], (k + 1) * mine.shape[1])
        factors[pl.ds(here, rank), span] = mine[:rank].astype(jnp.float32)
        factors[pl.ds(there, rank), span] = other[:rank].astype(jnp.float32)
        weights[:, span] = mine[rank:].astype(jnp.float32)[:1]


def block_pairs(mine, other):
    return [(mine.at[k], other.at[k]) for k in range(mine.shape[0])]


def weigh_rows(row_count, factors, weights, weighted):
    rank = factors.shape[0] // 2
    act, weight = factors[:rank, :], weights[...]
    first = rank + lax.axis_index("dp") * row_count
    for i in range(row_count):
        left = (factors[pl.ds(first + i, 1), :] * act).astype(jnp.bfloat16)
        left = (weight * left.astype(jnp.float32)).astype(jnp.bfloat16)
        weighted[i * rank : (i + 1) * rank, :] = left


def range_scale(values):
    top = jnp.max(jnp.abs(values), keepdims=True)
    scale = jnp.ones_like(top)
    for low in (16, 48, 80, 112):
        scale = jnp.where(top > 2.0**low, 2.0 ** -min(low + 16, 126), scale)
        scale = jnp.where(top < 2.0**-low, 2.0 ** min(low + 16, 126), scale)
    return scale


def share_kernel(row_count, own, own_other, mine, other, query_ref, near_query_ref, *refs):
    factors, weights, features = refs[-3:]
    out_refs = refs[:-3]
    lay_out_factors([(own, own_other)] + block_pairs(mine, other), factors, weights)
    rank = factors.shape[0] // 2
    tokens = factors.shape[1]
    tok = tokens // len(out_refs)
    act = factors[:rank, :]
    plain = 0.0
    for near, queries in ((0, query_ref), (1, near_query_ref)):
        first = rank + (lax.axis_index("dp") ^ near) * row_count
        for i in range(row_count):
            row = factors[pl.ds(first + i, 1), :]
            features[near, i * rank : (i + 1) * rank, :] = (row * act).astype(jnp.bfloat16)
        plain += jnp.dot(queries[...], features[near], preferred_element_type=jnp.float32)
    weight = weights[...]
    live = weight > 0.0
    act = jnp.where(live, act, 0.0)
    grad = jnp.where(live, factors[rank:, :], 0.0)
    act_scale, grad_scale = range_scale(act), range_scale(grad)
    act, grad = act * act_scale, grad * grad_scale
    norms = jnp.sum(act * act, axis=0, keepdims=True) * jnp.sum(grad * grad, axis=0, keepdims=True)
    level = jnp.sum(weight * norms, axis=1, keepdims=True) / (tokens * rank * rank)
    step = 1.1 * level
    act_b, grad_b = act.astype(jnp.bfloat16), grad.astype(jnp.bfloat16)
    gram = jnp.dot(act.T.astype(jnp.bfloat16), act_b, preferred_element_type=jnp.float32) * jnp.dot(
        grad.T.astype(jnp.bfloat16), grad_b, preferred_element_type=jnp.float32
    )
    gram = (gram * (1.0 / (tokens * step))).astype(jnp.bfloat16)
    image = jnp.dot((plain * weight).astype(jnp.bfloat16), gram, preferred_element_type=jnp.float32)
    scale = act_scale * grad_scale
    share = ((2.0 - 0.1 / 1.1) * plain - image) * scale * (scale / step)
    for k, out_ref in enumerate(out_refs):
        out_ref[...] = share[:, k * tok : (k + 1) * tok].astype(jnp.bfloat16)


def score_shares(own, own_other, mine, other, queries_t, near_queries_t, rank, row_count):
    blocks, tok = mine.shape[0] + 1, mine.shape[2]
    count, rows = queries_t.shape
    out = jax.ShapeDtypeStruct((count, tok), jnp.bfloat16)
    return pl.pallas_call(
        functools.partial(share_kernel, row_count),
        out_shape=[out] * blocks,
        scratch_shapes=[
            pltpu.VMEM((2 * rank, tok * blocks), jnp.float32),
            pltpu.VMEM((1, tok * blocks), jnp.float32),
            pltpu.VMEM((2, rows, tok * blocks), jnp.bfloat16),
        ],
        compiler_params=params(30),
    )(own, own_other, mine, other, queries_t, near_queries_t)


def build_columns(first, act, factors, right):
    rank = act.shape[0]
    for i in range(right.shape[0] // rank):
        row = rank + first + i
        right[i * rank : (i + 1) * rank, :] = (factors[row : row + 1, :] * act).astype(jnp.bfloat16)


def own_kernel(row_count, col_count, own, own_other, out, factors, weights, weighted, *rights):
    rank = factors.shape[0] // 2
    cols = col_count * rank
    lay_out_factors([(own, own_other)], factors, weights)
    weigh_rows(row_count, factors, weights, weighted)
    act = factors[:rank, :]
    build_columns(0, act, factors, rights[0])
    for step in range(rank // col_count):
        if (step + 1) * col_count < rank:
            build_columns((step + 1) * col_count, act, factors, rights[(step + 1) % 2])
        out[:, step * cols : (step + 1) * cols] = lax.dot_general(
            weighted[...], rights[step % 2][...], NT, preferred_element_type=jnp.float32
        )


def own_tokens_sum(own, own_other, rank, row_count, col_count=8):
    tok = own.shape[1]
    rows, cols = row_count * rank, col_count * rank
    return pl.pallas_call(
        functools.partial(own_kernel, row_count, col_count),
        out_shape=jax.ShapeDtypeStruct((rows, rank * rank), jnp.float32),
        scratch_shapes=[
            pltpu.VMEM((2 * rank, tok), jnp.float32),
            pltpu.VMEM((1, tok), jnp.float32),
            pltpu.VMEM((rows, tok), jnp.bfloat16),
            pltpu.VMEM((cols, tok), jnp.bfloat16),
            pltpu.VMEM((cols, tok), jnp.bfloat16),
        ],
        compiler_params=params(16),
    )(own, own_other)


def hessian_kernel(row_count, col_count, mine, other, own_sum, out, *scratch):
    factors, weights, weighted, rights = *scratch[:3], scratch[3:5]
    result, sems = scratch[5:]
    rank = factors.shape[0] // 2
    blocks = mine.shape[0]
    tokens = factors.shape[1] // blocks * (blocks + 1)
    rows, cols = row_count * rank, col_count * rank
    lay_out_factors(block_pairs(mine, other), factors, weights)
    weigh_rows(row_count, factors, weights, weighted)
    act = factors[:rank, :]
    copies = []
    build_columns(0, act, factors, rights[0])
    for step in range(rank // col_count):
        if (step + 1) * col_count < rank:
            build_columns((step + 1) * col_count, act, factors, rights[(step + 1) % 2])
        for row in range(0, rows, TILE):
            here = pl.ds(row, TILE), pl.ds(step * cols, cols)
            tile = lax.dot_general(
                weighted[row : row + TILE, :],
                rights[step % 2][...],
                NT,
                preferred_element_type=jnp.float32,
            )
            result[here] = (own_sum[here] + tile) * (1.0 / tokens)
            copy = pltpu.make_async_copy(result.at[here], out.at[here], sems.at[len(copies)])
            copy.start()
            copies.append(copy)
    for copy in copies:
        copy.wait()


def hessian_rows(mine, other, own_sum, rank, row_count, col_count=8):
    blocks, _, tok = mine.shape
    feat = rank * rank
    rows, cols = row_count * rank, col_count * rank
    return pl.pallas_call(
        functools.partial(hessian_kernel, row_count, col_count),
        out_specs=pl.BlockSpec(memory_space=pl.ANY),
        out_shape=jax.ShapeDtypeStruct((rows, feat), jnp.float32),
        scratch_shapes=[
            pltpu.VMEM((2 * rank, tok * blocks), jnp.float32),
            pltpu.VMEM((1, tok * blocks), jnp.float32),
            pltpu.VMEM((rows, tok * blocks), jnp.bfloat16),
            pltpu.VMEM((cols, tok * blocks), jnp.bfloat16),
            pltpu.VMEM((cols, tok * blocks), jnp.bfloat16),
            pltpu.VMEM((rows, feat), jnp.float32),
            pltpu.SemaphoreType.DMA((feat // cols * (rows // TILE),)),
        ],
        compiler_params=params(30),
    )(mine, other, own_sum)


def finish_kernel(payload_ref, *refs):
    shares, out_ref = refs[:-1], refs[-1]
    weight = payload_ref[...].astype(jnp.float32)[-1:]
    totals = []
    for near in range(2):
        total = shares[near][...].astype(jnp.float32)
        for ref in shares[near + 2 :: 2]:
            total = total + ref[...].astype(jnp.float32)
        totals.append(jnp.where(weight > 0.0, total, 0.0).T.astype(out_ref.dtype))
    even = lax.rem(lax.axis_index("dp"), 2) == 0
    half = totals[0].shape[1]
    out_ref[:, :half] = jnp.where(even, totals[0], totals[1])
    out_ref[:, half:] = jnp.where(even, totals[1], totals[0])


def finish_scores(payload, shares):
    half, tok = shares[0].shape
    return pl.pallas_call(
        finish_kernel,
        out_shape=jax.ShapeDtypeStruct((tok, 2 * half), jnp.bfloat16),
        compiler_params=params(40),
    )(payload, *shares)


def swapped(array, axis, distance):
    return lax.ppermute(array, axis, [(i, i ^ distance) for i in range(lax.axis_size(axis))])


def few_tokens(activations, out_grads, proj_in, proj_out, queries, lengths, credit):
    dp_count = lax.axis_size("dp")
    query_count = lax.axis_size("query")
    rank = proj_in.shape[1]
    row_count = rank // dp_count
    seq_len = activations.shape[0] // lengths.shape[0]
    live = jnp.arange(seq_len, dtype=jnp.int32)[None, :] < lengths[:, None]
    weight = jnp.where(live, credit[:, None], 0).astype(jnp.float32).reshape(1, -1)
    keep, send, send_queries = project(
        activations, out_grads, proj_in.T, proj_out.T, queries
    )
    other = swapped(send, "query", 1)
    near_queries = swapped(send_queries, "dp", 1)
    distance = 2
    while distance < query_count:
        keep = add(keep, other)
        other = swapped(keep, "query", distance)
        distance *= 2
    own = add_to_payload(keep, other, weight)
    own_other = swapped(own, "query", 1)
    others = [swapped(own, "dp", k) for k in reversed(range(1, dp_count))]
    own_sum = own_tokens_sum(own, own_other, rank, row_count)
    queries_t, near_queries_t = turn_queries(queries, near_queries)
    mine = stack(others[::-1], (own_sum, queries_t))
    other = swapped(mine, "query", 1)
    shares = score_shares(
        own, own_other, mine, other, queries_t, near_queries_t, rank, row_count
    )
    arrived = [swapped(shares[k], "dp", k) for k in reversed(range(1, dp_count))]
    hessian = hessian_rows(mine, other, own_sum, rank, row_count)
    return hessian, finish_scores(own, [shares[0]] + arrived[::-1])


def power_of_two(count):
    return count & (count - 1) == 0


def per_device(activations, *others):
    rank = others[1].shape[1]
    dp_count, query_count = lax.axis_size("dp"), lax.axis_size("query")
    pairs = min(dp_count, query_count) > 1 and power_of_two(dp_count) and power_of_two(query_count)
    if pairs and activations.shape[0] * dp_count <= rank * rank:
        return few_tokens(activations, *others)
    return many_tokens(activations, *others)


def solution(mesh):
    placed = (
        P(("groups", "dp"), "query"),
        P(("groups", "dp"), "query"),
        P("query", None),
        P("query", None),
        P(("groups", "dp"), "query"),
        P(("groups", "dp")),
        P(("groups", "dp")),
    )
    return jax.shard_map(
        per_device,
        mesh=mesh,
        in_specs=placed,
        out_specs=(P(("groups", "dp"), None), P(("groups", "dp"), "query")),
        check_vma=False,
    )
```

```python
import functools
import jax
import jax.numpy as jnp
from jax import lax
from jax.experimental import pallas as pl
from jax.experimental.pallas import tpu as pltpu
from jax.sharding import PartitionSpec as P


def kron_columns(grad_rows, act_rows, start, count):
    rank = grad_rows.shape[1]
    tokens_here = grad_rows.shape[0]
    grad_cols = lax.dynamic_slice_in_dim(grad_rows, start // rank, count // rank, 1)
    outer = grad_cols.astype(jnp.float32)[:, :, None] * act_rows.astype(jnp.float32)[:, None, :]
    return outer.reshape(tokens_here, count).astype(jnp.bfloat16)


def hessian_block(total, pieces, row_start, rows_own, col_start, col_count):
    grad_rows, act_rows, weights = pieces
    left = kron_columns(grad_rows, act_rows, row_start, rows_own)
    weighted = (weights.astype(jnp.float32)[:, None] * left.astype(jnp.float32)).astype(
        jnp.bfloat16
    )
    right = kron_columns(grad_rows, act_rows, col_start, col_count)
    return total + lax.dot_general(
        weighted, right, (((0,), (0,)), ((), ())), preferred_element_type=jnp.float32
    )


def fold_blocks(total, pieces, step_fn):
    count = pieces[0].shape[0]
    shaped = tuple((p.reshape((count // 512, 512) + p.shape[1:]) for p in pieces))

    def inner(carry, block):
        return (step_fn(carry, block), None)

    return lax.scan(inner, total, shaped)[0]


def split_parts(matrix):
    high_part = matrix.astype(jnp.bfloat16)
    first_rest = matrix - high_part.astype(jnp.float32)
    middle_part = first_rest.astype(jnp.bfloat16)
    low_part = (first_rest - middle_part.astype(jnp.float32)).astype(jnp.bfloat16)
    return (high_part, middle_part, low_part)


def many_tokens(activations, out_grads, proj_in, proj_out, queries, lengths, credit):
    tok_rows = activations.shape[0]
    seq_len = tok_rows // lengths.shape[0]
    dp_count = lax.axis_size("dp")
    query_count = lax.axis_size("query")
    dp_index = lax.axis_index("dp")
    query_index = lax.axis_index("query")
    part_act = jnp.dot(activations, proj_in, preferred_element_type=jnp.float32)
    part_grad = jnp.dot(out_grads, proj_out, preferred_element_type=jnp.float32)
    sum_act, sum_grad = lax.psum((part_act, part_grad), "query")
    act_proj = sum_act.astype(jnp.bfloat16)
    grad_proj = sum_grad.astype(jnp.bfloat16)
    rank = act_proj.shape[1]
    feat = rank * rank
    live = jnp.arange(seq_len, dtype=jnp.int32)[None, :] < lengths[:, None]
    weight = (credit[:, None].astype(jnp.float32) * live.astype(jnp.float32)).reshape(-1)
    mask = live.astype(jnp.float32).reshape(-1)
    weight_wire = weight.astype(jnp.bfloat16)
    rows_own = feat // dp_count
    row_start = dp_index * rows_own
    all_tokens = tok_rows * dp_count
    col_count = feat // query_count
    col_start = query_index * col_count
    owned = fold_blocks(
        jnp.zeros((rows_own, col_count), jnp.float32),
        (
            lax.all_gather(grad_proj, "dp", axis=0, tiled=True),
            lax.all_gather(act_proj, "dp", axis=0, tiled=True),
            lax.all_gather(weight_wire, "dp", axis=0, tiled=True),
        ),
        lambda carry, block: hessian_block(carry, block, row_start, rows_own, col_start, col_count),
    )
    hessian = lax.all_gather(owned, "query", axis=1, tiled=True) / all_tokens
    diagonal_block = lax.dynamic_slice_in_dim(hessian, row_start, rows_own, 1)
    level = lax.psum(jnp.trace(diagonal_block), "dp") / feat
    step = 1.1 * level
    high_part, middle_part, low_part = split_parts(hessian)
    piece = lax.all_gather(queries, "dp", axis=0, tiled=True)
    result = jnp.zeros(queries.shape, jnp.float32)
    for part_matrix in (low_part, middle_part, high_part):
        columns = part_matrix
        result = result + jnp.dot(columns, piece, preferred_element_type=jnp.float32)
    query_f = queries.astype(jnp.float32)
    precond = ((2.0 * query_f - (result + 0.1 * level * query_f) / step) / step).astype(
        jnp.bfloat16
    )
    local_features = kron_columns(grad_proj, act_proj, 0, feat)
    piece = lax.all_gather(precond, "dp", axis=0, tiled=True)
    columns = lax.slice_in_dim(local_features, 0, piece.shape[0], axis=1)
    scores = jnp.zeros((tok_rows, precond.shape[1]), jnp.float32) + jnp.dot(
        columns, piece, preferred_element_type=jnp.float32
    )
    return (hessian, (scores * mask[:, None]).astype(jnp.bfloat16))


MIB = 1024 * 1024
TILE = 256
NT = (((1,), (1,)), ((), ()))


def params(mib):
    return pltpu.CompilerParams(vmem_limit_bytes=int(mib * MIB))


def project_kernel(
    act, grad, pin, pout, query, keep_ref, send_ref, send_query, act_v, grad_v, pin_v, pout_v, query_v, sems
):
    chunk = act.shape[1]
    while grad.shape[1] % chunk:
        chunk //= 2
    spans = [pl.ds(c, chunk) for c in range(0, grad.shape[1], chunk)]
    copies = [pltpu.make_async_copy(s, d, sems.at[n]) for n, (s, d) in enumerate(((pin, pin_v), (act, act_v), (pout, pout_v)))]
    copies += [
        pltpu.make_async_copy(grad.at[:, span], grad_v.at[:, span], sems.at[3 + n])
        for n, span in enumerate(spans)
    ]
    half = send_query.shape[1]
    even = lax.rem(lax.axis_index("dp"), 2) == 0
    span = pl.ds(pl.multiple_of(jnp.where(even, half, 0), half), half)
    fetch = pltpu.make_async_copy(query.at[:, span], query_v, sems.at[len(copies)])
    fetch.start()
    for copy in copies:
        copy.start()
    copies[0].wait()
    copies[1].wait()
    part_act = lax.dot_general(pin_v[...], act_v[...], NT, preferred_element_type=jnp.float32)
    fetch.wait()
    hand_out = pltpu.make_async_copy(query_v, send_query, sems.at[len(copies)])
    hand_out.start()
    copies[2].wait()
    part_grad = jnp.zeros_like(part_act)
    for copy, span in zip(copies[3:], spans):
        copy.wait()
        part_grad += lax.dot_general(
            pout_v[:, span], grad_v[:, span], NT, preferred_element_type=jnp.float32
        )
    even = lax.rem(lax.axis_index("query"), 2) == 0
    keep_ref[...] = jnp.where(even, part_act, part_grad)
    send_ref[...] = jnp.where(even, part_grad, part_act)
    hand_out.wait()


def project(activations, out_grads, proj_in_t, proj_out_t, queries):
    tok, d_here = activations.shape
    f_here = out_grads.shape[1]
    rank = proj_in_t.shape[0]
    out = jax.ShapeDtypeStruct((rank, tok), jnp.float32)
    out_query = jax.ShapeDtypeStruct((queries.shape[0], queries.shape[1] // 2), queries.dtype)
    whole = pl.BlockSpec(memory_space=pltpu.VMEM)
    return pl.pallas_call(
        project_kernel,
        in_specs=[pl.BlockSpec(memory_space=pl.ANY)] * 5,
        out_specs=[whole, whole, pl.BlockSpec(memory_space=pl.ANY)],
        out_shape=[out, out, out_query],
        scratch_shapes=[
            pltpu.VMEM((tok, d_here), jnp.bfloat16),
            pltpu.VMEM((tok, f_here), jnp.bfloat16),
            pltpu.VMEM((rank, d_here), jnp.bfloat16),
            pltpu.VMEM((rank, f_here), jnp.bfloat16),
            pltpu.VMEM(out_query.shape, out_query.dtype),
            pltpu.SemaphoreType.DMA((4 + f_here // 128,)),
        ],
        compiler_params=params(53.75),
    )(activations, out_grads, proj_in_t, proj_out_t, queries)


def turn_kernel(query, near_query, out_ref, near_out_ref, query_v, sem):
    half = query_v.shape[1]
    odd = lax.rem(lax.axis_index("dp"), 2)
    span = pl.ds(pl.multiple_of(odd * half, half), half)
    fetch = pltpu.make_async_copy(query.at[:, span], query_v, sem)
    fetch.start()
    near_out_ref[...] = near_query[...].T
    fetch.wait()
    out_ref[...] = query_v[...].T


def turn_queries(queries, near_queries):
    rows, half = near_queries.shape
    out = jax.ShapeDtypeStruct((half, rows), queries.dtype)
    return pl.pallas_call(
        turn_kernel,
        in_specs=[pl.BlockSpec(memory_space=pl.ANY), pl.BlockSpec(memory_space=pltpu.VMEM)],
        out_shape=[out, out],
        scratch_shapes=[pltpu.VMEM((rows, half), queries.dtype), pltpu.SemaphoreType.DMA],
        compiler_params=params(30),
    )(queries, near_queries)


def add_kernel(one_ref, other_ref, out_ref):
    out_ref[...] = one_ref[...] + other_ref[...]


def add(one, other):
    return pl.pallas_call(
        add_kernel,
        out_shape=jax.ShapeDtypeStruct(one.shape, one.dtype),
        compiler_params=params(40),
    )(one, other)


def payload_kernel(one_ref, other_ref, weight_ref, out_ref):
    total = one_ref[...] + other_ref[...]
    weight = jnp.broadcast_to(weight_ref[...], (16, weight_ref.shape[1]))
    out_ref[...] = jnp.concatenate([total, weight], axis=0).astype(out_ref.dtype)


def add_to_payload(one, other, weight):
    rows, tok = one.shape
    return pl.pallas_call(
        payload_kernel,
        out_shape=jax.ShapeDtypeStruct((rows + 16, tok), jnp.bfloat16),
        compiler_params=params(40),
    )(one, other, weight)


def stack_kernel(_, __, *refs):
    parts, (out_ref, factors_ref) = refs[:-2], refs[-2:]
    for k, ref in enumerate(parts):
        out_ref[k] = ref[...]
        factors_ref[k] = ref[: factors_ref.shape[1]]


def stack(parts, rank, after):
    rows, tok = parts[0].shape
    whole = pl.BlockSpec(memory_space=pltpu.VMEM)
    return pl.pallas_call(
        stack_kernel,
        in_specs=[pl.BlockSpec(memory_space=pl.ANY)] * 2 + [whole] * len(parts),
        out_shape=[
            jax.ShapeDtypeStruct((len(parts), rows, tok), parts[0].dtype),
            jax.ShapeDtypeStruct((len(parts), rank, tok), parts[0].dtype),
        ],
        compiler_params=params(30),
    )(*after, *parts)


def lay_out_factors(blocks, factors, weights):
    rank = factors.shape[0] // 2
    here = pl.multiple_of(lax.rem(lax.axis_index("query"), 2) * rank, rank)
    there = pl.multiple_of(rank - here, rank)
    for k, (mine, other) in enumerate(blocks):
        span = slice(k * mine.shape[1], (k + 1) * mine.shape[1])
        factors[pl.ds(here, rank), span] = mine[:rank].astype(jnp.float32)
        factors[pl.ds(there, rank), span] = other[:rank].astype(jnp.float32)
        weights[:, span] = mine[rank:].astype(jnp.float32)[:1]


def block_pairs(mine, other):
    return [(mine.at[k], other.at[k]) for k in reversed(range(mine.shape[0]))]


def weigh_rows(first_row, end_row, row_count, factors, weights, weighted):
    rank = factors.shape[0] // 2
    act, weight = factors[:rank, :], weights[...]
    first = rank + lax.axis_index("dp") * row_count
    for i in range(first_row // rank, end_row // rank):
        left = (factors[pl.ds(first + i, 1), :] * act).astype(jnp.bfloat16)
        left = (weight * left.astype(jnp.float32)).astype(jnp.bfloat16)
        weighted[i * rank : (i + 1) * rank, :] = left


def range_scale(values):
    top = jnp.max(jnp.abs(values), keepdims=True)
    scale = jnp.ones_like(top)
    for low in (16, 48, 80, 112):
        scale = jnp.where(top > 2.0**low, 2.0 ** -min(low + 16, 126), scale)
        scale = jnp.where(top < 2.0**-low, 2.0 ** min(low + 16, 126), scale)
    return scale


def share_kernel(row_count, own, own_other, mine, other, query_ref, near_query_ref, *refs):
    factors, weights, features = refs[-3:]
    out_refs = refs[:-3]
    lay_out_factors([(own, own_other)] + block_pairs(mine, other), factors, weights)
    rank = factors.shape[0] // 2
    tokens = factors.shape[1]
    tok = tokens // len(out_refs)
    act = factors[:rank, :]
    plain = 0.0
    for near, queries in ((0, query_ref), (1, near_query_ref)):
        first = rank + (lax.axis_index("dp") ^ near) * row_count
        for i in range(row_count):
            row = factors[pl.ds(first + i, 1), :]
            features[near, i * rank : (i + 1) * rank, :] = (row * act).astype(jnp.bfloat16)
        plain += jnp.dot(queries[...], features[near], preferred_element_type=jnp.float32)
    weight = weights[...]
    live = weight > 0.0
    act = jnp.where(live, act, 0.0)
    grad = jnp.where(live, factors[rank:, :], 0.0)
    act_scale, grad_scale = range_scale(act), range_scale(grad)
    act, grad = act * act_scale, grad * grad_scale
    norms = jnp.sum(act * act, axis=0, keepdims=True) * jnp.sum(grad * grad, axis=0, keepdims=True)
    level = jnp.sum(weight * norms, axis=1, keepdims=True) / (tokens * rank * rank)
    step = 1.1 * level
    act_b, grad_b = act.astype(jnp.bfloat16), grad.astype(jnp.bfloat16)
    gram = jnp.dot(act.T.astype(jnp.bfloat16), act_b, preferred_element_type=jnp.float32) * jnp.dot(
        grad.T.astype(jnp.bfloat16), grad_b, preferred_element_type=jnp.float32
    )
    weighted = (plain * (weight * (1.0 / (tokens * step)))).astype(jnp.bfloat16)
    image = jnp.dot(weighted, gram.astype(jnp.bfloat16), preferred_element_type=jnp.float32)
    scale = act_scale * grad_scale
    share = ((2.0 - 0.1 / 1.1) * plain - image) * scale * (scale / step)
    for k, out_ref in enumerate(out_refs):
        out_ref[...] = share[:, k * tok : (k + 1) * tok].astype(jnp.bfloat16)


def score_shares(own, own_other, mine, other, queries_t, near_queries_t, rank, row_count):
    blocks, tok = mine.shape[0] + 1, mine.shape[2]
    count, rows = queries_t.shape
    out = jax.ShapeDtypeStruct((count, tok), jnp.bfloat16)
    return pl.pallas_call(
        functools.partial(share_kernel, row_count),
        out_shape=[out] * blocks,
        scratch_shapes=[
            pltpu.VMEM((2 * rank, tok * blocks), jnp.float32),
            pltpu.VMEM((1, tok * blocks), jnp.float32),
            pltpu.VMEM((2, rows, tok * blocks), jnp.bfloat16),
        ],
        compiler_params=params(30),
    )(own, own_other, mine, other, queries_t, near_queries_t)


def build_columns(first, act, factors, right):
    rank = act.shape[0]
    for i in range(right.shape[0] // rank):
        row = rank + first + i
        right[i * rank : (i + 1) * rank, :] = (factors[row : row + 1, :] * act).astype(jnp.bfloat16)


def own_kernel(row_count, col_count, own, own_other, out, factors, weights, weighted, *rights):
    rank = factors.shape[0] // 2
    cols = col_count * rank
    lay_out_factors([(own, own_other)], factors, weights)
    weigh_rows(0, weighted.shape[0], row_count, factors, weights, weighted)
    act = factors[:rank, :]
    build_columns(0, act, factors, rights[0])
    for step in range(rank // col_count):
        if (step + 1) * col_count < rank:
            build_columns((step + 1) * col_count, act, factors, rights[(step + 1) % 2])
        out[:, step * cols : (step + 1) * cols] = lax.dot_general(
            weighted[...], rights[step % 2][...], NT, preferred_element_type=jnp.float32
        )


def own_tokens_sum(own, own_other, rank, row_count, col_count=8):
    tok = own.shape[1]
    rows, cols = row_count * rank, col_count * rank
    return pl.pallas_call(
        functools.partial(own_kernel, row_count, col_count),
        out_shape=jax.ShapeDtypeStruct((rows, rank * rank), jnp.float32),
        scratch_shapes=[
            pltpu.VMEM((2 * rank, tok), jnp.float32),
            pltpu.VMEM((1, tok), jnp.float32),
            pltpu.VMEM((rows, tok), jnp.bfloat16),
            pltpu.VMEM((cols, tok), jnp.bfloat16),
            pltpu.VMEM((cols, tok), jnp.bfloat16),
        ],
        compiler_params=params(16),
    )(own, own_other)


def hessian_kernel(row_count, col_count, mine, other, own_sum, out, *scratch):
    factors, weights, weighted, rights = *scratch[:3], scratch[3:5]
    result, sems = scratch[5:]
    rank = factors.shape[0] // 2
    blocks = mine.shape[0]
    tokens = factors.shape[1] // blocks * (blocks + 1)
    rows, cols = row_count * rank, col_count * rank
    lay_out_factors(block_pairs(mine, other), factors, weights)
    act = factors[:rank, :]
    copies = []
    build_columns(0, act, factors, rights[0])
    for step in range(rank // col_count):
        if (step + 1) * col_count < rank:
            build_columns((step + 1) * col_count, act, factors, rights[(step + 1) % 2])
        for row in range(0, rows, TILE):
            if step == 0:
                weigh_rows(row, row + TILE, row_count, factors, weights, weighted)
            here = pl.ds(row, TILE), pl.ds(step * cols, cols)
            tile = lax.dot_general(
                weighted[row : row + TILE, :],
                rights[step % 2][...],
                NT,
                preferred_element_type=jnp.float32,
            )
            result[here] = (own_sum[here] + tile) * (1.0 / tokens)
            copy = pltpu.make_async_copy(result.at[here], out.at[here], sems.at[len(copies)])
            copy.start()
            copies.append(copy)
    for copy in copies:
        copy.wait()


def hessian_rows(mine, other, own_sum, rank, row_count, col_count=8):
    blocks, _, tok = mine.shape
    feat = rank * rank
    rows, cols = row_count * rank, col_count * rank
    return pl.pallas_call(
        functools.partial(hessian_kernel, row_count, col_count),
        out_specs=pl.BlockSpec(memory_space=pl.ANY),
        out_shape=jax.ShapeDtypeStruct((rows, feat), jnp.float32),
        scratch_shapes=[
            pltpu.VMEM((2 * rank, tok * blocks), jnp.float32),
            pltpu.VMEM((1, tok * blocks), jnp.float32),
            pltpu.VMEM((rows, tok * blocks), jnp.bfloat16),
            pltpu.VMEM((cols, tok * blocks), jnp.bfloat16),
            pltpu.VMEM((cols, tok * blocks), jnp.bfloat16),
            pltpu.VMEM((rows, feat), jnp.float32),
            pltpu.SemaphoreType.DMA((feat // cols * (rows // TILE),)),
        ],
        compiler_params=params(30),
    )(mine, other, own_sum)


def finish_kernel(payload_ref, *refs):
    shares, out_ref = refs[:-1], refs[-1]
    weight = payload_ref[...].astype(jnp.float32)[-1:]
    totals = []
    for near in range(2):
        total = shares[near][...].astype(jnp.float32)
        for ref in shares[near + 2 :: 2]:
            total = total + ref[...].astype(jnp.float32)
        totals.append(jnp.where(weight > 0.0, total, 0.0).T.astype(out_ref.dtype))
    even = lax.rem(lax.axis_index("dp"), 2) == 0
    half = totals[0].shape[1]
    out_ref[:, :half] = jnp.where(even, totals[0], totals[1])
    out_ref[:, half:] = jnp.where(even, totals[1], totals[0])


def finish_scores(payload, shares):
    half, tok = shares[0].shape
    return pl.pallas_call(
        finish_kernel,
        out_shape=jax.ShapeDtypeStruct((tok, 2 * half), jnp.bfloat16),
        compiler_params=params(40),
    )(payload, *shares)


def swapped(array, axis, distance):
    return lax.ppermute(array, axis, [(i, i ^ distance) for i in range(lax.axis_size(axis))])


def few_tokens(activations, out_grads, proj_in, proj_out, queries, lengths, credit):
    dp_count = lax.axis_size("dp")
    query_count = lax.axis_size("query")
    rank = proj_in.shape[1]
    row_count = rank // dp_count
    seq_len = activations.shape[0] // lengths.shape[0]
    live = jnp.arange(seq_len, dtype=jnp.int32)[None, :] < lengths[:, None]
    weight = jnp.where(live, credit[:, None], 0).astype(jnp.float32).reshape(1, -1)
    keep, send, send_queries = project(
        activations, out_grads, proj_in.T, proj_out.T, queries
    )
    other = swapped(send, "query", 1)
    near_queries = swapped(send_queries, "dp", 1)
    distance = 2
    while distance < query_count:
        keep = add(keep, other)
        other = swapped(keep, "query", distance)
        distance *= 2
    own = add_to_payload(keep, other, weight)
    own_other = swapped(own, "query", 1)
    others = [swapped(own, "dp", k) for k in reversed(range(1, dp_count))]
    own_sum = own_tokens_sum(own, own_other, rank, row_count)
    queries_t, near_queries_t = turn_queries(queries, near_queries)
    mine, factors = stack(others, rank, (own_sum, queries_t))
    other = swapped(factors, "query", 1)
    shares = score_shares(
        own, own_other, mine, other, queries_t, near_queries_t, rank, row_count
    )
    arrived = [swapped(shares[k], "dp", k) for k in reversed(range(1, dp_count))]
    hessian = hessian_rows(mine, other, own_sum, rank, row_count)
    return hessian, finish_scores(own, [shares[0]] + arrived[::-1])


def power_of_two(count):
    return count & (count - 1) == 0


def per_device(activations, *others):
    rank = others[1].shape[1]
    dp_count, query_count = lax.axis_size("dp"), lax.axis_size("query")
    pairs = min(dp_count, query_count) > 1 and power_of_two(dp_count) and power_of_two(query_count)
    if pairs and activations.shape[0] * dp_count <= rank * rank:
        return few_tokens(activations, *others)
    return many_tokens(activations, *others)


def solution(mesh):
    placed = (
        P(("groups", "dp"), "query"),
        P(("groups", "dp"), "query"),
        P("query", None),
        P("query", None),
        P(("groups", "dp"), "query"),
        P(("groups", "dp")),
        P(("groups", "dp")),
    )
    return jax.shard_map(
        per_device,
        mesh=mesh,
        in_specs=placed,
        out_specs=(P(("groups", "dp"), None), P(("groups", "dp"), "query")),
        check_vma=False,
    )
```

```python
import functools
import jax
import jax.numpy as jnp
from jax import lax
from jax.experimental import pallas as pl
from jax.experimental.pallas import tpu as pltpu
from jax.sharding import PartitionSpec as P


def kron_columns(grad_rows, act_rows, start, count):
    rank = grad_rows.shape[1]
    tokens_here = grad_rows.shape[0]
    grad_cols = lax.dynamic_slice_in_dim(grad_rows, start // rank, count // rank, 1)
    outer = grad_cols.astype(jnp.float32)[:, :, None] * act_rows.astype(jnp.float32)[:, None, :]
    return outer.reshape(tokens_here, count).astype(jnp.bfloat16)


def hessian_block(total, pieces, row_start, rows_own, col_start, col_count):
    grad_rows, act_rows, weights = pieces
    left = kron_columns(grad_rows, act_rows, row_start, rows_own)
    weighted = (weights.astype(jnp.float32)[:, None] * left.astype(jnp.float32)).astype(
        jnp.bfloat16
    )
    right = kron_columns(grad_rows, act_rows, col_start, col_count)
    return total + lax.dot_general(
        weighted, right, (((0,), (0,)), ((), ())), preferred_element_type=jnp.float32
    )


def fold_blocks(total, pieces, step_fn):
    count = pieces[0].shape[0]
    shaped = tuple((p.reshape((count // 512, 512) + p.shape[1:]) for p in pieces))

    def inner(carry, block):
        return (step_fn(carry, block), None)

    return lax.scan(inner, total, shaped)[0]


def split_parts(matrix):
    high_part = matrix.astype(jnp.bfloat16)
    first_rest = matrix - high_part.astype(jnp.float32)
    middle_part = first_rest.astype(jnp.bfloat16)
    low_part = (first_rest - middle_part.astype(jnp.float32)).astype(jnp.bfloat16)
    return (high_part, middle_part, low_part)


def many_tokens(activations, out_grads, proj_in, proj_out, queries, lengths, credit):
    tok_rows = activations.shape[0]
    seq_len = tok_rows // lengths.shape[0]
    dp_count = lax.axis_size("dp")
    query_count = lax.axis_size("query")
    dp_index = lax.axis_index("dp")
    query_index = lax.axis_index("query")
    part_act = jnp.dot(activations, proj_in, preferred_element_type=jnp.float32)
    part_grad = jnp.dot(out_grads, proj_out, preferred_element_type=jnp.float32)
    sum_act, sum_grad = lax.psum((part_act, part_grad), "query")
    act_proj = sum_act.astype(jnp.bfloat16)
    grad_proj = sum_grad.astype(jnp.bfloat16)
    rank = act_proj.shape[1]
    feat = rank * rank
    live = jnp.arange(seq_len, dtype=jnp.int32)[None, :] < lengths[:, None]
    weight = (credit[:, None].astype(jnp.float32) * live.astype(jnp.float32)).reshape(-1)
    mask = live.astype(jnp.float32).reshape(-1)
    weight_wire = weight.astype(jnp.bfloat16)
    rows_own = feat // dp_count
    row_start = dp_index * rows_own
    all_tokens = tok_rows * dp_count
    col_count = feat // query_count
    col_start = query_index * col_count
    owned = fold_blocks(
        jnp.zeros((rows_own, col_count), jnp.float32),
        (
            lax.all_gather(grad_proj, "dp", axis=0, tiled=True),
            lax.all_gather(act_proj, "dp", axis=0, tiled=True),
            lax.all_gather(weight_wire, "dp", axis=0, tiled=True),
        ),
        lambda carry, block: hessian_block(carry, block, row_start, rows_own, col_start, col_count),
    )
    hessian = lax.all_gather(owned, "query", axis=1, tiled=True) / all_tokens
    diagonal_block = lax.dynamic_slice_in_dim(hessian, row_start, rows_own, 1)
    level = lax.psum(jnp.trace(diagonal_block), "dp") / feat
    step = 1.1 * level
    high_part, middle_part, low_part = split_parts(hessian)
    piece = lax.all_gather(queries, "dp", axis=0, tiled=True)
    result = jnp.zeros(queries.shape, jnp.float32)
    for part_matrix in (low_part, middle_part, high_part):
        columns = part_matrix
        result = result + jnp.dot(columns, piece, preferred_element_type=jnp.float32)
    query_f = queries.astype(jnp.float32)
    precond = ((2.0 * query_f - (result + 0.1 * level * query_f) / step) / step).astype(
        jnp.bfloat16
    )
    local_features = kron_columns(grad_proj, act_proj, 0, feat)
    piece = lax.all_gather(precond, "dp", axis=0, tiled=True)
    columns = lax.slice_in_dim(local_features, 0, piece.shape[0], axis=1)
    scores = jnp.zeros((tok_rows, precond.shape[1]), jnp.float32) + jnp.dot(
        columns, piece, preferred_element_type=jnp.float32
    )
    return (hessian, (scores * mask[:, None]).astype(jnp.bfloat16))


MIB = 1024 * 1024
TILE = 256
NT = (((1,), (1,)), ((), ()))


def params(mib):
    return pltpu.CompilerParams(vmem_limit_bytes=int(mib * MIB))


def project_kernel(
    act, grad, pin, pout, query, keep_ref, send_ref, send_query, act_v, grad_v, pin_v, pout_v, query_v, sems
):
    chunk = act.shape[1]
    while grad.shape[1] % chunk:
        chunk //= 2
    spans = [pl.ds(c, chunk) for c in range(0, grad.shape[1], chunk)]
    copies = [pltpu.make_async_copy(s, d, sems.at[n]) for n, (s, d) in enumerate(((pin, pin_v), (act, act_v), (pout, pout_v)))]
    copies += [
        pltpu.make_async_copy(grad.at[:, span], grad_v.at[:, span], sems.at[3 + n])
        for n, span in enumerate(spans)
    ]
    half = send_query.shape[1]
    even = lax.rem(lax.axis_index("dp"), 2) == 0
    span = pl.ds(pl.multiple_of(jnp.where(even, half, 0), half), half)
    fetch = pltpu.make_async_copy(query.at[:, span], query_v, sems.at[len(copies)])
    fetch.start()
    for copy in copies:
        copy.start()
    copies[0].wait()
    copies[1].wait()
    part_act = lax.dot_general(act_v[...], pin_v[...], NT, preferred_element_type=jnp.float32)
    fetch.wait()
    hand_out = pltpu.make_async_copy(query_v, send_query, sems.at[len(copies)])
    hand_out.start()
    copies[2].wait()
    part_grad = jnp.zeros_like(part_act)
    for copy, span in zip(copies[3:], spans):
        copy.wait()
        part_grad += lax.dot_general(
            grad_v[:, span], pout_v[:, span], NT, preferred_element_type=jnp.float32
        )
    even = lax.rem(lax.axis_index("query"), 2) == 0
    keep_ref[...] = jnp.where(even, part_act, part_grad).T
    send_ref[...] = jnp.where(even, part_grad, part_act).T
    hand_out.wait()


def project(activations, out_grads, proj_in_t, proj_out_t, queries):
    tok, d_here = activations.shape
    f_here = out_grads.shape[1]
    rank = proj_in_t.shape[0]
    out = jax.ShapeDtypeStruct((rank, tok), jnp.float32)
    out_query = jax.ShapeDtypeStruct((queries.shape[0], queries.shape[1] // 2), queries.dtype)
    whole = pl.BlockSpec(memory_space=pltpu.VMEM)
    return pl.pallas_call(
        project_kernel,
        in_specs=[pl.BlockSpec(memory_space=pl.ANY)] * 5,
        out_specs=[whole, whole, pl.BlockSpec(memory_space=pl.ANY)],
        out_shape=[out, out, out_query],
        scratch_shapes=[
            pltpu.VMEM((tok, d_here), jnp.bfloat16),
            pltpu.VMEM((tok, f_here), jnp.bfloat16),
            pltpu.VMEM((rank, d_here), jnp.bfloat16),
            pltpu.VMEM((rank, f_here), jnp.bfloat16),
            pltpu.VMEM(out_query.shape, out_query.dtype),
            pltpu.SemaphoreType.DMA((4 + f_here // 128,)),
        ],
        compiler_params=params(53.75),
    )(activations, out_grads, proj_in_t, proj_out_t, queries)


def turn_kernel(query, near_query, out_ref, near_out_ref, query_v, sem):
    half = query_v.shape[1]
    odd = lax.rem(lax.axis_index("dp"), 2)
    span = pl.ds(pl.multiple_of(odd * half, half), half)
    fetch = pltpu.make_async_copy(query.at[:, span], query_v, sem)
    fetch.start()
    near_out_ref[...] = near_query[...].T
    fetch.wait()
    out_ref[...] = query_v[...].T


def turn_queries(queries, near_queries):
    rows, half = near_queries.shape
    out = jax.ShapeDtypeStruct((half, rows), queries.dtype)
    return pl.pallas_call(
        turn_kernel,
        in_specs=[pl.BlockSpec(memory_space=pl.ANY), pl.BlockSpec(memory_space=pltpu.VMEM)],
        out_shape=[out, out],
        scratch_shapes=[pltpu.VMEM((rows, half), queries.dtype), pltpu.SemaphoreType.DMA],
        compiler_params=params(30),
    )(queries, near_queries)


def add_kernel(one_ref, other_ref, out_ref):
    out_ref[...] = one_ref[...] + other_ref[...]


def add(one, other):
    return pl.pallas_call(
        add_kernel,
        out_shape=jax.ShapeDtypeStruct(one.shape, one.dtype),
        compiler_params=params(40),
    )(one, other)


def payload_kernel(one_ref, other_ref, weight_ref, out_ref):
    total = one_ref[...] + other_ref[...]
    weight = jnp.broadcast_to(weight_ref[...], (16, weight_ref.shape[1]))
    out_ref[...] = jnp.concatenate([total, weight], axis=0).astype(out_ref.dtype)


def add_to_payload(one, other, weight):
    rows, tok = one.shape
    return pl.pallas_call(
        payload_kernel,
        out_shape=jax.ShapeDtypeStruct((rows + 16, tok), jnp.bfloat16),
        compiler_params=params(40),
    )(one, other, weight)


def stack_kernel(_, __, *refs):
    parts, (out_ref, factors_ref) = refs[:-2], refs[-2:]
    for k, ref in enumerate(parts):
        out_ref[k] = ref[...]
        factors_ref[k] = ref[: factors_ref.shape[1]]


def stack(parts, rank, after):
    rows, tok = parts[0].shape
    whole = pl.BlockSpec(memory_space=pltpu.VMEM)
    return pl.pallas_call(
        stack_kernel,
        in_specs=[pl.BlockSpec(memory_space=pl.ANY)] * 2 + [whole] * len(parts),
        out_shape=[
            jax.ShapeDtypeStruct((len(parts), rows, tok), parts[0].dtype),
            jax.ShapeDtypeStruct((len(parts), rank, tok), parts[0].dtype),
        ],
        compiler_params=params(30),
    )(*after, *parts)


def lay_out_factors(blocks, factors, weights):
    rank = factors.shape[0] // 2
    here = pl.multiple_of(lax.rem(lax.axis_index("query"), 2) * rank, rank)
    there = pl.multiple_of(rank - here, rank)
    for k, (mine, other) in enumerate(blocks):
        span = slice(k * mine.shape[1], (k + 1) * mine.shape[1])
        factors[pl.ds(here, rank), span] = mine[:rank].astype(jnp.float32)
        factors[pl.ds(there, rank), span] = other[:rank].astype(jnp.float32)
        weights[:, span] = mine[rank:].astype(jnp.float32)[:1]


def block_pairs(mine, other):
    return [(mine.at[k], other.at[k]) for k in reversed(range(mine.shape[0]))]


def weigh_rows(first_row, end_row, row_count, factors, weights, weighted):
    rank = factors.shape[0] // 2
    act, weight = factors[:rank, :], weights[...]
    first = rank + lax.axis_index("dp") * row_count
    for i in range(first_row // rank, end_row // rank):
        left = (factors[pl.ds(first + i, 1), :] * act).astype(jnp.bfloat16)
        left = (weight * left.astype(jnp.float32)).astype(jnp.bfloat16)
        weighted[i * rank : (i + 1) * rank, :] = left


def range_scale(values):
    top = jnp.max(jnp.abs(values), keepdims=True)
    scale = jnp.ones_like(top)
    for low in (16, 48, 80, 112):
        scale = jnp.where(top > 2.0**low, 2.0 ** -min(low + 16, 126), scale)
        scale = jnp.where(top < 2.0**-low, 2.0 ** min(low + 16, 126), scale)
    return scale


def share_kernel(row_count, own, own_other, mine, other, query_ref, near_query_ref, *refs):
    factors, weights, features = refs[-3:]
    out_refs = refs[:-3]
    lay_out_factors([(own, own_other)] + block_pairs(mine, other), factors, weights)
    rank = factors.shape[0] // 2
    tokens = factors.shape[1]
    tok = tokens // len(out_refs)
    act = factors[:rank, :]
    plain = 0.0
    for near, queries in ((0, query_ref), (1, near_query_ref)):
        first = rank + (lax.axis_index("dp") ^ near) * row_count
        for i in range(row_count):
            row = factors[pl.ds(first + i, 1), :]
            features[near, i * rank : (i + 1) * rank, :] = (row * act).astype(jnp.bfloat16)
        plain += jnp.dot(queries[...], features[near], preferred_element_type=jnp.float32)
    weight = weights[...]
    live = weight > 0.0
    act = jnp.where(live, act, 0.0)
    grad = jnp.where(live, factors[rank:, :], 0.0)
    act_scale, grad_scale = range_scale(act), range_scale(grad)
    act, grad = act * act_scale, grad * grad_scale
    norms = jnp.sum(act * act, axis=0, keepdims=True) * jnp.sum(grad * grad, axis=0, keepdims=True)
    level = jnp.sum(weight * norms, axis=1, keepdims=True) / (tokens * rank * rank)
    step = 1.1 * level
    act_b, grad_b = act.astype(jnp.bfloat16), grad.astype(jnp.bfloat16)
    act_rows, grad_rows = act.T.astype(jnp.bfloat16), grad.T.astype(jnp.bfloat16)
    weighted = (plain * (weight * (1.0 / (tokens * step)))).astype(jnp.bfloat16)
    images = [0.0] * (tokens // TILE)
    for p in range(tokens // TILE):
        here = slice(p * TILE, (p + 1) * TILE)
        gram = jnp.dot(
            act_rows[here], act_b[:, p * TILE :], preferred_element_type=jnp.float32
        ) * jnp.dot(grad_rows[here], grad_b[:, p * TILE :], preferred_element_type=jnp.float32)
        gram = gram.astype(jnp.bfloat16)
        forward = jnp.dot(weighted[:, here], gram, preferred_element_type=jnp.float32)
        for q in range(p, tokens // TILE):
            images[q] += forward[:, (q - p) * TILE : (q - p + 1) * TILE]
        if p + 1 < tokens // TILE:
            images[p] += lax.dot_general(
                weighted[:, (p + 1) * TILE :],
                gram[:, TILE:],
                NT,
                preferred_element_type=jnp.float32,
            )
    image = jnp.concatenate(images, axis=1)
    scale = act_scale * grad_scale
    share = ((2.0 - 0.1 / 1.1) * plain - image) * scale * (scale / step)
    for k, out_ref in enumerate(out_refs):
        out_ref[...] = share[:, k * tok : (k + 1) * tok].astype(jnp.bfloat16)


def score_shares(own, own_other, mine, other, queries_t, near_queries_t, rank, row_count):
    blocks, tok = mine.shape[0] + 1, mine.shape[2]
    count, rows = queries_t.shape
    out = jax.ShapeDtypeStruct((count, tok), jnp.bfloat16)
    return pl.pallas_call(
        functools.partial(share_kernel, row_count),
        out_shape=[out] * blocks,
        scratch_shapes=[
            pltpu.VMEM((2 * rank, tok * blocks), jnp.float32),
            pltpu.VMEM((1, tok * blocks), jnp.float32),
            pltpu.VMEM((2, rows, tok * blocks), jnp.bfloat16),
        ],
        compiler_params=params(30),
    )(own, own_other, mine, other, queries_t, near_queries_t)


def build_columns(first, act, factors, right):
    rank = act.shape[0]
    for i in range(right.shape[0] // rank):
        row = rank + first + i
        right[i * rank : (i + 1) * rank, :] = (factors[row : row + 1, :] * act).astype(jnp.bfloat16)


def own_kernel(row_count, col_count, own, own_other, out, factors, weights, weighted, *rights):
    rank = factors.shape[0] // 2
    cols = col_count * rank
    lay_out_factors([(own, own_other)], factors, weights)
    weigh_rows(0, weighted.shape[0], row_count, factors, weights, weighted)
    act = factors[:rank, :]
    build_columns(0, act, factors, rights[0])
    for step in range(rank // col_count):
        if (step + 1) * col_count < rank:
            build_columns((step + 1) * col_count, act, factors, rights[(step + 1) % 2])
        out[:, step * cols : (step + 1) * cols] = lax.dot_general(
            weighted[...], rights[step % 2][...], NT, preferred_element_type=jnp.float32
        )


def own_tokens_sum(own, own_other, rank, row_count, col_count=8):
    tok = own.shape[1]
    rows, cols = row_count * rank, col_count * rank
    return pl.pallas_call(
        functools.partial(own_kernel, row_count, col_count),
        out_shape=jax.ShapeDtypeStruct((rows, rank * rank), jnp.float32),
        scratch_shapes=[
            pltpu.VMEM((2 * rank, tok), jnp.float32),
            pltpu.VMEM((1, tok), jnp.float32),
            pltpu.VMEM((rows, tok), jnp.bfloat16),
            pltpu.VMEM((cols, tok), jnp.bfloat16),
            pltpu.VMEM((cols, tok), jnp.bfloat16),
        ],
        compiler_params=params(16),
    )(own, own_other)


def hessian_kernel(row_count, col_count, mine, other, own_sum, out, *scratch):
    factors, weights, weighted, rights = *scratch[:3], scratch[3:5]
    result, sems = scratch[5:]
    rank = factors.shape[0] // 2
    blocks = mine.shape[0]
    tokens = factors.shape[1] // blocks * (blocks + 1)
    rows, cols = row_count * rank, col_count * rank
    lay_out_factors(block_pairs(mine, other), factors, weights)
    act = factors[:rank, :]
    copies = []
    build_columns(0, act, factors, rights[0])
    for step in range(rank // col_count):
        if (step + 1) * col_count < rank:
            build_columns((step + 1) * col_count, act, factors, rights[(step + 1) % 2])
        for row in range(0, rows, TILE):
            if step == 0:
                weigh_rows(row, row + TILE, row_count, factors, weights, weighted)
            here = pl.ds(row, TILE), pl.ds(step * cols, cols)
            tile = lax.dot_general(
                weighted[row : row + TILE, :],
                rights[step % 2][...],
                NT,
                preferred_element_type=jnp.float32,
            )
            result[here] = (own_sum[here] + tile) * (1.0 / tokens)
            copy = pltpu.make_async_copy(result.at[here], out.at[here], sems.at[len(copies)])
            copy.start()
            copies.append(copy)
    for copy in copies:
        copy.wait()


def hessian_rows(mine, other, own_sum, rank, row_count, col_count=8):
    blocks, _, tok = mine.shape
    feat = rank * rank
    rows, cols = row_count * rank, col_count * rank
    return pl.pallas_call(
        functools.partial(hessian_kernel, row_count, col_count),
        out_specs=pl.BlockSpec(memory_space=pl.ANY),
        out_shape=jax.ShapeDtypeStruct((rows, feat), jnp.float32),
        scratch_shapes=[
            pltpu.VMEM((2 * rank, tok * blocks), jnp.float32),
            pltpu.VMEM((1, tok * blocks), jnp.float32),
            pltpu.VMEM((rows, tok * blocks), jnp.bfloat16),
            pltpu.VMEM((cols, tok * blocks), jnp.bfloat16),
            pltpu.VMEM((cols, tok * blocks), jnp.bfloat16),
            pltpu.VMEM((rows, feat), jnp.float32),
            pltpu.SemaphoreType.DMA((feat // cols * (rows // TILE),)),
        ],
        compiler_params=params(30),
    )(mine, other, own_sum)


def finish_kernel(payload_ref, *refs):
    shares, out_ref = refs[:-1], refs[-1]
    weight = payload_ref[...].astype(jnp.float32)[-1:]
    totals = []
    for near in range(2):
        total = shares[near][...].astype(jnp.float32)
        for ref in shares[near + 2 :: 2]:
            total = total + ref[...].astype(jnp.float32)
        totals.append(jnp.where(weight > 0.0, total, 0.0).T.astype(out_ref.dtype))
    even = lax.rem(lax.axis_index("dp"), 2) == 0
    half = totals[0].shape[1]
    out_ref[:, :half] = jnp.where(even, totals[0], totals[1])
    out_ref[:, half:] = jnp.where(even, totals[1], totals[0])


def finish_scores(payload, shares):
    half, tok = shares[0].shape
    return pl.pallas_call(
        finish_kernel,
        out_shape=jax.ShapeDtypeStruct((tok, 2 * half), jnp.bfloat16),
        compiler_params=params(40),
    )(payload, *shares)


def swapped(array, axis, distance):
    return lax.ppermute(array, axis, [(i, i ^ distance) for i in range(lax.axis_size(axis))])


def few_tokens(activations, out_grads, proj_in, proj_out, queries, lengths, credit):
    dp_count = lax.axis_size("dp")
    query_count = lax.axis_size("query")
    rank = proj_in.shape[1]
    row_count = rank // dp_count
    seq_len = activations.shape[0] // lengths.shape[0]
    live = jnp.arange(seq_len, dtype=jnp.int32)[None, :] < lengths[:, None]
    weight = jnp.where(live, credit[:, None], 0).astype(jnp.float32).reshape(1, -1)
    keep, send, send_queries = project(
        activations, out_grads, proj_in.T, proj_out.T, queries
    )
    other = swapped(send, "query", 1)
    near_queries = swapped(send_queries, "dp", 1)
    distance = 2
    while distance < query_count:
        keep = add(keep, other)
        other = swapped(keep, "query", distance)
        distance *= 2
    own = add_to_payload(keep, other, weight)
    own_other = swapped(own, "query", 1)
    others = [swapped(own, "dp", k) for k in reversed(range(1, dp_count))]
    own_sum = own_tokens_sum(own, own_other, rank, row_count)
    queries_t, near_queries_t = turn_queries(queries, near_queries)
    mine, factors = stack(others, rank, (own_sum, queries_t))
    other = swapped(factors, "query", 1)
    shares = score_shares(
        own, own_other, mine, other, queries_t, near_queries_t, rank, row_count
    )
    arrived = [swapped(shares[k], "dp", k) for k in reversed(range(1, dp_count))]
    hessian = hessian_rows(mine, other, own_sum, rank, row_count)
    return hessian, finish_scores(own, [shares[0]] + arrived[::-1])


def power_of_two(count):
    return count & (count - 1) == 0


def per_device(activations, *others):
    rank = others[1].shape[1]
    dp_count, query_count = lax.axis_size("dp"), lax.axis_size("query")
    pairs = min(dp_count, query_count) > 1 and power_of_two(dp_count) and power_of_two(query_count)
    if pairs and activations.shape[0] * dp_count <= rank * rank:
        return few_tokens(activations, *others)
    return many_tokens(activations, *others)


def solution(mesh):
    placed = (
        P(("groups", "dp"), "query"),
        P(("groups", "dp"), "query"),
        P("query", None),
        P("query", None),
        P(("groups", "dp"), "query"),
        P(("groups", "dp")),
        P(("groups", "dp")),
    )
    return jax.shard_map(
        per_device,
        mesh=mesh,
        in_specs=placed,
        out_specs=(P(("groups", "dp"), None), P(("groups", "dp"), "query")),
        check_vma=False,
    )
```

```python
import functools
import jax
import jax.numpy as jnp
from jax import lax
from jax.experimental import pallas as pl
from jax.experimental.pallas import tpu as pltpu
from jax.sharding import PartitionSpec as P


def kron_columns(grad_rows, act_rows, start, count):
    rank = grad_rows.shape[1]
    tokens_here = grad_rows.shape[0]
    grad_cols = lax.dynamic_slice_in_dim(grad_rows, start // rank, count // rank, 1)
    outer = grad_cols.astype(jnp.float32)[:, :, None] * act_rows.astype(jnp.float32)[:, None, :]
    return outer.reshape(tokens_here, count).astype(jnp.bfloat16)


def hessian_block(total, pieces, row_start, rows_own, col_start, col_count):
    grad_rows, act_rows, weights = pieces
    left = kron_columns(grad_rows, act_rows, row_start, rows_own)
    weighted = (weights.astype(jnp.float32)[:, None] * left.astype(jnp.float32)).astype(
        jnp.bfloat16
    )
    right = kron_columns(grad_rows, act_rows, col_start, col_count)
    return total + lax.dot_general(
        weighted, right, (((0,), (0,)), ((), ())), preferred_element_type=jnp.float32
    )


def fold_blocks(total, pieces, step_fn):
    count = pieces[0].shape[0]
    shaped = tuple((p.reshape((count // 512, 512) + p.shape[1:]) for p in pieces))

    def inner(carry, block):
        return (step_fn(carry, block), None)

    return lax.scan(inner, total, shaped)[0]


def split_parts(matrix):
    high_part = matrix.astype(jnp.bfloat16)
    first_rest = matrix - high_part.astype(jnp.float32)
    middle_part = first_rest.astype(jnp.bfloat16)
    low_part = (first_rest - middle_part.astype(jnp.float32)).astype(jnp.bfloat16)
    return (high_part, middle_part, low_part)


def many_tokens(activations, out_grads, proj_in, proj_out, queries, lengths, credit):
    tok_rows = activations.shape[0]
    seq_len = tok_rows // lengths.shape[0]
    dp_count = lax.axis_size("dp")
    query_count = lax.axis_size("query")
    dp_index = lax.axis_index("dp")
    query_index = lax.axis_index("query")
    part_act = jnp.dot(activations, proj_in, preferred_element_type=jnp.float32)
    part_grad = jnp.dot(out_grads, proj_out, preferred_element_type=jnp.float32)
    sum_act, sum_grad = lax.psum((part_act, part_grad), "query")
    act_proj = sum_act.astype(jnp.bfloat16)
    grad_proj = sum_grad.astype(jnp.bfloat16)
    rank = act_proj.shape[1]
    feat = rank * rank
    live = jnp.arange(seq_len, dtype=jnp.int32)[None, :] < lengths[:, None]
    weight = (credit[:, None].astype(jnp.float32) * live.astype(jnp.float32)).reshape(-1)
    mask = live.astype(jnp.float32).reshape(-1)
    weight_wire = weight.astype(jnp.bfloat16)
    rows_own = feat // dp_count
    row_start = dp_index * rows_own
    all_tokens = tok_rows * dp_count
    col_count = feat // query_count
    col_start = query_index * col_count
    owned = fold_blocks(
        jnp.zeros((rows_own, col_count), jnp.float32),
        (
            lax.all_gather(grad_proj, "dp", axis=0, tiled=True),
            lax.all_gather(act_proj, "dp", axis=0, tiled=True),
            lax.all_gather(weight_wire, "dp", axis=0, tiled=True),
        ),
        lambda carry, block: hessian_block(carry, block, row_start, rows_own, col_start, col_count),
    )
    hessian = lax.all_gather(owned, "query", axis=1, tiled=True) / all_tokens
    diagonal_block = lax.dynamic_slice_in_dim(hessian, row_start, rows_own, 1)
    level = lax.psum(jnp.trace(diagonal_block), "dp") / feat
    step = 1.1 * level
    high_part, middle_part, low_part = split_parts(hessian)
    piece = lax.all_gather(queries, "dp", axis=0, tiled=True)
    result = jnp.zeros(queries.shape, jnp.float32)
    for part_matrix in (low_part, middle_part, high_part):
        columns = part_matrix
        result = result + jnp.dot(columns, piece, preferred_element_type=jnp.float32)
    query_f = queries.astype(jnp.float32)
    precond = ((2.0 * query_f - (result + 0.1 * level * query_f) / step) / step).astype(
        jnp.bfloat16
    )
    local_features = kron_columns(grad_proj, act_proj, 0, feat)
    piece = lax.all_gather(precond, "dp", axis=0, tiled=True)
    columns = lax.slice_in_dim(local_features, 0, piece.shape[0], axis=1)
    scores = jnp.zeros((tok_rows, precond.shape[1]), jnp.float32) + jnp.dot(
        columns, piece, preferred_element_type=jnp.float32
    )
    return (hessian, (scores * mask[:, None]).astype(jnp.bfloat16))


MIB = 1024 * 1024
TILE = 256
NT = (((1,), (1,)), ((), ()))


def params(mib):
    return pltpu.CompilerParams(vmem_limit_bytes=int(mib * MIB))


def project_kernel(act, grad, pin, pout, keep_ref, send_ref, act_v, grad_v, pin_v, pout_v, sems):
    chunk = act.shape[1]
    while grad.shape[1] % chunk:
        chunk //= 2
    spans = [pl.ds(c, chunk) for c in range(0, grad.shape[1], chunk)]
    copies = [pltpu.make_async_copy(s, d, sems.at[n]) for n, (s, d) in enumerate(((pin, pin_v), (act, act_v), (pout, pout_v)))]
    copies += [
        pltpu.make_async_copy(grad.at[:, span], grad_v.at[:, span], sems.at[3 + n])
        for n, span in enumerate(spans)
    ]
    for copy in copies:
        copy.start()
    copies[0].wait()
    copies[1].wait()
    part_act = lax.dot_general(pin_v[...], act_v[...], NT, preferred_element_type=jnp.float32)
    copies[2].wait()
    part_grad = jnp.zeros_like(part_act)
    for copy, span in zip(copies[3:], spans):
        copy.wait()
        part_grad += lax.dot_general(
            pout_v[:, span], grad_v[:, span], NT, preferred_element_type=jnp.float32
        )
    even = lax.rem(lax.axis_index("query"), 2) == 0
    keep_ref[...] = jnp.where(even, part_act, part_grad)
    send_ref[...] = jnp.where(even, part_grad, part_act)


def project(activations, out_grads, proj_in_t, proj_out_t):
    tok, d_here = activations.shape
    f_here = out_grads.shape[1]
    rank = proj_in_t.shape[0]
    out = jax.ShapeDtypeStruct((rank, tok), jnp.float32)
    return pl.pallas_call(
        project_kernel,
        in_specs=[pl.BlockSpec(memory_space=pl.ANY)] * 4,
        out_shape=[out, out],
        scratch_shapes=[
            pltpu.VMEM((tok, d_here), jnp.bfloat16),
            pltpu.VMEM((tok, f_here), jnp.bfloat16),
            pltpu.VMEM((rank, d_here), jnp.bfloat16),
            pltpu.VMEM((rank, f_here), jnp.bfloat16),
            pltpu.SemaphoreType.DMA((3 + f_here // 128,)),
        ],
        compiler_params=params(53.75),
    )(activations, out_grads, proj_in_t, proj_out_t)


def turn_kernel(query, near_query, out_ref, near_out_ref):
    out_ref[...] = query[...].T
    near_out_ref[...] = near_query[...].T


def turn_queries(queries, near_queries):
    out = jax.ShapeDtypeStruct(queries.shape[::-1], queries.dtype)
    return pl.pallas_call(
        turn_kernel,
        out_shape=[out, out],
        compiler_params=params(30),
    )(queries, near_queries)


def add_kernel(one_ref, other_ref, out_ref):
    out_ref[...] = one_ref[...] + other_ref[...]


def add(one, other):
    return pl.pallas_call(
        add_kernel,
        out_shape=jax.ShapeDtypeStruct(one.shape, one.dtype),
        compiler_params=params(40),
    )(one, other)


def payload_kernel(one_ref, other_ref, weight_ref, out_ref):
    total = one_ref[...] + other_ref[...]
    weight = jnp.broadcast_to(weight_ref[...], (16, weight_ref.shape[1]))
    out_ref[...] = jnp.concatenate([total, weight], axis=0).astype(out_ref.dtype)


def add_to_payload(one, other, weight):
    rows, tok = one.shape
    return pl.pallas_call(
        payload_kernel,
        out_shape=jax.ShapeDtypeStruct((rows + 16, tok), jnp.bfloat16),
        compiler_params=params(40),
    )(one, other, weight)


def stack_kernel(_, __, *refs):
    parts, (out_ref, factors_ref) = refs[:-2], refs[-2:]
    for k, ref in enumerate(parts):
        out_ref[k] = ref[...]
        factors_ref[k] = ref[: factors_ref.shape[1]]


def stack(parts, rank, after):
    rows, tok = parts[0].shape
    whole = pl.BlockSpec(memory_space=pltpu.VMEM)
    return pl.pallas_call(
        stack_kernel,
        in_specs=[pl.BlockSpec(memory_space=pl.ANY)] * 2 + [whole] * len(parts),
        out_shape=[
            jax.ShapeDtypeStruct((len(parts), rows, tok), parts[0].dtype),
            jax.ShapeDtypeStruct((len(parts), rank, tok), parts[0].dtype),
        ],
        compiler_params=params(30),
    )(*after, *parts)


def lay_out_factors(blocks, factors, weights):
    rank = factors.shape[0] // 2
    here = pl.multiple_of(lax.rem(lax.axis_index("query"), 2) * rank, rank)
    there = pl.multiple_of(rank - here, rank)
    for k, (mine, other) in enumerate(blocks):
        span = slice(k * mine.shape[1], (k + 1) * mine.shape[1])
        factors[pl.ds(here, rank), span] = mine[:rank].astype(jnp.float32)
        factors[pl.ds(there, rank), span] = other[:rank].astype(jnp.float32)
        weights[:, span] = mine[rank:].astype(jnp.float32)[:1]


def block_pairs(mine, other):
    return [(mine.at[k], other.at[k]) for k in reversed(range(mine.shape[0]))]


def weigh_rows(first_row, end_row, row_count, factors, weights, weighted):
    rank = factors.shape[0] // 2
    act, weight = factors[:rank, :], weights[...]
    first = rank + lax.axis_index("dp") * row_count
    for i in range(first_row // rank, end_row // rank):
        left = (factors[pl.ds(first + i, 1), :] * act).astype(jnp.bfloat16)
        left = (weight * left.astype(jnp.float32)).astype(jnp.bfloat16)
        weighted[i * rank : (i + 1) * rank, :] = left


def range_scale(values):
    top = jnp.max(jnp.abs(values), keepdims=True)
    scale = jnp.ones_like(top)
    for low in (16, 48, 80, 112):
        scale = jnp.where(top > 2.0**low, 2.0 ** -min(low + 16, 126), scale)
        scale = jnp.where(top < 2.0**-low, 2.0 ** min(low + 16, 126), scale)
    return scale


def share_kernel(row_count, own, own_other, mine, other, query_ref, near_query_ref, *refs):
    factors, weights, features, gram = refs[-4:]
    out_refs = refs[:-4]
    lay_out_factors([(own, own_other)] + block_pairs(mine, other), factors, weights)
    rank = factors.shape[0] // 2
    tokens = factors.shape[1]
    tok = own.shape[1]
    act = factors[:rank, :]
    plain = 0.0
    for near, queries in enumerate((query_ref, near_query_ref)):
        first = rank + (lax.axis_index("dp") ^ near) * row_count
        for i in range(row_count):
            row = factors[pl.ds(first + i, 1), :]
            features[near, i * rank : (i + 1) * rank, :] = (row * act).astype(jnp.bfloat16)
        plain += jnp.dot(queries[...], features[near], preferred_element_type=jnp.float32)
    weight = weights[...]
    live = weight > 0.0
    act = jnp.where(live, act, 0.0)
    grad = jnp.where(live, factors[rank:, :], 0.0)
    act_scale, grad_scale = range_scale(act), range_scale(grad)
    act, grad = act * act_scale, grad * grad_scale
    norms = jnp.sum(act * act, axis=0, keepdims=True) * jnp.sum(grad * grad, axis=0, keepdims=True)
    level = jnp.sum(weight * norms, axis=1, keepdims=True) / (tokens * rank * rank)
    step = 1.1 * level
    act_b, grad_b = act.astype(jnp.bfloat16), grad.astype(jnp.bfloat16)
    act_rows, grad_rows = act.T.astype(jnp.bfloat16), grad.T.astype(jnp.bfloat16)
    weighted = (plain * (weight * (1.0 / (tokens * step)))).astype(jnp.bfloat16)
    scale = act_scale * grad_scale
    for n, out_ref in enumerate(out_refs):
        block = slice(2 * n * tok, (2 * n + 1) * tok)
        for row in range(0, tokens, TILE // 2):
            here = slice(row, row + TILE // 2)
            tile = jnp.dot(act_rows[here], act_b[:, block], preferred_element_type=jnp.float32)
            tile *= jnp.dot(grad_rows[here], grad_b[:, block], preferred_element_type=jnp.float32)
            gram[n, here, :] = tile.astype(jnp.bfloat16)
        image = jnp.dot(weighted, gram[n], preferred_element_type=jnp.float32)
        share = ((2.0 - 0.1 / 1.1) * plain[:, block] - image) * scale * (scale / step)
        out_ref[...] = share.astype(out_ref.dtype)


def score_shares(own, own_other, mine, other, queries_t, near_queries_t, rank, row_count):
    blocks, tok = mine.shape[0] + 1, mine.shape[2]
    count, rows = queries_t.shape
    return pl.pallas_call(
        functools.partial(share_kernel, row_count),
        out_shape=[
            jax.ShapeDtypeStruct((count, tok), jnp.bfloat16 if k else jnp.float32)
            for k in range(0, blocks, 2)
        ],
        scratch_shapes=[
            pltpu.VMEM((2 * rank, tok * blocks), jnp.float32),
            pltpu.VMEM((1, tok * blocks), jnp.float32),
            pltpu.VMEM((2, rows, tok * blocks), jnp.bfloat16),
            pltpu.VMEM((blocks // 2, tok * blocks, tok), jnp.bfloat16),
        ],
        compiler_params=params(30),
    )(own, own_other, mine, other, queries_t, near_queries_t)


def build_columns(first, act, factors, right):
    rank = act.shape[0]
    for i in range(right.shape[0] // rank):
        row = rank + first + i
        right[i * rank : (i + 1) * rank, :] = (factors[row : row + 1, :] * act).astype(jnp.bfloat16)


def own_kernel(row_count, col_count, own, own_other, out, factors, weights, weighted, *rights):
    rank = factors.shape[0] // 2
    cols = col_count * rank
    lay_out_factors([(own, own_other)], factors, weights)
    weigh_rows(0, weighted.shape[0], row_count, factors, weights, weighted)
    act = factors[:rank, :]
    build_columns(0, act, factors, rights[0])
    for step in range(rank // col_count):
        if (step + 1) * col_count < rank:
            build_columns((step + 1) * col_count, act, factors, rights[(step + 1) % 2])
        out[:, step * cols : (step + 1) * cols] = lax.dot_general(
            weighted[...], rights[step % 2][...], NT, preferred_element_type=jnp.float32
        )


def own_tokens_sum(own, own_other, rank, row_count, col_count=8):
    tok = own.shape[1]
    rows, cols = row_count * rank, col_count * rank
    return pl.pallas_call(
        functools.partial(own_kernel, row_count, col_count),
        out_shape=jax.ShapeDtypeStruct((rows, rank * rank), jnp.float32),
        scratch_shapes=[
            pltpu.VMEM((2 * rank, tok), jnp.float32),
            pltpu.VMEM((1, tok), jnp.float32),
            pltpu.VMEM((rows, tok), jnp.bfloat16),
            pltpu.VMEM((cols, tok), jnp.bfloat16),
            pltpu.VMEM((cols, tok), jnp.bfloat16),
        ],
        compiler_params=params(16),
    )(own, own_other)


def hessian_kernel(row_count, col_count, mine, other, own_sum, out, *scratch):
    factors, weights, weighted, rights = *scratch[:3], scratch[3:5]
    result, sems = scratch[5:]
    rank = factors.shape[0] // 2
    blocks = mine.shape[0]
    tokens = factors.shape[1] // blocks * (blocks + 1)
    rows, cols = row_count * rank, col_count * rank
    lay_out_factors(block_pairs(mine, other), factors, weights)
    act = factors[:rank, :]
    copies = []
    build_columns(0, act, factors, rights[0])
    for step in range(rank // col_count):
        if (step + 1) * col_count < rank:
            build_columns((step + 1) * col_count, act, factors, rights[(step + 1) % 2])
        for row in range(0, rows, TILE):
            if step == 0:
                weigh_rows(row, row + TILE, row_count, factors, weights, weighted)
            here = pl.ds(row, TILE), pl.ds(step * cols, cols)
            tile = lax.dot_general(
                weighted[row : row + TILE, :],
                rights[step % 2][...],
                NT,
                preferred_element_type=jnp.float32,
            )
            result[here] = (own_sum[here] + tile) * (1.0 / tokens)
            copy = pltpu.make_async_copy(result.at[here], out.at[here], sems.at[len(copies)])
            copy.start()
            copies.append(copy)
    for copy in copies:
        copy.wait()


def hessian_rows(mine, other, own_sum, rank, row_count, col_count=8):
    blocks, _, tok = mine.shape
    feat = rank * rank
    rows, cols = row_count * rank, col_count * rank
    return pl.pallas_call(
        functools.partial(hessian_kernel, row_count, col_count),
        out_specs=pl.BlockSpec(memory_space=pl.ANY),
        out_shape=jax.ShapeDtypeStruct((rows, feat), jnp.float32),
        scratch_shapes=[
            pltpu.VMEM((2 * rank, tok * blocks), jnp.float32),
            pltpu.VMEM((1, tok * blocks), jnp.float32),
            pltpu.VMEM((rows, tok * blocks), jnp.bfloat16),
            pltpu.VMEM((cols, tok * blocks), jnp.bfloat16),
            pltpu.VMEM((cols, tok * blocks), jnp.bfloat16),
            pltpu.VMEM((rows, feat), jnp.float32),
            pltpu.SemaphoreType.DMA((feat // cols * (rows // TILE),)),
        ],
        compiler_params=params(30),
    )(mine, other, own_sum)


def finish_kernel(payload_ref, *refs):
    shares, out_ref = refs[:-1], refs[-1]
    total = shares[0][...]
    for ref in shares[1:]:
        total = total + ref[...].astype(jnp.float32)
    weight = payload_ref[...].astype(jnp.float32)[-1:]
    out_ref[...] = jnp.where(weight > 0.0, total, 0.0).T.astype(out_ref.dtype)


def finish_scores(payload, shares):
    count, tok = shares[0].shape
    return pl.pallas_call(
        finish_kernel,
        out_shape=jax.ShapeDtypeStruct((tok, count), jnp.bfloat16),
        compiler_params=params(40),
    )(payload, *shares)


def swapped(array, axis, distance):
    return lax.ppermute(array, axis, [(i, i ^ distance) for i in range(lax.axis_size(axis))])


def few_tokens(activations, out_grads, proj_in, proj_out, queries, lengths, credit):
    dp_count = lax.axis_size("dp")
    query_count = lax.axis_size("query")
    rank = proj_in.shape[1]
    row_count = rank // dp_count
    seq_len = activations.shape[0] // lengths.shape[0]
    live = jnp.arange(seq_len, dtype=jnp.int32)[None, :] < lengths[:, None]
    weight = jnp.where(live, credit[:, None], 0).astype(jnp.float32).reshape(1, -1)
    near_queries = swapped(queries, "dp", 1)
    keep, send = project(activations, out_grads, proj_in.T, proj_out.T)
    other = swapped(send, "query", 1)
    distance = 2
    while distance < query_count:
        keep = add(keep, other)
        other = swapped(keep, "query", distance)
        distance *= 2
    own = add_to_payload(keep, other, weight)
    own_other = swapped(own, "query", 1)
    others = [swapped(own, "dp", k) for k in reversed(range(1, dp_count))]
    own_sum = own_tokens_sum(own, own_other, rank, row_count)
    queries_t, near_queries_t = turn_queries(queries, near_queries)
    mine, factors = stack(others, rank, (own_sum, queries_t))
    other = swapped(factors, "query", 1)
    shares = score_shares(
        own, own_other, mine, other, queries_t, near_queries_t, rank, row_count
    )
    arrived = [swapped(share, "dp", 2 * n) for n, share in enumerate(shares) if n]
    hessian = hessian_rows(mine, other, own_sum, rank, row_count)
    return hessian, finish_scores(own, [shares[0]] + arrived)


def power_of_two(count):
    return count & (count - 1) == 0


def per_device(activations, *others):
    rank = others[1].shape[1]
    dp_count, query_count = lax.axis_size("dp"), lax.axis_size("query")
    pairs = min(dp_count, query_count) > 1 and power_of_two(dp_count) and power_of_two(query_count)
    if pairs and activations.shape[0] * dp_count <= rank * rank:
        return few_tokens(activations, *others)
    return many_tokens(activations, *others)


def solution(mesh):
    placed = (
        P(("groups", "dp"), "query"),
        P(("groups", "dp"), "query"),
        P("query", None),
        P("query", None),
        P(("groups", "dp"), "query"),
        P(("groups", "dp")),
        P(("groups", "dp")),
    )
    return jax.shard_map(
        per_device,
        mesh=mesh,
        in_specs=placed,
        out_specs=(P(("groups", "dp"), None), P(("groups", "dp"), "query")),
        check_vma=False,
    )
```

```python
import functools
import jax
import jax.numpy as jnp
from jax import lax
from jax.experimental import pallas as pl
from jax.experimental.pallas import tpu as pltpu
from jax.sharding import PartitionSpec as P


def kron_columns(grad_rows, act_rows, start, count):
    rank = grad_rows.shape[1]
    tokens_here = grad_rows.shape[0]
    grad_cols = lax.dynamic_slice_in_dim(grad_rows, start // rank, count // rank, 1)
    outer = grad_cols.astype(jnp.float32)[:, :, None] * act_rows.astype(jnp.float32)[:, None, :]
    return outer.reshape(tokens_here, count).astype(jnp.bfloat16)


def hessian_block(total, pieces, row_start, rows_own, col_start, col_count):
    grad_rows, act_rows, weights = pieces
    left = kron_columns(grad_rows, act_rows, row_start, rows_own)
    weighted = (weights.astype(jnp.float32)[:, None] * left.astype(jnp.float32)).astype(
        jnp.bfloat16
    )
    right = kron_columns(grad_rows, act_rows, col_start, col_count)
    return total + lax.dot_general(
        weighted, right, (((0,), (0,)), ((), ())), preferred_element_type=jnp.float32
    )


def fold_blocks(total, pieces, step_fn):
    count = pieces[0].shape[0]
    shaped = tuple((p.reshape((count // 512, 512) + p.shape[1:]) for p in pieces))

    def inner(carry, block):
        return (step_fn(carry, block), None)

    return lax.scan(inner, total, shaped)[0]


def split_parts(matrix):
    high_part = matrix.astype(jnp.bfloat16)
    first_rest = matrix - high_part.astype(jnp.float32)
    middle_part = first_rest.astype(jnp.bfloat16)
    low_part = (first_rest - middle_part.astype(jnp.float32)).astype(jnp.bfloat16)
    return (high_part, middle_part, low_part)


def many_tokens(activations, out_grads, proj_in, proj_out, queries, lengths, credit):
    tok_rows = activations.shape[0]
    seq_len = tok_rows // lengths.shape[0]
    dp_count = lax.axis_size("dp")
    query_count = lax.axis_size("query")
    dp_index = lax.axis_index("dp")
    query_index = lax.axis_index("query")
    part_act = jnp.dot(activations, proj_in, preferred_element_type=jnp.float32)
    part_grad = jnp.dot(out_grads, proj_out, preferred_element_type=jnp.float32)
    sum_act, sum_grad = lax.psum((part_act, part_grad), "query")
    act_proj = sum_act.astype(jnp.bfloat16)
    grad_proj = sum_grad.astype(jnp.bfloat16)
    rank = act_proj.shape[1]
    feat = rank * rank
    live = jnp.arange(seq_len, dtype=jnp.int32)[None, :] < lengths[:, None]
    weight = (credit[:, None].astype(jnp.float32) * live.astype(jnp.float32)).reshape(-1)
    mask = live.astype(jnp.float32).reshape(-1)
    weight_wire = weight.astype(jnp.bfloat16)
    rows_own = feat // dp_count
    row_start = dp_index * rows_own
    all_tokens = tok_rows * dp_count
    col_count = feat // query_count
    col_start = query_index * col_count
    owned = fold_blocks(
        jnp.zeros((rows_own, col_count), jnp.float32),
        (
            lax.all_gather(grad_proj, "dp", axis=0, tiled=True),
            lax.all_gather(act_proj, "dp", axis=0, tiled=True),
            lax.all_gather(weight_wire, "dp", axis=0, tiled=True),
        ),
        lambda carry, block: hessian_block(carry, block, row_start, rows_own, col_start, col_count),
    )
    hessian = lax.all_gather(owned, "query", axis=1, tiled=True) / all_tokens
    diagonal_block = lax.dynamic_slice_in_dim(hessian, row_start, rows_own, 1)
    level = lax.psum(jnp.trace(diagonal_block), "dp") / feat
    step = 1.1 * level
    high_part, middle_part, low_part = split_parts(hessian)
    piece = lax.all_gather(queries, "dp", axis=0, tiled=True)
    result = jnp.zeros(queries.shape, jnp.float32)
    for part_matrix in (low_part, middle_part, high_part):
        columns = part_matrix
        result = result + jnp.dot(columns, piece, preferred_element_type=jnp.float32)
    query_f = queries.astype(jnp.float32)
    precond = ((2.0 * query_f - (result + 0.1 * level * query_f) / step) / step).astype(
        jnp.bfloat16
    )
    local_features = kron_columns(grad_proj, act_proj, 0, feat)
    piece = lax.all_gather(precond, "dp", axis=0, tiled=True)
    columns = lax.slice_in_dim(local_features, 0, piece.shape[0], axis=1)
    scores = jnp.zeros((tok_rows, precond.shape[1]), jnp.float32) + jnp.dot(
        columns, piece, preferred_element_type=jnp.float32
    )
    return (hessian, (scores * mask[:, None]).astype(jnp.bfloat16))


MIB = 1024 * 1024
TILE = 256
NT = (((1,), (1,)), ((), ()))


def params(mib):
    return pltpu.CompilerParams(vmem_limit_bytes=int(mib * MIB))


def project_kernel(act, grad, pin, pout, keep_ref, send_ref, act_v, grad_v, pin_v, pout_v, sems):
    chunk = act.shape[1]
    while grad.shape[1] % chunk:
        chunk //= 2
    spans = [pl.ds(c, chunk) for c in range(0, grad.shape[1], chunk)]
    copies = [pltpu.make_async_copy(s, d, sems.at[n]) for n, (s, d) in enumerate(((pin, pin_v), (act, act_v), (pout, pout_v)))]
    copies += [
        pltpu.make_async_copy(grad.at[:, span], grad_v.at[:, span], sems.at[3 + n])
        for n, span in enumerate(spans)
    ]
    for copy in copies[:6]:
        copy.start()
    copies[0].wait()
    copies[1].wait()
    part_act = lax.dot_general(pin_v[...], act_v[...], NT, preferred_element_type=jnp.float32)
    copies[2].wait()
    part_grad = jnp.zeros_like(part_act)
    for n, span in enumerate(spans):
        copies[3 + n].wait()
        if n + 3 < len(spans):
            copies[6 + n].start()
        part_grad += lax.dot_general(
            pout_v[:, span], grad_v[:, span], NT, preferred_element_type=jnp.float32
        )
    even = lax.rem(lax.axis_index("query"), 2) == 0
    keep_ref[...] = jnp.where(even, part_act, part_grad)
    send_ref[...] = jnp.where(even, part_grad, part_act)


def project(activations, out_grads, proj_in_t, proj_out_t):
    tok, d_here = activations.shape
    f_here = out_grads.shape[1]
    rank = proj_in_t.shape[0]
    out = jax.ShapeDtypeStruct((rank, tok), jnp.float32)
    return pl.pallas_call(
        project_kernel,
        in_specs=[pl.BlockSpec(memory_space=pl.ANY)] * 4,
        out_shape=[out, out],
        scratch_shapes=[
            pltpu.VMEM((tok, d_here), jnp.bfloat16),
            pltpu.VMEM((tok, f_here), jnp.bfloat16),
            pltpu.VMEM((rank, d_here), jnp.bfloat16),
            pltpu.VMEM((rank, f_here), jnp.bfloat16),
            pltpu.SemaphoreType.DMA((3 + f_here // 128,)),
        ],
        compiler_params=params(53.75),
    )(activations, out_grads, proj_in_t, proj_out_t)


def add_kernel(one_ref, other_ref, out_ref):
    out_ref[...] = one_ref[...] + other_ref[...]


def add(one, other):
    return pl.pallas_call(
        add_kernel,
        out_shape=jax.ShapeDtypeStruct(one.shape, one.dtype),
        compiler_params=params(40),
    )(one, other)


def payload_kernel(one_ref, other_ref, weight_ref, out_ref):
    total = one_ref[...] + other_ref[...]
    weight = jnp.broadcast_to(weight_ref[...], (16, weight_ref.shape[1]))
    out_ref[...] = jnp.concatenate([total, weight], axis=0).astype(out_ref.dtype)


def add_to_payload(one, other, weight):
    rows, tok = one.shape
    return pl.pallas_call(
        payload_kernel,
        out_shape=jax.ShapeDtypeStruct((rows + 16, tok), jnp.bfloat16),
        compiler_params=params(40),
    )(one, other, weight)


def stack_kernel(_, __, *refs):
    parts, (out_ref, factors_ref) = refs[:-2], refs[-2:]
    for k, ref in enumerate(parts):
        out_ref[k] = ref[...]
        factors_ref[k] = ref[: factors_ref.shape[1]]


def stack(parts, rank, after):
    rows, tok = parts[0].shape
    whole = pl.BlockSpec(memory_space=pltpu.VMEM)
    return pl.pallas_call(
        stack_kernel,
        in_specs=[pl.BlockSpec(memory_space=pl.ANY)] * 2 + [whole] * len(parts),
        out_shape=[
            jax.ShapeDtypeStruct((len(parts), rows, tok), parts[0].dtype),
            jax.ShapeDtypeStruct((len(parts), rank, tok), parts[0].dtype),
        ],
        compiler_params=params(30),
    )(*after, *parts)


def lay_out_factors(blocks, factors, weights):
    rank = factors.shape[0] // 2
    here = pl.multiple_of(lax.rem(lax.axis_index("query"), 2) * rank, rank)
    there = pl.multiple_of(rank - here, rank)
    for k, (mine, other) in enumerate(blocks):
        span = slice(k * mine.shape[1], (k + 1) * mine.shape[1])
        factors[pl.ds(here, rank), span] = mine[:rank].astype(jnp.float32)
        factors[pl.ds(there, rank), span] = other[:rank].astype(jnp.float32)
        weights[:, span] = mine[rank:].astype(jnp.float32)[:1]


def block_pairs(mine, other):
    return [(mine.at[k], other.at[k]) for k in reversed(range(mine.shape[0]))]


def weigh_rows(first_row, end_row, row_count, factors, weights, weighted):
    rank = factors.shape[0] // 2
    act, weight = factors[:rank, :], weights[...]
    first = rank + lax.axis_index("dp") * row_count
    for i in range(first_row // rank, end_row // rank):
        left = (factors[pl.ds(first + i, 1), :] * act).astype(jnp.bfloat16)
        left = (weight * left.astype(jnp.float32)).astype(jnp.bfloat16)
        weighted[i * rank : (i + 1) * rank, :] = left


def range_scale(values):
    top = jnp.max(jnp.abs(values), keepdims=True)
    scale = jnp.ones_like(top)
    for low in (16, 48, 80, 112):
        scale = jnp.where(top > 2.0**low, 2.0 ** -min(low + 16, 126), scale)
        scale = jnp.where(top < 2.0**-low, 2.0 ** min(low + 16, 126), scale)
    return scale


def project_queries(row_count, factors, features, queries):
    rank = factors.shape[0] // 2
    act = factors[:rank, :]
    total = 0.0
    for near, query_ref in enumerate(queries):
        first = rank + (lax.axis_index("dp") ^ near) * row_count
        for i in range(row_count):
            row = factors[pl.ds(first + i, 1), :]
            features[near, i * rank : (i + 1) * rank, :] = (row * act).astype(jnp.bfloat16)
        total += jnp.dot(query_ref[...], features[near], preferred_element_type=jnp.float32)
    return total


def turn_kernel(row_count, query, near_query, own, own_other, *refs):
    out_ref, near_out_ref, plain_ref, factors, weights, features = refs
    out_ref[...] = query[...].T
    near_out_ref[...] = near_query[...].T
    lay_out_factors([(own, own_other)], factors, weights)
    plain_ref[...] = project_queries(row_count, factors, features, (out_ref, near_out_ref))


def turn_queries(queries, near_queries, own, own_other, rank, row_count):
    rows, count = queries.shape
    tok = own.shape[1]
    out = jax.ShapeDtypeStruct((count, rows), queries.dtype)
    return pl.pallas_call(
        functools.partial(turn_kernel, row_count),
        out_shape=[out, out, jax.ShapeDtypeStruct((count, tok), jnp.float32)],
        scratch_shapes=[
            pltpu.VMEM((2 * rank, tok), jnp.float32),
            pltpu.VMEM((1, tok), jnp.float32),
            pltpu.VMEM((2, rows, tok), jnp.bfloat16),
        ],
        compiler_params=params(30),
    )(queries, near_queries, own, own_other)


def share_kernel(
    row_count, own, own_other, mine, other, query_ref, near_query_ref, own_plain_ref, *refs
):
    factors, weights, features, gram = refs[-4:]
    out_refs = refs[:-4]
    lay_out_factors([(own, own_other)] + block_pairs(mine, other), factors, weights)
    rank = factors.shape[0] // 2
    tokens = factors.shape[1]
    tok = own.shape[1]
    plain = project_queries(
        row_count, factors.at[:, tok:], features, (query_ref, near_query_ref)
    )
    plain = jnp.concatenate([own_plain_ref[...], plain], axis=1)
    act = factors[:rank, :]
    weight = weights[...]
    live = weight > 0.0
    act = jnp.where(live, act, 0.0)
    grad = jnp.where(live, factors[rank:, :], 0.0)
    act_scale, grad_scale = range_scale(act), range_scale(grad)
    act, grad = act * act_scale, grad * grad_scale
    norms = jnp.sum(act * act, axis=0, keepdims=True) * jnp.sum(grad * grad, axis=0, keepdims=True)
    level = jnp.sum(weight * norms, axis=1, keepdims=True) / (tokens * rank * rank)
    step = 1.1 * level
    act_b, grad_b = act.astype(jnp.bfloat16), grad.astype(jnp.bfloat16)
    act_rows, grad_rows = act.T.astype(jnp.bfloat16), grad.T.astype(jnp.bfloat16)
    weighted = (plain * (weight * (1.0 / (tokens * step)))).astype(jnp.bfloat16)
    scale = act_scale * grad_scale
    for n, out_ref in enumerate(out_refs):
        block = slice(2 * n * tok, (2 * n + 1) * tok)
        for row in range(0, tokens, TILE // 2):
            here = slice(row, row + TILE // 2)
            tile = jnp.dot(act_rows[here], act_b[:, block], preferred_element_type=jnp.float32)
            tile *= jnp.dot(grad_rows[here], grad_b[:, block], preferred_element_type=jnp.float32)
            gram[n, here, :] = tile.astype(jnp.bfloat16)
        image = jnp.dot(weighted, gram[n], preferred_element_type=jnp.float32)
        share = ((2.0 - 0.1 / 1.1) * plain[:, block] - image) * scale * (scale / step)
        out_ref[...] = share.astype(out_ref.dtype)


def score_shares(
    own, own_other, mine, other, queries_t, near_queries_t, own_plain, rank, row_count
):
    blocks, tok = mine.shape[0] + 1, mine.shape[2]
    count, rows = queries_t.shape
    return pl.pallas_call(
        functools.partial(share_kernel, row_count),
        out_shape=[
            jax.ShapeDtypeStruct((count, tok), jnp.bfloat16 if k else jnp.float32)
            for k in range(0, blocks, 2)
        ],
        scratch_shapes=[
            pltpu.VMEM((2 * rank, tok * blocks), jnp.float32),
            pltpu.VMEM((1, tok * blocks), jnp.float32),
            pltpu.VMEM((2, rows, tok * (blocks - 1)), jnp.bfloat16),
            pltpu.VMEM((blocks // 2, tok * blocks, tok), jnp.bfloat16),
        ],
        compiler_params=params(30),
    )(own, own_other, mine, other, queries_t, near_queries_t, own_plain)


def build_columns(first, act, factors, right):
    rank = act.shape[0]
    for i in range(right.shape[0] // rank):
        row = rank + first + i
        right[i * rank : (i + 1) * rank, :] = (factors[row : row + 1, :] * act).astype(jnp.bfloat16)


def own_kernel(row_count, col_count, own, own_other, out, factors, weights, weighted, *rights):
    rank = factors.shape[0] // 2
    cols = col_count * rank
    lay_out_factors([(own, own_other)], factors, weights)
    weigh_rows(0, weighted.shape[0], row_count, factors, weights, weighted)
    act = factors[:rank, :]
    build_columns(0, act, factors, rights[0])
    for step in range(rank // col_count):
        if (step + 1) * col_count < rank:
            build_columns((step + 1) * col_count, act, factors, rights[(step + 1) % 2])
        out[:, step * cols : (step + 1) * cols] = lax.dot_general(
            weighted[...], rights[step % 2][...], NT, preferred_element_type=jnp.float32
        )


def own_tokens_sum(own, own_other, rank, row_count, col_count=8):
    tok = own.shape[1]
    rows, cols = row_count * rank, col_count * rank
    return pl.pallas_call(
        functools.partial(own_kernel, row_count, col_count),
        out_shape=jax.ShapeDtypeStruct((rows, rank * rank), jnp.float32),
        scratch_shapes=[
            pltpu.VMEM((2 * rank, tok), jnp.float32),
            pltpu.VMEM((1, tok), jnp.float32),
            pltpu.VMEM((rows, tok), jnp.bfloat16),
            pltpu.VMEM((cols, tok), jnp.bfloat16),
            pltpu.VMEM((cols, tok), jnp.bfloat16),
        ],
        compiler_params=params(16),
    )(own, own_other)


def hessian_kernel(row_count, col_count, mine, other, own_sum, out, *scratch):
    factors, weights, weighted, rights = *scratch[:3], scratch[3:5]
    result, sems = scratch[5:]
    rank = factors.shape[0] // 2
    blocks = mine.shape[0]
    tokens = factors.shape[1] // blocks * (blocks + 1)
    rows, cols = row_count * rank, col_count * rank
    lay_out_factors(block_pairs(mine, other), factors, weights)
    act = factors[:rank, :]
    copies = []
    build_columns(0, act, factors, rights[0])
    for step in range(rank // col_count):
        if (step + 1) * col_count < rank:
            build_columns((step + 1) * col_count, act, factors, rights[(step + 1) % 2])
        for row in range(0, rows, TILE):
            if step == 0:
                weigh_rows(row, row + TILE, row_count, factors, weights, weighted)
            here = pl.ds(row, TILE), pl.ds(step * cols, cols)
            tile = lax.dot_general(
                weighted[row : row + TILE, :],
                rights[step % 2][...],
                NT,
                preferred_element_type=jnp.float32,
            )
            result[here] = (own_sum[here] + tile) * (1.0 / tokens)
            copy = pltpu.make_async_copy(result.at[here], out.at[here], sems.at[len(copies)])
            copy.start()
            copies.append(copy)
    for copy in copies:
        copy.wait()


def hessian_rows(mine, other, own_sum, rank, row_count, col_count=8):
    blocks, _, tok = mine.shape
    feat = rank * rank
    rows, cols = row_count * rank, col_count * rank
    return pl.pallas_call(
        functools.partial(hessian_kernel, row_count, col_count),
        out_specs=pl.BlockSpec(memory_space=pl.ANY),
        out_shape=jax.ShapeDtypeStruct((rows, feat), jnp.float32),
        scratch_shapes=[
            pltpu.VMEM((2 * rank, tok * blocks), jnp.float32),
            pltpu.VMEM((1, tok * blocks), jnp.float32),
            pltpu.VMEM((rows, tok * blocks), jnp.bfloat16),
            pltpu.VMEM((cols, tok * blocks), jnp.bfloat16),
            pltpu.VMEM((cols, tok * blocks), jnp.bfloat16),
            pltpu.VMEM((rows, feat), jnp.float32),
            pltpu.SemaphoreType.DMA((feat // cols * (rows // TILE),)),
        ],
        compiler_params=params(30),
    )(mine, other, own_sum)


def finish_kernel(payload_ref, *refs):
    shares, out_ref = refs[:-1], refs[-1]
    total = shares[0][...]
    for ref in shares[1:]:
        total = total + ref[...].astype(jnp.float32)
    weight = payload_ref[...].astype(jnp.float32)[-1:]
    out_ref[...] = jnp.where(weight > 0.0, total, 0.0).T.astype(out_ref.dtype)


def finish_scores(payload, shares):
    count, tok = shares[0].shape
    return pl.pallas_call(
        finish_kernel,
        out_shape=jax.ShapeDtypeStruct((tok, count), jnp.bfloat16),
        compiler_params=params(40),
    )(payload, *shares)


def swapped(array, axis, distance):
    return lax.ppermute(array, axis, [(i, i ^ distance) for i in range(lax.axis_size(axis))])


def few_tokens(activations, out_grads, proj_in, proj_out, queries, lengths, credit):
    dp_count = lax.axis_size("dp")
    query_count = lax.axis_size("query")
    rank = proj_in.shape[1]
    row_count = rank // dp_count
    seq_len = activations.shape[0] // lengths.shape[0]
    live = jnp.arange(seq_len, dtype=jnp.int32)[None, :] < lengths[:, None]
    weight = jnp.where(live, credit[:, None], 0).astype(jnp.float32).reshape(1, -1)
    near_queries = swapped(queries, "dp", 1)
    keep, send = project(activations, out_grads, proj_in.T, proj_out.T)
    other = swapped(send, "query", 1)
    distance = 2
    while distance < query_count:
        keep = add(keep, other)
        other = swapped(keep, "query", distance)
        distance *= 2
    own = add_to_payload(keep, other, weight)
    own_other = swapped(own, "query", 1)
    others = [swapped(own, "dp", k) for k in reversed(range(1, dp_count))]
    own_sum = own_tokens_sum(own, own_other, rank, row_count)
    queries_t, near_queries_t, own_plain = turn_queries(
        queries, near_queries, own, own_other, rank, row_count
    )
    mine, factors = stack(others, rank, (own_sum, queries_t))
    other = swapped(factors, "query", 1)
    shares = score_shares(
        own, own_other, mine, other, queries_t, near_queries_t, own_plain, rank, row_count
    )
    arrived = [swapped(share, "dp", 2 * n) for n, share in enumerate(shares) if n]
    hessian = hessian_rows(mine, other, own_sum, rank, row_count)
    return hessian, finish_scores(own, [shares[0]] + arrived)


def power_of_two(count):
    return count & (count - 1) == 0


def per_device(activations, *others):
    rank = others[1].shape[1]
    dp_count, query_count = lax.axis_size("dp"), lax.axis_size("query")
    pairs = min(dp_count, query_count) > 1 and power_of_two(dp_count) and power_of_two(query_count)
    if pairs and activations.shape[0] * dp_count <= rank * rank:
        return few_tokens(activations, *others)
    return many_tokens(activations, *others)


def solution(mesh):
    placed = (
        P(("groups", "dp"), "query"),
        P(("groups", "dp"), "query"),
        P("query", None),
        P("query", None),
        P(("groups", "dp"), "query"),
        P(("groups", "dp")),
        P(("groups", "dp")),
    )
    return jax.shard_map(
        per_device,
        mesh=mesh,
        in_specs=placed,
        out_specs=(P(("groups", "dp"), None), P(("groups", "dp"), "query")),
        check_vma=False,
    )
```

```python
import functools
import jax
import jax.numpy as jnp
from jax import lax
from jax.experimental import pallas as pl
from jax.experimental.pallas import tpu as pltpu
from jax.sharding import PartitionSpec as P


def kron_columns(grad_rows, act_rows, start, count):
    rank = grad_rows.shape[1]
    tokens_here = grad_rows.shape[0]
    grad_cols = lax.dynamic_slice_in_dim(grad_rows, start // rank, count // rank, 1)
    outer = grad_cols.astype(jnp.float32)[:, :, None] * act_rows.astype(jnp.float32)[:, None, :]
    return outer.reshape(tokens_here, count).astype(jnp.bfloat16)


def hessian_block(total, pieces, row_start, rows_own, col_start, col_count):
    grad_rows, act_rows, weights = pieces
    left = kron_columns(grad_rows, act_rows, row_start, rows_own)
    weighted = (weights.astype(jnp.float32)[:, None] * left.astype(jnp.float32)).astype(
        jnp.bfloat16
    )
    right = kron_columns(grad_rows, act_rows, col_start, col_count)
    return total + lax.dot_general(
        weighted, right, (((0,), (0,)), ((), ())), preferred_element_type=jnp.float32
    )


def fold_blocks(total, pieces, step_fn):
    count = pieces[0].shape[0]
    shaped = tuple((p.reshape((count // 512, 512) + p.shape[1:]) for p in pieces))

    def inner(carry, block):
        return (step_fn(carry, block), None)

    return lax.scan(inner, total, shaped)[0]


def split_parts(matrix):
    high_part = matrix.astype(jnp.bfloat16)
    first_rest = matrix - high_part.astype(jnp.float32)
    middle_part = first_rest.astype(jnp.bfloat16)
    low_part = (first_rest - middle_part.astype(jnp.float32)).astype(jnp.bfloat16)
    return (high_part, middle_part, low_part)


def many_tokens(activations, out_grads, proj_in, proj_out, queries, lengths, credit):
    tok_rows = activations.shape[0]
    seq_len = tok_rows // lengths.shape[0]
    dp_count = lax.axis_size("dp")
    query_count = lax.axis_size("query")
    dp_index = lax.axis_index("dp")
    query_index = lax.axis_index("query")
    part_act = jnp.dot(activations, proj_in, preferred_element_type=jnp.float32)
    part_grad = jnp.dot(out_grads, proj_out, preferred_element_type=jnp.float32)
    sum_act, sum_grad = lax.psum((part_act, part_grad), "query")
    act_proj = sum_act.astype(jnp.bfloat16)
    grad_proj = sum_grad.astype(jnp.bfloat16)
    rank = act_proj.shape[1]
    feat = rank * rank
    live = jnp.arange(seq_len, dtype=jnp.int32)[None, :] < lengths[:, None]
    weight = (credit[:, None].astype(jnp.float32) * live.astype(jnp.float32)).reshape(-1)
    mask = live.astype(jnp.float32).reshape(-1)
    weight_wire = weight.astype(jnp.bfloat16)
    rows_own = feat // dp_count
    row_start = dp_index * rows_own
    all_tokens = tok_rows * dp_count
    col_count = feat // query_count
    col_start = query_index * col_count
    owned = fold_blocks(
        jnp.zeros((rows_own, col_count), jnp.float32),
        (
            lax.all_gather(grad_proj, "dp", axis=0, tiled=True),
            lax.all_gather(act_proj, "dp", axis=0, tiled=True),
            lax.all_gather(weight_wire, "dp", axis=0, tiled=True),
        ),
        lambda carry, block: hessian_block(carry, block, row_start, rows_own, col_start, col_count),
    )
    hessian = lax.all_gather(owned, "query", axis=1, tiled=True) / all_tokens
    diagonal_block = lax.dynamic_slice_in_dim(hessian, row_start, rows_own, 1)
    level = lax.psum(jnp.trace(diagonal_block), "dp") / feat
    step = 1.1 * level
    high_part, middle_part, low_part = split_parts(hessian)
    piece = lax.all_gather(queries, "dp", axis=0, tiled=True)
    result = jnp.zeros(queries.shape, jnp.float32)
    for part_matrix in (low_part, middle_part, high_part):
        columns = part_matrix
        result = result + jnp.dot(columns, piece, preferred_element_type=jnp.float32)
    query_f = queries.astype(jnp.float32)
    precond = ((2.0 * query_f - (result + 0.1 * level * query_f) / step) / step).astype(
        jnp.bfloat16
    )
    local_features = kron_columns(grad_proj, act_proj, 0, feat)
    piece = lax.all_gather(precond, "dp", axis=0, tiled=True)
    columns = lax.slice_in_dim(local_features, 0, piece.shape[0], axis=1)
    scores = jnp.zeros((tok_rows, precond.shape[1]), jnp.float32) + jnp.dot(
        columns, piece, preferred_element_type=jnp.float32
    )
    return (hessian, (scores * mask[:, None]).astype(jnp.bfloat16))


MIB = 1024 * 1024
TILE = 256
NT = (((1,), (1,)), ((), ()))


def params(mib):
    return pltpu.CompilerParams(vmem_limit_bytes=int(mib * MIB))


def project_kernel(act, grad, pin, pout, keep_ref, send_ref, act_v, grad_v, pin_v, pout_v, sems):
    chunk = grad.shape[1] // 2
    spans = [pl.ds(0, chunk), pl.ds(chunk, chunk)]
    pairs = [(pin, pin_v), (act, act_v), (pout, pout_v)]
    pairs += [(grad.at[:, span], grad_v.at[:, span]) for span in spans]
    copies = [pltpu.make_async_copy(s, d, sems.at[n]) for n, (s, d) in enumerate(pairs)]
    for copy in copies:
        copy.start()
    copies[0].wait()
    copies[1].wait()
    part_act = lax.dot_general(pin_v[...], act_v[...], NT, preferred_element_type=jnp.float32)
    copies[2].wait()
    part_grad = jnp.zeros_like(part_act)
    for copy, span in zip(copies[3:], spans):
        copy.wait()
        part_grad += lax.dot_general(
            pout_v[:, span], grad_v[:, span], NT, preferred_element_type=jnp.float32
        )
    even = lax.rem(lax.axis_index("query"), 2) == 0
    keep_ref[...] = jnp.where(even, part_act, part_grad)
    send_ref[...] = jnp.where(even, part_grad, part_act)


def project(activations, out_grads, proj_in_t, proj_out_t):
    tok, d_here = activations.shape
    f_here = out_grads.shape[1]
    rank = proj_in_t.shape[0]
    out = jax.ShapeDtypeStruct((rank, tok), jnp.float32)
    return pl.pallas_call(
        project_kernel,
        in_specs=[pl.BlockSpec(memory_space=pl.ANY)] * 4,
        out_shape=[out, out],
        scratch_shapes=[
            pltpu.VMEM((tok, d_here), jnp.bfloat16),
            pltpu.VMEM((tok, f_here), jnp.bfloat16),
            pltpu.VMEM((rank, d_here), jnp.bfloat16),
            pltpu.VMEM((rank, f_here), jnp.bfloat16),
            pltpu.SemaphoreType.DMA((5,)),
        ],
        compiler_params=params(53.75),
    )(activations, out_grads, proj_in_t, proj_out_t)


def add_kernel(one_ref, other_ref, out_ref):
    out_ref[...] = one_ref[...] + other_ref[...]


def add(one, other):
    return pl.pallas_call(
        add_kernel,
        out_shape=jax.ShapeDtypeStruct(one.shape, one.dtype),
        compiler_params=params(40),
    )(one, other)


def payload_kernel(one_ref, other_ref, weight_ref, out_ref):
    total = one_ref[...] + other_ref[...]
    weight = jnp.broadcast_to(weight_ref[...], (16, weight_ref.shape[1]))
    out_ref[...] = jnp.concatenate([total, weight], axis=0).astype(out_ref.dtype)


def add_to_payload(one, other, weight):
    rows, tok = one.shape
    return pl.pallas_call(
        payload_kernel,
        out_shape=jax.ShapeDtypeStruct((rows + 16, tok), jnp.bfloat16),
        compiler_params=params(40),
    )(one, other, weight)


def stack_kernel(_, __, *refs):
    parts, (out_ref, factors_ref) = refs[:-2], refs[-2:]
    for k, ref in enumerate(parts):
        out_ref[k] = ref[...]
        factors_ref[k] = ref[: factors_ref.shape[1]]


def stack(parts, rank, after):
    rows, tok = parts[0].shape
    whole = pl.BlockSpec(memory_space=pltpu.VMEM)
    return pl.pallas_call(
        stack_kernel,
        in_specs=[pl.BlockSpec(memory_space=pl.ANY)] * 2 + [whole] * len(parts),
        out_shape=[
            jax.ShapeDtypeStruct((len(parts), rows, tok), parts[0].dtype),
            jax.ShapeDtypeStruct((len(parts), rank, tok), parts[0].dtype),
        ],
        compiler_params=params(26),
    )(*after, *parts)


def lay_out_factors(blocks, factors, weights):
    rank = factors.shape[0] // 2
    here = pl.multiple_of(lax.rem(lax.axis_index("query"), 2) * rank, rank)
    there = pl.multiple_of(rank - here, rank)
    for k, (mine, other) in enumerate(blocks):
        span = slice(k * mine.shape[1], (k + 1) * mine.shape[1])
        factors[pl.ds(here, rank), span] = mine[:rank].astype(jnp.float32)
        factors[pl.ds(there, rank), span] = other[:rank].astype(jnp.float32)
        weights[:, span] = mine[rank:].astype(jnp.float32)[:1]


def block_pairs(mine, other):
    return [(mine.at[k], other.at[k]) for k in range(mine.shape[0])]


def weigh_rows(first_row, end_row, row_count, factors, weights, weighted):
    rank = factors.shape[0] // 2
    act, weight = factors[:rank, :], weights[...]
    first = rank + lax.axis_index("dp") * row_count
    for i in range(first_row // rank, end_row // rank):
        left = (factors[pl.ds(first + i, 1), :] * act).astype(jnp.bfloat16)
        left = (weight * left.astype(jnp.float32)).astype(jnp.bfloat16)
        weighted[i * rank : (i + 1) * rank, :] = left


def range_scale(values):
    top = jnp.max(jnp.abs(values), keepdims=True)
    scale = jnp.ones_like(top)
    for low in (16, 48, 80, 112):
        scale = jnp.where(top > 2.0**low, 2.0 ** -min(low + 16, 126), scale)
        scale = jnp.where(top < 2.0**-low, 2.0 ** min(low + 16, 126), scale)
    return scale


def project_queries(row_count, factors, features, queries):
    rank = factors.shape[0] // 2
    act = factors[:rank, :]
    total = 0.0
    for near, query_ref in enumerate(queries):
        first = rank + (lax.axis_index("dp") ^ near) * row_count
        for i in range(row_count):
            row = factors[pl.ds(first + i, 1), :]
            features[near, i * rank : (i + 1) * rank, :] = (row * act).astype(jnp.bfloat16)
        total += jnp.dot(query_ref[...], features[near], preferred_element_type=jnp.float32)
    return total


def turn_kernel(row_count, query, near_query, own, own_other, *refs):
    out_ref, near_out_ref, plain_ref, factors, weights, features = refs
    out_ref[...] = query[...].T
    near_out_ref[...] = near_query[...].T
    lay_out_factors([(own, own_other)], factors, weights)
    plain_ref[...] = project_queries(row_count, factors, features, (out_ref, near_out_ref))


def turn_queries(queries, near_queries, own, own_other, rank, row_count):
    rows, count = queries.shape
    tok = own.shape[1]
    out = jax.ShapeDtypeStruct((count, rows), queries.dtype)
    return pl.pallas_call(
        functools.partial(turn_kernel, row_count),
        out_shape=[out, out, jax.ShapeDtypeStruct((count, tok), jnp.float32)],
        scratch_shapes=[
            pltpu.VMEM((2 * rank, tok), jnp.float32),
            pltpu.VMEM((1, tok), jnp.float32),
            pltpu.VMEM((2, rows, tok), jnp.bfloat16),
        ],
        compiler_params=params(26),
    )(queries, near_queries, own, own_other)


def block_share(plain, weighted, act_rows, grad_rows, act, grad, scales, gram):
    for row in range(0, gram.shape[0], TILE // 2):
        here = slice(row, row + TILE // 2)
        tile = jnp.dot(act_rows[here], act, preferred_element_type=jnp.float32)
        tile *= jnp.dot(grad_rows[here], grad, preferred_element_type=jnp.float32)
        gram[here, :] = tile.astype(jnp.bfloat16)
    image = jnp.dot(weighted, gram[...], preferred_element_type=jnp.float32)
    return ((2.0 - 0.1 / 1.1) * plain - image) * scales[:1, :1] * scales[1:2, :1]


def share_kernel(
    row_count, own, own_other, mine, other, query_ref, near_query_ref, own_plain_ref, *refs
):
    weighted_ref, act_rows, grad_rows, act_own, grad_own, scales = refs[:6]
    out_refs = refs[6:-4]
    factors, weights, features, gram = refs[-4:]
    lay_out_factors([(own, own_other)] + block_pairs(mine, other), factors, weights)
    rank = factors.shape[0] // 2
    tokens = factors.shape[1]
    tok = own.shape[1]
    plain = project_queries(
        row_count, factors.at[:, tok:], features, (query_ref, near_query_ref)
    )
    plain = jnp.concatenate([own_plain_ref[...], plain], axis=1)
    weight = weights[...]
    live = weight > 0.0
    act = jnp.where(live, factors[:rank, :], 0.0)
    grad = jnp.where(live, factors[rank:, :], 0.0)
    act_scale, grad_scale = range_scale(act), range_scale(grad)
    act, grad = act * act_scale, grad * grad_scale
    norms = jnp.sum(act * act, axis=0, keepdims=True) * jnp.sum(grad * grad, axis=0, keepdims=True)
    level = jnp.sum(weight * norms, axis=1, keepdims=True) / (tokens * rank * rank)
    step = 1.1 * level
    scale = act_scale * grad_scale
    scales[:1, :] = jnp.broadcast_to(scale, (1, scales.shape[1]))
    scales[1:2, :] = jnp.broadcast_to(scale / step, (1, scales.shape[1]))
    act_b, grad_b = act.astype(jnp.bfloat16), grad.astype(jnp.bfloat16)
    act_rows[...] = act.T.astype(jnp.bfloat16)
    grad_rows[...] = grad.T.astype(jnp.bfloat16)
    act_own[...] = act_b[:, :tok]
    grad_own[...] = grad_b[:, :tok]
    weighted_ref[...] = (plain * (weight * (1.0 / (tokens * step)))).astype(jnp.bfloat16)
    for n, out_ref in enumerate(out_refs):
        block = slice(2 * (n + 1) * tok, (2 * (n + 1) + 1) * tok)
        share = block_share(
            plain[:, block],
            weighted_ref[...],
            act_rows,
            grad_rows,
            act_b[:, block],
            grad_b[:, block],
            scales,
            gram,
        )
        out_ref[...] = share.astype(out_ref.dtype)


def score_shares(
    own, own_other, mine, other, queries_t, near_queries_t, own_plain, rank, row_count
):
    blocks, tok = mine.shape[0] + 1, mine.shape[2]
    count, rows = queries_t.shape
    tokens = tok * blocks
    return pl.pallas_call(
        functools.partial(share_kernel, row_count),
        out_shape=[
            jax.ShapeDtypeStruct((count, tokens), jnp.bfloat16),
            jax.ShapeDtypeStruct((tokens, rank), jnp.bfloat16),
            jax.ShapeDtypeStruct((tokens, rank), jnp.bfloat16),
            jax.ShapeDtypeStruct((rank, tok), jnp.bfloat16),
            jax.ShapeDtypeStruct((rank, tok), jnp.bfloat16),
            jax.ShapeDtypeStruct((8, 128), jnp.float32),
        ]
        + [jax.ShapeDtypeStruct((count, tok), jnp.bfloat16)] * (blocks // 2 - 1),
        scratch_shapes=[
            pltpu.VMEM((2 * rank, tokens), jnp.float32),
            pltpu.VMEM((1, tokens), jnp.float32),
            pltpu.VMEM((2, rows, tokens - tok), jnp.bfloat16),
            pltpu.VMEM((tokens, tok), jnp.bfloat16),
        ],
        compiler_params=params(26),
    )(own, own_other, mine, other, queries_t, near_queries_t, own_plain)


def build_columns(first, act, factors, right):
    rank = act.shape[0]
    for i in range(right.shape[0] // rank):
        row = rank + first + i
        right[i * rank : (i + 1) * rank, :] = (factors[row : row + 1, :] * act).astype(jnp.bfloat16)


def own_kernel(row_count, col_count, own, own_other, out, factors, weights, weighted, *rights):
    rank = factors.shape[0] // 2
    cols = col_count * rank
    lay_out_factors([(own, own_other)], factors, weights)
    weigh_rows(0, weighted.shape[0], row_count, factors, weights, weighted)
    act = factors[:rank, :]
    build_columns(0, act, factors, rights[0])
    for step in range(rank // col_count):
        if (step + 1) * col_count < rank:
            build_columns((step + 1) * col_count, act, factors, rights[(step + 1) % 2])
        out[:, step * cols : (step + 1) * cols] = lax.dot_general(
            weighted[...], rights[step % 2][...], NT, preferred_element_type=jnp.float32
        )


def own_tokens_sum(own, own_other, rank, row_count, col_count=8):
    tok = own.shape[1]
    rows, cols = row_count * rank, col_count * rank
    return pl.pallas_call(
        functools.partial(own_kernel, row_count, col_count),
        out_shape=jax.ShapeDtypeStruct((rows, rank * rank), jnp.float32),
        scratch_shapes=[
            pltpu.VMEM((2 * rank, tok), jnp.float32),
            pltpu.VMEM((1, tok), jnp.float32),
            pltpu.VMEM((rows, tok), jnp.bfloat16),
            pltpu.VMEM((cols, tok), jnp.bfloat16),
            pltpu.VMEM((cols, tok), jnp.bfloat16),
        ],
        compiler_params=params(16),
    )(own, own_other)


def hessian_kernel(row_count, col_count, mine, other, own_sum, own_plain, *refs):
    share_parts, out, share_ref = refs[:6], refs[6], refs[7]
    factors, weights, weighted, rights = *refs[8:11], refs[11:13]
    result, gram, sems = refs[13:]
    rank = factors.shape[0] // 2
    blocks = mine.shape[0]
    tokens = factors.shape[1] // blocks * (blocks + 1)
    rows, cols = row_count * rank, col_count * rank
    lay_out_factors(block_pairs(mine, other), factors, weights)
    act = factors[:rank, :]
    copies = []
    build_columns(0, act, factors, rights[0])
    for step in range(rank // col_count):
        if (step + 1) * col_count < rank:
            build_columns((step + 1) * col_count, act, factors, rights[(step + 1) % 2])
        for row in range(0, rows, TILE):
            if step == 0:
                weigh_rows(row, row + TILE, row_count, factors, weights, weighted)
            here = pl.ds(row, TILE), pl.ds(step * cols, cols)
            tile = lax.dot_general(
                weighted[row : row + TILE, :],
                rights[step % 2][...],
                NT,
                preferred_element_type=jnp.float32,
            )
            result[here] = (own_sum[here] + tile) * (1.0 / tokens)
            copy = pltpu.make_async_copy(result.at[here], out.at[here], sems.at[len(copies)])
            copy.start()
            copies.append(copy)
    share_weighted, act_rows, grad_rows, act_own, grad_own, scales = share_parts
    share_ref[...] = block_share(
        own_plain[...],
        share_weighted[...],
        act_rows,
        grad_rows,
        act_own[...],
        grad_own[...],
        scales,
        gram,
    )
    for copy in copies:
        copy.wait()


def hessian_rows(mine, other, own_sum, own_plain, share_parts, rank, row_count, col_count=8):
    blocks, _, tok = mine.shape
    feat = rank * rank
    rows, cols = row_count * rank, col_count * rank
    return pl.pallas_call(
        functools.partial(hessian_kernel, row_count, col_count),
        out_specs=[
            pl.BlockSpec(memory_space=pl.ANY),
            pl.BlockSpec(memory_space=pltpu.VMEM),
        ],
        out_shape=[
            jax.ShapeDtypeStruct((rows, feat), jnp.float32),
            jax.ShapeDtypeStruct(own_plain.shape, jnp.float32),
        ],
        scratch_shapes=[
            pltpu.VMEM((2 * rank, tok * blocks), jnp.float32),
            pltpu.VMEM((1, tok * blocks), jnp.float32),
            pltpu.VMEM((rows, tok * blocks), jnp.bfloat16),
            pltpu.VMEM((cols, tok * blocks), jnp.bfloat16),
            pltpu.VMEM((cols, tok * blocks), jnp.bfloat16),
            pltpu.VMEM((rows, feat), jnp.float32),
            pltpu.VMEM((tok * (blocks + 1), tok), jnp.bfloat16),
            pltpu.SemaphoreType.DMA((feat // cols * (rows // TILE),)),
        ],
        compiler_params=params(26),
    )(mine, other, own_sum, own_plain, *share_parts)


def finish_kernel(payload_ref, *refs):
    shares, out_ref = refs[:-1], refs[-1]
    total = shares[0][...]
    for ref in shares[1:]:
        total = total + ref[...].astype(jnp.float32)
    weight = payload_ref[...].astype(jnp.float32)[-1:]
    out_ref[...] = jnp.where(weight > 0.0, total, 0.0).T.astype(out_ref.dtype)


def finish_scores(payload, shares):
    count, tok = shares[0].shape
    return pl.pallas_call(
        finish_kernel,
        out_shape=jax.ShapeDtypeStruct((tok, count), jnp.bfloat16),
        compiler_params=params(40),
    )(payload, *shares)


def swapped(array, axis, distance):
    return lax.ppermute(array, axis, [(i, i ^ distance) for i in range(lax.axis_size(axis))])


def few_tokens(activations, out_grads, proj_in, proj_out, queries, lengths, credit):
    dp_count = lax.axis_size("dp")
    query_count = lax.axis_size("query")
    rank = proj_in.shape[1]
    row_count = rank // dp_count
    seq_len = activations.shape[0] // lengths.shape[0]
    live = jnp.arange(seq_len, dtype=jnp.int32)[None, :] < lengths[:, None]
    weight = jnp.where(live, credit[:, None], 0).astype(jnp.float32).reshape(1, -1)
    near_queries = swapped(queries, "dp", 1)
    keep, send = project(activations, out_grads, proj_in.T, proj_out.T)
    other = swapped(send, "query", 1)
    distance = 2
    while distance < query_count:
        keep = add(keep, other)
        other = swapped(keep, "query", distance)
        distance *= 2
    own = add_to_payload(keep, other, weight)
    own_other = swapped(own, "query", 1)
    others = [swapped(own, "dp", k) for k in reversed(range(1, dp_count))]
    own_sum = own_tokens_sum(own, own_other, rank, row_count)
    queries_t, near_queries_t, own_plain = turn_queries(
        queries, near_queries, own, own_other, rank, row_count
    )
    mine, factors = stack(others[::-1], rank, (own_sum, queries_t))
    other = swapped(factors, "query", 1)
    parts = score_shares(
        own, own_other, mine, other, queries_t, near_queries_t, own_plain, rank, row_count
    )
    arrived = [swapped(share, "dp", 2 * (n + 1)) for n, share in enumerate(parts[6:])]
    hessian, share = hessian_rows(
        mine, other, own_sum, own_plain, parts[:6], rank, row_count
    )
    return hessian, finish_scores(own, [share] + arrived)


def power_of_two(count):
    return count & (count - 1) == 0


def per_device(activations, *others):
    rank = others[1].shape[1]
    dp_count, query_count = lax.axis_size("dp"), lax.axis_size("query")
    pairs = min(dp_count, query_count) > 1 and power_of_two(dp_count) and power_of_two(query_count)
    if pairs and activations.shape[0] * dp_count <= rank * rank:
        return few_tokens(activations, *others)
    return many_tokens(activations, *others)


def solution(mesh):
    placed = (
        P(("groups", "dp"), "query"),
        P(("groups", "dp"), "query"),
        P("query", None),
        P("query", None),
        P(("groups", "dp"), "query"),
        P(("groups", "dp")),
        P(("groups", "dp")),
    )
    return jax.shard_map(
        per_device,
        mesh=mesh,
        in_specs=placed,
        out_specs=(P(("groups", "dp"), None), P(("groups", "dp"), "query")),
        check_vma=False,
    )
```

```python
import functools
import jax
import jax.numpy as jnp
from jax import lax
from jax.experimental import pallas as pl
from jax.experimental.pallas import tpu as pltpu
from jax.sharding import PartitionSpec as P


def kron_columns(grad_rows, act_rows, start, count):
    rank = grad_rows.shape[1]
    tokens_here = grad_rows.shape[0]
    grad_cols = lax.dynamic_slice_in_dim(grad_rows, start // rank, count // rank, 1)
    outer = grad_cols.astype(jnp.float32)[:, :, None] * act_rows.astype(jnp.float32)[:, None, :]
    return outer.reshape(tokens_here, count).astype(jnp.bfloat16)


def hessian_block(total, pieces, row_start, rows_own, col_start, col_count):
    grad_rows, act_rows, weights = pieces
    left = kron_columns(grad_rows, act_rows, row_start, rows_own)
    weighted = (weights.astype(jnp.float32)[:, None] * left.astype(jnp.float32)).astype(
        jnp.bfloat16
    )
    right = kron_columns(grad_rows, act_rows, col_start, col_count)
    return total + lax.dot_general(
        weighted, right, (((0,), (0,)), ((), ())), preferred_element_type=jnp.float32
    )


def fold_blocks(total, pieces, step_fn):
    count = pieces[0].shape[0]
    shaped = tuple((p.reshape((count // 512, 512) + p.shape[1:]) for p in pieces))

    def inner(carry, block):
        return (step_fn(carry, block), None)

    return lax.scan(inner, total, shaped)[0]


def split_parts(matrix):
    high_part = matrix.astype(jnp.bfloat16)
    first_rest = matrix - high_part.astype(jnp.float32)
    middle_part = first_rest.astype(jnp.bfloat16)
    low_part = (first_rest - middle_part.astype(jnp.float32)).astype(jnp.bfloat16)
    return (high_part, middle_part, low_part)


def many_tokens(activations, out_grads, proj_in, proj_out, queries, lengths, credit):
    tok_rows = activations.shape[0]
    seq_len = tok_rows // lengths.shape[0]
    dp_count = lax.axis_size("dp")
    query_count = lax.axis_size("query")
    dp_index = lax.axis_index("dp")
    query_index = lax.axis_index("query")
    part_act = jnp.dot(activations, proj_in, preferred_element_type=jnp.float32)
    part_grad = jnp.dot(out_grads, proj_out, preferred_element_type=jnp.float32)
    sum_act, sum_grad = lax.psum((part_act, part_grad), "query")
    act_proj = sum_act.astype(jnp.bfloat16)
    grad_proj = sum_grad.astype(jnp.bfloat16)
    rank = act_proj.shape[1]
    feat = rank * rank
    live = jnp.arange(seq_len, dtype=jnp.int32)[None, :] < lengths[:, None]
    weight = (credit[:, None].astype(jnp.float32) * live.astype(jnp.float32)).reshape(-1)
    mask = live.astype(jnp.float32).reshape(-1)
    weight_wire = weight.astype(jnp.bfloat16)
    rows_own = feat // dp_count
    row_start = dp_index * rows_own
    all_tokens = tok_rows * dp_count
    col_count = feat // query_count
    col_start = query_index * col_count
    owned = fold_blocks(
        jnp.zeros((rows_own, col_count), jnp.float32),
        (
            lax.all_gather(grad_proj, "dp", axis=0, tiled=True),
            lax.all_gather(act_proj, "dp", axis=0, tiled=True),
            lax.all_gather(weight_wire, "dp", axis=0, tiled=True),
        ),
        lambda carry, block: hessian_block(carry, block, row_start, rows_own, col_start, col_count),
    )
    hessian = lax.all_gather(owned, "query", axis=1, tiled=True) / all_tokens
    diagonal_block = lax.dynamic_slice_in_dim(hessian, row_start, rows_own, 1)
    level = lax.psum(jnp.trace(diagonal_block), "dp") / feat
    step = 1.1 * level
    high_part, middle_part, low_part = split_parts(hessian)
    piece = lax.all_gather(queries, "dp", axis=0, tiled=True)
    result = jnp.zeros(queries.shape, jnp.float32)
    for part_matrix in (low_part, middle_part, high_part):
        columns = part_matrix
        result = result + jnp.dot(columns, piece, preferred_element_type=jnp.float32)
    query_f = queries.astype(jnp.float32)
    precond = ((2.0 * query_f - (result + 0.1 * level * query_f) / step) / step).astype(
        jnp.bfloat16
    )
    local_features = kron_columns(grad_proj, act_proj, 0, feat)
    piece = lax.all_gather(precond, "dp", axis=0, tiled=True)
    columns = lax.slice_in_dim(local_features, 0, piece.shape[0], axis=1)
    scores = jnp.zeros((tok_rows, precond.shape[1]), jnp.float32) + jnp.dot(
        columns, piece, preferred_element_type=jnp.float32
    )
    return (hessian, (scores * mask[:, None]).astype(jnp.bfloat16))


MIB = 1024 * 1024
TILE = 256
NT = (((1,), (1,)), ((), ()))


def params(mib):
    return pltpu.CompilerParams(vmem_limit_bytes=int(mib * MIB))


def project_kernel(act, grad, pin, pout, keep_ref, send_ref, act_v, grad_v, pin_v, pout_v, sems):
    chunk = grad.shape[1] // 2
    spans = [pl.ds(0, chunk), pl.ds(chunk, chunk)]
    pairs = [(pin, pin_v), (act, act_v), (pout, pout_v)]
    pairs += [(grad.at[:, span], grad_v.at[:, span]) for span in spans]
    copies = [pltpu.make_async_copy(s, d, sems.at[n]) for n, (s, d) in enumerate(pairs)]
    for copy in copies:
        copy.start()
    copies[0].wait()
    copies[1].wait()
    part_act = lax.dot_general(pin_v[...], act_v[...], NT, preferred_element_type=jnp.float32)
    copies[2].wait()
    part_grad = jnp.zeros_like(part_act)
    for copy, span in zip(copies[3:], spans):
        copy.wait()
        part_grad += lax.dot_general(
            pout_v[:, span], grad_v[:, span], NT, preferred_element_type=jnp.float32
        )
    even = lax.rem(lax.axis_index("query"), 2) == 0
    keep_ref[...] = jnp.where(even, part_act, part_grad)
    send_ref[...] = jnp.where(even, part_grad, part_act)


def project(activations, out_grads, proj_in_t, proj_out_t):
    tok, d_here = activations.shape
    f_here = out_grads.shape[1]
    rank = proj_in_t.shape[0]
    out = jax.ShapeDtypeStruct((rank, tok), jnp.float32)
    return pl.pallas_call(
        project_kernel,
        in_specs=[pl.BlockSpec(memory_space=pl.ANY)] * 4,
        out_shape=[out, out],
        scratch_shapes=[
            pltpu.VMEM((tok, d_here), jnp.bfloat16),
            pltpu.VMEM((tok, f_here), jnp.bfloat16),
            pltpu.VMEM((rank, d_here), jnp.bfloat16),
            pltpu.VMEM((rank, f_here), jnp.bfloat16),
            pltpu.SemaphoreType.DMA((5,)),
        ],
        compiler_params=params(53.75),
    )(activations, out_grads, proj_in_t, proj_out_t)


def add_kernel(one_ref, other_ref, out_ref):
    out_ref[...] = one_ref[...] + other_ref[...]


def add(one, other):
    return pl.pallas_call(
        add_kernel,
        out_shape=jax.ShapeDtypeStruct(one.shape, one.dtype),
        compiler_params=params(40),
    )(one, other)


def payload_kernel(one_ref, other_ref, weight_ref, out_ref):
    total = one_ref[...] + other_ref[...]
    weight = jnp.broadcast_to(weight_ref[...], (16, weight_ref.shape[1]))
    out_ref[...] = jnp.concatenate([total, weight], axis=0).astype(out_ref.dtype)


def add_to_payload(one, other, weight):
    rows, tok = one.shape
    return pl.pallas_call(
        payload_kernel,
        out_shape=jax.ShapeDtypeStruct((rows + 16, tok), jnp.bfloat16),
        compiler_params=params(40),
    )(one, other, weight)


def stack_kernel(_, __, *refs):
    parts, (out_ref, factors_ref) = refs[:-2], refs[-2:]
    for k, ref in enumerate(parts):
        out_ref[k] = ref[...]
        factors_ref[k] = ref[: factors_ref.shape[1]]


def stack(parts, rank, after):
    rows, tok = parts[0].shape
    whole = pl.BlockSpec(memory_space=pltpu.VMEM)
    return pl.pallas_call(
        stack_kernel,
        in_specs=[pl.BlockSpec(memory_space=pl.ANY)] * 2 + [whole] * len(parts),
        out_shape=[
            jax.ShapeDtypeStruct((len(parts), rows, tok), parts[0].dtype),
            jax.ShapeDtypeStruct((len(parts), rank, tok), parts[0].dtype),
        ],
        compiler_params=params(26),
    )(*after, *parts)


def lay_out_factors(blocks, factors, weights):
    rank = factors.shape[0] // 2
    here = pl.multiple_of(lax.rem(lax.axis_index("query"), 2) * rank, rank)
    there = pl.multiple_of(rank - here, rank)
    for k, (mine, other) in enumerate(blocks):
        span = slice(k * mine.shape[1], (k + 1) * mine.shape[1])
        factors[pl.ds(here, rank), span] = mine[:rank].astype(jnp.float32)
        factors[pl.ds(there, rank), span] = other[:rank].astype(jnp.float32)
        weights[:, span] = mine[rank:].astype(jnp.float32)[:1]


def block_pairs(mine, other):
    return [(mine.at[k], other.at[k]) for k in reversed(range(mine.shape[0]))]


def weigh_rows(first_row, end_row, row_count, factors, weights, weighted):
    rank = factors.shape[0] // 2
    act, weight = factors[:rank, :], weights[...]
    first = rank + lax.axis_index("dp") * row_count
    for i in range(first_row // rank, end_row // rank):
        left = (factors[pl.ds(first + i, 1), :] * act).astype(jnp.bfloat16)
        left = (weight * left.astype(jnp.float32)).astype(jnp.bfloat16)
        weighted[i * rank : (i + 1) * rank, :] = left


def range_scale(values):
    top = jnp.max(jnp.abs(values), keepdims=True)
    scale = jnp.ones_like(top)
    for low in (16, 48, 80, 112):
        scale = jnp.where(top > 2.0**low, 2.0 ** -min(low + 16, 126), scale)
        scale = jnp.where(top < 2.0**-low, 2.0 ** min(low + 16, 126), scale)
    return scale


def project_queries(row_count, factors, features, queries):
    rank = factors.shape[0] // 2
    act = factors[:rank, :]
    total = 0.0
    for near, query_ref in enumerate(queries):
        first = rank + (lax.axis_index("dp") ^ near) * row_count
        for i in range(row_count):
            row = factors[pl.ds(first + i, 1), :]
            features[near, i * rank : (i + 1) * rank, :] = (row * act).astype(jnp.bfloat16)
        total += jnp.dot(query_ref[...], features[near], preferred_element_type=jnp.float32)
    return total


def turn_kernel(row_count, query, near_query, own, own_other, *refs):
    out_ref, near_out_ref, plain_ref, factors, weights, features = refs
    out_ref[...] = query[...].T
    near_out_ref[...] = near_query[...].T
    lay_out_factors([(own, own_other)], factors, weights)
    plain_ref[...] = project_queries(row_count, factors, features, (out_ref, near_out_ref))


def turn_queries(queries, near_queries, own, own_other, rank, row_count):
    rows, count = queries.shape
    tok = own.shape[1]
    out = jax.ShapeDtypeStruct((count, rows), queries.dtype)
    return pl.pallas_call(
        functools.partial(turn_kernel, row_count),
        out_shape=[out, out, jax.ShapeDtypeStruct((count, tok), jnp.float32)],
        scratch_shapes=[
            pltpu.VMEM((2 * rank, tok), jnp.float32),
            pltpu.VMEM((1, tok), jnp.float32),
            pltpu.VMEM((2, rows, tok), jnp.bfloat16),
        ],
        compiler_params=params(26),
    )(queries, near_queries, own, own_other)


def share_kernel(
    row_count, own, own_other, mine, other, query_ref, near_query_ref, own_plain_ref, *refs
):
    factors, weights, features, gram = refs[-4:]
    out_refs = refs[:-4]
    lay_out_factors([(own, own_other)] + block_pairs(mine, other), factors, weights)
    rank = factors.shape[0] // 2
    tokens = factors.shape[1]
    tok = own.shape[1]
    plain = project_queries(
        row_count, factors.at[:, tok:], features, (query_ref, near_query_ref)
    )
    plain = jnp.concatenate([own_plain_ref[...], plain], axis=1)
    act = factors[:rank, :]
    weight = weights[...]
    live = weight > 0.0
    act = jnp.where(live, act, 0.0)
    grad = jnp.where(live, factors[rank:, :], 0.0)
    act_scale, grad_scale = range_scale(act), range_scale(grad)
    act, grad = act * act_scale, grad * grad_scale
    norms = jnp.sum(act * act, axis=0, keepdims=True) * jnp.sum(grad * grad, axis=0, keepdims=True)
    level = jnp.sum(weight * norms, axis=1, keepdims=True) / (tokens * rank * rank)
    step = 1.1 * level
    act_b, grad_b = act.astype(jnp.bfloat16), grad.astype(jnp.bfloat16)
    act_rows, grad_rows = act.T.astype(jnp.bfloat16), grad.T.astype(jnp.bfloat16)
    weighted = (plain * (weight * (1.0 / (tokens * step)))).astype(jnp.bfloat16)
    scale = act_scale * grad_scale
    for n, out_ref in enumerate(out_refs):
        block = slice(2 * n * tok, (2 * n + 1) * tok)
        for row in range(0, tokens, TILE // 2):
            here = slice(row, row + TILE // 2)
            tile = jnp.dot(act_rows[here], act_b[:, block], preferred_element_type=jnp.float32)
            tile *= jnp.dot(grad_rows[here], grad_b[:, block], preferred_element_type=jnp.float32)
            gram[n, here, :] = tile.astype(jnp.bfloat16)
        image = jnp.dot(weighted, gram[n], preferred_element_type=jnp.float32)
        share = ((2.0 - 0.1 / 1.1) * plain[:, block] - image) * scale * (scale / step)
        out_ref[...] = share.astype(out_ref.dtype)


def score_shares(
    own, own_other, mine, other, queries_t, near_queries_t, own_plain, rank, row_count
):
    blocks, tok = mine.shape[0] + 1, mine.shape[2]
    count, rows = queries_t.shape
    return pl.pallas_call(
        functools.partial(share_kernel, row_count),
        out_shape=[
            jax.ShapeDtypeStruct((count, tok), jnp.bfloat16 if k else jnp.float32)
            for k in range(0, blocks, 2)
        ],
        scratch_shapes=[
            pltpu.VMEM((2 * rank, tok * blocks), jnp.float32),
            pltpu.VMEM((1, tok * blocks), jnp.float32),
            pltpu.VMEM((2, rows, tok * (blocks - 1)), jnp.bfloat16),
            pltpu.VMEM((blocks // 2, tok * blocks, tok), jnp.bfloat16),
        ],
        compiler_params=params(26),
    )(own, own_other, mine, other, queries_t, near_queries_t, own_plain)


def build_columns(first, act, factors, right):
    rank = act.shape[0]
    for i in range(right.shape[0] // rank):
        row = rank + first + i
        right[i * rank : (i + 1) * rank, :] = (factors[row : row + 1, :] * act).astype(jnp.bfloat16)


def own_kernel(row_count, col_count, own, own_other, out, factors, weights, weighted, *rights):
    rank = factors.shape[0] // 2
    cols = col_count * rank
    lay_out_factors([(own, own_other)], factors, weights)
    weigh_rows(0, weighted.shape[0], row_count, factors, weights, weighted)
    act = factors[:rank, :]
    build_columns(0, act, factors, rights[0])
    for step in range(rank // col_count):
        if (step + 1) * col_count < rank:
            build_columns((step + 1) * col_count, act, factors, rights[(step + 1) % 2])
        out[:, step * cols : (step + 1) * cols] = lax.dot_general(
            weighted[...], rights[step % 2][...], NT, preferred_element_type=jnp.float32
        )


def own_tokens_sum(own, own_other, rank, row_count, col_count=8):
    tok = own.shape[1]
    rows, cols = row_count * rank, col_count * rank
    return pl.pallas_call(
        functools.partial(own_kernel, row_count, col_count),
        out_shape=jax.ShapeDtypeStruct((rows, rank * rank), jnp.float32),
        scratch_shapes=[
            pltpu.VMEM((2 * rank, tok), jnp.float32),
            pltpu.VMEM((1, tok), jnp.float32),
            pltpu.VMEM((rows, tok), jnp.bfloat16),
            pltpu.VMEM((cols, tok), jnp.bfloat16),
            pltpu.VMEM((cols, tok), jnp.bfloat16),
        ],
        compiler_params=params(16),
    )(own, own_other)


def hessian_kernel(row_count, col_count, mine, other, own_sum, out, *scratch):
    factors, weights, weighted, rights = *scratch[:3], scratch[3:5]
    result, sems = scratch[5:]
    rank = factors.shape[0] // 2
    blocks = mine.shape[0]
    tokens = factors.shape[1] // blocks * (blocks + 1)
    rows, cols = row_count * rank, col_count * rank
    lay_out_factors(block_pairs(mine, other), factors, weights)
    act = factors[:rank, :]
    copies = []
    build_columns(0, act, factors, rights[0])
    for step in range(rank // col_count):
        if (step + 1) * col_count < rank:
            build_columns((step + 1) * col_count, act, factors, rights[(step + 1) % 2])
        height = 2 * TILE if step and rows % (2 * TILE) == 0 else TILE
        for row in range(0, rows, height):
            if step == 0:
                weigh_rows(row, row + height, row_count, factors, weights, weighted)
            here = pl.ds(row, height), pl.ds(step * cols, cols)
            tile = lax.dot_general(
                weighted[row : row + height, :],
                rights[step % 2][...],
                NT,
                preferred_element_type=jnp.float32,
            )
            result[here] = (own_sum[here] + tile) * (1.0 / tokens)
            copy = pltpu.make_async_copy(result.at[here], out.at[here], sems.at[len(copies)])
            copy.start()
            copies.append(copy)
    for copy in copies:
        copy.wait()


def hessian_rows(mine, other, own_sum, rank, row_count, col_count=8):
    blocks, _, tok = mine.shape
    feat = rank * rank
    rows, cols = row_count * rank, col_count * rank
    return pl.pallas_call(
        functools.partial(hessian_kernel, row_count, col_count),
        out_specs=pl.BlockSpec(memory_space=pl.ANY),
        out_shape=jax.ShapeDtypeStruct((rows, feat), jnp.float32),
        scratch_shapes=[
            pltpu.VMEM((2 * rank, tok * blocks), jnp.float32),
            pltpu.VMEM((1, tok * blocks), jnp.float32),
            pltpu.VMEM((rows, tok * blocks), jnp.bfloat16),
            pltpu.VMEM((cols, tok * blocks), jnp.bfloat16),
            pltpu.VMEM((cols, tok * blocks), jnp.bfloat16),
            pltpu.VMEM((rows, feat), jnp.float32),
            pltpu.SemaphoreType.DMA((feat // cols * (rows // TILE),)),
        ],
        compiler_params=params(26),
    )(mine, other, own_sum)


def finish_kernel(payload_ref, *refs):
    shares, out_ref = refs[:-1], refs[-1]
    total = shares[0][...]
    for ref in shares[1:]:
        total = total + ref[...].astype(jnp.float32)
    weight = payload_ref[...].astype(jnp.float32)[-1:]
    out_ref[...] = jnp.where(weight > 0.0, total, 0.0).T.astype(out_ref.dtype)


def finish_scores(payload, shares):
    count, tok = shares[0].shape
    return pl.pallas_call(
        finish_kernel,
        out_shape=jax.ShapeDtypeStruct((tok, count), jnp.bfloat16),
        compiler_params=params(40),
    )(payload, *shares)


def swapped(array, axis, distance):
    return lax.ppermute(array, axis, [(i, i ^ distance) for i in range(lax.axis_size(axis))])


def few_tokens(activations, out_grads, proj_in, proj_out, queries, lengths, credit):
    dp_count = lax.axis_size("dp")
    query_count = lax.axis_size("query")
    rank = proj_in.shape[1]
    row_count = rank // dp_count
    seq_len = activations.shape[0] // lengths.shape[0]
    live = jnp.arange(seq_len, dtype=jnp.int32)[None, :] < lengths[:, None]
    weight = jnp.where(live, credit[:, None], 0).astype(jnp.float32).reshape(1, -1)
    near_queries = swapped(queries, "dp", 1)
    keep, send = project(activations, out_grads, proj_in.T, proj_out.T)
    other = swapped(send, "query", 1)
    distance = 2
    while distance < query_count:
        keep = add(keep, other)
        other = swapped(keep, "query", distance)
        distance *= 2
    own = add_to_payload(keep, other, weight)
    own_other = swapped(own, "query", 1)
    others = [swapped(own, "dp", k) for k in reversed(range(1, dp_count))]
    own_sum = own_tokens_sum(own, own_other, rank, row_count)
    queries_t, near_queries_t, own_plain = turn_queries(
        queries, near_queries, own, own_other, rank, row_count
    )
    mine, factors = stack(others, rank, (own_sum, queries_t))
    other = swapped(factors, "query", 1)
    shares = score_shares(
        own, own_other, mine, other, queries_t, near_queries_t, own_plain, rank, row_count
    )
    arrived = [swapped(share, "dp", 2 * n) for n, share in enumerate(shares) if n]
    hessian = hessian_rows(mine, other, own_sum, rank, row_count)
    return hessian, finish_scores(own, [shares[0]] + arrived)


def power_of_two(count):
    return count & (count - 1) == 0


def per_device(activations, *others):
    rank = others[1].shape[1]
    dp_count, query_count = lax.axis_size("dp"), lax.axis_size("query")
    pairs = min(dp_count, query_count) > 1 and power_of_two(dp_count) and power_of_two(query_count)
    if pairs and activations.shape[0] * dp_count <= rank * rank:
        return few_tokens(activations, *others)
    return many_tokens(activations, *others)


def solution(mesh):
    placed = (
        P(("groups", "dp"), "query"),
        P(("groups", "dp"), "query"),
        P("query", None),
        P("query", None),
        P(("groups", "dp"), "query"),
        P(("groups", "dp")),
        P(("groups", "dp")),
    )
    return jax.shard_map(
        per_device,
        mesh=mesh,
        in_specs=placed,
        out_specs=(P(("groups", "dp"), None), P(("groups", "dp"), "query")),
        check_vma=False,
    )
```

```python
import functools
import jax
import jax.numpy as jnp
from jax import lax
from jax.experimental import pallas as pl
from jax.experimental.pallas import tpu as pltpu
from jax.sharding import PartitionSpec as P


def kron_columns(grad_rows, act_rows, start, count):
    rank = grad_rows.shape[1]
    tokens_here = grad_rows.shape[0]
    grad_cols = lax.dynamic_slice_in_dim(grad_rows, start // rank, count // rank, 1)
    outer = grad_cols.astype(jnp.float32)[:, :, None] * act_rows.astype(jnp.float32)[:, None, :]
    return outer.reshape(tokens_here, count).astype(jnp.bfloat16)


def hessian_block(total, pieces, row_start, rows_own, col_start, col_count):
    grad_rows, act_rows, weights = pieces
    left = kron_columns(grad_rows, act_rows, row_start, rows_own)
    weighted = (weights.astype(jnp.float32)[:, None] * left.astype(jnp.float32)).astype(
        jnp.bfloat16
    )
    right = kron_columns(grad_rows, act_rows, col_start, col_count)
    return total + lax.dot_general(
        weighted, right, (((0,), (0,)), ((), ())), preferred_element_type=jnp.float32
    )


def fold_blocks(total, pieces, step_fn):
    count = pieces[0].shape[0]
    shaped = tuple((p.reshape((count // 512, 512) + p.shape[1:]) for p in pieces))

    def inner(carry, block):
        return (step_fn(carry, block), None)

    return lax.scan(inner, total, shaped)[0]


def split_parts(matrix):
    high_part = matrix.astype(jnp.bfloat16)
    first_rest = matrix - high_part.astype(jnp.float32)
    middle_part = first_rest.astype(jnp.bfloat16)
    low_part = (first_rest - middle_part.astype(jnp.float32)).astype(jnp.bfloat16)
    return (high_part, middle_part, low_part)


def many_tokens(activations, out_grads, proj_in, proj_out, queries, lengths, credit):
    tok_rows = activations.shape[0]
    seq_len = tok_rows // lengths.shape[0]
    dp_count = lax.axis_size("dp")
    query_count = lax.axis_size("query")
    dp_index = lax.axis_index("dp")
    query_index = lax.axis_index("query")
    part_act = jnp.dot(activations, proj_in, preferred_element_type=jnp.float32)
    part_grad = jnp.dot(out_grads, proj_out, preferred_element_type=jnp.float32)
    sum_act, sum_grad = lax.psum((part_act, part_grad), "query")
    act_proj = sum_act.astype(jnp.bfloat16)
    grad_proj = sum_grad.astype(jnp.bfloat16)
    rank = act_proj.shape[1]
    feat = rank * rank
    live = jnp.arange(seq_len, dtype=jnp.int32)[None, :] < lengths[:, None]
    weight = (credit[:, None].astype(jnp.float32) * live.astype(jnp.float32)).reshape(-1)
    mask = live.astype(jnp.float32).reshape(-1)
    weight_wire = weight.astype(jnp.bfloat16)
    rows_own = feat // dp_count
    row_start = dp_index * rows_own
    all_tokens = tok_rows * dp_count
    col_count = feat // query_count
    col_start = query_index * col_count
    owned = fold_blocks(
        jnp.zeros((rows_own, col_count), jnp.float32),
        (
            lax.all_gather(grad_proj, "dp", axis=0, tiled=True),
            lax.all_gather(act_proj, "dp", axis=0, tiled=True),
            lax.all_gather(weight_wire, "dp", axis=0, tiled=True),
        ),
        lambda carry, block: hessian_block(carry, block, row_start, rows_own, col_start, col_count),
    )
    hessian = lax.all_gather(owned, "query", axis=1, tiled=True) / all_tokens
    diagonal_block = lax.dynamic_slice_in_dim(hessian, row_start, rows_own, 1)
    level = lax.psum(jnp.trace(diagonal_block), "dp") / feat
    step = 1.1 * level
    high_part, middle_part, low_part = split_parts(hessian)
    piece = lax.all_gather(queries, "dp", axis=0, tiled=True)
    result = jnp.zeros(queries.shape, jnp.float32)
    for part_matrix in (low_part, middle_part, high_part):
        columns = part_matrix
        result = result + jnp.dot(columns, piece, preferred_element_type=jnp.float32)
    query_f = queries.astype(jnp.float32)
    precond = ((2.0 * query_f - (result + 0.1 * level * query_f) / step) / step).astype(
        jnp.bfloat16
    )
    local_features = kron_columns(grad_proj, act_proj, 0, feat)
    piece = lax.all_gather(precond, "dp", axis=0, tiled=True)
    columns = lax.slice_in_dim(local_features, 0, piece.shape[0], axis=1)
    scores = jnp.zeros((tok_rows, precond.shape[1]), jnp.float32) + jnp.dot(
        columns, piece, preferred_element_type=jnp.float32
    )
    return (hessian, (scores * mask[:, None]).astype(jnp.bfloat16))


MIB = 1024 * 1024
TILE = 256
NT = (((1,), (1,)), ((), ()))


def params(mib):
    return pltpu.CompilerParams(vmem_limit_bytes=int(mib * MIB))


def project_kernel(act, grad, pin, pout, keep_ref, send_ref, act_v, grad_v, pin_v, pout_v, sems):
    chunk = grad.shape[1] // 2
    spans = [pl.ds(0, chunk), pl.ds(chunk, chunk)]
    pairs = [(pin, pin_v), (act, act_v), (pout, pout_v)]
    pairs += [(grad.at[:, span], grad_v.at[:, span]) for span in spans]
    copies = [pltpu.make_async_copy(s, d, sems.at[n]) for n, (s, d) in enumerate(pairs)]
    for copy in copies:
        copy.start()
    copies[0].wait()
    copies[1].wait()
    part_act = lax.dot_general(pin_v[...], act_v[...], NT, preferred_element_type=jnp.float32)
    copies[2].wait()
    part_grad = jnp.zeros_like(part_act)
    for copy, span in zip(copies[3:], spans):
        copy.wait()
        part_grad += lax.dot_general(
            pout_v[:, span], grad_v[:, span], NT, preferred_element_type=jnp.float32
        )
    factors = jnp.concatenate([part_act, part_grad], axis=0)
    half = factors.shape[1] // 2
    even = lax.rem(lax.axis_index("query"), 2) == 0
    keep_ref[...] = jnp.where(even, factors[:, :half], factors[:, half:])
    send_ref[...] = jnp.where(even, factors[:, half:], factors[:, :half])


def project(activations, out_grads, proj_in_t, proj_out_t):
    tok, d_here = activations.shape
    f_here = out_grads.shape[1]
    rank = proj_in_t.shape[0]
    out = jax.ShapeDtypeStruct((2 * rank, tok // 2), jnp.float32)
    return pl.pallas_call(
        project_kernel,
        in_specs=[pl.BlockSpec(memory_space=pl.ANY)] * 4,
        out_shape=[out, out],
        scratch_shapes=[
            pltpu.VMEM((tok, d_here), jnp.bfloat16),
            pltpu.VMEM((tok, f_here), jnp.bfloat16),
            pltpu.VMEM((rank, d_here), jnp.bfloat16),
            pltpu.VMEM((rank, f_here), jnp.bfloat16),
            pltpu.SemaphoreType.DMA((5,)),
        ],
        compiler_params=params(53.75),
    )(activations, out_grads, proj_in_t, proj_out_t)


def add_kernel(one_ref, other_ref, out_ref):
    out_ref[...] = one_ref[...] + other_ref[...]


def add(one, other):
    return pl.pallas_call(
        add_kernel,
        out_shape=jax.ShapeDtypeStruct(one.shape, one.dtype),
        compiler_params=params(40),
    )(one, other)


def payload_kernel(one_ref, other_ref, weight_ref, out_ref):
    total = one_ref[...] + other_ref[...]
    half = total.shape[1]
    even = lax.rem(lax.axis_index("query"), 2) == 0
    weight = jnp.where(even, weight_ref[:, :half], weight_ref[:, half:])
    weight = jnp.broadcast_to(weight, (16, half))
    out_ref[...] = jnp.concatenate([total, weight], axis=0).astype(out_ref.dtype)


def add_to_payload(one, other, weight):
    rows, tok = one.shape
    return pl.pallas_call(
        payload_kernel,
        out_shape=jax.ShapeDtypeStruct((rows + 16, tok), jnp.bfloat16),
        compiler_params=params(40),
    )(one, other, weight)


def stack_kernel(_, __, *refs):
    for k, ref in enumerate(refs[:-1]):
        refs[-1][k] = ref[...]


def stack(parts, after):
    whole = pl.BlockSpec(memory_space=pltpu.VMEM)
    return pl.pallas_call(
        stack_kernel,
        in_specs=[pl.BlockSpec(memory_space=pl.ANY)] * 2 + [whole] * len(parts),
        out_shape=jax.ShapeDtypeStruct((len(parts),) + parts[0].shape, parts[0].dtype),
        compiler_params=params(26),
    )(*after, *parts)


def lay_out_factors(parts, factors, weights):
    rows = factors.shape[0]
    for k, part in enumerate(parts):
        span = slice(k * part.shape[1], (k + 1) * part.shape[1])
        factors[:, span] = part[:rows].astype(jnp.float32)
        weights[:, span] = part[rows:].astype(jnp.float32)[:1]


def parts_of(stacked):
    return [stacked.at[k] for k in reversed(range(stacked.shape[0]))]


def weigh_rows(first_row, end_row, row_count, factors, weights, weighted):
    rank = factors.shape[0] // 2
    act, weight = factors[:rank, :], weights[...]
    first = rank + lax.axis_index("dp") * row_count
    for i in range(first_row // rank, end_row // rank):
        left = (factors[pl.ds(first + i, 1), :] * act).astype(jnp.bfloat16)
        left = (weight * left.astype(jnp.float32)).astype(jnp.bfloat16)
        weighted[i * rank : (i + 1) * rank, :] = left


def range_scale(values):
    top = jnp.max(jnp.abs(values), keepdims=True)
    scale = jnp.ones_like(top)
    for low in (16, 48, 80, 112):
        scale = jnp.where(top > 2.0**low, 2.0 ** -min(low + 16, 126), scale)
        scale = jnp.where(top < 2.0**-low, 2.0 ** min(low + 16, 126), scale)
    return scale


def project_queries(row_count, factors, features, queries):
    rank = factors.shape[0] // 2
    act = factors[:rank, :]
    total = 0.0
    for near, query_ref in enumerate(queries):
        first = rank + (lax.axis_index("dp") ^ near) * row_count
        for i in range(row_count):
            row = factors[pl.ds(first + i, 1), :]
            features[near, i * rank : (i + 1) * rank, :] = (row * act).astype(jnp.bfloat16)
        total += jnp.dot(query_ref[...], features[near], preferred_element_type=jnp.float32)
    return total


def turn_kernel(row_count, query, near_query, own, own_other, *refs):
    out_ref, near_out_ref, plain_ref, factors, weights, features = refs
    out_ref[...] = query[...].T
    near_out_ref[...] = near_query[...].T
    lay_out_factors([own, own_other], factors, weights)
    plain_ref[...] = project_queries(row_count, factors, features, (out_ref, near_out_ref))


def turn_queries(queries, near_queries, own, own_other, rank, row_count):
    rows, count = queries.shape
    tok = 2 * own.shape[1]
    out = jax.ShapeDtypeStruct((count, rows), queries.dtype)
    return pl.pallas_call(
        functools.partial(turn_kernel, row_count),
        out_shape=[out, out, jax.ShapeDtypeStruct((count, tok), jnp.float32)],
        scratch_shapes=[
            pltpu.VMEM((2 * rank, tok), jnp.float32),
            pltpu.VMEM((1, tok), jnp.float32),
            pltpu.VMEM((2, rows, tok), jnp.bfloat16),
        ],
        compiler_params=params(26),
    )(queries, near_queries, own, own_other)


def half_kernel(row_count, mine, query_ref, near_query_ref, plain_ref, factors, weights, features):
    lay_out_factors(parts_of(mine), factors, weights)
    plain_ref[...] = project_queries(row_count, factors, features, (query_ref, near_query_ref))


def project_half(mine, queries_t, near_queries_t, rank, row_count):
    count, rows = queries_t.shape
    tokens = mine.shape[0] * mine.shape[2]
    return pl.pallas_call(
        functools.partial(half_kernel, row_count),
        out_shape=jax.ShapeDtypeStruct((count, tokens), jnp.float32),
        scratch_shapes=[
            pltpu.VMEM((2 * rank, tokens), jnp.float32),
            pltpu.VMEM((1, tokens), jnp.float32),
            pltpu.VMEM((2, rows, tokens), jnp.bfloat16),
        ],
        compiler_params=params(26),
    )(mine, queries_t, near_queries_t)


def share_kernel(row_count, own, own_other, mine, other, query_ref, near_query_ref, *refs):
    own_plain_ref, half_plain_ref = refs[:2]
    out_refs = refs[2:-4]
    factors, weights, features, gram = refs[-4:]
    half = own.shape[1]
    blocks = mine.shape[0] + 1
    lay_out_factors(
        [own] + parts_of(mine) + [own_other] + parts_of(other), factors, weights
    )
    rank = factors.shape[0] // 2
    tokens = factors.shape[1]
    plain = project_queries(
        row_count,
        factors.at[:, (blocks + 1) * half :],
        features,
        (query_ref, near_query_ref),
    )
    plain = jnp.concatenate(
        [own_plain_ref[:, :half], half_plain_ref[...], own_plain_ref[:, half:], plain], axis=1
    )
    weight = weights[...]
    live = weight > 0.0
    act = jnp.where(live, factors[:rank, :], 0.0)
    grad = jnp.where(live, factors[rank:, :], 0.0)
    act_scale, grad_scale = range_scale(act), range_scale(grad)
    act, grad = act * act_scale, grad * grad_scale
    norms = jnp.sum(act * act, axis=0, keepdims=True) * jnp.sum(grad * grad, axis=0, keepdims=True)
    level = jnp.sum(weight * norms, axis=1, keepdims=True) / (tokens * rank * rank)
    step = 1.1 * level
    act_b, grad_b = act.astype(jnp.bfloat16), grad.astype(jnp.bfloat16)
    act_rows, grad_rows = act.T.astype(jnp.bfloat16), grad.T.astype(jnp.bfloat16)
    weighted = (plain * (weight * (1.0 / (tokens * step)))).astype(jnp.bfloat16)
    scale = act_scale * grad_scale

    def block_of(array, k):
        starts = (k * half, (blocks + k) * half)
        return jnp.concatenate([array[:, i : i + half] for i in starts], axis=1)

    for n, out_ref in enumerate(out_refs):
        act_block, grad_block = block_of(act_b, 2 * n), block_of(grad_b, 2 * n)
        for row in range(0, tokens, TILE // 2):
            here = slice(row, row + TILE // 2)
            tile = jnp.dot(act_rows[here], act_block, preferred_element_type=jnp.float32)
            tile *= jnp.dot(grad_rows[here], grad_block, preferred_element_type=jnp.float32)
            gram[n, here, :] = tile.astype(jnp.bfloat16)
        image = jnp.dot(weighted, gram[n], preferred_element_type=jnp.float32)
        share = ((2.0 - 0.1 / 1.1) * block_of(plain, 2 * n) - image) * scale * (scale / step)
        out_ref[...] = share.astype(out_ref.dtype)


def score_shares(own, own_other, mine, other, queries_t, near_queries_t, plains, rank, row_count):
    blocks, half = mine.shape[0] + 1, mine.shape[2]
    count, rows = queries_t.shape
    tokens = 2 * half * blocks
    return pl.pallas_call(
        functools.partial(share_kernel, row_count),
        out_shape=[
            jax.ShapeDtypeStruct((count, 2 * half), jnp.bfloat16 if k else jnp.float32)
            for k in range(0, blocks, 2)
        ],
        scratch_shapes=[
            pltpu.VMEM((2 * rank, tokens), jnp.float32),
            pltpu.VMEM((1, tokens), jnp.float32),
            pltpu.VMEM((2, rows, (blocks - 1) * half), jnp.bfloat16),
            pltpu.VMEM((blocks // 2, tokens, 2 * half), jnp.bfloat16),
        ],
        compiler_params=params(26),
    )(own, own_other, mine, other, queries_t, near_queries_t, *plains)


def build_columns(first, act, factors, right):
    rank = act.shape[0]
    for i in range(right.shape[0] // rank):
        row = rank + first + i
        right[i * rank : (i + 1) * rank, :] = (factors[row : row + 1, :] * act).astype(jnp.bfloat16)


def own_kernel(row_count, col_count, own, own_other, out, factors, weights, weighted, *rights):
    rank = factors.shape[0] // 2
    cols = col_count * rank
    lay_out_factors([own, own_other], factors, weights)
    weigh_rows(0, weighted.shape[0], row_count, factors, weights, weighted)
    act = factors[:rank, :]
    build_columns(0, act, factors, rights[0])
    for step in range(rank // col_count):
        if (step + 1) * col_count < rank:
            build_columns((step + 1) * col_count, act, factors, rights[(step + 1) % 2])
        out[:, step * cols : (step + 1) * cols] = lax.dot_general(
            weighted[...], rights[step % 2][...], NT, preferred_element_type=jnp.float32
        )


def own_tokens_sum(own, own_other, rank, row_count, col_count=8):
    tok = 2 * own.shape[1]
    rows, cols = row_count * rank, col_count * rank
    return pl.pallas_call(
        functools.partial(own_kernel, row_count, col_count),
        out_shape=jax.ShapeDtypeStruct((rows, rank * rank), jnp.float32),
        scratch_shapes=[
            pltpu.VMEM((2 * rank, tok), jnp.float32),
            pltpu.VMEM((1, tok), jnp.float32),
            pltpu.VMEM((rows, tok), jnp.bfloat16),
            pltpu.VMEM((cols, tok), jnp.bfloat16),
            pltpu.VMEM((cols, tok), jnp.bfloat16),
        ],
        compiler_params=params(16),
    )(own, own_other)


def hessian_kernel(row_count, col_count, mine, other, own_sum, out, *scratch):
    factors, weights, weighted, rights = *scratch[:3], scratch[3:5]
    result, sems = scratch[5:]
    rank = factors.shape[0] // 2
    blocks = mine.shape[0]
    tokens = factors.shape[1] // blocks * (blocks + 1)
    rows, cols = row_count * rank, col_count * rank
    lay_out_factors(parts_of(mine) + parts_of(other), factors, weights)
    act = factors[:rank, :]
    copies = []
    build_columns(0, act, factors, rights[0])
    for step in range(rank // col_count):
        if (step + 1) * col_count < rank:
            build_columns((step + 1) * col_count, act, factors, rights[(step + 1) % 2])
        for row in range(0, rows, TILE):
            if step == 0:
                weigh_rows(row, row + TILE, row_count, factors, weights, weighted)
            here = pl.ds(row, TILE), pl.ds(step * cols, cols)
            tile = lax.dot_general(
                weighted[row : row + TILE, :],
                rights[step % 2][...],
                NT,
                preferred_element_type=jnp.float32,
            )
            result[here] = (own_sum[here] + tile) * (1.0 / tokens)
            copy = pltpu.make_async_copy(result.at[here], out.at[here], sems.at[len(copies)])
            copy.start()
            copies.append(copy)
    for copy in copies:
        copy.wait()


def hessian_rows(mine, other, own_sum, rank, row_count, col_count=8):
    blocks, _, half = mine.shape
    tok = 2 * half
    feat = rank * rank
    rows, cols = row_count * rank, col_count * rank
    return pl.pallas_call(
        functools.partial(hessian_kernel, row_count, col_count),
        out_specs=pl.BlockSpec(memory_space=pl.ANY),
        out_shape=jax.ShapeDtypeStruct((rows, feat), jnp.float32),
        scratch_shapes=[
            pltpu.VMEM((2 * rank, tok * blocks), jnp.float32),
            pltpu.VMEM((1, tok * blocks), jnp.float32),
            pltpu.VMEM((rows, tok * blocks), jnp.bfloat16),
            pltpu.VMEM((cols, tok * blocks), jnp.bfloat16),
            pltpu.VMEM((cols, tok * blocks), jnp.bfloat16),
            pltpu.VMEM((rows, feat), jnp.float32),
            pltpu.SemaphoreType.DMA((feat // cols * (rows // TILE),)),
        ],
        compiler_params=params(26),
    )(mine, other, own_sum)


def finish_kernel(own, own_other, *refs):
    shares, out_ref = refs[:-1], refs[-1]
    total = shares[0][...]
    for ref in shares[1:]:
        total = total + ref[...].astype(jnp.float32)
    weight = jnp.concatenate([part[...].astype(jnp.float32)[-1:] for part in (own, own_other)], axis=1)
    scores = jnp.where(weight > 0.0, total, 0.0).T.astype(out_ref.dtype)
    half = own.shape[1]
    here = pl.multiple_of(lax.rem(lax.axis_index("query"), 2) * half, half)
    out_ref[pl.ds(here, half), :] = scores[:half]
    out_ref[pl.ds(pl.multiple_of(half - here, half), half), :] = scores[half:]


def finish_scores(own, own_other, shares):
    count, tok = shares[0].shape
    return pl.pallas_call(
        finish_kernel,
        out_shape=jax.ShapeDtypeStruct((tok, count), jnp.bfloat16),
        compiler_params=params(40),
    )(own, own_other, *shares)


def swapped(array, axis, distance):
    return lax.ppermute(array, axis, [(i, i ^ distance) for i in range(lax.axis_size(axis))])


def few_tokens(activations, out_grads, proj_in, proj_out, queries, lengths, credit):
    dp_count = lax.axis_size("dp")
    query_count = lax.axis_size("query")
    rank = proj_in.shape[1]
    row_count = rank // dp_count
    seq_len = activations.shape[0] // lengths.shape[0]
    live = jnp.arange(seq_len, dtype=jnp.int32)[None, :] < lengths[:, None]
    weight = jnp.where(live, credit[:, None], 0).astype(jnp.float32).reshape(1, -1)
    near_queries = swapped(queries, "dp", 1)
    keep, send = project(activations, out_grads, proj_in.T, proj_out.T)
    other = swapped(send, "query", 1)
    distance = 2
    while distance < query_count:
        keep = add(keep, other)
        other = swapped(keep, "query", distance)
        distance *= 2
    own = add_to_payload(keep, other, weight)
    own_other = swapped(own, "query", 1)
    others = [swapped(own, "dp", k) for k in reversed(range(1, dp_count))]
    own_sum = own_tokens_sum(own, own_other, rank, row_count)
    queries_t, near_queries_t, own_plain = turn_queries(
        queries, near_queries, own, own_other, rank, row_count
    )
    mine = stack(others, (own_sum, queries_t))
    other = swapped(mine, "query", 1)
    half_plain = project_half(mine, queries_t, near_queries_t, rank, row_count)
    plains = (own_plain, half_plain)
    shares = score_shares(
        own, own_other, mine, other, queries_t, near_queries_t, plains, rank, row_count
    )
    arrived = [swapped(share, "dp", 2 * n) for n, share in enumerate(shares) if n]
    hessian = hessian_rows(mine, other, own_sum, rank, row_count)
    return hessian, finish_scores(own, own_other, [shares[0]] + arrived)


def power_of_two(count):
    return count & (count - 1) == 0


def per_device(activations, *others):
    rank = others[1].shape[1]
    dp_count, query_count = lax.axis_size("dp"), lax.axis_size("query")
    pairs = activations.shape[0] % 256 == 0 and min(dp_count, query_count) > 1 and power_of_two(dp_count) and power_of_two(query_count)
    if pairs and activations.shape[0] * dp_count <= rank * rank:
        return few_tokens(activations, *others)
    return many_tokens(activations, *others)


def solution(mesh):
    placed = (
        P(("groups", "dp"), "query"),
        P(("groups", "dp"), "query"),
        P("query", None),
        P("query", None),
        P(("groups", "dp"), "query"),
        P(("groups", "dp")),
        P(("groups", "dp")),
    )
    return jax.shard_map(
        per_device,
        mesh=mesh,
        in_specs=placed,
        out_specs=(P(("groups", "dp"), None), P(("groups", "dp"), "query")),
        check_vma=False,
    )
```

```python
import functools
import jax
import jax.numpy as jnp
from jax import lax
from jax.experimental import pallas as pl
from jax.experimental.pallas import tpu as pltpu
from jax.sharding import PartitionSpec as P


def kron_columns(grad_rows, act_rows, start, count):
    rank = grad_rows.shape[1]
    tokens_here = grad_rows.shape[0]
    grad_cols = lax.dynamic_slice_in_dim(grad_rows, start // rank, count // rank, 1)
    outer = grad_cols.astype(jnp.float32)[:, :, None] * act_rows.astype(jnp.float32)[:, None, :]
    return outer.reshape(tokens_here, count).astype(jnp.bfloat16)


def hessian_block(total, pieces, row_start, rows_own, col_start, col_count):
    grad_rows, act_rows, weights = pieces
    left = kron_columns(grad_rows, act_rows, row_start, rows_own)
    weighted = (weights.astype(jnp.float32)[:, None] * left.astype(jnp.float32)).astype(
        jnp.bfloat16
    )
    right = kron_columns(grad_rows, act_rows, col_start, col_count)
    return total + lax.dot_general(
        weighted, right, (((0,), (0,)), ((), ())), preferred_element_type=jnp.float32
    )


def fold_blocks(total, pieces, step_fn):
    count = pieces[0].shape[0]
    shaped = tuple((p.reshape((count // 512, 512) + p.shape[1:]) for p in pieces))

    def inner(carry, block):
        return (step_fn(carry, block), None)

    return lax.scan(inner, total, shaped)[0]


def split_parts(matrix):
    high_part = matrix.astype(jnp.bfloat16)
    first_rest = matrix - high_part.astype(jnp.float32)
    middle_part = first_rest.astype(jnp.bfloat16)
    low_part = (first_rest - middle_part.astype(jnp.float32)).astype(jnp.bfloat16)
    return (high_part, middle_part, low_part)


def many_tokens(activations, out_grads, proj_in, proj_out, queries, lengths, credit):
    tok_rows = activations.shape[0]
    seq_len = tok_rows // lengths.shape[0]
    dp_count = lax.axis_size("dp")
    query_count = lax.axis_size("query")
    dp_index = lax.axis_index("dp")
    query_index = lax.axis_index("query")
    part_act = jnp.dot(activations, proj_in, preferred_element_type=jnp.float32)
    part_grad = jnp.dot(out_grads, proj_out, preferred_element_type=jnp.float32)
    sum_act, sum_grad = lax.psum((part_act, part_grad), "query")
    act_proj = sum_act.astype(jnp.bfloat16)
    grad_proj = sum_grad.astype(jnp.bfloat16)
    rank = act_proj.shape[1]
    feat = rank * rank
    live = jnp.arange(seq_len, dtype=jnp.int32)[None, :] < lengths[:, None]
    weight = (credit[:, None].astype(jnp.float32) * live.astype(jnp.float32)).reshape(-1)
    mask = live.astype(jnp.float32).reshape(-1)
    weight_wire = weight.astype(jnp.bfloat16)
    rows_own = feat // dp_count
    row_start = dp_index * rows_own
    all_tokens = tok_rows * dp_count
    col_count = feat // query_count
    col_start = query_index * col_count
    owned = fold_blocks(
        jnp.zeros((rows_own, col_count), jnp.float32),
        (
            lax.all_gather(grad_proj, "dp", axis=0, tiled=True),
            lax.all_gather(act_proj, "dp", axis=0, tiled=True),
            lax.all_gather(weight_wire, "dp", axis=0, tiled=True),
        ),
        lambda carry, block: hessian_block(carry, block, row_start, rows_own, col_start, col_count),
    )
    hessian = lax.all_gather(owned, "query", axis=1, tiled=True) / all_tokens
    diagonal_block = lax.dynamic_slice_in_dim(hessian, row_start, rows_own, 1)
    level = lax.psum(jnp.trace(diagonal_block), "dp") / feat
    step = 1.1 * level
    high_part, middle_part, low_part = split_parts(hessian)
    piece = lax.all_gather(queries, "dp", axis=0, tiled=True)
    result = jnp.zeros(queries.shape, jnp.float32)
    for part_matrix in (low_part, middle_part, high_part):
        columns = part_matrix
        result = result + jnp.dot(columns, piece, preferred_element_type=jnp.float32)
    query_f = queries.astype(jnp.float32)
    precond = ((2.0 * query_f - (result + 0.1 * level * query_f) / step) / step).astype(
        jnp.bfloat16
    )
    local_features = kron_columns(grad_proj, act_proj, 0, feat)
    piece = lax.all_gather(precond, "dp", axis=0, tiled=True)
    columns = lax.slice_in_dim(local_features, 0, piece.shape[0], axis=1)
    scores = jnp.zeros((tok_rows, precond.shape[1]), jnp.float32) + jnp.dot(
        columns, piece, preferred_element_type=jnp.float32
    )
    return (hessian, (scores * mask[:, None]).astype(jnp.bfloat16))


MIB = 1024 * 1024
TILE = 256
NT = (((1,), (1,)), ((), ()))


def params(mib):
    return pltpu.CompilerParams(vmem_limit_bytes=int(mib * MIB))


def project_kernel(act, grad, pin, pout, keep_ref, send_ref, act_v, grad_v, pin_v, pout_v, sems):
    chunk = grad.shape[1] // 2
    spans = [pl.ds(0, chunk), pl.ds(chunk, chunk)]
    pairs = [(pin, pin_v), (act, act_v), (pout, pout_v)]
    pairs += [(grad.at[:, span], grad_v.at[:, span]) for span in spans]
    copies = [pltpu.make_async_copy(s, d, sems.at[n]) for n, (s, d) in enumerate(pairs)]
    for copy in copies:
        copy.start()
    copies[0].wait()
    copies[1].wait()
    part_act = lax.dot_general(pin_v[...], act_v[...], NT, preferred_element_type=jnp.float32)
    copies[2].wait()
    part_grad = jnp.zeros_like(part_act)
    for copy, span in zip(copies[3:], spans):
        copy.wait()
        part_grad += lax.dot_general(
            pout_v[:, span], grad_v[:, span], NT, preferred_element_type=jnp.float32
        )
    factors = jnp.concatenate([part_act, part_grad], axis=0)
    half = factors.shape[1] // 2
    even = lax.rem(lax.axis_index("query"), 2) == 0
    keep_ref[...] = jnp.where(even, factors[:, :half], factors[:, half:])
    send_ref[...] = jnp.where(even, factors[:, half:], factors[:, :half])


def project(activations, out_grads, proj_in_t, proj_out_t):
    tok, d_here = activations.shape
    f_here = out_grads.shape[1]
    rank = proj_in_t.shape[0]
    out = jax.ShapeDtypeStruct((2 * rank, tok // 2), jnp.float32)
    return pl.pallas_call(
        project_kernel,
        in_specs=[pl.BlockSpec(memory_space=pl.ANY)] * 4,
        out_shape=[out, out],
        scratch_shapes=[
            pltpu.VMEM((tok, d_here), jnp.bfloat16),
            pltpu.VMEM((tok, f_here), jnp.bfloat16),
            pltpu.VMEM((rank, d_here), jnp.bfloat16),
            pltpu.VMEM((rank, f_here), jnp.bfloat16),
            pltpu.SemaphoreType.DMA((5,)),
        ],
        compiler_params=params(53.75),
    )(activations, out_grads, proj_in_t, proj_out_t)


def add_kernel(one_ref, other_ref, out_ref):
    out_ref[...] = one_ref[...] + other_ref[...]


def add(one, other):
    return pl.pallas_call(
        add_kernel,
        out_shape=jax.ShapeDtypeStruct(one.shape, one.dtype),
        compiler_params=params(40),
    )(one, other)


def payload_kernel(one_ref, other_ref, weight_ref, out_ref):
    total = one_ref[...] + other_ref[...]
    half = total.shape[1]
    even = lax.rem(lax.axis_index("query"), 2) == 0
    weight = jnp.where(even, weight_ref[:, :half], weight_ref[:, half:])
    weight = jnp.broadcast_to(weight, (16, half))
    out_ref[...] = jnp.concatenate([total, weight], axis=0).astype(out_ref.dtype)


def add_to_payload(one, other, weight):
    rows, tok = one.shape
    return pl.pallas_call(
        payload_kernel,
        out_shape=jax.ShapeDtypeStruct((rows + 16, tok), jnp.bfloat16),
        compiler_params=params(40),
    )(one, other, weight)


def stack_kernel(_, __, *refs):
    for k, ref in enumerate(refs[:-1]):
        refs[-1][k] = ref[...]


def stack(parts, after):
    whole = pl.BlockSpec(memory_space=pltpu.VMEM)
    return pl.pallas_call(
        stack_kernel,
        in_specs=[pl.BlockSpec(memory_space=pl.ANY)] * 2 + [whole] * len(parts),
        out_shape=jax.ShapeDtypeStruct((len(parts),) + parts[0].shape, parts[0].dtype),
        compiler_params=params(26),
    )(*after, *parts)


def lay_out_factors(parts, factors, weights):
    rows = factors.shape[0]
    for k, part in enumerate(parts):
        span = slice(k * part.shape[1], (k + 1) * part.shape[1])
        factors[:, span] = part[:rows].astype(jnp.float32)
        weights[:, span] = part[rows:].astype(jnp.float32)[:1]


def parts_of(stacked):
    return [stacked.at[k] for k in reversed(range(stacked.shape[0]))]


def weigh_rows(first_row, end_row, row_count, factors, weights, weighted):
    rank = factors.shape[0] // 2
    act, weight = factors[:rank, :], weights[...]
    first = rank + lax.axis_index("dp") * row_count
    for i in range(first_row // rank, end_row // rank):
        left = (factors[pl.ds(first + i, 1), :] * act).astype(jnp.bfloat16)
        left = (weight * left.astype(jnp.float32)).astype(jnp.bfloat16)
        weighted[i * rank : (i + 1) * rank, :] = left


def range_scale(values):
    top = jnp.max(jnp.abs(values), keepdims=True)
    scale = jnp.ones_like(top)
    for low in (16, 48, 80, 112):
        scale = jnp.where(top > 2.0**low, 2.0 ** -min(low + 16, 126), scale)
        scale = jnp.where(top < 2.0**-low, 2.0 ** min(low + 16, 126), scale)
    return scale


def project_queries(row_count, factors, features, queries):
    rank = factors.shape[0] // 2
    act = factors[:rank, :]
    total = 0.0
    for near, query_ref in enumerate(queries):
        first = rank + (lax.axis_index("dp") ^ near) * row_count
        for i in range(row_count):
            row = factors[pl.ds(first + i, 1), :]
            features[near, i * rank : (i + 1) * rank, :] = (row * act).astype(jnp.bfloat16)
        total += jnp.dot(query_ref[...], features[near], preferred_element_type=jnp.float32)
    return total


def turn_kernel(row_count, query, near_query, own, own_other, *refs):
    out_ref, near_out_ref, plain_ref, factors, weights, features = refs
    out_ref[...] = query[...].T
    near_out_ref[...] = near_query[...].T
    lay_out_factors([own, own_other], factors, weights)
    plain_ref[...] = project_queries(row_count, factors, features, (out_ref, near_out_ref))


def turn_queries(queries, near_queries, own, own_other, rank, row_count):
    rows, count = queries.shape
    tok = 2 * own.shape[1]
    out = jax.ShapeDtypeStruct((count, rows), queries.dtype)
    return pl.pallas_call(
        functools.partial(turn_kernel, row_count),
        out_shape=[out, out, jax.ShapeDtypeStruct((count, tok), jnp.float32)],
        scratch_shapes=[
            pltpu.VMEM((2 * rank, tok), jnp.float32),
            pltpu.VMEM((1, tok), jnp.float32),
            pltpu.VMEM((2, rows, tok), jnp.bfloat16),
        ],
        compiler_params=params(26),
    )(queries, near_queries, own, own_other)


def half_kernel(row_count, mine, query_ref, near_query_ref, plain_ref, factors, weights, features):
    lay_out_factors(parts_of(mine), factors, weights)
    plain_ref[...] = project_queries(row_count, factors, features, (query_ref, near_query_ref))


def project_half(mine, queries_t, near_queries_t, rank, row_count):
    count, rows = queries_t.shape
    tokens = mine.shape[0] * mine.shape[2]
    return pl.pallas_call(
        functools.partial(half_kernel, row_count),
        out_shape=jax.ShapeDtypeStruct((count, tokens), jnp.float32),
        scratch_shapes=[
            pltpu.VMEM((2 * rank, tokens), jnp.float32),
            pltpu.VMEM((1, tokens), jnp.float32),
            pltpu.VMEM((2, rows, tokens), jnp.bfloat16),
        ],
        compiler_params=params(26),
    )(mine, queries_t, near_queries_t)


def share_kernel(row_count, own, own_other, mine, other, query_ref, near_query_ref, *refs):
    own_plain_ref, half_plain_ref = refs[:2]
    out_refs = refs[2:-4]
    factors, weights, features, gram = refs[-4:]
    half = own.shape[1]
    blocks = mine.shape[0] + 1
    lay_out_factors(
        [own] + parts_of(mine) + [own_other] + parts_of(other), factors, weights
    )
    rank = factors.shape[0] // 2
    tokens = factors.shape[1]
    plain = project_queries(
        row_count,
        factors.at[:, (blocks + 1) * half :],
        features,
        (query_ref, near_query_ref),
    )
    plain = jnp.concatenate(
        [own_plain_ref[:, :half], half_plain_ref[...], own_plain_ref[:, half:], plain], axis=1
    )
    weight = weights[...]
    live = weight > 0.0
    act = jnp.where(live, factors[:rank, :], 0.0)
    grad = jnp.where(live, factors[rank:, :], 0.0)
    act_scale, grad_scale = range_scale(act), range_scale(grad)
    act, grad = act * act_scale, grad * grad_scale
    norms = jnp.sum(act * act, axis=0, keepdims=True) * jnp.sum(grad * grad, axis=0, keepdims=True)
    level = jnp.sum(weight * norms, axis=1, keepdims=True) / (tokens * rank * rank)
    step = 1.1 * level
    act_b, grad_b = act.astype(jnp.bfloat16), grad.astype(jnp.bfloat16)
    act_rows, grad_rows = act.T.astype(jnp.bfloat16), grad.T.astype(jnp.bfloat16)
    weighted = (plain * (weight * (1.0 / (tokens * step)))).astype(jnp.bfloat16)
    scale = act_scale * grad_scale

    def block_of(array, k):
        starts = (k * half, (blocks + k) * half)
        return jnp.concatenate([array[:, i : i + half] for i in starts], axis=1)

    for n, out_ref in enumerate(out_refs):
        act_block, grad_block = block_of(act_b, 2 * n), block_of(grad_b, 2 * n)
        for row in range(0, tokens, TILE // 2):
            here = slice(row, row + TILE // 2)
            tile = jnp.dot(act_rows[here], act_block, preferred_element_type=jnp.float32)
            tile *= jnp.dot(grad_rows[here], grad_block, preferred_element_type=jnp.float32)
            gram[n, here, :] = tile.astype(jnp.bfloat16)
        image = jnp.dot(weighted, gram[n], preferred_element_type=jnp.float32)
        share = ((2.0 - 0.1 / 1.1) * block_of(plain, 2 * n) - image) * scale * (scale / step)
        out_ref[...] = share.astype(out_ref.dtype)


def score_shares(own, own_other, mine, other, queries_t, near_queries_t, plains, rank, row_count):
    blocks, half = mine.shape[0] + 1, mine.shape[2]
    count, rows = queries_t.shape
    tokens = 2 * half * blocks
    return pl.pallas_call(
        functools.partial(share_kernel, row_count),
        out_shape=[
            jax.ShapeDtypeStruct((count, 2 * half), jnp.bfloat16 if k else jnp.float32)
            for k in range(0, blocks, 2)
        ],
        scratch_shapes=[
            pltpu.VMEM((2 * rank, tokens), jnp.float32),
            pltpu.VMEM((1, tokens), jnp.float32),
            pltpu.VMEM((2, rows, (blocks - 1) * half), jnp.bfloat16),
            pltpu.VMEM((blocks // 2, tokens, 2 * half), jnp.bfloat16),
        ],
        compiler_params=params(26),
    )(own, own_other, mine, other, queries_t, near_queries_t, *plains)


def build_columns(first, act, factors, right):
    rank = act.shape[0]
    for i in range(right.shape[0] // rank):
        row = rank + first + i
        right[i * rank : (i + 1) * rank, :] = (factors[row : row + 1, :] * act).astype(jnp.bfloat16)


def own_kernel(row_count, col_count, own, own_other, out, factors, weights, weighted, *rights):
    rank = factors.shape[0] // 2
    cols = col_count * rank
    lay_out_factors([own, own_other], factors, weights)
    weigh_rows(0, weighted.shape[0], row_count, factors, weights, weighted)
    act = factors[:rank, :]
    build_columns(0, act, factors, rights[0])
    for step in range(rank // col_count):
        if (step + 1) * col_count < rank:
            build_columns((step + 1) * col_count, act, factors, rights[(step + 1) % 2])
        out[:, step * cols : (step + 1) * cols] = lax.dot_general(
            weighted[...], rights[step % 2][...], NT, preferred_element_type=jnp.float32
        )


def own_tokens_sum(own, own_other, rank, row_count, col_count=8):
    tok = 2 * own.shape[1]
    rows, cols = row_count * rank, col_count * rank
    return pl.pallas_call(
        functools.partial(own_kernel, row_count, col_count),
        out_shape=jax.ShapeDtypeStruct((rows, rank * rank), jnp.float32),
        scratch_shapes=[
            pltpu.VMEM((2 * rank, tok), jnp.float32),
            pltpu.VMEM((1, tok), jnp.float32),
            pltpu.VMEM((rows, tok), jnp.bfloat16),
            pltpu.VMEM((cols, tok), jnp.bfloat16),
            pltpu.VMEM((cols, tok), jnp.bfloat16),
        ],
        compiler_params=params(16),
    )(own, own_other)


def hessian_kernel(row_count, col_count, mine, other, own_sum, out, *scratch):
    factors, weights, weighted, rights = *scratch[:3], scratch[3:5]
    result, sems = scratch[5:]
    rank = factors.shape[0] // 2
    blocks = mine.shape[0]
    tokens = factors.shape[1] // blocks * (blocks + 1)
    rows, cols = row_count * rank, col_count * rank
    lay_out_factors(parts_of(mine) + parts_of(other), factors, weights)
    act = factors[:rank, :]
    copies = []
    build_columns(0, act, factors, rights[0])
    for step in range(rank // col_count):
        if (step + 1) * col_count < rank:
            build_columns((step + 1) * col_count, act, factors, rights[(step + 1) % 2])
        for row in range(0, rows, TILE):
            if step == 0:
                weigh_rows(row, row + TILE, row_count, factors, weights, weighted)
            here = pl.ds(row, TILE), pl.ds(step * cols, cols)
            tile = lax.dot_general(
                weighted[row : row + TILE, :],
                rights[step % 2][...],
                NT,
                preferred_element_type=jnp.float32,
            )
            result[here] = (own_sum[here] + tile) * (1.0 / tokens)
            copy = pltpu.make_async_copy(result.at[here], out.at[here], sems.at[len(copies)])
            copy.start()
            copies.append(copy)
    for copy in copies:
        copy.wait()


def hessian_rows(mine, other, own_sum, rank, row_count, col_count=8):
    blocks, _, half = mine.shape
    tok = 2 * half
    feat = rank * rank
    rows, cols = row_count * rank, col_count * rank
    return pl.pallas_call(
        functools.partial(hessian_kernel, row_count, col_count),
        out_specs=pl.BlockSpec(memory_space=pl.ANY),
        out_shape=jax.ShapeDtypeStruct((rows, feat), jnp.float32),
        scratch_shapes=[
            pltpu.VMEM((2 * rank, tok * blocks), jnp.float32),
            pltpu.VMEM((1, tok * blocks), jnp.float32),
            pltpu.VMEM((rows, tok * blocks), jnp.bfloat16),
            pltpu.VMEM((cols, tok * blocks), jnp.bfloat16),
            pltpu.VMEM((cols, tok * blocks), jnp.bfloat16),
            pltpu.VMEM((rows, feat), jnp.float32),
            pltpu.SemaphoreType.DMA((feat // cols * (rows // TILE),)),
        ],
        compiler_params=params(30),
    )(mine, other, own_sum)


def finish_kernel(own, own_other, *refs):
    shares, out_ref = refs[:-1], refs[-1]
    total = shares[0][...]
    for ref in shares[1:]:
        total = total + ref[...].astype(jnp.float32)
    weight = jnp.concatenate([part[...].astype(jnp.float32)[-1:] for part in (own, own_other)], axis=1)
    scores = jnp.where(weight > 0.0, total, 0.0).T.astype(out_ref.dtype)
    half = own.shape[1]
    here = pl.multiple_of(lax.rem(lax.axis_index("query"), 2) * half, half)
    out_ref[pl.ds(here, half), :] = scores[:half]
    out_ref[pl.ds(pl.multiple_of(half - here, half), half), :] = scores[half:]


def finish_scores(own, own_other, shares):
    count, tok = shares[0].shape
    return pl.pallas_call(
        finish_kernel,
        out_shape=jax.ShapeDtypeStruct((tok, count), jnp.bfloat16),
        compiler_params=params(40),
    )(own, own_other, *shares)


def swapped(array, axis, distance):
    return lax.ppermute(array, axis, [(i, i ^ distance) for i in range(lax.axis_size(axis))])


def few_tokens(activations, out_grads, proj_in, proj_out, queries, lengths, credit):
    dp_count = lax.axis_size("dp")
    query_count = lax.axis_size("query")
    rank = proj_in.shape[1]
    row_count = rank // dp_count
    seq_len = activations.shape[0] // lengths.shape[0]
    live = jnp.arange(seq_len, dtype=jnp.int32)[None, :] < lengths[:, None]
    weight = jnp.where(live, credit[:, None], 0).astype(jnp.float32).reshape(1, -1)
    near_queries = swapped(queries, "dp", 1)
    keep, send = project(activations, out_grads, proj_in.T, proj_out.T)
    other = swapped(send, "query", 1)
    distance = 2
    while distance < query_count:
        keep = add(keep, other)
        other = swapped(keep, "query", distance)
        distance *= 2
    own = add_to_payload(keep, other, weight)
    own_other = swapped(own, "query", 1)
    others = [swapped(own, "dp", k) for k in reversed(range(1, dp_count))]
    own_sum = own_tokens_sum(own, own_other, rank, row_count)
    queries_t, near_queries_t, own_plain = turn_queries(
        queries, near_queries, own, own_other, rank, row_count
    )
    mine = stack(others, (own_sum, queries_t))
    other = swapped(mine, "query", 1)
    half_plain = project_half(mine, queries_t, near_queries_t, rank, row_count)
    plains = (own_plain, half_plain)
    shares = score_shares(
        own, own_other, mine, other, queries_t, near_queries_t, plains, rank, row_count
    )
    arrived = [swapped(share, "dp", 2 * n) for n, share in enumerate(shares) if n]
    hessian = hessian_rows(mine, other, own_sum, rank, row_count)
    return hessian, finish_scores(own, own_other, [shares[0]] + arrived)


def power_of_two(count):
    return count & (count - 1) == 0


def per_device(activations, *others):
    rank = others[1].shape[1]
    dp_count, query_count = lax.axis_size("dp"), lax.axis_size("query")
    pairs = activations.shape[0] % 256 == 0 and min(dp_count, query_count) > 1 and power_of_two(dp_count) and power_of_two(query_count)
    if pairs and activations.shape[0] * dp_count <= rank * rank:
        return few_tokens(activations, *others)
    return many_tokens(activations, *others)


def solution(mesh):
    placed = (
        P(("groups", "dp"), "query"),
        P(("groups", "dp"), "query"),
        P("query", None),
        P("query", None),
        P(("groups", "dp"), "query"),
        P(("groups", "dp")),
        P(("groups", "dp")),
    )
    return jax.shard_map(
        per_device,
        mesh=mesh,
        in_specs=placed,
        out_specs=(P(("groups", "dp"), None), P(("groups", "dp"), "query")),
        check_vma=False,
    )
```

```python
import functools
import jax
import jax.numpy as jnp
from jax import lax
from jax.experimental import pallas as pl
from jax.experimental.pallas import tpu as pltpu
from jax.sharding import PartitionSpec as P


def kron_columns(grad_rows, act_rows, start, count):
    rank = grad_rows.shape[1]
    tokens_here = grad_rows.shape[0]
    grad_cols = lax.dynamic_slice_in_dim(grad_rows, start // rank, count // rank, 1)
    outer = grad_cols.astype(jnp.float32)[:, :, None] * act_rows.astype(jnp.float32)[:, None, :]
    return outer.reshape(tokens_here, count).astype(jnp.bfloat16)


def hessian_block(total, pieces, row_start, rows_own, col_start, col_count):
    grad_rows, act_rows, weights = pieces
    left = kron_columns(grad_rows, act_rows, row_start, rows_own)
    weighted = (weights.astype(jnp.float32)[:, None] * left.astype(jnp.float32)).astype(
        jnp.bfloat16
    )
    right = kron_columns(grad_rows, act_rows, col_start, col_count)
    return total + lax.dot_general(
        weighted, right, (((0,), (0,)), ((), ())), preferred_element_type=jnp.float32
    )


def fold_blocks(total, pieces, step_fn):
    count = pieces[0].shape[0]
    shaped = tuple((p.reshape((count // 512, 512) + p.shape[1:]) for p in pieces))

    def inner(carry, block):
        return (step_fn(carry, block), None)

    return lax.scan(inner, total, shaped)[0]


def split_parts(matrix):
    high_part = matrix.astype(jnp.bfloat16)
    first_rest = matrix - high_part.astype(jnp.float32)
    middle_part = first_rest.astype(jnp.bfloat16)
    low_part = (first_rest - middle_part.astype(jnp.float32)).astype(jnp.bfloat16)
    return (high_part, middle_part, low_part)


def many_tokens(activations, out_grads, proj_in, proj_out, queries, lengths, credit):
    tok_rows = activations.shape[0]
    seq_len = tok_rows // lengths.shape[0]
    dp_count = lax.axis_size("dp")
    query_count = lax.axis_size("query")
    dp_index = lax.axis_index("dp")
    query_index = lax.axis_index("query")
    part_act = jnp.dot(activations, proj_in, preferred_element_type=jnp.float32)
    part_grad = jnp.dot(out_grads, proj_out, preferred_element_type=jnp.float32)
    sum_act, sum_grad = lax.psum((part_act, part_grad), "query")
    act_proj = sum_act.astype(jnp.bfloat16)
    grad_proj = sum_grad.astype(jnp.bfloat16)
    rank = act_proj.shape[1]
    feat = rank * rank
    live = jnp.arange(seq_len, dtype=jnp.int32)[None, :] < lengths[:, None]
    weight = (credit[:, None].astype(jnp.float32) * live.astype(jnp.float32)).reshape(-1)
    mask = live.astype(jnp.float32).reshape(-1)
    weight_wire = weight.astype(jnp.bfloat16)
    rows_own = feat // dp_count
    row_start = dp_index * rows_own
    all_tokens = tok_rows * dp_count
    col_count = feat // query_count
    col_start = query_index * col_count
    owned = fold_blocks(
        jnp.zeros((rows_own, col_count), jnp.float32),
        (
            lax.all_gather(grad_proj, "dp", axis=0, tiled=True),
            lax.all_gather(act_proj, "dp", axis=0, tiled=True),
            lax.all_gather(weight_wire, "dp", axis=0, tiled=True),
        ),
        lambda carry, block: hessian_block(carry, block, row_start, rows_own, col_start, col_count),
    )
    hessian = lax.all_gather(owned, "query", axis=1, tiled=True) / all_tokens
    diagonal_block = lax.dynamic_slice_in_dim(hessian, row_start, rows_own, 1)
    level = lax.psum(jnp.trace(diagonal_block), "dp") / feat
    step = 1.1 * level
    high_part, middle_part, low_part = split_parts(hessian)
    piece = lax.all_gather(queries, "dp", axis=0, tiled=True)
    result = jnp.zeros(queries.shape, jnp.float32)
    for part_matrix in (low_part, middle_part, high_part):
        columns = part_matrix
        result = result + jnp.dot(columns, piece, preferred_element_type=jnp.float32)
    query_f = queries.astype(jnp.float32)
    precond = ((2.0 * query_f - (result + 0.1 * level * query_f) / step) / step).astype(
        jnp.bfloat16
    )
    local_features = kron_columns(grad_proj, act_proj, 0, feat)
    piece = lax.all_gather(precond, "dp", axis=0, tiled=True)
    columns = lax.slice_in_dim(local_features, 0, piece.shape[0], axis=1)
    scores = jnp.zeros((tok_rows, precond.shape[1]), jnp.float32) + jnp.dot(
        columns, piece, preferred_element_type=jnp.float32
    )
    return (hessian, (scores * mask[:, None]).astype(jnp.bfloat16))


MIB = 1024 * 1024
TILE = 256
NT = (((1,), (1,)), ((), ()))


def params(mib):
    return pltpu.CompilerParams(vmem_limit_bytes=int(mib * MIB))


def project_kernel(act, grad, pin, pout, keep_ref, send_ref, act_v, grad_v, pin_v, pout_v, sems):
    chunk = grad.shape[1] // 2
    spans = [pl.ds(0, chunk), pl.ds(chunk, chunk)]
    pairs = [(pin, pin_v), (act, act_v), (pout, pout_v)]
    pairs += [(grad.at[:, span], grad_v.at[:, span]) for span in spans]
    copies = [pltpu.make_async_copy(s, d, sems.at[n]) for n, (s, d) in enumerate(pairs)]
    for copy in copies:
        copy.start()
    copies[0].wait()
    copies[1].wait()
    part_act = lax.dot_general(pin_v[...], act_v[...], NT, preferred_element_type=jnp.float32)
    copies[2].wait()
    part_grad = jnp.zeros_like(part_act)
    for copy, span in zip(copies[3:], spans):
        copy.wait()
        part_grad += lax.dot_general(
            pout_v[:, span], grad_v[:, span], NT, preferred_element_type=jnp.float32
        )
    even = lax.rem(lax.axis_index("query"), 2) == 0
    keep_ref[...] = jnp.where(even, part_act, part_grad)
    send_ref[...] = jnp.where(even, part_grad, part_act)


def project(activations, out_grads, proj_in_t, proj_out_t):
    tok, d_here = activations.shape
    f_here = out_grads.shape[1]
    rank = proj_in_t.shape[0]
    out = jax.ShapeDtypeStruct((rank, tok), jnp.float32)
    return pl.pallas_call(
        project_kernel,
        in_specs=[pl.BlockSpec(memory_space=pl.ANY)] * 4,
        out_shape=[out, out],
        scratch_shapes=[
            pltpu.VMEM((tok, d_here), jnp.bfloat16),
            pltpu.VMEM((tok, f_here), jnp.bfloat16),
            pltpu.VMEM((rank, d_here), jnp.bfloat16),
            pltpu.VMEM((rank, f_here), jnp.bfloat16),
            pltpu.SemaphoreType.DMA((5,)),
        ],
        compiler_params=params(53.75),
    )(activations, out_grads, proj_in_t, proj_out_t)


def add_kernel(one_ref, other_ref, out_ref):
    out_ref[...] = one_ref[...] + other_ref[...]


def add(one, other):
    return pl.pallas_call(
        add_kernel,
        out_shape=jax.ShapeDtypeStruct(one.shape, one.dtype),
        compiler_params=params(40),
    )(one, other)


def payload_kernel(one_ref, other_ref, weight_ref, out_ref):
    total = jnp.where(weight_ref[...] > 0.0, one_ref[...] + other_ref[...], 0.0)
    weight = jnp.broadcast_to(weight_ref[...], (16, weight_ref.shape[1]))
    out_ref[...] = jnp.concatenate([total, weight], axis=0).astype(out_ref.dtype)


def add_to_payload(one, other, weight):
    rows, tok = one.shape
    return pl.pallas_call(
        payload_kernel,
        out_shape=jax.ShapeDtypeStruct((rows + 16, tok), jnp.bfloat16),
        compiler_params=params(40),
    )(one, other, weight)


def stack_kernel(_, __, *refs):
    parts, (out_ref, factors_ref) = refs[:-2], refs[-2:]
    for k, ref in enumerate(parts):
        out_ref[k] = ref[...]
        factors_ref[k] = ref[: factors_ref.shape[1]]


def stack(parts, rank, after):
    rows, tok = parts[0].shape
    whole = pl.BlockSpec(memory_space=pltpu.VMEM)
    return pl.pallas_call(
        stack_kernel,
        in_specs=[pl.BlockSpec(memory_space=pl.ANY)] * 2 + [whole] * len(parts),
        out_shape=[
            jax.ShapeDtypeStruct((len(parts), rows, tok), parts[0].dtype),
            jax.ShapeDtypeStruct((len(parts), rank, tok), parts[0].dtype),
        ],
        compiler_params=params(26),
    )(*after, *parts)


def lay_out_factors(blocks, factors, weights):
    rank = factors.shape[0] // 2
    here = pl.multiple_of(lax.rem(lax.axis_index("query"), 2) * rank, rank)
    there = pl.multiple_of(rank - here, rank)
    for k, (mine, other) in enumerate(blocks):
        span = slice(k * mine.shape[1], (k + 1) * mine.shape[1])
        factors[pl.ds(here, rank), span] = mine[:rank].astype(jnp.float32)
        factors[pl.ds(there, rank), span] = other[:rank].astype(jnp.float32)
        weights[:, span] = mine[rank:].astype(jnp.float32)[:1]


def block_pairs(mine, other):
    return [(mine.at[k], other.at[k]) for k in reversed(range(mine.shape[0]))]


def weigh_rows(first_row, end_row, row_count, factors, weights, weighted):
    rank = factors.shape[0] // 2
    act, weight = factors[:rank, :], weights[...]
    first = rank + lax.axis_index("dp") * row_count
    for i in range(first_row // rank, end_row // rank):
        left = (factors[pl.ds(first + i, 1), :] * act).astype(jnp.bfloat16)
        left = (weight * left.astype(jnp.float32)).astype(jnp.bfloat16)
        weighted[i * rank : (i + 1) * rank, :] = left


def range_scale(values):
    top = jnp.max(jnp.abs(values), keepdims=True)
    scale = jnp.ones_like(top)
    for low in (16, 48, 80, 112):
        scale = jnp.where(top > 2.0**low, 2.0 ** -min(low + 16, 126), scale)
        scale = jnp.where(top < 2.0**-low, 2.0 ** min(low + 16, 126), scale)
    return scale


def project_queries(row_count, factors, features, queries):
    rank = factors.shape[0] // 2
    act = factors[:rank, :]
    total = 0.0
    for near, query_ref in enumerate(queries):
        first = rank + (lax.axis_index("dp") ^ near) * row_count
        for i in range(row_count):
            row = factors[pl.ds(first + i, 1), :]
            features[near, i * rank : (i + 1) * rank, :] = (row * act).astype(jnp.bfloat16)
        total += jnp.dot(query_ref[...], features[near], preferred_element_type=jnp.float32)
    return total


def turn_kernel(row_count, query, near_query, own, own_other, *refs):
    out_ref, near_out_ref, plain_ref, factors, weights, features = refs
    out_ref[...] = query[...].T
    near_out_ref[...] = near_query[...].T
    lay_out_factors([(own, own_other)], factors, weights)
    plain_ref[...] = project_queries(row_count, factors, features, (out_ref, near_out_ref))


def turn_queries(queries, near_queries, own, own_other, rank, row_count):
    rows, count = queries.shape
    tok = own.shape[1]
    out = jax.ShapeDtypeStruct((count, rows), queries.dtype)
    return pl.pallas_call(
        functools.partial(turn_kernel, row_count),
        out_shape=[out, out, jax.ShapeDtypeStruct((count, tok), jnp.float32)],
        scratch_shapes=[
            pltpu.VMEM((2 * rank, tok), jnp.float32),
            pltpu.VMEM((1, tok), jnp.float32),
            pltpu.VMEM((2, rows, tok), jnp.bfloat16),
        ],
        compiler_params=params(26),
    )(queries, near_queries, own, own_other)


def share_kernel(
    row_count, own, own_other, mine, other, query_ref, near_query_ref, own_plain_ref, *refs
):
    factors, weights, features, gram = refs[-4:]
    out_refs = refs[:-4]
    lay_out_factors([(own, own_other)] + block_pairs(mine, other), factors, weights)
    rank = factors.shape[0] // 2
    tokens = factors.shape[1]
    tok = own.shape[1]
    plain = project_queries(
        row_count, factors.at[:, tok:], features, (query_ref, near_query_ref)
    )
    plain = jnp.concatenate([own_plain_ref[...], plain], axis=1)
    act = factors[:rank, :]
    weight = weights[...]
    act, grad = factors[:rank, :], factors[rank:, :]
    act_scale, grad_scale = range_scale(act), range_scale(grad)
    act, grad = act * act_scale, grad * grad_scale
    norms = jnp.sum(act * act, axis=0, keepdims=True) * jnp.sum(grad * grad, axis=0, keepdims=True)
    level = jnp.sum(weight * norms, axis=1, keepdims=True) / (tokens * rank * rank)
    step = 1.1 * level
    act_b, grad_b = act.astype(jnp.bfloat16), grad.astype(jnp.bfloat16)
    weighted = (plain * (weight * (1.0 / (tokens * step)))).astype(jnp.bfloat16)
    scale = act_scale * grad_scale
    for n, out_ref in enumerate(out_refs):
        block = slice(2 * n * tok, (2 * n + 1) * tok)
        act_rows, grad_rows = act_b[:, block].T, grad_b[:, block].T
        for col in range(0, tokens, TILE):
            there = slice(col, col + TILE)
            for row in range(0, tok, TILE // 2):
                here = slice(row, row + TILE // 2)
                tile = jnp.dot(act_rows[here], act_b[:, there], preferred_element_type=jnp.float32)
                tile *= jnp.dot(
                    grad_rows[here], grad_b[:, there], preferred_element_type=jnp.float32
                )
                gram[n, here, there] = tile.astype(jnp.bfloat16)
        image = lax.dot_general(weighted, gram[n], NT, preferred_element_type=jnp.float32)
        share = ((2.0 - 0.1 / 1.1) * plain[:, block] - image) * scale * (scale / step)
        out_ref[...] = share.astype(out_ref.dtype)


def score_shares(
    own, own_other, mine, other, queries_t, near_queries_t, own_plain, rank, row_count
):
    blocks, tok = mine.shape[0] + 1, mine.shape[2]
    count, rows = queries_t.shape
    return pl.pallas_call(
        functools.partial(share_kernel, row_count),
        out_shape=[
            jax.ShapeDtypeStruct((count, tok), jnp.bfloat16 if k else jnp.float32)
            for k in range(0, blocks, 2)
        ],
        scratch_shapes=[
            pltpu.VMEM((2 * rank, tok * blocks), jnp.float32),
            pltpu.VMEM((1, tok * blocks), jnp.float32),
            pltpu.VMEM((2, rows, tok * (blocks - 1)), jnp.bfloat16),
            pltpu.VMEM((blocks // 2, tok, tok * blocks), jnp.bfloat16),
        ],
        compiler_params=params(26),
    )(own, own_other, mine, other, queries_t, near_queries_t, own_plain)


def build_columns(first, act, factors, right):
    rank = act.shape[0]
    for i in range(right.shape[0] // rank):
        row = rank + first + i
        right[i * rank : (i + 1) * rank, :] = (factors[row : row + 1, :] * act).astype(jnp.bfloat16)


def own_kernel(row_count, col_count, own, own_other, out, factors, weights, weighted, *rights):
    rank = factors.shape[0] // 2
    cols = col_count * rank
    lay_out_factors([(own, own_other)], factors, weights)
    weigh_rows(0, weighted.shape[0], row_count, factors, weights, weighted)
    act = factors[:rank, :]
    build_columns(0, act, factors, rights[0])
    for step in range(rank // col_count):
        if (step + 1) * col_count < rank:
            build_columns((step + 1) * col_count, act, factors, rights[(step + 1) % 2])
        out[:, step * cols : (step + 1) * cols] = lax.dot_general(
            weighted[...], rights[step % 2][...], NT, preferred_element_type=jnp.float32
        )


def own_tokens_sum(own, own_other, rank, row_count, col_count=8):
    tok = own.shape[1]
    rows, cols = row_count * rank, col_count * rank
    return pl.pallas_call(
        functools.partial(own_kernel, row_count, col_count),
        out_shape=jax.ShapeDtypeStruct((rows, rank * rank), jnp.float32),
        scratch_shapes=[
            pltpu.VMEM((2 * rank, tok), jnp.float32),
            pltpu.VMEM((1, tok), jnp.float32),
            pltpu.VMEM((rows, tok), jnp.bfloat16),
            pltpu.VMEM((cols, tok), jnp.bfloat16),
            pltpu.VMEM((cols, tok), jnp.bfloat16),
        ],
        compiler_params=params(16),
    )(own, own_other)


def hessian_kernel(row_count, col_count, mine, other, own_sum, out, *scratch):
    factors, weights, weighted, rights = *scratch[:3], scratch[3:5]
    result, sems = scratch[5:]
    rank = factors.shape[0] // 2
    blocks = mine.shape[0]
    tokens = factors.shape[1] // blocks * (blocks + 1)
    rows, cols = row_count * rank, col_count * rank
    lay_out_factors(block_pairs(mine, other), factors, weights)
    act = factors[:rank, :]
    copies = []
    build_columns(0, act, factors, rights[0])
    for step in range(rank // col_count):
        if (step + 1) * col_count < rank:
            build_columns((step + 1) * col_count, act, factors, rights[(step + 1) % 2])
        for row in range(0, rows, TILE):
            if step == 0:
                weigh_rows(row, row + TILE, row_count, factors, weights, weighted)
            here = pl.ds(row, TILE), pl.ds(step * cols, cols)
            tile = lax.dot_general(
                weighted[row : row + TILE, :],
                rights[step % 2][...],
                NT,
                preferred_element_type=jnp.float32,
            )
            result[here] = (own_sum[here] + tile) * (1.0 / tokens)
            copy = pltpu.make_async_copy(result.at[here], out.at[here], sems.at[len(copies)])
            copy.start()
            copies.append(copy)
    for copy in copies:
        copy.wait()


def hessian_rows(mine, other, own_sum, rank, row_count, col_count=8):
    blocks, _, tok = mine.shape
    feat = rank * rank
    rows, cols = row_count * rank, col_count * rank
    return pl.pallas_call(
        functools.partial(hessian_kernel, row_count, col_count),
        out_specs=pl.BlockSpec(memory_space=pl.ANY),
        out_shape=jax.ShapeDtypeStruct((rows, feat), jnp.float32),
        scratch_shapes=[
            pltpu.VMEM((2 * rank, tok * blocks), jnp.float32),
            pltpu.VMEM((1, tok * blocks), jnp.float32),
            pltpu.VMEM((rows, tok * blocks), jnp.bfloat16),
            pltpu.VMEM((cols, tok * blocks), jnp.bfloat16),
            pltpu.VMEM((cols, tok * blocks), jnp.bfloat16),
            pltpu.VMEM((rows, feat), jnp.float32),
            pltpu.SemaphoreType.DMA((feat // cols * (rows // TILE),)),
        ],
        compiler_params=params(26),
    )(mine, other, own_sum)


def finish_kernel(payload_ref, *refs):
    shares, out_ref = refs[:-1], refs[-1]
    total = shares[0][...]
    for ref in shares[1:]:
        total = total + ref[...].astype(jnp.float32)
    weight = payload_ref[...].astype(jnp.float32)[-1:]
    out_ref[...] = jnp.where(weight > 0.0, total, 0.0).T.astype(out_ref.dtype)


def finish_scores(payload, shares):
    count, tok = shares[0].shape
    return pl.pallas_call(
        finish_kernel,
        out_shape=jax.ShapeDtypeStruct((tok, count), jnp.bfloat16),
        compiler_params=params(40),
    )(payload, *shares)


def swapped(array, axis, distance):
    return lax.ppermute(array, axis, [(i, i ^ distance) for i in range(lax.axis_size(axis))])


def few_tokens(activations, out_grads, proj_in, proj_out, queries, lengths, credit):
    dp_count = lax.axis_size("dp")
    query_count = lax.axis_size("query")
    rank = proj_in.shape[1]
    row_count = rank // dp_count
    seq_len = activations.shape[0] // lengths.shape[0]
    live = jnp.arange(seq_len, dtype=jnp.int32)[None, :] < lengths[:, None]
    weight = jnp.where(live, credit[:, None], 0).astype(jnp.float32).reshape(1, -1)
    near_queries = swapped(queries, "dp", 1)
    keep, send = project(activations, out_grads, proj_in.T, proj_out.T)
    other = swapped(send, "query", 1)
    distance = 2
    while distance < query_count:
        keep = add(keep, other)
        other = swapped(keep, "query", distance)
        distance *= 2
    own = add_to_payload(keep, other, weight)
    own_other = swapped(own, "query", 1)
    others = [swapped(own, "dp", k) for k in reversed(range(1, dp_count))]
    own_sum = own_tokens_sum(own, own_other, rank, row_count)
    queries_t, near_queries_t, own_plain = turn_queries(
        queries, near_queries, own, own_other, rank, row_count
    )
    mine, factors = stack(others, rank, (own_sum, queries_t))
    other = swapped(factors, "query", 1)
    shares = score_shares(
        own, own_other, mine, other, queries_t, near_queries_t, own_plain, rank, row_count
    )
    arrived = [swapped(share, "dp", 2 * n) for n, share in enumerate(shares) if n]
    hessian = hessian_rows(mine, other, own_sum, rank, row_count)
    return hessian, finish_scores(own, [shares[0]] + arrived)


def power_of_two(count):
    return count & (count - 1) == 0


def per_device(activations, *others):
    rank = others[1].shape[1]
    dp_count, query_count = lax.axis_size("dp"), lax.axis_size("query")
    pairs = min(dp_count, query_count) > 1 and power_of_two(dp_count) and power_of_two(query_count)
    if pairs and activations.shape[0] * dp_count <= rank * rank:
        return few_tokens(activations, *others)
    return many_tokens(activations, *others)


def solution(mesh):
    placed = (
        P(("groups", "dp"), "query"),
        P(("groups", "dp"), "query"),
        P("query", None),
        P("query", None),
        P(("groups", "dp"), "query"),
        P(("groups", "dp")),
        P(("groups", "dp")),
    )
    return jax.shard_map(
        per_device,
        mesh=mesh,
        in_specs=placed,
        out_specs=(P(("groups", "dp"), None), P(("groups", "dp"), "query")),
        check_vma=False,
    )
```

```python
import functools
import jax
import jax.numpy as jnp
from jax import lax
from jax.experimental import pallas as pl
from jax.experimental.pallas import tpu as pltpu
from jax.sharding import PartitionSpec as P


def kron_columns(grad_rows, act_rows, start, count):
    rank = grad_rows.shape[1]
    tokens_here = grad_rows.shape[0]
    grad_cols = lax.dynamic_slice_in_dim(grad_rows, start // rank, count // rank, 1)
    outer = grad_cols.astype(jnp.float32)[:, :, None] * act_rows.astype(jnp.float32)[:, None, :]
    return outer.reshape(tokens_here, count).astype(jnp.bfloat16)


def hessian_block(total, pieces, row_start, rows_own, col_start, col_count):
    grad_rows, act_rows, weights = pieces
    left = kron_columns(grad_rows, act_rows, row_start, rows_own)
    weighted = (weights.astype(jnp.float32)[:, None] * left.astype(jnp.float32)).astype(
        jnp.bfloat16
    )
    right = kron_columns(grad_rows, act_rows, col_start, col_count)
    return total + lax.dot_general(
        weighted, right, (((0,), (0,)), ((), ())), preferred_element_type=jnp.float32
    )


def fold_blocks(total, pieces, step_fn):
    count = pieces[0].shape[0]
    shaped = tuple((p.reshape((count // 512, 512) + p.shape[1:]) for p in pieces))

    def inner(carry, block):
        return (step_fn(carry, block), None)

    return lax.scan(inner, total, shaped)[0]


def split_parts(matrix):
    high_part = matrix.astype(jnp.bfloat16)
    first_rest = matrix - high_part.astype(jnp.float32)
    middle_part = first_rest.astype(jnp.bfloat16)
    low_part = (first_rest - middle_part.astype(jnp.float32)).astype(jnp.bfloat16)
    return (high_part, middle_part, low_part)


def many_tokens(activations, out_grads, proj_in, proj_out, queries, lengths, credit):
    tok_rows = activations.shape[0]
    seq_len = tok_rows // lengths.shape[0]
    dp_count = lax.axis_size("dp")
    query_count = lax.axis_size("query")
    dp_index = lax.axis_index("dp")
    query_index = lax.axis_index("query")
    part_act = jnp.dot(activations, proj_in, preferred_element_type=jnp.float32)
    part_grad = jnp.dot(out_grads, proj_out, preferred_element_type=jnp.float32)
    sum_act, sum_grad = lax.psum((part_act, part_grad), "query")
    act_proj = sum_act.astype(jnp.bfloat16)
    grad_proj = sum_grad.astype(jnp.bfloat16)
    rank = act_proj.shape[1]
    feat = rank * rank
    live = jnp.arange(seq_len, dtype=jnp.int32)[None, :] < lengths[:, None]
    weight = (credit[:, None].astype(jnp.float32) * live.astype(jnp.float32)).reshape(-1)
    mask = live.astype(jnp.float32).reshape(-1)
    weight_wire = weight.astype(jnp.bfloat16)
    rows_own = feat // dp_count
    row_start = dp_index * rows_own
    all_tokens = tok_rows * dp_count
    col_count = feat // query_count
    col_start = query_index * col_count
    owned = fold_blocks(
        jnp.zeros((rows_own, col_count), jnp.float32),
        (
            lax.all_gather(grad_proj, "dp", axis=0, tiled=True),
            lax.all_gather(act_proj, "dp", axis=0, tiled=True),
            lax.all_gather(weight_wire, "dp", axis=0, tiled=True),
        ),
        lambda carry, block: hessian_block(carry, block, row_start, rows_own, col_start, col_count),
    )
    hessian = lax.all_gather(owned, "query", axis=1, tiled=True) / all_tokens
    diagonal_block = lax.dynamic_slice_in_dim(hessian, row_start, rows_own, 1)
    level = lax.psum(jnp.trace(diagonal_block), "dp") / feat
    step = 1.1 * level
    high_part, middle_part, low_part = split_parts(hessian)
    piece = lax.all_gather(queries, "dp", axis=0, tiled=True)
    result = jnp.zeros(queries.shape, jnp.float32)
    for part_matrix in (low_part, middle_part, high_part):
        columns = part_matrix
        result = result + jnp.dot(columns, piece, preferred_element_type=jnp.float32)
    query_f = queries.astype(jnp.float32)
    precond = ((2.0 * query_f - (result + 0.1 * level * query_f) / step) / step).astype(
        jnp.bfloat16
    )
    local_features = kron_columns(grad_proj, act_proj, 0, feat)
    piece = lax.all_gather(precond, "dp", axis=0, tiled=True)
    columns = lax.slice_in_dim(local_features, 0, piece.shape[0], axis=1)
    scores = jnp.zeros((tok_rows, precond.shape[1]), jnp.float32) + jnp.dot(
        columns, piece, preferred_element_type=jnp.float32
    )
    return (hessian, (scores * mask[:, None]).astype(jnp.bfloat16))


MIB = 1024 * 1024
TILE = 256
NT = (((1,), (1,)), ((), ()))


def params(mib):
    return pltpu.CompilerParams(vmem_limit_bytes=int(mib * MIB))


def project_kernel(act, grad, pin, pout, keep_ref, send_ref, act_v, grad_v, pin_v, pout_v, sems):
    chunk = grad.shape[1] // 2
    spans = [pl.ds(0, chunk), pl.ds(chunk, chunk)]
    pairs = [(pin, pin_v), (act, act_v), (pout, pout_v)]
    pairs += [(grad.at[:, span], grad_v.at[:, span]) for span in spans]
    copies = [pltpu.make_async_copy(s, d, sems.at[n]) for n, (s, d) in enumerate(pairs)]
    for copy in copies:
        copy.start()
    copies[0].wait()
    copies[1].wait()
    part_act = lax.dot_general(pin_v[...], act_v[...], NT, preferred_element_type=jnp.float32)
    copies[2].wait()
    part_grad = jnp.zeros_like(part_act)
    for copy, span in zip(copies[3:], spans):
        copy.wait()
        part_grad += lax.dot_general(
            pout_v[:, span], grad_v[:, span], NT, preferred_element_type=jnp.float32
        )
    even = lax.rem(lax.axis_index("query"), 2) == 0
    keep_ref[...] = jnp.where(even, part_act, part_grad)
    send_ref[...] = jnp.where(even, part_grad, part_act)


def project(activations, out_grads, proj_in_t, proj_out_t):
    tok, d_here = activations.shape
    f_here = out_grads.shape[1]
    rank = proj_in_t.shape[0]
    out = jax.ShapeDtypeStruct((rank, tok), jnp.float32)
    return pl.pallas_call(
        project_kernel,
        in_specs=[pl.BlockSpec(memory_space=pl.ANY)] * 4,
        out_shape=[out, out],
        scratch_shapes=[
            pltpu.VMEM((tok, d_here), jnp.bfloat16),
            pltpu.VMEM((tok, f_here), jnp.bfloat16),
            pltpu.VMEM((rank, d_here), jnp.bfloat16),
            pltpu.VMEM((rank, f_here), jnp.bfloat16),
            pltpu.SemaphoreType.DMA((5,)),
        ],
        compiler_params=params(53.75),
    )(activations, out_grads, proj_in_t, proj_out_t)


def add_kernel(one_ref, other_ref, out_ref):
    out_ref[...] = one_ref[...] + other_ref[...]


def add(one, other):
    return pl.pallas_call(
        add_kernel,
        out_shape=jax.ShapeDtypeStruct(one.shape, one.dtype),
        compiler_params=params(40),
    )(one, other)


def payload_kernel(one_ref, other_ref, weight_ref, out_ref):
    total = jnp.where(weight_ref[...] > 0.0, one_ref[...] + other_ref[...], 0.0)
    weight = jnp.broadcast_to(weight_ref[...], (16, weight_ref.shape[1]))
    out_ref[...] = jnp.concatenate([total, weight], axis=0).astype(out_ref.dtype)


def add_to_payload(one, other, weight):
    rows, tok = one.shape
    return pl.pallas_call(
        payload_kernel,
        out_shape=jax.ShapeDtypeStruct((rows + 16, tok), jnp.bfloat16),
        compiler_params=params(40),
    )(one, other, weight)


def stack_kernel(_, __, *refs):
    parts, (out_ref, factors_ref) = refs[:-2], refs[-2:]
    for k, ref in enumerate(parts):
        out_ref[k] = ref[...]
        factors_ref[k] = ref[: factors_ref.shape[1]]


def stack(parts, rank, after):
    rows, tok = parts[0].shape
    whole = pl.BlockSpec(memory_space=pltpu.VMEM)
    return pl.pallas_call(
        stack_kernel,
        in_specs=[pl.BlockSpec(memory_space=pl.ANY)] * 2 + [whole] * len(parts),
        out_shape=[
            jax.ShapeDtypeStruct((len(parts), rows, tok), parts[0].dtype),
            jax.ShapeDtypeStruct((len(parts), rank, tok), parts[0].dtype),
        ],
        compiler_params=params(26),
    )(*after, *parts)


def lay_out_factors(blocks, factors, weights):
    rank = factors.shape[0] // 2
    here = pl.multiple_of(lax.rem(lax.axis_index("query"), 2) * rank, rank)
    there = pl.multiple_of(rank - here, rank)
    for k, (mine, other) in enumerate(blocks):
        span = slice(k * mine.shape[1], (k + 1) * mine.shape[1])
        factors[pl.ds(here, rank), span] = mine[:rank].astype(jnp.float32)
        factors[pl.ds(there, rank), span] = other[:rank].astype(jnp.float32)
        weights[:, span] = mine[rank:].astype(jnp.float32)[:1]


def block_pairs(mine, other):
    return [(mine.at[k], other.at[k]) for k in reversed(range(mine.shape[0]))]


def weigh_rows(first_row, end_row, row_count, factors, weights, weighted):
    rank = factors.shape[0] // 2
    act, weight = factors[:rank, :], weights[...]
    first = rank + lax.axis_index("dp") * row_count
    for i in range(first_row // rank, end_row // rank):
        left = (factors[pl.ds(first + i, 1), :] * act).astype(jnp.bfloat16)
        left = (weight * left.astype(jnp.float32)).astype(jnp.bfloat16)
        weighted[i * rank : (i + 1) * rank, :] = left


def range_scale(values):
    top = jnp.max(jnp.abs(values), keepdims=True)
    scale = jnp.ones_like(top)
    for low in (16, 48, 80, 112):
        scale = jnp.where(top > 2.0**low, 2.0 ** -min(low + 16, 126), scale)
        scale = jnp.where(top < 2.0**-low, 2.0 ** min(low + 16, 126), scale)
    return scale


def project_queries(row_count, factors, features, query_ref):
    rank = factors.shape[0] // 2
    act = factors[:rank, :]
    for near in range(2):
        first = rank + (lax.axis_index("dp") ^ near) * row_count
        for i in range(row_count):
            row = factors[pl.ds(first + i, 1), :]
            start = (near * row_count + i) * rank
            features[start : start + rank, :] = (row * act).astype(jnp.bfloat16)
    return jnp.dot(query_ref[...], features[...], preferred_element_type=jnp.float32)


def turn_kernel(row_count, query, near_query, own, own_other, *refs):
    out_ref, plain_ref, factors, weights, features = refs
    rows = query.shape[0]
    out_ref[:, :rows] = query[...].T
    out_ref[:, rows:] = near_query[...].T
    lay_out_factors([(own, own_other)], factors, weights)
    plain_ref[...] = project_queries(row_count, factors, features, out_ref)


def turn_queries(queries, near_queries, own, own_other, rank, row_count):
    rows, count = queries.shape
    tok = own.shape[1]
    out = jax.ShapeDtypeStruct((count, 2 * rows), queries.dtype)
    return pl.pallas_call(
        functools.partial(turn_kernel, row_count),
        out_shape=[out, jax.ShapeDtypeStruct((count, tok), jnp.float32)],
        scratch_shapes=[
            pltpu.VMEM((2 * rank, tok), jnp.float32),
            pltpu.VMEM((1, tok), jnp.float32),
            pltpu.VMEM((2 * rows, tok), jnp.bfloat16),
        ],
        compiler_params=params(26),
    )(queries, near_queries, own, own_other)


def share_kernel(row_count, own, own_other, mine, other, query_ref, own_plain_ref, *refs):
    factors, weights, features, gram, plain, weighted = refs[-6:]
    out_refs = refs[:-6]
    lay_out_factors([(own, own_other)] + block_pairs(mine, other), factors, weights)
    rank = factors.shape[0] // 2
    tokens = factors.shape[1]
    tok = own.shape[1]
    weight = weights[...]
    act, grad = factors[:rank, :], factors[rank:, :]
    act_scale, grad_scale = range_scale(act), range_scale(grad)
    act, grad = act * act_scale, grad * grad_scale
    norms = jnp.sum(act * act, axis=0, keepdims=True) * jnp.sum(grad * grad, axis=0, keepdims=True)
    level = jnp.sum(weight * norms, axis=1, keepdims=True) / (tokens * rank * rank)
    step = 1.1 * level
    act_b, grad_b = act.astype(jnp.bfloat16), grad.astype(jnp.bfloat16)
    act_rows, grad_rows = act.T.astype(jnp.bfloat16), grad.T.astype(jnp.bfloat16)
    scale = act_scale * grad_scale
    per_token = weight * (1.0 / (tokens * step))
    for start in range(0, tokens, tok):
        here = slice(start, start + tok)
        if start:
            plain[:, here] = project_queries(
                row_count, factors.at[:, here], features.at[start // tok - 1], query_ref
            )
        else:
            plain[:, here] = own_plain_ref[...]
        weighted[:, here] = (plain[:, here] * per_token[:, here]).astype(jnp.bfloat16)
    for n, out_ref in enumerate(out_refs):
        block = slice(2 * n * tok, (2 * n + 1) * tok)
        for row in range(0, tokens, TILE // 2):
            here = slice(row, row + TILE // 2)
            tile = jnp.dot(act_rows[here], act_b[:, block], preferred_element_type=jnp.float32)
            tile *= jnp.dot(grad_rows[here], grad_b[:, block], preferred_element_type=jnp.float32)
            gram[n, here, :] = tile.astype(jnp.bfloat16)
        image = jnp.dot(weighted[...], gram[n], preferred_element_type=jnp.float32)
        share = ((2.0 - 0.1 / 1.1) * plain[:, block] - image) * scale * (scale / step)
        out_ref[...] = share.astype(out_ref.dtype)


def score_shares(own, own_other, mine, other, queries_t, own_plain, rank, row_count):
    blocks, tok = mine.shape[0] + 1, mine.shape[2]
    count, depth = queries_t.shape
    return pl.pallas_call(
        functools.partial(share_kernel, row_count),
        out_shape=[
            jax.ShapeDtypeStruct((count, tok), jnp.bfloat16 if k else jnp.float32)
            for k in range(0, blocks, 2)
        ],
        scratch_shapes=[
            pltpu.VMEM((2 * rank, tok * blocks), jnp.float32),
            pltpu.VMEM((1, tok * blocks), jnp.float32),
            pltpu.VMEM((blocks - 1, depth, tok), jnp.bfloat16),
            pltpu.VMEM((blocks // 2, tok * blocks, tok), jnp.bfloat16),
            pltpu.VMEM((count, tok * blocks), jnp.float32),
            pltpu.VMEM((count, tok * blocks), jnp.bfloat16),
        ],
        compiler_params=params(26),
    )(own, own_other, mine, other, queries_t, own_plain)


def build_columns(first, act, factors, right):
    rank = act.shape[0]
    for i in range(right.shape[0] // rank):
        row = rank + first + i
        right[i * rank : (i + 1) * rank, :] = (factors[row : row + 1, :] * act).astype(jnp.bfloat16)


def own_kernel(row_count, col_count, own, own_other, out, factors, weights, weighted, *rights):
    rank = factors.shape[0] // 2
    cols = col_count * rank
    lay_out_factors([(own, own_other)], factors, weights)
    weigh_rows(0, weighted.shape[0], row_count, factors, weights, weighted)
    act = factors[:rank, :]
    build_columns(0, act, factors, rights[0])
    for step in range(rank // col_count):
        if (step + 1) * col_count < rank:
            build_columns((step + 1) * col_count, act, factors, rights[(step + 1) % 2])
        out[:, step * cols : (step + 1) * cols] = lax.dot_general(
            weighted[...], rights[step % 2][...], NT, preferred_element_type=jnp.float32
        )


def own_tokens_sum(own, own_other, rank, row_count, col_count=8):
    tok = own.shape[1]
    rows, cols = row_count * rank, col_count * rank
    return pl.pallas_call(
        functools.partial(own_kernel, row_count, col_count),
        out_shape=jax.ShapeDtypeStruct((rows, rank * rank), jnp.float32),
        scratch_shapes=[
            pltpu.VMEM((2 * rank, tok), jnp.float32),
            pltpu.VMEM((1, tok), jnp.float32),
            pltpu.VMEM((rows, tok), jnp.bfloat16),
            pltpu.VMEM((cols, tok), jnp.bfloat16),
            pltpu.VMEM((cols, tok), jnp.bfloat16),
        ],
        compiler_params=params(16),
    )(own, own_other)


def hessian_kernel(row_count, col_count, mine, other, own_sum, out, *scratch):
    factors, weights, weighted, rights = *scratch[:3], scratch[3:5]
    result, sems = scratch[5:]
    rank = factors.shape[0] // 2
    blocks = mine.shape[0]
    tokens = factors.shape[1] // blocks * (blocks + 1)
    rows, cols = row_count * rank, col_count * rank
    lay_out_factors(block_pairs(mine, other), factors, weights)
    act = factors[:rank, :]
    copies = []
    build_columns(0, act, factors, rights[0])
    for step in range(rank // col_count):
        if (step + 1) * col_count < rank:
            build_columns((step + 1) * col_count, act, factors, rights[(step + 1) % 2])
        for row in range(0, rows, TILE):
            if step == 0:
                weigh_rows(row, row + TILE, row_count, factors, weights, weighted)
            here = pl.ds(row, TILE), pl.ds(step * cols, cols)
            tile = lax.dot_general(
                weighted[row : row + TILE, :],
                rights[step % 2][...],
                NT,
                preferred_element_type=jnp.float32,
            )
            result[here] = (own_sum[here] + tile) * (1.0 / tokens)
            copy = pltpu.make_async_copy(result.at[here], out.at[here], sems.at[len(copies)])
            copy.start()
            copies.append(copy)
    for copy in copies:
        copy.wait()


def hessian_rows(mine, other, own_sum, rank, row_count, col_count=8):
    blocks, _, tok = mine.shape
    feat = rank * rank
    rows, cols = row_count * rank, col_count * rank
    return pl.pallas_call(
        functools.partial(hessian_kernel, row_count, col_count),
        out_specs=pl.BlockSpec(memory_space=pl.ANY),
        out_shape=jax.ShapeDtypeStruct((rows, feat), jnp.float32),
        scratch_shapes=[
            pltpu.VMEM((2 * rank, tok * blocks), jnp.float32),
            pltpu.VMEM((1, tok * blocks), jnp.float32),
            pltpu.VMEM((rows, tok * blocks), jnp.bfloat16),
            pltpu.VMEM((cols, tok * blocks), jnp.bfloat16),
            pltpu.VMEM((cols, tok * blocks), jnp.bfloat16),
            pltpu.VMEM((rows, feat), jnp.float32),
            pltpu.SemaphoreType.DMA((feat // cols * (rows // TILE),)),
        ],
        compiler_params=params(26),
    )(mine, other, own_sum)


def finish_kernel(payload_ref, *refs):
    shares, out_ref = refs[:-1], refs[-1]
    total = shares[0][...]
    for ref in shares[1:]:
        total = total + ref[...].astype(jnp.float32)
    weight = payload_ref[...].astype(jnp.float32)[-1:]
    out_ref[...] = jnp.where(weight > 0.0, total, 0.0).T.astype(out_ref.dtype)


def finish_scores(payload, shares):
    count, tok = shares[0].shape
    return pl.pallas_call(
        finish_kernel,
        out_shape=jax.ShapeDtypeStruct((tok, count), jnp.bfloat16),
        compiler_params=params(40),
    )(payload, *shares)


def swapped(array, axis, distance):
    return lax.ppermute(array, axis, [(i, i ^ distance) for i in range(lax.axis_size(axis))])


def few_tokens(activations, out_grads, proj_in, proj_out, queries, lengths, credit):
    dp_count = lax.axis_size("dp")
    query_count = lax.axis_size("query")
    rank = proj_in.shape[1]
    row_count = rank // dp_count
    seq_len = activations.shape[0] // lengths.shape[0]
    live = jnp.arange(seq_len, dtype=jnp.int32)[None, :] < lengths[:, None]
    weight = jnp.where(live, credit[:, None], 0).astype(jnp.float32).reshape(1, -1)
    near_queries = swapped(queries, "dp", 1)
    keep, send = project(activations, out_grads, proj_in.T, proj_out.T)
    other = swapped(send, "query", 1)
    distance = 2
    while distance < query_count:
        keep = add(keep, other)
        other = swapped(keep, "query", distance)
        distance *= 2
    own = add_to_payload(keep, other, weight)
    own_other = swapped(own, "query", 1)
    others = [swapped(own, "dp", k) for k in reversed(range(1, dp_count))]
    own_sum = own_tokens_sum(own, own_other, rank, row_count)
    queries_t, own_plain = turn_queries(
        queries, near_queries, own, own_other, rank, row_count
    )
    mine, factors = stack(others, rank, (own_sum, queries_t))
    other = swapped(factors, "query", 1)
    shares = score_shares(own, own_other, mine, other, queries_t, own_plain, rank, row_count)
    arrived = [swapped(share, "dp", 2 * n) for n, share in enumerate(shares) if n]
    hessian = hessian_rows(mine, other, own_sum, rank, row_count)
    return hessian, finish_scores(own, [shares[0]] + arrived)


def power_of_two(count):
    return count & (count - 1) == 0


def per_device(activations, *others):
    rank = others[1].shape[1]
    dp_count, query_count = lax.axis_size("dp"), lax.axis_size("query")
    pairs = min(dp_count, query_count) > 1 and power_of_two(dp_count) and power_of_two(query_count)
    if pairs and activations.shape[0] * dp_count <= rank * rank:
        return few_tokens(activations, *others)
    return many_tokens(activations, *others)


def solution(mesh):
    placed = (
        P(("groups", "dp"), "query"),
        P(("groups", "dp"), "query"),
        P("query", None),
        P("query", None),
        P(("groups", "dp"), "query"),
        P(("groups", "dp")),
        P(("groups", "dp")),
    )
    return jax.shard_map(
        per_device,
        mesh=mesh,
        in_specs=placed,
        out_specs=(P(("groups", "dp"), None), P(("groups", "dp"), "query")),
        check_vma=False,
    )
```

```python
import functools
import jax
import jax.numpy as jnp
from jax import lax
from jax.experimental import pallas as pl
from jax.experimental.pallas import tpu as pltpu
from jax.sharding import PartitionSpec as P


def kron_columns(grad_rows, act_rows, start, count):
    rank = grad_rows.shape[1]
    tokens_here = grad_rows.shape[0]
    grad_cols = lax.dynamic_slice_in_dim(grad_rows, start // rank, count // rank, 1)
    outer = grad_cols.astype(jnp.float32)[:, :, None] * act_rows.astype(jnp.float32)[:, None, :]
    return outer.reshape(tokens_here, count).astype(jnp.bfloat16)


def hessian_block(total, pieces, row_start, rows_own, col_start, col_count):
    grad_rows, act_rows, weights = pieces
    left = kron_columns(grad_rows, act_rows, row_start, rows_own)
    weighted = (weights.astype(jnp.float32)[:, None] * left.astype(jnp.float32)).astype(
        jnp.bfloat16
    )
    right = kron_columns(grad_rows, act_rows, col_start, col_count)
    return total + lax.dot_general(
        weighted, right, (((0,), (0,)), ((), ())), preferred_element_type=jnp.float32
    )


def fold_blocks(total, pieces, step_fn):
    count = pieces[0].shape[0]
    shaped = tuple((p.reshape((count // 512, 512) + p.shape[1:]) for p in pieces))

    def inner(carry, block):
        return (step_fn(carry, block), None)

    return lax.scan(inner, total, shaped)[0]


def split_parts(matrix):
    high_part = matrix.astype(jnp.bfloat16)
    first_rest = matrix - high_part.astype(jnp.float32)
    middle_part = first_rest.astype(jnp.bfloat16)
    low_part = (first_rest - middle_part.astype(jnp.float32)).astype(jnp.bfloat16)
    return (high_part, middle_part, low_part)


def many_tokens(activations, out_grads, proj_in, proj_out, queries, lengths, credit):
    tok_rows = activations.shape[0]
    seq_len = tok_rows // lengths.shape[0]
    dp_count = lax.axis_size("dp")
    query_count = lax.axis_size("query")
    dp_index = lax.axis_index("dp")
    query_index = lax.axis_index("query")
    part_act = jnp.dot(activations, proj_in, preferred_element_type=jnp.float32)
    part_grad = jnp.dot(out_grads, proj_out, preferred_element_type=jnp.float32)
    sum_act, sum_grad = lax.psum((part_act, part_grad), "query")
    act_proj = sum_act.astype(jnp.bfloat16)
    grad_proj = sum_grad.astype(jnp.bfloat16)
    rank = act_proj.shape[1]
    feat = rank * rank
    live = jnp.arange(seq_len, dtype=jnp.int32)[None, :] < lengths[:, None]
    weight = (credit[:, None].astype(jnp.float32) * live.astype(jnp.float32)).reshape(-1)
    mask = live.astype(jnp.float32).reshape(-1)
    weight_wire = weight.astype(jnp.bfloat16)
    rows_own = feat // dp_count
    row_start = dp_index * rows_own
    all_tokens = tok_rows * dp_count
    col_count = feat // query_count
    col_start = query_index * col_count
    owned = fold_blocks(
        jnp.zeros((rows_own, col_count), jnp.float32),
        (
            lax.all_gather(grad_proj, "dp", axis=0, tiled=True),
            lax.all_gather(act_proj, "dp", axis=0, tiled=True),
            lax.all_gather(weight_wire, "dp", axis=0, tiled=True),
        ),
        lambda carry, block: hessian_block(carry, block, row_start, rows_own, col_start, col_count),
    )
    hessian = lax.all_gather(owned, "query", axis=1, tiled=True) / all_tokens
    diagonal_block = lax.dynamic_slice_in_dim(hessian, row_start, rows_own, 1)
    level = lax.psum(jnp.trace(diagonal_block), "dp") / feat
    step = 1.1 * level
    high_part, middle_part, low_part = split_parts(hessian)
    piece = lax.all_gather(queries, "dp", axis=0, tiled=True)
    result = jnp.zeros(queries.shape, jnp.float32)
    for part_matrix in (low_part, middle_part, high_part):
        columns = part_matrix
        result = result + jnp.dot(columns, piece, preferred_element_type=jnp.float32)
    query_f = queries.astype(jnp.float32)
    precond = ((2.0 * query_f - (result + 0.1 * level * query_f) / step) / step).astype(
        jnp.bfloat16
    )
    local_features = kron_columns(grad_proj, act_proj, 0, feat)
    piece = lax.all_gather(precond, "dp", axis=0, tiled=True)
    columns = lax.slice_in_dim(local_features, 0, piece.shape[0], axis=1)
    scores = jnp.zeros((tok_rows, precond.shape[1]), jnp.float32) + jnp.dot(
        columns, piece, preferred_element_type=jnp.float32
    )
    return (hessian, (scores * mask[:, None]).astype(jnp.bfloat16))


MIB = 1024 * 1024
TILE = 256
NT = (((1,), (1,)), ((), ()))


def params(mib):
    return pltpu.CompilerParams(vmem_limit_bytes=int(mib * MIB))


def project_kernel(act, grad, pin, pout, keep_ref, send_ref, act_v, grad_v, pin_v, pout_v, sems):
    chunk = grad.shape[1] // 2
    spans = [pl.ds(0, chunk), pl.ds(chunk, chunk)]
    pairs = [(pin, pin_v), (act, act_v), (pout, pout_v)]
    pairs += [(grad.at[:, span], grad_v.at[:, span]) for span in spans]
    copies = [pltpu.make_async_copy(s, d, sems.at[n]) for n, (s, d) in enumerate(pairs)]
    for copy in copies:
        copy.start()
    copies[0].wait()
    copies[1].wait()
    part_act = lax.dot_general(pin_v[...], act_v[...], NT, preferred_element_type=jnp.float32)
    copies[2].wait()
    part_grad = jnp.zeros_like(part_act)
    for copy, span in zip(copies[3:], spans):
        copy.wait()
        part_grad += lax.dot_general(
            pout_v[:, span], grad_v[:, span], NT, preferred_element_type=jnp.float32
        )
    even = lax.rem(lax.axis_index("query"), 2) == 0
    keep_ref[...] = jnp.where(even, part_act, part_grad)
    send_ref[...] = jnp.where(even, part_grad, part_act)


def project(activations, out_grads, proj_in_t, proj_out_t):
    tok, d_here = activations.shape
    f_here = out_grads.shape[1]
    rank = proj_in_t.shape[0]
    out = jax.ShapeDtypeStruct((rank, tok), jnp.float32)
    return pl.pallas_call(
        project_kernel,
        in_specs=[pl.BlockSpec(memory_space=pl.ANY)] * 4,
        out_shape=[out, out],
        scratch_shapes=[
            pltpu.VMEM((tok, d_here), jnp.bfloat16),
            pltpu.VMEM((tok, f_here), jnp.bfloat16),
            pltpu.VMEM((rank, d_here), jnp.bfloat16),
            pltpu.VMEM((rank, f_here), jnp.bfloat16),
            pltpu.SemaphoreType.DMA((5,)),
        ],
        compiler_params=params(53.75),
    )(activations, out_grads, proj_in_t, proj_out_t)


def add_kernel(one_ref, other_ref, out_ref):
    out_ref[...] = one_ref[...] + other_ref[...]


def add(one, other):
    return pl.pallas_call(
        add_kernel,
        out_shape=jax.ShapeDtypeStruct(one.shape, one.dtype),
        compiler_params=params(40),
    )(one, other)


def payload_kernel(one_ref, other_ref, weight_ref, out_ref):
    total = jnp.where(weight_ref[...] > 0.0, one_ref[...] + other_ref[...], 0.0)
    weight = jnp.broadcast_to(weight_ref[...], (16, weight_ref.shape[1]))
    out_ref[...] = jnp.concatenate([total, weight], axis=0).astype(out_ref.dtype)


def add_to_payload(one, other, weight):
    rows, tok = one.shape
    return pl.pallas_call(
        payload_kernel,
        out_shape=jax.ShapeDtypeStruct((rows + 16, tok), jnp.bfloat16),
        compiler_params=params(40),
    )(one, other, weight)


def stack_kernel(_, __, *refs):
    parts, (out_ref, factors_ref) = refs[:-2], refs[-2:]
    for k, ref in enumerate(parts):
        out_ref[k] = ref[...]
        factors_ref[k] = ref[: factors_ref.shape[1]]


def stack(parts, rank, after):
    rows, tok = parts[0].shape
    whole = pl.BlockSpec(memory_space=pltpu.VMEM)
    return pl.pallas_call(
        stack_kernel,
        in_specs=[pl.BlockSpec(memory_space=pl.ANY)] * 2 + [whole] * len(parts),
        out_shape=[
            jax.ShapeDtypeStruct((len(parts), rows, tok), parts[0].dtype),
            jax.ShapeDtypeStruct((len(parts), rank, tok), parts[0].dtype),
        ],
        compiler_params=params(26),
    )(*after, *parts)


def lay_out_factors(blocks, factors, weights):
    rank = factors.shape[0] // 2
    here = pl.multiple_of(lax.rem(lax.axis_index("query"), 2) * rank, rank)
    there = pl.multiple_of(rank - here, rank)
    for k, (mine, other) in enumerate(blocks):
        span = slice(k * mine.shape[1], (k + 1) * mine.shape[1])
        factors[pl.ds(here, rank), span] = mine[:rank].astype(jnp.float32)
        factors[pl.ds(there, rank), span] = other[:rank].astype(jnp.float32)
        weights[:, span] = mine[rank:].astype(jnp.float32)[:1]


def block_pairs(mine, other):
    return [(mine.at[k], other.at[k]) for k in reversed(range(mine.shape[0]))]


def weigh_rows(first_row, end_row, row_count, factors, weights, weighted):
    rank = factors.shape[0] // 2
    act, weight = factors[:rank, :], weights[...]
    first = rank + lax.axis_index("dp") * row_count
    for i in range(first_row // rank, end_row // rank):
        left = (factors[pl.ds(first + i, 1), :] * act).astype(jnp.bfloat16)
        left = (weight * left.astype(jnp.float32)).astype(jnp.bfloat16)
        weighted[i * rank : (i + 1) * rank, :] = left


def range_scale(values):
    top = jnp.max(jnp.abs(values), keepdims=True)
    scale = jnp.ones_like(top)
    for low in (16, 48, 80, 112):
        scale = jnp.where(top > 2.0**low, 2.0 ** -min(low + 16, 126), scale)
        scale = jnp.where(top < 2.0**-low, 2.0 ** min(low + 16, 126), scale)
    return scale


def project_queries(row_count, factors, features, query_ref):
    rank = factors.shape[0] // 2
    act = factors[:rank, :]
    for near in range(2):
        first = rank + (lax.axis_index("dp") ^ near) * row_count
        for i in range(row_count):
            row = factors[pl.ds(first + i, 1), :]
            start = (near * row_count + i) * rank
            features[start : start + rank, :] = (row * act).astype(jnp.bfloat16)
    return jnp.dot(query_ref[...], features[...], preferred_element_type=jnp.float32)


def turn_kernel(row_count, query, near_query, own, own_other, *refs):
    out_ref, plain_ref, factors, weights, features = refs
    rows = query.shape[0]
    out_ref[:, :rows] = query[...].T
    out_ref[:, rows:] = near_query[...].T
    lay_out_factors([(own, own_other)], factors, weights)
    plain_ref[...] = project_queries(row_count, factors, features, out_ref)


def turn_queries(queries, near_queries, own, own_other, rank, row_count):
    rows, count = queries.shape
    tok = own.shape[1]
    out = jax.ShapeDtypeStruct((count, 2 * rows), queries.dtype)
    return pl.pallas_call(
        functools.partial(turn_kernel, row_count),
        out_shape=[out, jax.ShapeDtypeStruct((count, tok), jnp.float32)],
        scratch_shapes=[
            pltpu.VMEM((2 * rank, tok), jnp.float32),
            pltpu.VMEM((1, tok), jnp.float32),
            pltpu.VMEM((2 * rows, tok), jnp.bfloat16),
        ],
        compiler_params=params(26),
    )(queries, near_queries, own, own_other)


def share_kernel(row_count, own, own_other, mine, other, query_ref, own_plain_ref, *refs):
    factors, weights, features, gram, plain, weighted = refs[-6:]
    out_refs = refs[:-6]
    lay_out_factors([(own, own_other)] + block_pairs(mine, other), factors, weights)
    rank = factors.shape[0] // 2
    tokens = factors.shape[1]
    tok = own.shape[1]

    def project_block(k):
        here = slice(k * tok, (k + 1) * tok)
        plain[:, here] = project_queries(
            row_count, factors.at[:, here], features.at[k - 1], query_ref
        )

    plain[:, :tok] = own_plain_ref[...]
    blocks = tokens // tok
    for k in range(1, blocks // 2):
        project_block(k)
    weight = weights[...]
    act, grad = factors[:rank, :], factors[rank:, :]
    act_scale, grad_scale = range_scale(act), range_scale(grad)
    act, grad = act * act_scale, grad * grad_scale
    act_b, grad_b = act.astype(jnp.bfloat16), grad.astype(jnp.bfloat16)
    norms = jnp.sum(act * act, axis=0, keepdims=True) * jnp.sum(grad * grad, axis=0, keepdims=True)
    level = jnp.sum(weight * norms, axis=1, keepdims=True) / (tokens * rank * rank)
    for k in range(max(blocks // 2, 1), blocks - 1):
        project_block(k)
    step = 1.1 * level
    scale = act_scale * grad_scale
    act_rows, grad_rows = act.T.astype(jnp.bfloat16), grad.T.astype(jnp.bfloat16)
    project_block(blocks - 1)
    weighted[...] = (plain[...] * (weight * (1.0 / (tokens * step)))).astype(jnp.bfloat16)
    for n, out_ref in enumerate(out_refs):
        block = slice(2 * n * tok, (2 * n + 1) * tok)
        for row in range(0, tokens, TILE // 2):
            here = slice(row, row + TILE // 2)
            tile = jnp.dot(act_rows[here], act_b[:, block], preferred_element_type=jnp.float32)
            tile *= jnp.dot(grad_rows[here], grad_b[:, block], preferred_element_type=jnp.float32)
            gram[n, here, :] = tile.astype(jnp.bfloat16)
        image = jnp.dot(weighted[...], gram[n], preferred_element_type=jnp.float32)
        share = ((2.0 - 0.1 / 1.1) * plain[:, block] - image) * scale * (scale / step)
        out_ref[...] = share.astype(out_ref.dtype)


def score_shares(own, own_other, mine, other, queries_t, own_plain, rank, row_count):
    blocks, tok = mine.shape[0] + 1, mine.shape[2]
    count, depth = queries_t.shape
    return pl.pallas_call(
        functools.partial(share_kernel, row_count),
        out_shape=[
            jax.ShapeDtypeStruct((count, tok), jnp.bfloat16 if k else jnp.float32)
            for k in range(0, blocks, 2)
        ],
        scratch_shapes=[
            pltpu.VMEM((2 * rank, tok * blocks), jnp.float32),
            pltpu.VMEM((1, tok * blocks), jnp.float32),
            pltpu.VMEM((blocks - 1, depth, tok), jnp.bfloat16),
            pltpu.VMEM((blocks // 2, tok * blocks, tok), jnp.bfloat16),
            pltpu.VMEM((count, tok * blocks), jnp.float32),
            pltpu.VMEM((count, tok * blocks), jnp.bfloat16),
        ],
        compiler_params=params(26),
    )(own, own_other, mine, other, queries_t, own_plain)


def build_columns(first, act, factors, right):
    rank = act.shape[0]
    for i in range(right.shape[0] // rank):
        row = rank + first + i
        right[i * rank : (i + 1) * rank, :] = (factors[row : row + 1, :] * act).astype(jnp.bfloat16)


def own_kernel(row_count, col_count, own, own_other, out, factors, weights, weighted, *rights):
    rank = factors.shape[0] // 2
    cols = col_count * rank
    lay_out_factors([(own, own_other)], factors, weights)
    weigh_rows(0, weighted.shape[0], row_count, factors, weights, weighted)
    act = factors[:rank, :]
    build_columns(0, act, factors, rights[0])
    for step in range(rank // col_count):
        if (step + 1) * col_count < rank:
            build_columns((step + 1) * col_count, act, factors, rights[(step + 1) % 2])
        out[:, step * cols : (step + 1) * cols] = lax.dot_general(
            weighted[...], rights[step % 2][...], NT, preferred_element_type=jnp.float32
        )


def own_tokens_sum(own, own_other, rank, row_count, col_count=8):
    tok = own.shape[1]
    rows, cols = row_count * rank, col_count * rank
    return pl.pallas_call(
        functools.partial(own_kernel, row_count, col_count),
        out_shape=jax.ShapeDtypeStruct((rows, rank * rank), jnp.float32),
        scratch_shapes=[
            pltpu.VMEM((2 * rank, tok), jnp.float32),
            pltpu.VMEM((1, tok), jnp.float32),
            pltpu.VMEM((rows, tok), jnp.bfloat16),
            pltpu.VMEM((cols, tok), jnp.bfloat16),
            pltpu.VMEM((cols, tok), jnp.bfloat16),
        ],
        compiler_params=params(16),
    )(own, own_other)


def hessian_kernel(row_count, col_count, mine, other, own_sum, out, *scratch):
    factors, weights, weighted, rights = *scratch[:3], scratch[3:5]
    result, sems = scratch[5:]
    rank = factors.shape[0] // 2
    blocks = mine.shape[0]
    tokens = factors.shape[1] // blocks * (blocks + 1)
    rows, cols = row_count * rank, col_count * rank
    lay_out_factors(block_pairs(mine, other), factors, weights)
    act = factors[:rank, :]
    copies = []
    build_columns(0, act, factors, rights[0])
    for step in range(rank // col_count):
        if (step + 1) * col_count < rank:
            build_columns((step + 1) * col_count, act, factors, rights[(step + 1) % 2])
        for row in range(0, rows, TILE):
            if step == 0:
                weigh_rows(row, row + TILE, row_count, factors, weights, weighted)
            here = pl.ds(row, TILE), pl.ds(step * cols, cols)
            tile = lax.dot_general(
                weighted[row : row + TILE, :],
                rights[step % 2][...],
                NT,
                preferred_element_type=jnp.float32,
            )
            result[here] = (own_sum[here] + tile) * (1.0 / tokens)
            copy = pltpu.make_async_copy(result.at[here], out.at[here], sems.at[len(copies)])
            copy.start()
            copies.append(copy)
    for copy in copies:
        copy.wait()


def hessian_rows(mine, other, own_sum, rank, row_count, col_count=8):
    blocks, _, tok = mine.shape
    feat = rank * rank
    rows, cols = row_count * rank, col_count * rank
    return pl.pallas_call(
        functools.partial(hessian_kernel, row_count, col_count),
        out_specs=pl.BlockSpec(memory_space=pl.ANY),
        out_shape=jax.ShapeDtypeStruct((rows, feat), jnp.float32),
        scratch_shapes=[
            pltpu.VMEM((2 * rank, tok * blocks), jnp.float32),
            pltpu.VMEM((1, tok * blocks), jnp.float32),
            pltpu.VMEM((rows, tok * blocks), jnp.bfloat16),
            pltpu.VMEM((cols, tok * blocks), jnp.bfloat16),
            pltpu.VMEM((cols, tok * blocks), jnp.bfloat16),
            pltpu.VMEM((rows, feat), jnp.float32),
            pltpu.SemaphoreType.DMA((feat // cols * (rows // TILE),)),
        ],
        compiler_params=params(26),
    )(mine, other, own_sum)


def finish_kernel(payload_ref, *refs):
    shares, out_ref = refs[:-1], refs[-1]
    total = shares[0][...]
    for ref in shares[1:]:
        total = total + ref[...].astype(jnp.float32)
    weight = payload_ref[...].astype(jnp.float32)[-1:]
    out_ref[...] = jnp.where(weight > 0.0, total, 0.0).T.astype(out_ref.dtype)


def finish_scores(payload, shares):
    count, tok = shares[0].shape
    return pl.pallas_call(
        finish_kernel,
        out_shape=jax.ShapeDtypeStruct((tok, count), jnp.bfloat16),
        compiler_params=params(40),
    )(payload, *shares)


def swapped(array, axis, distance):
    return lax.ppermute(array, axis, [(i, i ^ distance) for i in range(lax.axis_size(axis))])


def few_tokens(activations, out_grads, proj_in, proj_out, queries, lengths, credit):
    dp_count = lax.axis_size("dp")
    query_count = lax.axis_size("query")
    rank = proj_in.shape[1]
    row_count = rank // dp_count
    seq_len = activations.shape[0] // lengths.shape[0]
    live = jnp.arange(seq_len, dtype=jnp.int32)[None, :] < lengths[:, None]
    weight = jnp.where(live, credit[:, None], 0).astype(jnp.float32).reshape(1, -1)
    near_queries = swapped(queries, "dp", 1)
    keep, send = project(activations, out_grads, proj_in.T, proj_out.T)
    other = swapped(send, "query", 1)
    distance = 2
    while distance < query_count:
        keep = add(keep, other)
        other = swapped(keep, "query", distance)
        distance *= 2
    own = add_to_payload(keep, other, weight)
    own_other = swapped(own, "query", 1)
    others = [swapped(own, "dp", k) for k in reversed(range(1, dp_count))]
    own_sum = own_tokens_sum(own, own_other, rank, row_count)
    queries_t, own_plain = turn_queries(
        queries, near_queries, own, own_other, rank, row_count
    )
    mine, factors = stack(others, rank, (own_sum, queries_t))
    other = swapped(factors, "query", 1)
    shares = score_shares(own, own_other, mine, other, queries_t, own_plain, rank, row_count)
    arrived = [swapped(share, "dp", 2 * n) for n, share in enumerate(shares) if n]
    hessian = hessian_rows(mine, other, own_sum, rank, row_count)
    return hessian, finish_scores(own, [shares[0]] + arrived)


def power_of_two(count):
    return count & (count - 1) == 0


def per_device(activations, *others):
    rank = others[1].shape[1]
    dp_count, query_count = lax.axis_size("dp"), lax.axis_size("query")
    pairs = min(dp_count, query_count) > 1 and power_of_two(dp_count) and power_of_two(query_count)
    if pairs and activations.shape[0] * dp_count <= rank * rank:
        return few_tokens(activations, *others)
    return many_tokens(activations, *others)


def solution(mesh):
    placed = (
        P(("groups", "dp"), "query"),
        P(("groups", "dp"), "query"),
        P("query", None),
        P("query", None),
        P(("groups", "dp"), "query"),
        P(("groups", "dp")),
        P(("groups", "dp")),
    )
    return jax.shard_map(
        per_device,
        mesh=mesh,
        in_specs=placed,
        out_specs=(P(("groups", "dp"), None), P(("groups", "dp"), "query")),
        check_vma=False,
    )
```

```python
import functools
import jax
import jax.numpy as jnp
from jax import lax
from jax.experimental import pallas as pl
from jax.experimental.pallas import tpu as pltpu
from jax.sharding import PartitionSpec as P


def kron_columns(grad_rows, act_rows, start, count):
    rank = grad_rows.shape[1]
    tokens_here = grad_rows.shape[0]
    grad_cols = lax.dynamic_slice_in_dim(grad_rows, start // rank, count // rank, 1)
    outer = grad_cols.astype(jnp.float32)[:, :, None] * act_rows.astype(jnp.float32)[:, None, :]
    return outer.reshape(tokens_here, count).astype(jnp.bfloat16)


def hessian_block(total, pieces, row_start, rows_own, col_start, col_count):
    grad_rows, act_rows, weights = pieces
    left = kron_columns(grad_rows, act_rows, row_start, rows_own)
    weighted = (weights.astype(jnp.float32)[:, None] * left.astype(jnp.float32)).astype(
        jnp.bfloat16
    )
    right = kron_columns(grad_rows, act_rows, col_start, col_count)
    return total + lax.dot_general(
        weighted, right, (((0,), (0,)), ((), ())), preferred_element_type=jnp.float32
    )


def fold_blocks(total, pieces, step_fn):
    count = pieces[0].shape[0]
    shaped = tuple((p.reshape((count // 512, 512) + p.shape[1:]) for p in pieces))

    def inner(carry, block):
        return (step_fn(carry, block), None)

    return lax.scan(inner, total, shaped)[0]


def split_parts(matrix):
    high_part = matrix.astype(jnp.bfloat16)
    first_rest = matrix - high_part.astype(jnp.float32)
    middle_part = first_rest.astype(jnp.bfloat16)
    low_part = (first_rest - middle_part.astype(jnp.float32)).astype(jnp.bfloat16)
    return (high_part, middle_part, low_part)


def many_tokens(activations, out_grads, proj_in, proj_out, queries, lengths, credit):
    tok_rows = activations.shape[0]
    seq_len = tok_rows // lengths.shape[0]
    dp_count = lax.axis_size("dp")
    query_count = lax.axis_size("query")
    dp_index = lax.axis_index("dp")
    query_index = lax.axis_index("query")
    part_act = jnp.dot(activations, proj_in, preferred_element_type=jnp.float32)
    part_grad = jnp.dot(out_grads, proj_out, preferred_element_type=jnp.float32)
    sum_act, sum_grad = lax.psum((part_act, part_grad), "query")
    act_proj = sum_act.astype(jnp.bfloat16)
    grad_proj = sum_grad.astype(jnp.bfloat16)
    rank = act_proj.shape[1]
    feat = rank * rank
    live = jnp.arange(seq_len, dtype=jnp.int32)[None, :] < lengths[:, None]
    weight = (credit[:, None].astype(jnp.float32) * live.astype(jnp.float32)).reshape(-1)
    mask = live.astype(jnp.float32).reshape(-1)
    weight_wire = weight.astype(jnp.bfloat16)
    rows_own = feat // dp_count
    row_start = dp_index * rows_own
    all_tokens = tok_rows * dp_count
    col_count = feat // query_count
    col_start = query_index * col_count
    owned = fold_blocks(
        jnp.zeros((rows_own, col_count), jnp.float32),
        (
            lax.all_gather(grad_proj, "dp", axis=0, tiled=True),
            lax.all_gather(act_proj, "dp", axis=0, tiled=True),
            lax.all_gather(weight_wire, "dp", axis=0, tiled=True),
        ),
        lambda carry, block: hessian_block(carry, block, row_start, rows_own, col_start, col_count),
    )
    hessian = lax.all_gather(owned, "query", axis=1, tiled=True) / all_tokens
    diagonal_block = lax.dynamic_slice_in_dim(hessian, row_start, rows_own, 1)
    level = lax.psum(jnp.trace(diagonal_block), "dp") / feat
    step = 1.1 * level
    high_part, middle_part, low_part = split_parts(hessian)
    piece = lax.all_gather(queries, "dp", axis=0, tiled=True)
    result = jnp.zeros(queries.shape, jnp.float32)
    for part_matrix in (low_part, middle_part, high_part):
        columns = part_matrix
        result = result + jnp.dot(columns, piece, preferred_element_type=jnp.float32)
    query_f = queries.astype(jnp.float32)
    precond = ((2.0 * query_f - (result + 0.1 * level * query_f) / step) / step).astype(
        jnp.bfloat16
    )
    local_features = kron_columns(grad_proj, act_proj, 0, feat)
    piece = lax.all_gather(precond, "dp", axis=0, tiled=True)
    columns = lax.slice_in_dim(local_features, 0, piece.shape[0], axis=1)
    scores = jnp.zeros((tok_rows, precond.shape[1]), jnp.float32) + jnp.dot(
        columns, piece, preferred_element_type=jnp.float32
    )
    return (hessian, (scores * mask[:, None]).astype(jnp.bfloat16))


MIB = 1024 * 1024
TILE = 256
NT = (((1,), (1,)), ((), ()))


def params(mib):
    return pltpu.CompilerParams(vmem_limit_bytes=int(mib * MIB))


def project_kernel(act, grad, pin, pout, keep_ref, send_ref, act_v, grad_v, pin_v, pout_v, sems):
    chunk = grad.shape[1] // 2
    spans = [pl.ds(0, chunk), pl.ds(chunk, chunk)]
    pairs = [(pin, pin_v), (act, act_v), (pout, pout_v)]
    pairs += [(grad.at[:, span], grad_v.at[:, span]) for span in spans]
    copies = [pltpu.make_async_copy(s, d, sems.at[n]) for n, (s, d) in enumerate(pairs)]
    for copy in copies:
        copy.start()
    copies[0].wait()
    copies[1].wait()
    part_act = lax.dot_general(pin_v[...], act_v[...], NT, preferred_element_type=jnp.float32)
    copies[2].wait()
    part_grad = jnp.zeros_like(part_act)
    for copy, span in zip(copies[3:], spans):
        copy.wait()
        part_grad += lax.dot_general(
            pout_v[:, span], grad_v[:, span], NT, preferred_element_type=jnp.float32
        )
    even = lax.rem(lax.axis_index("query"), 2) == 0
    keep_ref[...] = jnp.where(even, part_act, part_grad)
    send_ref[...] = jnp.where(even, part_grad, part_act)


def project(activations, out_grads, proj_in_t, proj_out_t):
    tok, d_here = activations.shape
    f_here = out_grads.shape[1]
    rank = proj_in_t.shape[0]
    out = jax.ShapeDtypeStruct((rank, tok), jnp.float32)
    return pl.pallas_call(
        project_kernel,
        in_specs=[pl.BlockSpec(memory_space=pl.ANY)] * 4,
        out_shape=[out, out],
        scratch_shapes=[
            pltpu.VMEM((tok, d_here), jnp.bfloat16),
            pltpu.VMEM((tok, f_here), jnp.bfloat16),
            pltpu.VMEM((rank, d_here), jnp.bfloat16),
            pltpu.VMEM((rank, f_here), jnp.bfloat16),
            pltpu.SemaphoreType.DMA((5,)),
        ],
        compiler_params=params(53.75),
    )(activations, out_grads, proj_in_t, proj_out_t)


def add_kernel(one_ref, other_ref, out_ref):
    out_ref[...] = one_ref[...] + other_ref[...]


def add(one, other):
    return pl.pallas_call(
        add_kernel,
        out_shape=jax.ShapeDtypeStruct(one.shape, one.dtype),
        compiler_params=params(40),
    )(one, other)


def payload_kernel(one_ref, other_ref, weight_ref, out_ref):
    total = jnp.where(weight_ref[...] > 0.0, one_ref[...] + other_ref[...], 0.0)
    weight = jnp.broadcast_to(weight_ref[...], (16, weight_ref.shape[1]))
    out_ref[...] = jnp.concatenate([total, weight], axis=0).astype(out_ref.dtype)


def add_to_payload(one, other, weight):
    rows, tok = one.shape
    return pl.pallas_call(
        payload_kernel,
        out_shape=jax.ShapeDtypeStruct((rows + 16, tok), jnp.bfloat16),
        compiler_params=params(40),
    )(one, other, weight)


def stack_kernel(_, __, *refs):
    parts, (out_ref, factors_ref) = refs[:-2], refs[-2:]
    for k, ref in enumerate(parts):
        out_ref[k] = ref[...]
        factors_ref[k] = ref[: factors_ref.shape[1]]


def stack(parts, rank, after):
    rows, tok = parts[0].shape
    whole = pl.BlockSpec(memory_space=pltpu.VMEM)
    return pl.pallas_call(
        stack_kernel,
        in_specs=[pl.BlockSpec(memory_space=pl.ANY)] * 2 + [whole] * len(parts),
        out_shape=[
            jax.ShapeDtypeStruct((len(parts), rows, tok), parts[0].dtype),
            jax.ShapeDtypeStruct((len(parts), rank, tok), parts[0].dtype),
        ],
        compiler_params=params(26),
    )(*after, *parts)


def lay_out_factors(blocks, factors, weights):
    rank = factors.shape[0] // 2
    here = pl.multiple_of(lax.rem(lax.axis_index("query"), 2) * rank, rank)
    there = pl.multiple_of(rank - here, rank)
    for k, (mine, other) in enumerate(blocks):
        span = slice(k * mine.shape[1], (k + 1) * mine.shape[1])
        factors[pl.ds(here, rank), span] = mine[:rank].astype(jnp.float32)
        factors[pl.ds(there, rank), span] = other[:rank].astype(jnp.float32)
        weights[:, span] = mine[rank:].astype(jnp.float32)[:1]


def block_pairs(mine, other):
    return [(mine.at[k], other.at[k]) for k in reversed(range(mine.shape[0]))]


def weigh_rows(first_row, end_row, row_count, factors, weights, weighted):
    rank = factors.shape[0] // 2
    act, weight = factors[:rank, :], weights[...]
    first = rank + lax.axis_index("dp") * row_count
    for i in range(first_row // rank, end_row // rank):
        left = (factors[pl.ds(first + i, 1), :] * act).astype(jnp.bfloat16)
        left = (weight * left.astype(jnp.float32)).astype(jnp.bfloat16)
        weighted[i * rank : (i + 1) * rank, :] = left


def range_scale(values):
    top = jnp.max(jnp.abs(values), keepdims=True)
    scale = jnp.ones_like(top)
    for low in (16, 48, 80, 112):
        scale = jnp.where(top > 2.0**low, 2.0 ** -min(low + 16, 126), scale)
        scale = jnp.where(top < 2.0**-low, 2.0 ** min(low + 16, 126), scale)
    return scale


def project_queries(row_count, factors, features, queries):
    rank = factors.shape[0] // 2
    act = factors[:rank, :]
    total = 0.0
    for near, query_ref in enumerate(queries):
        first = rank + (lax.axis_index("dp") ^ near) * row_count
        for i in range(row_count):
            row = factors[pl.ds(first + i, 1), :]
            features[near, i * rank : (i + 1) * rank, :] = (row * act).astype(jnp.bfloat16)
        total += jnp.dot(query_ref[...], features[near], preferred_element_type=jnp.float32)
    return total


def turn_kernel(row_count, query, near_query, own, own_other, *refs):
    out_ref, near_out_ref, plain_ref, factors, weights, features = refs
    out_ref[...] = query[...].T
    near_out_ref[...] = near_query[...].T
    lay_out_factors([(own, own_other)], factors, weights)
    plain_ref[...] = project_queries(row_count, factors, features, (out_ref, near_out_ref))


def turn_queries(queries, near_queries, own, own_other, rank, row_count):
    rows, count = queries.shape
    tok = own.shape[1]
    out = jax.ShapeDtypeStruct((count, rows), queries.dtype)
    return pl.pallas_call(
        functools.partial(turn_kernel, row_count),
        out_shape=[out, out, jax.ShapeDtypeStruct((count, tok), jnp.float32)],
        scratch_shapes=[
            pltpu.VMEM((2 * rank, tok), jnp.float32),
            pltpu.VMEM((1, tok), jnp.float32),
            pltpu.VMEM((2, rows, tok), jnp.bfloat16),
        ],
        compiler_params=params(26),
    )(queries, near_queries, own, own_other)


def scaled(values):
    scale = range_scale(values)
    return values * scale, scale


def half_kernel(own, mine, gram_ref, norm_ref, scale_ref, values):
    rank, tok = values.shape[0], own.shape[1]
    for k, part in enumerate([own] + [mine.at[k] for k in reversed(range(mine.shape[0]))]):
        values[:, k * tok : (k + 1) * tok] = part[:rank].astype(jnp.float32)
    factor, scale = scaled(values[...])
    scale_ref[...] = jnp.broadcast_to(scale, scale_ref.shape)
    norm = jnp.sum(factor * factor, axis=0, keepdims=True)
    norm_ref[...] = jnp.broadcast_to(norm, norm_ref.shape)
    factor_b, factor_rows = factor.astype(jnp.bfloat16), factor.T.astype(jnp.bfloat16)
    for n in range(gram_ref.shape[0]):
        block = slice(2 * n * tok, (2 * n + 1) * tok)
        for row in range(0, values.shape[1], TILE // 2):
            here = slice(row, row + TILE // 2)
            gram_ref[n, here, :] = jnp.dot(
                factor_rows[here], factor_b[:, block], preferred_element_type=jnp.float32
            )


def half_gram(own, mine, rank):
    blocks, tok = mine.shape[0] + 1, own.shape[1]
    tokens = blocks * tok
    return pl.pallas_call(
        half_kernel,
        out_shape=[
            jax.ShapeDtypeStruct((blocks // 2, tokens, tok), jnp.float32),
            jax.ShapeDtypeStruct((8, tokens), jnp.float32),
            jax.ShapeDtypeStruct((8, 128), jnp.float32),
        ],
        scratch_shapes=[pltpu.VMEM((rank, tokens), jnp.float32)],
        compiler_params=params(26),
    )(own, mine)


def share_kernel(
    row_count, own, own_other, mine, other, query_ref, near_query_ref, own_plain_ref, *refs
):
    half_gram_ref, half_norm_ref, half_scale_ref = refs[:3]
    refs = refs[3:]
    factors, weights, features, gram = refs[-4:]
    out_refs = refs[:-4]
    lay_out_factors([(own, own_other)] + block_pairs(mine, other), factors, weights)
    rank = factors.shape[0] // 2
    tokens = factors.shape[1]
    tok = own.shape[1]
    plain = project_queries(
        row_count, factors.at[:, tok:], features, (query_ref, near_query_ref)
    )
    plain = jnp.concatenate([own_plain_ref[...], plain], axis=1)
    there = pl.multiple_of(rank - lax.rem(lax.axis_index("query"), 2) * rank, rank)
    factor, scale = scaled(factors[pl.ds(there, rank), :])
    weight = weights[...]
    norms = half_norm_ref[:1, :] * jnp.sum(factor * factor, axis=0, keepdims=True)
    level = jnp.sum(weight * norms, axis=1, keepdims=True) / (tokens * rank * rank)
    step = 1.1 * level
    factor_b, factor_rows = factor.astype(jnp.bfloat16), factor.T.astype(jnp.bfloat16)
    weighted = (plain * (weight * (1.0 / (tokens * step)))).astype(jnp.bfloat16)
    scale = scale * half_scale_ref[:1, :1]
    for n, out_ref in enumerate(out_refs):
        block = slice(2 * n * tok, (2 * n + 1) * tok)
        for row in range(0, tokens, TILE // 2):
            here = slice(row, row + TILE // 2)
            tile = jnp.dot(factor_rows[here], factor_b[:, block], preferred_element_type=jnp.float32)
            gram[n, here, :] = (tile * half_gram_ref[n, here, :]).astype(jnp.bfloat16)
        image = jnp.dot(weighted, gram[n], preferred_element_type=jnp.float32)
        share = ((2.0 - 0.1 / 1.1) * plain[:, block] - image) * scale * (scale / step)
        out_ref[...] = share.astype(out_ref.dtype)


def score_shares(
    own, own_other, mine, other, queries_t, near_queries_t, own_plain, half, rank, row_count
):
    blocks, tok = mine.shape[0] + 1, mine.shape[2]
    count, rows = queries_t.shape
    return pl.pallas_call(
        functools.partial(share_kernel, row_count),
        out_shape=[
            jax.ShapeDtypeStruct((count, tok), jnp.bfloat16 if k else jnp.float32)
            for k in range(0, blocks, 2)
        ],
        scratch_shapes=[
            pltpu.VMEM((2 * rank, tok * blocks), jnp.float32),
            pltpu.VMEM((1, tok * blocks), jnp.float32),
            pltpu.VMEM((2, rows, tok * (blocks - 1)), jnp.bfloat16),
            pltpu.VMEM((blocks // 2, tok * blocks, tok), jnp.bfloat16),
        ],
        compiler_params=params(26),
    )(own, own_other, mine, other, queries_t, near_queries_t, own_plain, *half)


def build_columns(first, act, factors, right):
    rank = act.shape[0]
    for i in range(right.shape[0] // rank):
        row = rank + first + i
        right[i * rank : (i + 1) * rank, :] = (factors[row : row + 1, :] * act).astype(jnp.bfloat16)


def own_kernel(row_count, col_count, own, own_other, out, factors, weights, weighted, *rights):
    rank = factors.shape[0] // 2
    cols = col_count * rank
    lay_out_factors([(own, own_other)], factors, weights)
    weigh_rows(0, weighted.shape[0], row_count, factors, weights, weighted)
    act = factors[:rank, :]
    build_columns(0, act, factors, rights[0])
    for step in range(rank // col_count):
        if (step + 1) * col_count < rank:
            build_columns((step + 1) * col_count, act, factors, rights[(step + 1) % 2])
        out[:, step * cols : (step + 1) * cols] = lax.dot_general(
            weighted[...], rights[step % 2][...], NT, preferred_element_type=jnp.float32
        )


def own_tokens_sum(own, own_other, rank, row_count, col_count=8):
    tok = own.shape[1]
    rows, cols = row_count * rank, col_count * rank
    return pl.pallas_call(
        functools.partial(own_kernel, row_count, col_count),
        out_shape=jax.ShapeDtypeStruct((rows, rank * rank), jnp.float32),
        scratch_shapes=[
            pltpu.VMEM((2 * rank, tok), jnp.float32),
            pltpu.VMEM((1, tok), jnp.float32),
            pltpu.VMEM((rows, tok), jnp.bfloat16),
            pltpu.VMEM((cols, tok), jnp.bfloat16),
            pltpu.VMEM((cols, tok), jnp.bfloat16),
        ],
        compiler_params=params(16),
    )(own, own_other)


def hessian_kernel(row_count, col_count, mine, other, own_sum, out, *scratch):
    factors, weights, weighted, rights = *scratch[:3], scratch[3:5]
    result, sems = scratch[5:]
    rank = factors.shape[0] // 2
    blocks = mine.shape[0]
    tokens = factors.shape[1] // blocks * (blocks + 1)
    rows, cols = row_count * rank, col_count * rank
    lay_out_factors(block_pairs(mine, other), factors, weights)
    act = factors[:rank, :]
    copies = []
    build_columns(0, act, factors, rights[0])
    for step in range(rank // col_count):
        if (step + 1) * col_count < rank:
            build_columns((step + 1) * col_count, act, factors, rights[(step + 1) % 2])
        for row in range(0, rows, TILE):
            if step == 0:
                weigh_rows(row, row + TILE, row_count, factors, weights, weighted)
            here = pl.ds(row, TILE), pl.ds(step * cols, cols)
            tile = lax.dot_general(
                weighted[row : row + TILE, :],
                rights[step % 2][...],
                NT,
                preferred_element_type=jnp.float32,
            )
            result[here] = (own_sum[here] + tile) * (1.0 / tokens)
            copy = pltpu.make_async_copy(result.at[here], out.at[here], sems.at[len(copies)])
            copy.start()
            copies.append(copy)
    for copy in copies:
        copy.wait()


def hessian_rows(mine, other, own_sum, rank, row_count, col_count=8):
    blocks, _, tok = mine.shape
    feat = rank * rank
    rows, cols = row_count * rank, col_count * rank
    return pl.pallas_call(
        functools.partial(hessian_kernel, row_count, col_count),
        out_specs=pl.BlockSpec(memory_space=pl.ANY),
        out_shape=jax.ShapeDtypeStruct((rows, feat), jnp.float32),
        scratch_shapes=[
            pltpu.VMEM((2 * rank, tok * blocks), jnp.float32),
            pltpu.VMEM((1, tok * blocks), jnp.float32),
            pltpu.VMEM((rows, tok * blocks), jnp.bfloat16),
            pltpu.VMEM((cols, tok * blocks), jnp.bfloat16),
            pltpu.VMEM((cols, tok * blocks), jnp.bfloat16),
            pltpu.VMEM((rows, feat), jnp.float32),
            pltpu.SemaphoreType.DMA((feat // cols * (rows // TILE),)),
        ],
        compiler_params=params(26),
    )(mine, other, own_sum)


def finish_kernel(payload_ref, *refs):
    shares, out_ref = refs[:-1], refs[-1]
    total = shares[0][...]
    for ref in shares[1:]:
        total = total + ref[...].astype(jnp.float32)
    weight = payload_ref[...].astype(jnp.float32)[-1:]
    out_ref[...] = jnp.where(weight > 0.0, total, 0.0).T.astype(out_ref.dtype)


def finish_scores(payload, shares):
    count, tok = shares[0].shape
    return pl.pallas_call(
        finish_kernel,
        out_shape=jax.ShapeDtypeStruct((tok, count), jnp.bfloat16),
        compiler_params=params(40),
    )(payload, *shares)


def swapped(array, axis, distance):
    return lax.ppermute(array, axis, [(i, i ^ distance) for i in range(lax.axis_size(axis))])


def few_tokens(activations, out_grads, proj_in, proj_out, queries, lengths, credit):
    dp_count = lax.axis_size("dp")
    query_count = lax.axis_size("query")
    rank = proj_in.shape[1]
    row_count = rank // dp_count
    seq_len = activations.shape[0] // lengths.shape[0]
    live = jnp.arange(seq_len, dtype=jnp.int32)[None, :] < lengths[:, None]
    weight = jnp.where(live, credit[:, None], 0).astype(jnp.float32).reshape(1, -1)
    near_queries = swapped(queries, "dp", 1)
    keep, send = project(activations, out_grads, proj_in.T, proj_out.T)
    other = swapped(send, "query", 1)
    distance = 2
    while distance < query_count:
        keep = add(keep, other)
        other = swapped(keep, "query", distance)
        distance *= 2
    own = add_to_payload(keep, other, weight)
    own_other = swapped(own, "query", 1)
    others = [swapped(own, "dp", k) for k in reversed(range(1, dp_count))]
    own_sum = own_tokens_sum(own, own_other, rank, row_count)
    queries_t, near_queries_t, own_plain = turn_queries(
        queries, near_queries, own, own_other, rank, row_count
    )
    mine, factors = stack(others, rank, (own_sum, queries_t))
    other = swapped(factors, "query", 1)
    half = half_gram(own, mine, rank)
    shares = score_shares(
        own, own_other, mine, other, queries_t, near_queries_t, own_plain, half, rank, row_count
    )
    arrived = [swapped(share, "dp", 2 * n) for n, share in enumerate(shares) if n]
    hessian = hessian_rows(mine, other, own_sum, rank, row_count)
    return hessian, finish_scores(own, [shares[0]] + arrived)


def power_of_two(count):
    return count & (count - 1) == 0


def per_device(activations, *others):
    rank = others[1].shape[1]
    dp_count, query_count = lax.axis_size("dp"), lax.axis_size("query")
    pairs = min(dp_count, query_count) > 1 and power_of_two(dp_count) and power_of_two(query_count)
    if pairs and activations.shape[0] * dp_count <= rank * rank:
        return few_tokens(activations, *others)
    return many_tokens(activations, *others)


def solution(mesh):
    placed = (
        P(("groups", "dp"), "query"),
        P(("groups", "dp"), "query"),
        P("query", None),
        P("query", None),
        P(("groups", "dp"), "query"),
        P(("groups", "dp")),
        P(("groups", "dp")),
    )
    return jax.shard_map(
        per_device,
        mesh=mesh,
        in_specs=placed,
        out_specs=(P(("groups", "dp"), None), P(("groups", "dp"), "query")),
        check_vma=False,
    )
```

```python
import functools
import jax
import jax.numpy as jnp
from jax import lax
from jax.experimental import pallas as pl
from jax.experimental.pallas import tpu as pltpu
from jax.sharding import PartitionSpec as P


def kron_columns(grad_rows, act_rows, start, count):
    rank = grad_rows.shape[1]
    tokens_here = grad_rows.shape[0]
    grad_cols = lax.dynamic_slice_in_dim(grad_rows, start // rank, count // rank, 1)
    outer = grad_cols.astype(jnp.float32)[:, :, None] * act_rows.astype(jnp.float32)[:, None, :]
    return outer.reshape(tokens_here, count).astype(jnp.bfloat16)


def hessian_block(total, pieces, row_start, rows_own, col_start, col_count):
    grad_rows, act_rows, weights = pieces
    left = kron_columns(grad_rows, act_rows, row_start, rows_own)
    weighted = (weights.astype(jnp.float32)[:, None] * left.astype(jnp.float32)).astype(
        jnp.bfloat16
    )
    right = kron_columns(grad_rows, act_rows, col_start, col_count)
    return total + lax.dot_general(
        weighted, right, (((0,), (0,)), ((), ())), preferred_element_type=jnp.float32
    )


def fold_blocks(total, pieces, step_fn):
    count = pieces[0].shape[0]
    shaped = tuple((p.reshape((count // 512, 512) + p.shape[1:]) for p in pieces))

    def inner(carry, block):
        return (step_fn(carry, block), None)

    return lax.scan(inner, total, shaped)[0]


def split_parts(matrix):
    high_part = matrix.astype(jnp.bfloat16)
    first_rest = matrix - high_part.astype(jnp.float32)
    middle_part = first_rest.astype(jnp.bfloat16)
    low_part = (first_rest - middle_part.astype(jnp.float32)).astype(jnp.bfloat16)
    return (high_part, middle_part, low_part)


def many_tokens(activations, out_grads, proj_in, proj_out, queries, lengths, credit):
    tok_rows = activations.shape[0]
    seq_len = tok_rows // lengths.shape[0]
    dp_count = lax.axis_size("dp")
    query_count = lax.axis_size("query")
    dp_index = lax.axis_index("dp")
    query_index = lax.axis_index("query")
    part_act = jnp.dot(activations, proj_in, preferred_element_type=jnp.float32)
    part_grad = jnp.dot(out_grads, proj_out, preferred_element_type=jnp.float32)
    sum_act, sum_grad = lax.psum((part_act, part_grad), "query")
    act_proj = sum_act.astype(jnp.bfloat16)
    grad_proj = sum_grad.astype(jnp.bfloat16)
    rank = act_proj.shape[1]
    feat = rank * rank
    live = jnp.arange(seq_len, dtype=jnp.int32)[None, :] < lengths[:, None]
    weight = (credit[:, None].astype(jnp.float32) * live.astype(jnp.float32)).reshape(-1)
    mask = live.astype(jnp.float32).reshape(-1)
    weight_wire = weight.astype(jnp.bfloat16)
    rows_own = feat // dp_count
    row_start = dp_index * rows_own
    all_tokens = tok_rows * dp_count
    col_count = feat // query_count
    col_start = query_index * col_count
    owned = fold_blocks(
        jnp.zeros((rows_own, col_count), jnp.float32),
        (
            lax.all_gather(grad_proj, "dp", axis=0, tiled=True),
            lax.all_gather(act_proj, "dp", axis=0, tiled=True),
            lax.all_gather(weight_wire, "dp", axis=0, tiled=True),
        ),
        lambda carry, block: hessian_block(carry, block, row_start, rows_own, col_start, col_count),
    )
    hessian = lax.all_gather(owned, "query", axis=1, tiled=True) / all_tokens
    diagonal_block = lax.dynamic_slice_in_dim(hessian, row_start, rows_own, 1)
    level = lax.psum(jnp.trace(diagonal_block), "dp") / feat
    step = 1.1 * level
    high_part, middle_part, low_part = split_parts(hessian)
    piece = lax.all_gather(queries, "dp", axis=0, tiled=True)
    result = jnp.zeros(queries.shape, jnp.float32)
    for part_matrix in (low_part, middle_part, high_part):
        columns = part_matrix
        result = result + jnp.dot(columns, piece, preferred_element_type=jnp.float32)
    query_f = queries.astype(jnp.float32)
    precond = ((2.0 * query_f - (result + 0.1 * level * query_f) / step) / step).astype(
        jnp.bfloat16
    )
    local_features = kron_columns(grad_proj, act_proj, 0, feat)
    piece = lax.all_gather(precond, "dp", axis=0, tiled=True)
    columns = lax.slice_in_dim(local_features, 0, piece.shape[0], axis=1)
    scores = jnp.zeros((tok_rows, precond.shape[1]), jnp.float32) + jnp.dot(
        columns, piece, preferred_element_type=jnp.float32
    )
    return (hessian, (scores * mask[:, None]).astype(jnp.bfloat16))


MIB = 1024 * 1024
TILE = 256
NT = (((1,), (1,)), ((), ()))


def params(mib):
    return pltpu.CompilerParams(vmem_limit_bytes=int(mib * MIB))


def project_kernel(act, grad, pin, pout, keep_ref, send_ref, act_v, grad_v, pin_v, pout_v, sems):
    half = grad.shape[0] // 2
    spans = [pl.ds(0, half), pl.ds(half, half)]
    pairs = [(pin, pin_v), (act, act_v), (pout, pout_v)]
    pairs += [(grad.at[span], grad_v.at[span]) for span in spans]
    copies = [pltpu.make_async_copy(s, d, sems.at[n]) for n, (s, d) in enumerate(pairs)]
    for copy in copies:
        copy.start()
    copies[0].wait()
    copies[1].wait()
    part_act = lax.dot_general(pin_v[...], act_v[...], NT, preferred_element_type=jnp.float32)
    copies[2].wait()
    parts = []
    for copy, span in zip(copies[3:], spans):
        copy.wait()
        parts.append(
            lax.dot_general(pout_v[...], grad_v[span], NT, preferred_element_type=jnp.float32)
        )
    part_grad = jnp.concatenate(parts, axis=1)
    even = lax.rem(lax.axis_index("query"), 2) == 0
    keep_ref[...] = jnp.where(even, part_act, part_grad)
    send_ref[...] = jnp.where(even, part_grad, part_act)


def project(activations, out_grads, proj_in_t, proj_out_t):
    tok, d_here = activations.shape
    f_here = out_grads.shape[1]
    rank = proj_in_t.shape[0]
    out = jax.ShapeDtypeStruct((rank, tok), jnp.float32)
    return pl.pallas_call(
        project_kernel,
        in_specs=[pl.BlockSpec(memory_space=pl.ANY)] * 4,
        out_shape=[out, out],
        scratch_shapes=[
            pltpu.VMEM((tok, d_here), jnp.bfloat16),
            pltpu.VMEM((tok, f_here), jnp.bfloat16),
            pltpu.VMEM((rank, d_here), jnp.bfloat16),
            pltpu.VMEM((rank, f_here), jnp.bfloat16),
            pltpu.SemaphoreType.DMA((5,)),
        ],
        compiler_params=params(53.75),
    )(activations, out_grads, proj_in_t, proj_out_t)


def add_kernel(one_ref, other_ref, out_ref):
    out_ref[...] = one_ref[...] + other_ref[...]


def add(one, other):
    return pl.pallas_call(
        add_kernel,
        out_shape=jax.ShapeDtypeStruct(one.shape, one.dtype),
        compiler_params=params(40),
    )(one, other)


def payload_kernel(one_ref, other_ref, weight_ref, out_ref):
    total = jnp.where(weight_ref[...] > 0.0, one_ref[...] + other_ref[...], 0.0)
    weight = jnp.broadcast_to(weight_ref[...], (16, weight_ref.shape[1]))
    out_ref[...] = jnp.concatenate([total, weight], axis=0).astype(out_ref.dtype)


def add_to_payload(one, other, weight):
    rows, tok = one.shape
    return pl.pallas_call(
        payload_kernel,
        out_shape=jax.ShapeDtypeStruct((rows + 16, tok), jnp.bfloat16),
        compiler_params=params(40),
    )(one, other, weight)


def stack_kernel(_, __, *refs):
    parts, (out_ref, factors_ref) = refs[:-2], refs[-2:]
    for k, ref in enumerate(parts):
        out_ref[k] = ref[...]
        factors_ref[k] = ref[: factors_ref.shape[1]]


def stack(parts, rank, after):
    rows, tok = parts[0].shape
    whole = pl.BlockSpec(memory_space=pltpu.VMEM)
    return pl.pallas_call(
        stack_kernel,
        in_specs=[pl.BlockSpec(memory_space=pl.ANY)] * 2 + [whole] * len(parts),
        out_shape=[
            jax.ShapeDtypeStruct((len(parts), rows, tok), parts[0].dtype),
            jax.ShapeDtypeStruct((len(parts), rank, tok), parts[0].dtype),
        ],
        compiler_params=params(26),
    )(*after, *parts)


def lay_out_factors(blocks, factors, weights):
    rank = factors.shape[0] // 2
    here = pl.multiple_of(lax.rem(lax.axis_index("query"), 2) * rank, rank)
    there = pl.multiple_of(rank - here, rank)
    for k, (mine, other) in enumerate(blocks):
        span = slice(k * mine.shape[1], (k + 1) * mine.shape[1])
        factors[pl.ds(here, rank), span] = mine[:rank].astype(jnp.float32)
        factors[pl.ds(there, rank), span] = other[:rank].astype(jnp.float32)
        weights[:, span] = mine[rank:].astype(jnp.float32)[:1]


def block_pairs(mine, other):
    return [(mine.at[k], other.at[k]) for k in reversed(range(mine.shape[0]))]


def weigh_rows(first_row, end_row, row_count, factors, weights, weighted):
    rank = factors.shape[0] // 2
    act, weight = factors[:rank, :], weights[...]
    first = rank + lax.axis_index("dp") * row_count
    for i in range(first_row // rank, end_row // rank):
        left = (factors[pl.ds(first + i, 1), :] * act).astype(jnp.bfloat16)
        left = (weight * left.astype(jnp.float32)).astype(jnp.bfloat16)
        weighted[i * rank : (i + 1) * rank, :] = left


def range_scale(values):
    top = jnp.max(jnp.abs(values), keepdims=True)
    scale = jnp.ones_like(top)
    for low in (16, 48, 80, 112):
        scale = jnp.where(top > 2.0**low, 2.0 ** -min(low + 16, 126), scale)
        scale = jnp.where(top < 2.0**-low, 2.0 ** min(low + 16, 126), scale)
    return scale


def project_queries(row_count, factors, features, query_ref):
    rank = factors.shape[0] // 2
    act = factors[:rank, :]
    for near in range(2):
        first = rank + (lax.axis_index("dp") ^ near) * row_count
        for i in range(row_count):
            row = factors[pl.ds(first + i, 1), :]
            start = (near * row_count + i) * rank
            features[start : start + rank, :] = (row * act).astype(jnp.bfloat16)
    return jnp.dot(query_ref[...], features[...], preferred_element_type=jnp.float32)


def turn_kernel(row_count, query, near_query, own, own_other, *refs):
    out_ref, plain_ref, factors, weights, features = refs
    rows = query.shape[0]
    out_ref[:, :rows] = query[...].T
    out_ref[:, rows:] = near_query[...].T
    lay_out_factors([(own, own_other)], factors, weights)
    plain_ref[...] = project_queries(row_count, factors, features, out_ref)


def turn_queries(queries, near_queries, own, own_other, rank, row_count):
    rows, count = queries.shape
    tok = own.shape[1]
    out = jax.ShapeDtypeStruct((count, 2 * rows), queries.dtype)
    return pl.pallas_call(
        functools.partial(turn_kernel, row_count),
        out_shape=[out, jax.ShapeDtypeStruct((count, tok), jnp.float32)],
        scratch_shapes=[
            pltpu.VMEM((2 * rank, tok), jnp.float32),
            pltpu.VMEM((1, tok), jnp.float32),
            pltpu.VMEM((2 * rows, tok), jnp.bfloat16),
        ],
        compiler_params=params(26),
    )(queries, near_queries, own, own_other)


def scaled(values):
    scale = range_scale(values)
    return values * scale, scale


def half_kernel(own, mine, gram_ref, norm_ref, scale_ref, values):
    rank, tok = values.shape[0], own.shape[1]
    for k, part in enumerate([own] + [mine.at[k] for k in reversed(range(mine.shape[0]))]):
        values[:, k * tok : (k + 1) * tok] = part[:rank].astype(jnp.float32)
    factor, scale = scaled(values[...])
    scale_ref[...] = jnp.broadcast_to(scale, scale_ref.shape)
    norm = jnp.sum(factor * factor, axis=0, keepdims=True)
    norm_ref[...] = jnp.broadcast_to(norm, norm_ref.shape)
    factor_b, factor_rows = factor.astype(jnp.bfloat16), factor.T.astype(jnp.bfloat16)
    for n in range(gram_ref.shape[0]):
        block = slice(2 * n * tok, (2 * n + 1) * tok)
        for row in range(0, values.shape[1], TILE // 2):
            here = slice(row, row + TILE // 2)
            gram_ref[n, here, :] = jnp.dot(
                factor_rows[here], factor_b[:, block], preferred_element_type=jnp.float32
            )


def half_gram(own, mine, rank):
    blocks, tok = mine.shape[0] + 1, own.shape[1]
    tokens = blocks * tok
    return pl.pallas_call(
        half_kernel,
        out_shape=[
            jax.ShapeDtypeStruct((blocks // 2, tokens, tok), jnp.float32),
            jax.ShapeDtypeStruct((8, tokens), jnp.float32),
            jax.ShapeDtypeStruct((8, 128), jnp.float32),
        ],
        scratch_shapes=[pltpu.VMEM((rank, tokens), jnp.float32)],
        compiler_params=params(26),
    )(own, mine)


def share_kernel(row_count, own, own_other, mine, other, query_ref, own_plain_ref, *refs):
    half_gram_ref, half_norm_ref, half_scale_ref = refs[:3]
    refs = refs[3:]
    factors, weights, features, gram = refs[-4:]
    out_refs = refs[:-4]
    lay_out_factors([(own, own_other)] + block_pairs(mine, other), factors, weights)
    rank = factors.shape[0] // 2
    tokens = factors.shape[1]
    tok = own.shape[1]
    plain = project_queries(row_count, factors.at[:, tok:], features, query_ref)
    plain = jnp.concatenate([own_plain_ref[...], plain], axis=1)
    there = pl.multiple_of(rank - lax.rem(lax.axis_index("query"), 2) * rank, rank)
    factor, scale = scaled(factors[pl.ds(there, rank), :])
    weight = weights[...]
    norms = half_norm_ref[:1, :] * jnp.sum(factor * factor, axis=0, keepdims=True)
    level = jnp.sum(weight * norms, axis=1, keepdims=True) / (tokens * rank * rank)
    step = 1.1 * level
    factor_b, factor_rows = factor.astype(jnp.bfloat16), factor.T.astype(jnp.bfloat16)
    weighted = (plain * (weight * (1.0 / (tokens * step)))).astype(jnp.bfloat16)
    scale = scale * half_scale_ref[:1, :1]
    for n, out_ref in enumerate(out_refs):
        block = slice(2 * n * tok, (2 * n + 1) * tok)
        for row in range(0, tokens, TILE // 2):
            here = slice(row, row + TILE // 2)
            tile = jnp.dot(factor_rows[here], factor_b[:, block], preferred_element_type=jnp.float32)
            gram[n, here, :] = (tile * half_gram_ref[n, here, :]).astype(jnp.bfloat16)
        image = jnp.dot(weighted, gram[n], preferred_element_type=jnp.float32)
        share = ((2.0 - 0.1 / 1.1) * plain[:, block] - image) * scale * (scale / step)
        out_ref[...] = share.astype(out_ref.dtype)


def score_shares(own, own_other, mine, other, queries_t, own_plain, half, rank, row_count):
    blocks, tok = mine.shape[0] + 1, mine.shape[2]
    count, depth = queries_t.shape
    return pl.pallas_call(
        functools.partial(share_kernel, row_count),
        out_shape=[
            jax.ShapeDtypeStruct((count, tok), jnp.bfloat16 if k else jnp.float32)
            for k in range(0, blocks, 2)
        ],
        scratch_shapes=[
            pltpu.VMEM((2 * rank, tok * blocks), jnp.float32),
            pltpu.VMEM((1, tok * blocks), jnp.float32),
            pltpu.VMEM((depth, tok * (blocks - 1)), jnp.bfloat16),
            pltpu.VMEM((blocks // 2, tok * blocks, tok), jnp.bfloat16),
        ],
        compiler_params=params(26),
    )(own, own_other, mine, other, queries_t, own_plain, *half)


def build_columns(first, act, factors, right):
    rank = act.shape[0]
    for i in range(right.shape[0] // rank):
        row = rank + first + i
        right[i * rank : (i + 1) * rank, :] = (factors[row : row + 1, :] * act).astype(jnp.bfloat16)


def own_kernel(row_count, col_count, own, own_other, out, factors, weights, weighted, *rights):
    rank = factors.shape[0] // 2
    cols = col_count * rank
    lay_out_factors([(own, own_other)], factors, weights)
    weigh_rows(0, weighted.shape[0], row_count, factors, weights, weighted)
    act = factors[:rank, :]
    build_columns(0, act, factors, rights[0])
    for step in range(rank // col_count):
        if (step + 1) * col_count < rank:
            build_columns((step + 1) * col_count, act, factors, rights[(step + 1) % 2])
        out[:, step * cols : (step + 1) * cols] = lax.dot_general(
            weighted[...], rights[step % 2][...], NT, preferred_element_type=jnp.float32
        )


def own_tokens_sum(own, own_other, rank, row_count, col_count=8):
    tok = own.shape[1]
    rows, cols = row_count * rank, col_count * rank
    return pl.pallas_call(
        functools.partial(own_kernel, row_count, col_count),
        out_shape=jax.ShapeDtypeStruct((rows, rank * rank), jnp.float32),
        scratch_shapes=[
            pltpu.VMEM((2 * rank, tok), jnp.float32),
            pltpu.VMEM((1, tok), jnp.float32),
            pltpu.VMEM((rows, tok), jnp.bfloat16),
            pltpu.VMEM((cols, tok), jnp.bfloat16),
            pltpu.VMEM((cols, tok), jnp.bfloat16),
        ],
        compiler_params=params(16),
    )(own, own_other)


def hessian_kernel(row_count, col_count, mine, other, own_sum, out, *scratch):
    factors, weights, weighted, rights = *scratch[:3], scratch[3:5]
    result, sems = scratch[5:]
    rank = factors.shape[0] // 2
    blocks = mine.shape[0]
    tokens = factors.shape[1] // blocks * (blocks + 1)
    rows, cols = row_count * rank, col_count * rank
    lay_out_factors(block_pairs(mine, other), factors, weights)
    act = factors[:rank, :]
    copies = []
    build_columns(0, act, factors, rights[0])
    for step in range(rank // col_count):
        if (step + 1) * col_count < rank:
            build_columns((step + 1) * col_count, act, factors, rights[(step + 1) % 2])
        for row in range(0, rows, TILE):
            if step == 0:
                weigh_rows(row, row + TILE, row_count, factors, weights, weighted)
            here = pl.ds(row, TILE), pl.ds(step * cols, cols)
            tile = lax.dot_general(
                weighted[row : row + TILE, :],
                rights[step % 2][...],
                NT,
                preferred_element_type=jnp.float32,
            )
            result[here] = (own_sum[here] + tile) * (1.0 / tokens)
            copy = pltpu.make_async_copy(result.at[here], out.at[here], sems.at[len(copies)])
            copy.start()
            copies.append(copy)
    for copy in copies:
        copy.wait()


def hessian_rows(mine, other, own_sum, rank, row_count, col_count=8):
    blocks, _, tok = mine.shape
    feat = rank * rank
    rows, cols = row_count * rank, col_count * rank
    return pl.pallas_call(
        functools.partial(hessian_kernel, row_count, col_count),
        out_specs=pl.BlockSpec(memory_space=pl.ANY),
        out_shape=jax.ShapeDtypeStruct((rows, feat), jnp.float32),
        scratch_shapes=[
            pltpu.VMEM((2 * rank, tok * blocks), jnp.float32),
            pltpu.VMEM((1, tok * blocks), jnp.float32),
            pltpu.VMEM((rows, tok * blocks), jnp.bfloat16),
            pltpu.VMEM((cols, tok * blocks), jnp.bfloat16),
            pltpu.VMEM((cols, tok * blocks), jnp.bfloat16),
            pltpu.VMEM((rows, feat), jnp.float32),
            pltpu.SemaphoreType.DMA((feat // cols * (rows // TILE),)),
        ],
        compiler_params=params(26),
    )(mine, other, own_sum)


def finish_kernel(payload_ref, *refs):
    shares, out_ref = refs[:-1], refs[-1]
    total = shares[0][...]
    for ref in shares[1:]:
        total = total + ref[...].astype(jnp.float32)
    weight = payload_ref[...].astype(jnp.float32)[-1:]
    out_ref[...] = jnp.where(weight > 0.0, total, 0.0).T.astype(out_ref.dtype)


def finish_scores(payload, shares):
    count, tok = shares[0].shape
    return pl.pallas_call(
        finish_kernel,
        out_shape=jax.ShapeDtypeStruct((tok, count), jnp.bfloat16),
        compiler_params=params(40),
    )(payload, *shares)


def swapped(array, axis, distance):
    return lax.ppermute(array, axis, [(i, i ^ distance) for i in range(lax.axis_size(axis))])


def few_tokens(activations, out_grads, proj_in, proj_out, queries, lengths, credit):
    dp_count = lax.axis_size("dp")
    query_count = lax.axis_size("query")
    rank = proj_in.shape[1]
    row_count = rank // dp_count
    seq_len = activations.shape[0] // lengths.shape[0]
    live = jnp.arange(seq_len, dtype=jnp.int32)[None, :] < lengths[:, None]
    weight = jnp.where(live, credit[:, None], 0).astype(jnp.float32).reshape(1, -1)
    near_queries = swapped(queries, "dp", 1)
    keep, send = project(activations, out_grads, proj_in.T, proj_out.T)
    other = swapped(send, "query", 1)
    distance = 2
    while distance < query_count:
        keep = add(keep, other)
        other = swapped(keep, "query", distance)
        distance *= 2
    own = add_to_payload(keep, other, weight)
    own_other = swapped(own, "query", 1)
    others = [swapped(own, "dp", k) for k in reversed(range(1, dp_count))]
    own_sum = own_tokens_sum(own, own_other, rank, row_count)
    queries_t, own_plain = turn_queries(
        queries, near_queries, own, own_other, rank, row_count
    )
    mine, factors = stack(others, rank, (own_sum, queries_t))
    other = swapped(factors, "query", 1)
    half = half_gram(own, mine, rank)
    shares = score_shares(
        own, own_other, mine, other, queries_t, own_plain, half, rank, row_count
    )
    arrived = [swapped(share, "dp", 2 * n) for n, share in enumerate(shares) if n]
    hessian = hessian_rows(mine, other, own_sum, rank, row_count)
    return hessian, finish_scores(own, [shares[0]] + arrived)


def power_of_two(count):
    return count & (count - 1) == 0


def per_device(activations, *others):
    rank = others[1].shape[1]
    dp_count, query_count = lax.axis_size("dp"), lax.axis_size("query")
    pairs = min(dp_count, query_count) > 1 and power_of_two(dp_count) and power_of_two(query_count)
    if pairs and activations.shape[0] * dp_count <= rank * rank:
        return few_tokens(activations, *others)
    return many_tokens(activations, *others)


def solution(mesh):
    placed = (
        P(("groups", "dp"), "query"),
        P(("groups", "dp"), "query"),
        P("query", None),
        P("query", None),
        P(("groups", "dp"), "query"),
        P(("groups", "dp")),
        P(("groups", "dp")),
    )
    return jax.shard_map(
        per_device,
        mesh=mesh,
        in_specs=placed,
        out_specs=(P(("groups", "dp"), None), P(("groups", "dp"), "query")),
        check_vma=False,
    )
```

```python
import functools
import jax
import jax.numpy as jnp
from jax import lax
from jax.experimental import pallas as pl
from jax.experimental.pallas import tpu as pltpu
from jax.sharding import PartitionSpec as P


def kron_columns(grad_rows, act_rows, start, count):
    rank = grad_rows.shape[1]
    tokens_here = grad_rows.shape[0]
    grad_cols = lax.dynamic_slice_in_dim(grad_rows, start // rank, count // rank, 1)
    outer = grad_cols.astype(jnp.float32)[:, :, None] * act_rows.astype(jnp.float32)[:, None, :]
    return outer.reshape(tokens_here, count).astype(jnp.bfloat16)


def hessian_block(total, pieces, row_start, rows_own, col_start, col_count):
    grad_rows, act_rows, weights = pieces
    left = kron_columns(grad_rows, act_rows, row_start, rows_own)
    weighted = (weights.astype(jnp.float32)[:, None] * left.astype(jnp.float32)).astype(
        jnp.bfloat16
    )
    right = kron_columns(grad_rows, act_rows, col_start, col_count)
    return total + lax.dot_general(
        weighted, right, (((0,), (0,)), ((), ())), preferred_element_type=jnp.float32
    )


def fold_blocks(total, pieces, step_fn):
    count = pieces[0].shape[0]
    shaped = tuple((p.reshape((count // 512, 512) + p.shape[1:]) for p in pieces))

    def inner(carry, block):
        return (step_fn(carry, block), None)

    return lax.scan(inner, total, shaped)[0]


def split_parts(matrix):
    high_part = matrix.astype(jnp.bfloat16)
    first_rest = matrix - high_part.astype(jnp.float32)
    middle_part = first_rest.astype(jnp.bfloat16)
    low_part = (first_rest - middle_part.astype(jnp.float32)).astype(jnp.bfloat16)
    return (high_part, middle_part, low_part)


def many_tokens(activations, out_grads, proj_in, proj_out, queries, lengths, credit):
    tok_rows = activations.shape[0]
    seq_len = tok_rows // lengths.shape[0]
    dp_count = lax.axis_size("dp")
    query_count = lax.axis_size("query")
    dp_index = lax.axis_index("dp")
    query_index = lax.axis_index("query")
    part_act = jnp.dot(activations, proj_in, preferred_element_type=jnp.float32)
    part_grad = jnp.dot(out_grads, proj_out, preferred_element_type=jnp.float32)
    sum_act, sum_grad = lax.psum((part_act, part_grad), "query")
    act_proj = sum_act.astype(jnp.bfloat16)
    grad_proj = sum_grad.astype(jnp.bfloat16)
    rank = act_proj.shape[1]
    feat = rank * rank
    live = jnp.arange(seq_len, dtype=jnp.int32)[None, :] < lengths[:, None]
    weight = (credit[:, None].astype(jnp.float32) * live.astype(jnp.float32)).reshape(-1)
    mask = live.astype(jnp.float32).reshape(-1)
    weight_wire = weight.astype(jnp.bfloat16)
    rows_own = feat // dp_count
    row_start = dp_index * rows_own
    all_tokens = tok_rows * dp_count
    col_count = feat // query_count
    col_start = query_index * col_count
    owned = fold_blocks(
        jnp.zeros((rows_own, col_count), jnp.float32),
        (
            lax.all_gather(grad_proj, "dp", axis=0, tiled=True),
            lax.all_gather(act_proj, "dp", axis=0, tiled=True),
            lax.all_gather(weight_wire, "dp", axis=0, tiled=True),
        ),
        lambda carry, block: hessian_block(carry, block, row_start, rows_own, col_start, col_count),
    )
    hessian = lax.all_gather(owned, "query", axis=1, tiled=True) / all_tokens
    diagonal_block = lax.dynamic_slice_in_dim(hessian, row_start, rows_own, 1)
    level = lax.psum(jnp.trace(diagonal_block), "dp") / feat
    step = 1.1 * level
    high_part, middle_part, low_part = split_parts(hessian)
    piece = lax.all_gather(queries, "dp", axis=0, tiled=True)
    result = jnp.zeros(queries.shape, jnp.float32)
    for part_matrix in (low_part, middle_part, high_part):
        columns = part_matrix
        result = result + jnp.dot(columns, piece, preferred_element_type=jnp.float32)
    query_f = queries.astype(jnp.float32)
    precond = ((2.0 * query_f - (result + 0.1 * level * query_f) / step) / step).astype(
        jnp.bfloat16
    )
    local_features = kron_columns(grad_proj, act_proj, 0, feat)
    piece = lax.all_gather(precond, "dp", axis=0, tiled=True)
    columns = lax.slice_in_dim(local_features, 0, piece.shape[0], axis=1)
    scores = jnp.zeros((tok_rows, precond.shape[1]), jnp.float32) + jnp.dot(
        columns, piece, preferred_element_type=jnp.float32
    )
    return (hessian, (scores * mask[:, None]).astype(jnp.bfloat16))


MIB = 1024 * 1024
TILE = 256
NT = (((1,), (1,)), ((), ()))


def params(mib):
    return pltpu.CompilerParams(vmem_limit_bytes=int(mib * MIB))


def project_kernel(act, grad, pin, pout, keep_ref, send_ref, act_v, grad_v, pin_v, pout_v, sems):
    chunk = grad.shape[1] // 2
    spans = [pl.ds(0, chunk), pl.ds(chunk, chunk)]
    pairs = [(pin, pin_v), (act, act_v), (pout, pout_v)]
    pairs += [(grad.at[:, span], grad_v.at[:, span]) for span in spans]
    copies = [pltpu.make_async_copy(s, d, sems.at[n]) for n, (s, d) in enumerate(pairs)]
    for copy in copies:
        copy.start()
    copies[0].wait()
    copies[1].wait()
    part_act = lax.dot_general(pin_v[...], act_v[...], NT, preferred_element_type=jnp.float32)
    copies[2].wait()
    part_grad = jnp.zeros_like(part_act)
    for copy, span in zip(copies[3:], spans):
        copy.wait()
        part_grad += lax.dot_general(
            pout_v[:, span], grad_v[:, span], NT, preferred_element_type=jnp.float32
        )
    even = lax.rem(lax.axis_index("query"), 2) == 0
    keep_ref[...] = jnp.where(even, part_act, part_grad)
    send_ref[...] = jnp.where(even, part_grad, part_act)


def project(activations, out_grads, proj_in_t, proj_out_t):
    tok, d_here = activations.shape
    f_here = out_grads.shape[1]
    rank = proj_in_t.shape[0]
    out = jax.ShapeDtypeStruct((rank, tok), jnp.float32)
    return pl.pallas_call(
        project_kernel,
        in_specs=[pl.BlockSpec(memory_space=pl.ANY)] * 4,
        out_shape=[out, out],
        scratch_shapes=[
            pltpu.VMEM((tok, d_here), jnp.bfloat16),
            pltpu.VMEM((tok, f_here), jnp.bfloat16),
            pltpu.VMEM((rank, d_here), jnp.bfloat16),
            pltpu.VMEM((rank, f_here), jnp.bfloat16),
            pltpu.SemaphoreType.DMA((5,)),
        ],
        compiler_params=params(53.75),
    )(activations, out_grads, proj_in_t, proj_out_t)


def add_kernel(one_ref, other_ref, out_ref):
    out_ref[...] = one_ref[...] + other_ref[...]


def add(one, other):
    return pl.pallas_call(
        add_kernel,
        out_shape=jax.ShapeDtypeStruct(one.shape, one.dtype),
        compiler_params=params(40),
    )(one, other)


def payload_kernel(one_ref, other_ref, weight_ref, out_ref):
    total = jnp.where(weight_ref[...] > 0.0, one_ref[...] + other_ref[...], 0.0)
    weight = jnp.broadcast_to(weight_ref[...], (16, weight_ref.shape[1]))
    out_ref[...] = jnp.concatenate([total, weight], axis=0).astype(out_ref.dtype)


def add_to_payload(one, other, weight):
    rows, tok = one.shape
    return pl.pallas_call(
        payload_kernel,
        out_shape=jax.ShapeDtypeStruct((rows + 16, tok), jnp.bfloat16),
        compiler_params=params(40),
    )(one, other, weight)


def pass_kernel(_, __, part, out_ref):
    out_ref[...] = part[: out_ref.shape[0]]


def pass_factors(part, rank, after):
    anywhere = pl.BlockSpec(memory_space=pl.ANY)
    return pl.pallas_call(
        pass_kernel,
        in_specs=[anywhere, anywhere, pl.BlockSpec(memory_space=pltpu.VMEM)],
        out_shape=jax.ShapeDtypeStruct((rank, part.shape[1]), part.dtype),
        compiler_params=params(26),
    )(*after, part)


def stack_kernel(_, __, *refs):
    parts, (out_ref, factors_ref) = refs[:-2], refs[-2:]
    for k, ref in enumerate(parts):
        out_ref[k] = ref[...]
        factors_ref[k] = ref[: factors_ref.shape[1]]


def stack(parts, rank, after):
    rows, tok = parts[0].shape
    whole = pl.BlockSpec(memory_space=pltpu.VMEM)
    return pl.pallas_call(
        stack_kernel,
        in_specs=[pl.BlockSpec(memory_space=pl.ANY)] * 2 + [whole] * len(parts),
        out_shape=[
            jax.ShapeDtypeStruct((len(parts), rows, tok), parts[0].dtype),
            jax.ShapeDtypeStruct((len(parts), rank, tok), parts[0].dtype),
        ],
        compiler_params=params(26),
    )(*after, *parts)


def lay_out_factors(blocks, factors, weights):
    rank = factors.shape[0] // 2
    here = pl.multiple_of(lax.rem(lax.axis_index("query"), 2) * rank, rank)
    there = pl.multiple_of(rank - here, rank)
    for k, (mine, other) in enumerate(blocks):
        span = slice(k * mine.shape[1], (k + 1) * mine.shape[1])
        factors[pl.ds(here, rank), span] = mine[:rank].astype(jnp.float32)
        factors[pl.ds(there, rank), span] = other[:rank].astype(jnp.float32)
        weights[:, span] = mine[rank:].astype(jnp.float32)[:1]


def block_pairs(far, far_other, mine, other):
    near = [(mine.at[k], other.at[k]) for k in reversed(range(mine.shape[0]))]
    return near + [(far, far_other)]


def weigh_rows(first_row, end_row, row_count, factors, weights, weighted):
    rank = factors.shape[0] // 2
    act, weight = factors[:rank, :], weights[...]
    first = rank + lax.axis_index("dp") * row_count
    for i in range(first_row // rank, end_row // rank):
        left = (factors[pl.ds(first + i, 1), :] * act).astype(jnp.bfloat16)
        left = (weight * left.astype(jnp.float32)).astype(jnp.bfloat16)
        weighted[i * rank : (i + 1) * rank, :] = left


def range_scale(values):
    top = jnp.max(jnp.abs(values), keepdims=True)
    scale = jnp.ones_like(top)
    for low in (16, 48, 80, 112):
        scale = jnp.where(top > 2.0**low, 2.0 ** -min(low + 16, 126), scale)
        scale = jnp.where(top < 2.0**-low, 2.0 ** min(low + 16, 126), scale)
    return scale


def project_queries(row_count, factors, features, query_ref):
    rank = factors.shape[0] // 2
    act = factors[:rank, :]
    for near in range(2):
        first = rank + (lax.axis_index("dp") ^ near) * row_count
        for i in range(row_count):
            row = factors[pl.ds(first + i, 1), :]
            start = (near * row_count + i) * rank
            features[start : start + rank, :] = (row * act).astype(jnp.bfloat16)
    return jnp.dot(query_ref[...], features[...], preferred_element_type=jnp.float32)


def turn_kernel(row_count, query, near_query, own, own_other, *refs):
    out_ref, plain_ref, factors, weights, features = refs
    rows = query.shape[0]
    out_ref[:, :rows] = query[...].T
    out_ref[:, rows:] = near_query[...].T
    lay_out_factors([(own, own_other)], factors, weights)
    plain_ref[...] = project_queries(row_count, factors, features, out_ref)


def turn_queries(queries, near_queries, own, own_other, rank, row_count):
    rows, count = queries.shape
    tok = own.shape[1]
    out = jax.ShapeDtypeStruct((count, 2 * rows), queries.dtype)
    return pl.pallas_call(
        functools.partial(turn_kernel, row_count),
        out_shape=[out, jax.ShapeDtypeStruct((count, tok), jnp.float32)],
        scratch_shapes=[
            pltpu.VMEM((2 * rank, tok), jnp.float32),
            pltpu.VMEM((1, tok), jnp.float32),
            pltpu.VMEM((2 * rows, tok), jnp.bfloat16),
        ],
        compiler_params=params(26),
    )(queries, near_queries, own, own_other)


def scaled(values):
    scale = range_scale(values)
    return values * scale, scale


def half_kernel(own, far, mine, gram_ref, norm_ref, scale_ref, values):
    rank, tok = values.shape[0], own.shape[1]
    near = [mine.at[k] for k in reversed(range(mine.shape[0]))]
    for k, part in enumerate([own] + near + [far]):
        values[:, k * tok : (k + 1) * tok] = part[:rank].astype(jnp.float32)
    factor, scale = scaled(values[...])
    scale_ref[...] = jnp.broadcast_to(scale, scale_ref.shape)
    norm = jnp.sum(factor * factor, axis=0, keepdims=True)
    norm_ref[...] = jnp.broadcast_to(norm, norm_ref.shape)
    factor_b, factor_rows = factor.astype(jnp.bfloat16), factor.T.astype(jnp.bfloat16)
    for n in range(gram_ref.shape[0]):
        block = slice(2 * n * tok, (2 * n + 1) * tok)
        for row in range(0, values.shape[1], TILE // 2):
            here = slice(row, row + TILE // 2)
            gram_ref[n, here, :] = jnp.dot(
                factor_rows[here], factor_b[:, block], preferred_element_type=jnp.float32
            )


def half_gram(own, far, mine, rank):
    blocks, tok = mine.shape[0] + 2, own.shape[1]
    tokens = blocks * tok
    return pl.pallas_call(
        half_kernel,
        out_shape=[
            jax.ShapeDtypeStruct((blocks // 2, tokens, tok), jnp.float32),
            jax.ShapeDtypeStruct((8, tokens), jnp.float32),
            jax.ShapeDtypeStruct((8, 128), jnp.float32),
        ],
        scratch_shapes=[pltpu.VMEM((rank, tokens), jnp.float32)],
        compiler_params=params(26),
    )(own, far, mine)


def share_kernel(row_count, own, own_other, far, far_other, mine, other, *refs):
    query_ref, own_plain_ref = refs[:2]
    half_gram_ref, half_norm_ref, half_scale_ref = refs[2:5]
    refs = refs[5:]
    factors, weights, features, gram = refs[-4:]
    out_refs = refs[:-4]
    lay_out_factors([(own, own_other)] + block_pairs(far, far_other, mine, other), factors, weights)
    rank = factors.shape[0] // 2
    tokens = factors.shape[1]
    tok = own.shape[1]
    plain = project_queries(row_count, factors.at[:, tok:], features, query_ref)
    plain = jnp.concatenate([own_plain_ref[...], plain], axis=1)
    there = pl.multiple_of(rank - lax.rem(lax.axis_index("query"), 2) * rank, rank)
    factor, scale = scaled(factors[pl.ds(there, rank), :])
    weight = weights[...]
    norms = half_norm_ref[:1, :] * jnp.sum(factor * factor, axis=0, keepdims=True)
    level = jnp.sum(weight * norms, axis=1, keepdims=True) / (tokens * rank * rank)
    step = 1.1 * level
    factor_b, factor_rows = factor.astype(jnp.bfloat16), factor.T.astype(jnp.bfloat16)
    weighted = (plain * (weight * (1.0 / (tokens * step)))).astype(jnp.bfloat16)
    scale = scale * half_scale_ref[:1, :1]
    for n, out_ref in enumerate(out_refs):
        block = slice(2 * n * tok, (2 * n + 1) * tok)
        for row in range(0, tokens, TILE // 2):
            here = slice(row, row + TILE // 2)
            tile = jnp.dot(factor_rows[here], factor_b[:, block], preferred_element_type=jnp.float32)
            gram[n, here, :] = (tile * half_gram_ref[n, here, :]).astype(jnp.bfloat16)
        image = jnp.dot(weighted, gram[n], preferred_element_type=jnp.float32)
        share = ((2.0 - 0.1 / 1.1) * plain[:, block] - image) * scale * (scale / step)
        out_ref[...] = share.astype(out_ref.dtype)


def score_shares(factors, queries_t, own_plain, half, rank, row_count):
    mine = factors[-1]
    blocks, tok = mine.shape[0] + 2, mine.shape[2]
    count, depth = queries_t.shape
    return pl.pallas_call(
        functools.partial(share_kernel, row_count),
        out_shape=[
            jax.ShapeDtypeStruct((count, tok), jnp.bfloat16 if k else jnp.float32)
            for k in range(0, blocks, 2)
        ],
        scratch_shapes=[
            pltpu.VMEM((2 * rank, tok * blocks), jnp.float32),
            pltpu.VMEM((1, tok * blocks), jnp.float32),
            pltpu.VMEM((depth, tok * (blocks - 1)), jnp.bfloat16),
            pltpu.VMEM((blocks // 2, tok * blocks, tok), jnp.bfloat16),
        ],
        compiler_params=params(26),
    )(*factors, queries_t, own_plain, *half)


def build_columns(first, act, factors, right):
    rank = act.shape[0]
    for i in range(right.shape[0] // rank):
        row = rank + first + i
        right[i * rank : (i + 1) * rank, :] = (factors[row : row + 1, :] * act).astype(jnp.bfloat16)


def own_kernel(row_count, col_count, own, own_other, out, factors, weights, weighted, *rights):
    rank = factors.shape[0] // 2
    cols = col_count * rank
    lay_out_factors([(own, own_other)], factors, weights)
    weigh_rows(0, weighted.shape[0], row_count, factors, weights, weighted)
    act = factors[:rank, :]
    build_columns(0, act, factors, rights[0])
    for step in range(rank // col_count):
        if (step + 1) * col_count < rank:
            build_columns((step + 1) * col_count, act, factors, rights[(step + 1) % 2])
        out[:, step * cols : (step + 1) * cols] = lax.dot_general(
            weighted[...], rights[step % 2][...], NT, preferred_element_type=jnp.float32
        )


def own_tokens_sum(own, own_other, rank, row_count, col_count=8):
    tok = own.shape[1]
    rows, cols = row_count * rank, col_count * rank
    return pl.pallas_call(
        functools.partial(own_kernel, row_count, col_count),
        out_shape=jax.ShapeDtypeStruct((rows, rank * rank), jnp.float32),
        scratch_shapes=[
            pltpu.VMEM((2 * rank, tok), jnp.float32),
            pltpu.VMEM((1, tok), jnp.float32),
            pltpu.VMEM((rows, tok), jnp.bfloat16),
            pltpu.VMEM((cols, tok), jnp.bfloat16),
            pltpu.VMEM((cols, tok), jnp.bfloat16),
        ],
        compiler_params=params(16),
    )(own, own_other)


def hessian_kernel(
    row_count, col_count, far, far_other, mine, other, own_sum, out, *scratch
):
    factors, weights, weighted, rights = *scratch[:3], scratch[3:5]
    result, sems = scratch[5:]
    rank = factors.shape[0] // 2
    blocks = mine.shape[0] + 1
    tokens = factors.shape[1] // blocks * (blocks + 1)
    rows, cols = row_count * rank, col_count * rank
    lay_out_factors(block_pairs(far, far_other, mine, other), factors, weights)
    act = factors[:rank, :]
    copies = []
    build_columns(0, act, factors, rights[0])
    for step in range(rank // col_count):
        if (step + 1) * col_count < rank:
            build_columns((step + 1) * col_count, act, factors, rights[(step + 1) % 2])
        for row in range(0, rows, TILE):
            if step == 0:
                weigh_rows(row, row + TILE, row_count, factors, weights, weighted)
            here = pl.ds(row, TILE), pl.ds(step * cols, cols)
            tile = lax.dot_general(
                weighted[row : row + TILE, :],
                rights[step % 2][...],
                NT,
                preferred_element_type=jnp.float32,
            )
            result[here] = (own_sum[here] + tile) * (1.0 / tokens)
            copy = pltpu.make_async_copy(result.at[here], out.at[here], sems.at[len(copies)])
            copy.start()
            copies.append(copy)
    for copy in copies:
        copy.wait()


def hessian_rows(factors, own_sum, rank, row_count, col_count=8):
    mine = factors[-1]
    blocks, tok = mine.shape[0] + 1, mine.shape[2]
    feat = rank * rank
    rows, cols = row_count * rank, col_count * rank
    return pl.pallas_call(
        functools.partial(hessian_kernel, row_count, col_count),
        out_specs=pl.BlockSpec(memory_space=pl.ANY),
        out_shape=jax.ShapeDtypeStruct((rows, feat), jnp.float32),
        scratch_shapes=[
            pltpu.VMEM((2 * rank, tok * blocks), jnp.float32),
            pltpu.VMEM((1, tok * blocks), jnp.float32),
            pltpu.VMEM((rows, tok * blocks), jnp.bfloat16),
            pltpu.VMEM((cols, tok * blocks), jnp.bfloat16),
            pltpu.VMEM((cols, tok * blocks), jnp.bfloat16),
            pltpu.VMEM((rows, feat), jnp.float32),
            pltpu.SemaphoreType.DMA((feat // cols * (rows // TILE),)),
        ],
        compiler_params=params(26),
    )(*factors, own_sum)


def finish_kernel(payload_ref, *refs):
    shares, out_ref = refs[:-1], refs[-1]
    total = shares[0][...]
    for ref in shares[1:]:
        total = total + ref[...].astype(jnp.float32)
    weight = payload_ref[...].astype(jnp.float32)[-1:]
    out_ref[...] = jnp.where(weight > 0.0, total, 0.0).T.astype(out_ref.dtype)


def finish_scores(payload, shares):
    count, tok = shares[0].shape
    return pl.pallas_call(
        finish_kernel,
        out_shape=jax.ShapeDtypeStruct((tok, count), jnp.bfloat16),
        compiler_params=params(40),
    )(payload, *shares)


def swapped(array, axis, distance):
    return lax.ppermute(array, axis, [(i, i ^ distance) for i in range(lax.axis_size(axis))])


def few_tokens(activations, out_grads, proj_in, proj_out, queries, lengths, credit):
    dp_count = lax.axis_size("dp")
    query_count = lax.axis_size("query")
    rank = proj_in.shape[1]
    row_count = rank // dp_count
    seq_len = activations.shape[0] // lengths.shape[0]
    live = jnp.arange(seq_len, dtype=jnp.int32)[None, :] < lengths[:, None]
    weight = jnp.where(live, credit[:, None], 0).astype(jnp.float32).reshape(1, -1)
    near_queries = swapped(queries, "dp", 1)
    keep, send = project(activations, out_grads, proj_in.T, proj_out.T)
    other = swapped(send, "query", 1)
    distance = 2
    while distance < query_count:
        keep = add(keep, other)
        other = swapped(keep, "query", distance)
        distance *= 2
    own = add_to_payload(keep, other, weight)
    own_other = swapped(own, "query", 1)
    others = [swapped(own, "dp", k) for k in reversed(range(1, dp_count))]
    own_sum = own_tokens_sum(own, own_other, rank, row_count)
    queries_t, own_plain = turn_queries(
        queries, near_queries, own, own_other, rank, row_count
    )
    far = others[0]
    far_send = pass_factors(far, rank, (own_sum, queries_t))
    far_other = swapped(far_send, "query", 1)
    mine, send = stack(others[1:], rank, (own_sum, far_other))
    other = swapped(send, "query", 1)
    half = half_gram(own, far, mine, rank)
    factors = (far, far_other, mine, other)
    shares = score_shares(
        (own, own_other) + factors, queries_t, own_plain, half, rank, row_count
    )
    arrived = [swapped(share, "dp", 2 * n) for n, share in enumerate(shares) if n]
    hessian = hessian_rows(factors, own_sum, rank, row_count)
    return hessian, finish_scores(own, [shares[0]] + arrived)


def power_of_two(count):
    return count & (count - 1) == 0


def per_device(activations, *others):
    rank = others[1].shape[1]
    dp_count, query_count = lax.axis_size("dp"), lax.axis_size("query")
    pairs = dp_count > 2 and query_count > 1 and power_of_two(dp_count) and power_of_two(query_count)
    if pairs and activations.shape[0] * dp_count <= rank * rank:
        return few_tokens(activations, *others)
    return many_tokens(activations, *others)


def solution(mesh):
    placed = (
        P(("groups", "dp"), "query"),
        P(("groups", "dp"), "query"),
        P("query", None),
        P("query", None),
        P(("groups", "dp"), "query"),
        P(("groups", "dp")),
        P(("groups", "dp")),
    )
    return jax.shard_map(
        per_device,
        mesh=mesh,
        in_specs=placed,
        out_specs=(P(("groups", "dp"), None), P(("groups", "dp"), "query")),
        check_vma=False,
    )
```

```python
import functools
import jax
import jax.numpy as jnp
from jax import lax
from jax.experimental import pallas as pl
from jax.experimental.pallas import tpu as pltpu
from jax.sharding import PartitionSpec as P


def kron_columns(grad_rows, act_rows, start, count):
    rank = grad_rows.shape[1]
    tokens_here = grad_rows.shape[0]
    grad_cols = lax.dynamic_slice_in_dim(grad_rows, start // rank, count // rank, 1)
    outer = grad_cols.astype(jnp.float32)[:, :, None] * act_rows.astype(jnp.float32)[:, None, :]
    return outer.reshape(tokens_here, count).astype(jnp.bfloat16)


def hessian_block(total, pieces, row_start, rows_own, col_start, col_count):
    grad_rows, act_rows, weights = pieces
    left = kron_columns(grad_rows, act_rows, row_start, rows_own)
    weighted = (weights.astype(jnp.float32)[:, None] * left.astype(jnp.float32)).astype(
        jnp.bfloat16
    )
    right = kron_columns(grad_rows, act_rows, col_start, col_count)
    return total + lax.dot_general(
        weighted, right, (((0,), (0,)), ((), ())), preferred_element_type=jnp.float32
    )


def fold_blocks(total, pieces, step_fn):
    count = pieces[0].shape[0]
    shaped = tuple((p.reshape((count // 512, 512) + p.shape[1:]) for p in pieces))

    def inner(carry, block):
        return (step_fn(carry, block), None)

    return lax.scan(inner, total, shaped)[0]


def split_parts(matrix):
    high_part = matrix.astype(jnp.bfloat16)
    first_rest = matrix - high_part.astype(jnp.float32)
    middle_part = first_rest.astype(jnp.bfloat16)
    low_part = (first_rest - middle_part.astype(jnp.float32)).astype(jnp.bfloat16)
    return (high_part, middle_part, low_part)


def many_tokens(activations, out_grads, proj_in, proj_out, queries, lengths, credit):
    tok_rows = activations.shape[0]
    seq_len = tok_rows // lengths.shape[0]
    dp_count = lax.axis_size("dp")
    query_count = lax.axis_size("query")
    dp_index = lax.axis_index("dp")
    query_index = lax.axis_index("query")
    part_act = jnp.dot(activations, proj_in, preferred_element_type=jnp.float32)
    part_grad = jnp.dot(out_grads, proj_out, preferred_element_type=jnp.float32)
    sum_act, sum_grad = lax.psum((part_act, part_grad), "query")
    act_proj = sum_act.astype(jnp.bfloat16)
    grad_proj = sum_grad.astype(jnp.bfloat16)
    rank = act_proj.shape[1]
    feat = rank * rank
    live = jnp.arange(seq_len, dtype=jnp.int32)[None, :] < lengths[:, None]
    weight = (credit[:, None].astype(jnp.float32) * live.astype(jnp.float32)).reshape(-1)
    mask = live.astype(jnp.float32).reshape(-1)
    weight_wire = weight.astype(jnp.bfloat16)
    rows_own = feat // dp_count
    row_start = dp_index * rows_own
    all_tokens = tok_rows * dp_count
    col_count = feat // query_count
    col_start = query_index * col_count
    owned = fold_blocks(
        jnp.zeros((rows_own, col_count), jnp.float32),
        (
            lax.all_gather(grad_proj, "dp", axis=0, tiled=True),
            lax.all_gather(act_proj, "dp", axis=0, tiled=True),
            lax.all_gather(weight_wire, "dp", axis=0, tiled=True),
        ),
        lambda carry, block: hessian_block(carry, block, row_start, rows_own, col_start, col_count),
    )
    hessian = lax.all_gather(owned, "query", axis=1, tiled=True) / all_tokens
    diagonal_block = lax.dynamic_slice_in_dim(hessian, row_start, rows_own, 1)
    level = lax.psum(jnp.trace(diagonal_block), "dp") / feat
    step = 1.1 * level
    high_part, middle_part, low_part = split_parts(hessian)
    piece = lax.all_gather(queries, "dp", axis=0, tiled=True)
    result = jnp.zeros(queries.shape, jnp.float32)
    for part_matrix in (low_part, middle_part, high_part):
        columns = part_matrix
        result = result + jnp.dot(columns, piece, preferred_element_type=jnp.float32)
    query_f = queries.astype(jnp.float32)
    precond = ((2.0 * query_f - (result + 0.1 * level * query_f) / step) / step).astype(
        jnp.bfloat16
    )
    local_features = kron_columns(grad_proj, act_proj, 0, feat)
    piece = lax.all_gather(precond, "dp", axis=0, tiled=True)
    columns = lax.slice_in_dim(local_features, 0, piece.shape[0], axis=1)
    scores = jnp.zeros((tok_rows, precond.shape[1]), jnp.float32) + jnp.dot(
        columns, piece, preferred_element_type=jnp.float32
    )
    return (hessian, (scores * mask[:, None]).astype(jnp.bfloat16))


MIB = 1024 * 1024
TILE = 256
NT = (((1,), (1,)), ((), ()))


def params(mib):
    return pltpu.CompilerParams(vmem_limit_bytes=int(mib * MIB))


def project_kernel(act, grad, pin, pout, keep_ref, send_ref, act_v, grad_v, pin_v, pout_v, sems):
    unit = grad.shape[1] // 7
    spans = [pl.ds(0, unit), pl.ds(unit, 2 * unit), pl.ds(3 * unit, 4 * unit)]
    if grad.shape[1] % 7 or unit % 128:
        spans = [pl.ds(0, grad.shape[1])]
    pairs = [(pin, pin_v), (act, act_v), (pout, pout_v)]
    pairs += [(grad.at[:, span], grad_v.at[:, span]) for span in spans]
    copies = [pltpu.make_async_copy(s, d, sems.at[n]) for n, (s, d) in enumerate(pairs)]
    for copy in copies:
        copy.start()
    copies[0].wait()
    copies[1].wait()
    part_act = lax.dot_general(pin_v[...], act_v[...], NT, preferred_element_type=jnp.float32)
    copies[2].wait()
    part_grad = jnp.zeros_like(part_act)
    for copy, span in zip(copies[3:], spans):
        copy.wait()
        part_grad += lax.dot_general(
            pout_v[:, span], grad_v[:, span], NT, preferred_element_type=jnp.float32
        )
    even = lax.rem(lax.axis_index("query"), 2) == 0
    keep_ref[...] = jnp.where(even, part_act, part_grad)
    send_ref[...] = jnp.where(even, part_grad, part_act)


def project(activations, out_grads, proj_in_t, proj_out_t):
    tok, d_here = activations.shape
    f_here = out_grads.shape[1]
    rank = proj_in_t.shape[0]
    out = jax.ShapeDtypeStruct((rank, tok), jnp.float32)
    return pl.pallas_call(
        project_kernel,
        in_specs=[pl.BlockSpec(memory_space=pl.ANY)] * 4,
        out_shape=[out, out],
        scratch_shapes=[
            pltpu.VMEM((tok, d_here), jnp.bfloat16),
            pltpu.VMEM((tok, f_here), jnp.bfloat16),
            pltpu.VMEM((rank, d_here), jnp.bfloat16),
            pltpu.VMEM((rank, f_here), jnp.bfloat16),
            pltpu.SemaphoreType.DMA((6,)),
        ],
        compiler_params=params(53.75),
    )(activations, out_grads, proj_in_t, proj_out_t)


def add_kernel(one_ref, other_ref, out_ref):
    out_ref[...] = one_ref[...] + other_ref[...]


def add(one, other):
    return pl.pallas_call(
        add_kernel,
        out_shape=jax.ShapeDtypeStruct(one.shape, one.dtype),
        compiler_params=params(40),
    )(one, other)


def payload_kernel(one_ref, other_ref, weight_ref, out_ref):
    total = jnp.where(weight_ref[...] > 0.0, one_ref[...] + other_ref[...], 0.0)
    weight = jnp.broadcast_to(weight_ref[...], (16, weight_ref.shape[1]))
    out_ref[...] = jnp.concatenate([total, weight], axis=0).astype(out_ref.dtype)


def add_to_payload(one, other, weight):
    rows, tok = one.shape
    return pl.pallas_call(
        payload_kernel,
        out_shape=jax.ShapeDtypeStruct((rows + 16, tok), jnp.bfloat16),
        compiler_params=params(40),
    )(one, other, weight)


def stack_kernel(_, __, *refs):
    parts, (out_ref, factors_ref) = refs[:-2], refs[-2:]
    for k, ref in enumerate(parts):
        out_ref[k] = ref[...]
        factors_ref[k] = ref[: factors_ref.shape[1]]


def stack(parts, rank, after):
    rows, tok = parts[0].shape
    whole = pl.BlockSpec(memory_space=pltpu.VMEM)
    return pl.pallas_call(
        stack_kernel,
        in_specs=[pl.BlockSpec(memory_space=pl.ANY)] * 2 + [whole] * len(parts),
        out_shape=[
            jax.ShapeDtypeStruct((len(parts), rows, tok), parts[0].dtype),
            jax.ShapeDtypeStruct((len(parts), rank, tok), parts[0].dtype),
        ],
        compiler_params=params(26),
    )(*after, *parts)


def lay_out_factors(blocks, factors, weights):
    rank = factors.shape[0] // 2
    here = pl.multiple_of(lax.rem(lax.axis_index("query"), 2) * rank, rank)
    there = pl.multiple_of(rank - here, rank)
    for k, (mine, other) in enumerate(blocks):
        span = slice(k * mine.shape[1], (k + 1) * mine.shape[1])
        factors[pl.ds(here, rank), span] = mine[:rank].astype(jnp.float32)
        factors[pl.ds(there, rank), span] = other[:rank].astype(jnp.float32)
        weights[:, span] = mine[rank:].astype(jnp.float32)[:1]


def block_pairs(mine, other):
    return [(mine.at[k], other.at[k]) for k in reversed(range(mine.shape[0]))]


def weigh_rows(first_row, end_row, row_count, factors, weights, weighted):
    rank = factors.shape[0] // 2
    act, weight = factors[:rank, :], weights[...]
    first = rank + lax.axis_index("dp") * row_count
    for i in range(first_row // rank, end_row // rank):
        left = (factors[pl.ds(first + i, 1), :] * act).astype(jnp.bfloat16)
        left = (weight * left.astype(jnp.float32)).astype(jnp.bfloat16)
        weighted[i * rank : (i + 1) * rank, :] = left


def range_scale(values):
    top = jnp.max(jnp.abs(values), keepdims=True)
    scale = jnp.ones_like(top)
    for low in (16, 48, 80, 112):
        scale = jnp.where(top > 2.0**low, 2.0 ** -min(low + 16, 126), scale)
        scale = jnp.where(top < 2.0**-low, 2.0 ** min(low + 16, 126), scale)
    return scale


def project_queries(row_count, factors, features, query_ref):
    rank = factors.shape[0] // 2
    act = factors[:rank, :]
    for near in range(2):
        first = rank + (lax.axis_index("dp") ^ near) * row_count
        for i in range(row_count):
            row = factors[pl.ds(first + i, 1), :]
            start = (near * row_count + i) * rank
            features[start : start + rank, :] = (row * act).astype(jnp.bfloat16)
    return jnp.dot(query_ref[...], features[...], preferred_element_type=jnp.float32)


def turn_kernel(row_count, query, near_query, own, own_other, *refs):
    out_ref, plain_ref, factors, weights, features = refs
    rows = query.shape[0]
    out_ref[:, :rows] = query[...].T
    out_ref[:, rows:] = near_query[...].T
    lay_out_factors([(own, own_other)], factors, weights)
    plain_ref[...] = project_queries(row_count, factors, features, out_ref)


def turn_queries(queries, near_queries, own, own_other, rank, row_count):
    rows, count = queries.shape
    tok = own.shape[1]
    out = jax.ShapeDtypeStruct((count, 2 * rows), queries.dtype)
    return pl.pallas_call(
        functools.partial(turn_kernel, row_count),
        out_shape=[out, jax.ShapeDtypeStruct((count, tok), jnp.float32)],
        scratch_shapes=[
            pltpu.VMEM((2 * rank, tok), jnp.float32),
            pltpu.VMEM((1, tok), jnp.float32),
            pltpu.VMEM((2 * rows, tok), jnp.bfloat16),
        ],
        compiler_params=params(26),
    )(queries, near_queries, own, own_other)


def scaled(values):
    scale = range_scale(values)
    return values * scale, scale


def half_kernel(own, mine, gram_ref, norm_ref, scale_ref, values):
    rank, tok = values.shape[0], own.shape[1]
    for k, part in enumerate([own] + [mine.at[k] for k in reversed(range(mine.shape[0]))]):
        values[:, k * tok : (k + 1) * tok] = part[:rank].astype(jnp.float32)
    factor, scale = scaled(values[...])
    scale_ref[...] = jnp.broadcast_to(scale, scale_ref.shape)
    norm = jnp.sum(factor * factor, axis=0, keepdims=True)
    norm_ref[...] = jnp.broadcast_to(norm, norm_ref.shape)
    factor_b, factor_rows = factor.astype(jnp.bfloat16), factor.T.astype(jnp.bfloat16)
    for n in range(gram_ref.shape[0]):
        block = slice(2 * n * tok, (2 * n + 1) * tok)
        for row in range(0, values.shape[1], TILE // 2):
            here = slice(row, row + TILE // 2)
            gram_ref[n, here, :] = jnp.dot(
                factor_rows[here], factor_b[:, block], preferred_element_type=jnp.float32
            )


def half_gram(own, mine, rank):
    blocks, tok = mine.shape[0] + 1, own.shape[1]
    tokens = blocks * tok
    return pl.pallas_call(
        half_kernel,
        out_shape=[
            jax.ShapeDtypeStruct((blocks // 2, tokens, tok), jnp.float32),
            jax.ShapeDtypeStruct((8, tokens), jnp.float32),
            jax.ShapeDtypeStruct((8, 128), jnp.float32),
        ],
        scratch_shapes=[pltpu.VMEM((rank, tokens), jnp.float32)],
        compiler_params=params(26),
    )(own, mine)


def share_kernel(row_count, own, own_other, mine, other, query_ref, own_plain_ref, *refs):
    half_gram_ref, half_norm_ref, half_scale_ref = refs[:3]
    refs = refs[3:]
    factors, weights, features, gram = refs[-4:]
    out_refs = refs[:-4]
    lay_out_factors([(own, own_other)] + block_pairs(mine, other), factors, weights)
    rank = factors.shape[0] // 2
    tokens = factors.shape[1]
    tok = own.shape[1]
    plain = project_queries(row_count, factors.at[:, tok:], features, query_ref)
    plain = jnp.concatenate([own_plain_ref[...], plain], axis=1)
    there = pl.multiple_of(rank - lax.rem(lax.axis_index("query"), 2) * rank, rank)
    factor, scale = scaled(factors[pl.ds(there, rank), :])
    weight = weights[...]
    norms = half_norm_ref[:1, :] * jnp.sum(factor * factor, axis=0, keepdims=True)
    level = jnp.sum(weight * norms, axis=1, keepdims=True) / (tokens * rank * rank)
    step = 1.1 * level
    factor_b, factor_rows = factor.astype(jnp.bfloat16), factor.T.astype(jnp.bfloat16)
    weighted = (plain * (weight * (1.0 / (tokens * step)))).astype(jnp.bfloat16)
    scale = scale * half_scale_ref[:1, :1]
    for n, out_ref in enumerate(out_refs):
        block = slice(2 * n * tok, (2 * n + 1) * tok)
        for row in range(0, tokens, TILE // 2):
            here = slice(row, row + TILE // 2)
            tile = jnp.dot(factor_rows[here], factor_b[:, block], preferred_element_type=jnp.float32)
            gram[n, here, :] = (tile * half_gram_ref[n, here, :]).astype(jnp.bfloat16)
        image = jnp.dot(weighted, gram[n], preferred_element_type=jnp.float32)
        share = ((2.0 - 0.1 / 1.1) * plain[:, block] - image) * scale * (scale / step)
        out_ref[...] = share.astype(out_ref.dtype)


def score_shares(own, own_other, mine, other, queries_t, own_plain, half, rank, row_count):
    blocks, tok = mine.shape[0] + 1, mine.shape[2]
    count, depth = queries_t.shape
    return pl.pallas_call(
        functools.partial(share_kernel, row_count),
        out_shape=[
            jax.ShapeDtypeStruct((count, tok), jnp.bfloat16 if k else jnp.float32)
            for k in range(0, blocks, 2)
        ],
        scratch_shapes=[
            pltpu.VMEM((2 * rank, tok * blocks), jnp.float32),
            pltpu.VMEM((1, tok * blocks), jnp.float32),
            pltpu.VMEM((depth, tok * (blocks - 1)), jnp.bfloat16),
            pltpu.VMEM((blocks // 2, tok * blocks, tok), jnp.bfloat16),
        ],
        compiler_params=params(26),
    )(own, own_other, mine, other, queries_t, own_plain, *half)


def build_columns(first, act, factors, right):
    rank = act.shape[0]
    for i in range(right.shape[0] // rank):
        row = rank + first + i
        right[i * rank : (i + 1) * rank, :] = (factors[row : row + 1, :] * act).astype(jnp.bfloat16)


def own_kernel(row_count, col_count, own, own_other, out, factors, weights, weighted, *rights):
    rank = factors.shape[0] // 2
    cols = col_count * rank
    lay_out_factors([(own, own_other)], factors, weights)
    weigh_rows(0, weighted.shape[0], row_count, factors, weights, weighted)
    act = factors[:rank, :]
    build_columns(0, act, factors, rights[0])
    for step in range(rank // col_count):
        if (step + 1) * col_count < rank:
            build_columns((step + 1) * col_count, act, factors, rights[(step + 1) % 2])
        out[:, step * cols : (step + 1) * cols] = lax.dot_general(
            weighted[...], rights[step % 2][...], NT, preferred_element_type=jnp.float32
        )


def own_tokens_sum(own, own_other, rank, row_count, col_count=8):
    tok = own.shape[1]
    rows, cols = row_count * rank, col_count * rank
    return pl.pallas_call(
        functools.partial(own_kernel, row_count, col_count),
        out_shape=jax.ShapeDtypeStruct((rows, rank * rank), jnp.float32),
        scratch_shapes=[
            pltpu.VMEM((2 * rank, tok), jnp.float32),
            pltpu.VMEM((1, tok), jnp.float32),
            pltpu.VMEM((rows, tok), jnp.bfloat16),
            pltpu.VMEM((cols, tok), jnp.bfloat16),
            pltpu.VMEM((cols, tok), jnp.bfloat16),
        ],
        compiler_params=params(16),
    )(own, own_other)


def hessian_kernel(row_count, col_count, mine, other, own_sum, out, *scratch):
    factors, weights, weighted, rights = *scratch[:3], scratch[3:5]
    result, sems = scratch[5:]
    rank = factors.shape[0] // 2
    blocks = mine.shape[0]
    tokens = factors.shape[1] // blocks * (blocks + 1)
    rows, cols = row_count * rank, col_count * rank
    lay_out_factors(block_pairs(mine, other), factors, weights)
    act = factors[:rank, :]
    copies = []
    build_columns(0, act, factors, rights[0])
    for step in range(rank // col_count):
        if (step + 1) * col_count < rank:
            build_columns((step + 1) * col_count, act, factors, rights[(step + 1) % 2])
        for row in range(0, rows, TILE):
            if step == 0:
                weigh_rows(row, row + TILE, row_count, factors, weights, weighted)
            here = pl.ds(row, TILE), pl.ds(step * cols, cols)
            tile = lax.dot_general(
                weighted[row : row + TILE, :],
                rights[step % 2][...],
                NT,
                preferred_element_type=jnp.float32,
            )
            result[here] = (own_sum[here] + tile) * (1.0 / tokens)
            copy = pltpu.make_async_copy(result.at[here], out.at[here], sems.at[len(copies)])
            copy.start()
            copies.append(copy)
    for copy in copies:
        copy.wait()


def hessian_rows(mine, other, own_sum, rank, row_count, col_count=8):
    blocks, _, tok = mine.shape
    feat = rank * rank
    rows, cols = row_count * rank, col_count * rank
    return pl.pallas_call(
        functools.partial(hessian_kernel, row_count, col_count),
        out_specs=pl.BlockSpec(memory_space=pl.ANY),
        out_shape=jax.ShapeDtypeStruct((rows, feat), jnp.float32),
        scratch_shapes=[
            pltpu.VMEM((2 * rank, tok * blocks), jnp.float32),
            pltpu.VMEM((1, tok * blocks), jnp.float32),
            pltpu.VMEM((rows, tok * blocks), jnp.bfloat16),
            pltpu.VMEM((cols, tok * blocks), jnp.bfloat16),
            pltpu.VMEM((cols, tok * blocks), jnp.bfloat16),
            pltpu.VMEM((rows, feat), jnp.float32),
            pltpu.SemaphoreType.DMA((feat // cols * (rows // TILE),)),
        ],
        compiler_params=params(26),
    )(mine, other, own_sum)


def finish_kernel(payload_ref, *refs):
    shares, out_ref = refs[:-1], refs[-1]
    total = shares[0][...]
    for ref in shares[1:]:
        total = total + ref[...].astype(jnp.float32)
    weight = payload_ref[...].astype(jnp.float32)[-1:]
    out_ref[...] = jnp.where(weight > 0.0, total, 0.0).T.astype(out_ref.dtype)


def finish_scores(payload, shares):
    count, tok = shares[0].shape
    return pl.pallas_call(
        finish_kernel,
        out_shape=jax.ShapeDtypeStruct((tok, count), jnp.bfloat16),
        compiler_params=params(40),
    )(payload, *shares)


def swapped(array, axis, distance):
    return lax.ppermute(array, axis, [(i, i ^ distance) for i in range(lax.axis_size(axis))])


def few_tokens(activations, out_grads, proj_in, proj_out, queries, lengths, credit):
    dp_count = lax.axis_size("dp")
    query_count = lax.axis_size("query")
    rank = proj_in.shape[1]
    row_count = rank // dp_count
    seq_len = activations.shape[0] // lengths.shape[0]
    live = jnp.arange(seq_len, dtype=jnp.int32)[None, :] < lengths[:, None]
    weight = jnp.where(live, credit[:, None], 0).astype(jnp.float32).reshape(1, -1)
    near_queries = swapped(queries, "dp", 1)
    keep, send = project(activations, out_grads, proj_in.T, proj_out.T)
    other = swapped(send, "query", 1)
    distance = 2
    while distance < query_count:
        keep = add(keep, other)
        other = swapped(keep, "query", distance)
        distance *= 2
    own = add_to_payload(keep, other, weight)
    own_other = swapped(own, "query", 1)
    others = [swapped(own, "dp", k) for k in reversed(range(1, dp_count))]
    own_sum = own_tokens_sum(own, own_other, rank, row_count)
    queries_t, own_plain = turn_queries(
        queries, near_queries, own, own_other, rank, row_count
    )
    mine, factors = stack(others, rank, (own_sum, queries_t))
    other = swapped(factors, "query", 1)
    half = half_gram(own, mine, rank)
    shares = score_shares(
        own, own_other, mine, other, queries_t, own_plain, half, rank, row_count
    )
    arrived = [swapped(share, "dp", 2 * n) for n, share in enumerate(shares) if n]
    hessian = hessian_rows(mine, other, own_sum, rank, row_count)
    return hessian, finish_scores(own, [shares[0]] + arrived)


def power_of_two(count):
    return count & (count - 1) == 0


def per_device(activations, *others):
    rank = others[1].shape[1]
    dp_count, query_count = lax.axis_size("dp"), lax.axis_size("query")
    pairs = min(dp_count, query_count) > 1 and power_of_two(dp_count) and power_of_two(query_count)
    if pairs and activations.shape[0] * dp_count <= rank * rank:
        return few_tokens(activations, *others)
    return many_tokens(activations, *others)


def solution(mesh):
    placed = (
        P(("groups", "dp"), "query"),
        P(("groups", "dp"), "query"),
        P("query", None),
        P("query", None),
        P(("groups", "dp"), "query"),
        P(("groups", "dp")),
        P(("groups", "dp")),
    )
    return jax.shard_map(
        per_device,
        mesh=mesh,
        in_specs=placed,
        out_specs=(P(("groups", "dp"), None), P(("groups", "dp"), "query")),
        check_vma=False,
    )
```

```python
import functools
import jax
import jax.numpy as jnp
from jax import lax
from jax.experimental import pallas as pl
from jax.experimental.pallas import tpu as pltpu
from jax.sharding import PartitionSpec as P


def kron_columns(grad_rows, act_rows, start, count):
    rank = grad_rows.shape[1]
    tokens_here = grad_rows.shape[0]
    grad_cols = lax.dynamic_slice_in_dim(grad_rows, start // rank, count // rank, 1)
    outer = grad_cols.astype(jnp.float32)[:, :, None] * act_rows.astype(jnp.float32)[:, None, :]
    return outer.reshape(tokens_here, count).astype(jnp.bfloat16)


def hessian_block(total, pieces, row_start, rows_own, col_start, col_count):
    grad_rows, act_rows, weights = pieces
    left = kron_columns(grad_rows, act_rows, row_start, rows_own)
    weighted = (weights.astype(jnp.float32)[:, None] * left.astype(jnp.float32)).astype(
        jnp.bfloat16
    )
    right = kron_columns(grad_rows, act_rows, col_start, col_count)
    return total + lax.dot_general(
        weighted, right, (((0,), (0,)), ((), ())), preferred_element_type=jnp.float32
    )


def fold_blocks(total, pieces, step_fn):
    count = pieces[0].shape[0]
    shaped = tuple((p.reshape((count // 512, 512) + p.shape[1:]) for p in pieces))

    def inner(carry, block):
        return (step_fn(carry, block), None)

    return lax.scan(inner, total, shaped)[0]


def split_parts(matrix):
    high_part = matrix.astype(jnp.bfloat16)
    first_rest = matrix - high_part.astype(jnp.float32)
    middle_part = first_rest.astype(jnp.bfloat16)
    low_part = (first_rest - middle_part.astype(jnp.float32)).astype(jnp.bfloat16)
    return (high_part, middle_part, low_part)


def many_tokens(activations, out_grads, proj_in, proj_out, queries, lengths, credit):
    tok_rows = activations.shape[0]
    seq_len = tok_rows // lengths.shape[0]
    dp_count = lax.axis_size("dp")
    query_count = lax.axis_size("query")
    dp_index = lax.axis_index("dp")
    query_index = lax.axis_index("query")
    part_act = jnp.dot(activations, proj_in, preferred_element_type=jnp.float32)
    part_grad = jnp.dot(out_grads, proj_out, preferred_element_type=jnp.float32)
    sum_act, sum_grad = lax.psum((part_act, part_grad), "query")
    act_proj = sum_act.astype(jnp.bfloat16)
    grad_proj = sum_grad.astype(jnp.bfloat16)
    rank = act_proj.shape[1]
    feat = rank * rank
    live = jnp.arange(seq_len, dtype=jnp.int32)[None, :] < lengths[:, None]
    weight = (credit[:, None].astype(jnp.float32) * live.astype(jnp.float32)).reshape(-1)
    mask = live.astype(jnp.float32).reshape(-1)
    weight_wire = weight.astype(jnp.bfloat16)
    rows_own = feat // dp_count
    row_start = dp_index * rows_own
    all_tokens = tok_rows * dp_count
    col_count = feat // query_count
    col_start = query_index * col_count
    owned = fold_blocks(
        jnp.zeros((rows_own, col_count), jnp.float32),
        (
            lax.all_gather(grad_proj, "dp", axis=0, tiled=True),
            lax.all_gather(act_proj, "dp", axis=0, tiled=True),
            lax.all_gather(weight_wire, "dp", axis=0, tiled=True),
        ),
        lambda carry, block: hessian_block(carry, block, row_start, rows_own, col_start, col_count),
    )
    hessian = lax.all_gather(owned, "query", axis=1, tiled=True) / all_tokens
    diagonal_block = lax.dynamic_slice_in_dim(hessian, row_start, rows_own, 1)
    level = lax.psum(jnp.trace(diagonal_block), "dp") / feat
    step = 1.1 * level
    high_part, middle_part, low_part = split_parts(hessian)
    piece = lax.all_gather(queries, "dp", axis=0, tiled=True)
    result = jnp.zeros(queries.shape, jnp.float32)
    for part_matrix in (low_part, middle_part, high_part):
        columns = part_matrix
        result = result + jnp.dot(columns, piece, preferred_element_type=jnp.float32)
    query_f = queries.astype(jnp.float32)
    precond = ((2.0 * query_f - (result + 0.1 * level * query_f) / step) / step).astype(
        jnp.bfloat16
    )
    local_features = kron_columns(grad_proj, act_proj, 0, feat)
    piece = lax.all_gather(precond, "dp", axis=0, tiled=True)
    columns = lax.slice_in_dim(local_features, 0, piece.shape[0], axis=1)
    scores = jnp.zeros((tok_rows, precond.shape[1]), jnp.float32) + jnp.dot(
        columns, piece, preferred_element_type=jnp.float32
    )
    return (hessian, (scores * mask[:, None]).astype(jnp.bfloat16))


MIB = 1024 * 1024
TILE = 256
NT = (((1,), (1,)), ((), ()))


def params(mib):
    return pltpu.CompilerParams(vmem_limit_bytes=int(mib * MIB))


def project_kernel(act, grad, pin, pout, keep_ref, send_ref, act_v, grad_v, pin_v, pout_v, sems):
    chunk = grad.shape[1] // 2
    spans = [pl.ds(0, chunk), pl.ds(chunk, chunk)]
    pairs = [(pin, pin_v), (act, act_v), (pout, pout_v)]
    pairs += [(grad.at[:, span], grad_v.at[:, span]) for span in spans]
    copies = [pltpu.make_async_copy(s, d, sems.at[n]) for n, (s, d) in enumerate(pairs)]
    for copy in copies:
        copy.start()
    copies[0].wait()
    copies[1].wait()
    part_act = lax.dot_general(pin_v[...], act_v[...], NT, preferred_element_type=jnp.float32)
    copies[2].wait()
    part_grad = jnp.zeros_like(part_act)
    for copy, span in zip(copies[3:], spans):
        copy.wait()
        part_grad += lax.dot_general(
            pout_v[:, span], grad_v[:, span], NT, preferred_element_type=jnp.float32
        )
    even = lax.rem(lax.axis_index("query"), 2) == 0
    keep_ref[...] = jnp.where(even, part_act, part_grad)
    send_ref[...] = jnp.where(even, part_grad, part_act)


def project(activations, out_grads, proj_in_t, proj_out_t):
    tok, d_here = activations.shape
    f_here = out_grads.shape[1]
    rank = proj_in_t.shape[0]
    out = jax.ShapeDtypeStruct((rank, tok), jnp.float32)
    return pl.pallas_call(
        project_kernel,
        in_specs=[pl.BlockSpec(memory_space=pl.ANY)] * 4,
        out_shape=[out, out],
        scratch_shapes=[
            pltpu.VMEM((tok, d_here), jnp.bfloat16),
            pltpu.VMEM((tok, f_here), jnp.bfloat16),
            pltpu.VMEM((rank, d_here), jnp.bfloat16),
            pltpu.VMEM((rank, f_here), jnp.bfloat16),
            pltpu.SemaphoreType.DMA((5,)),
        ],
        compiler_params=params(53.75),
    )(activations, out_grads, proj_in_t, proj_out_t)


def add_kernel(one_ref, other_ref, out_ref):
    out_ref[...] = one_ref[...] + other_ref[...]


def add(one, other):
    return pl.pallas_call(
        add_kernel,
        out_shape=jax.ShapeDtypeStruct(one.shape, one.dtype),
        compiler_params=params(40),
    )(one, other)


def payload_kernel(one_ref, other_ref, weight_ref, out_ref):
    total = jnp.where(weight_ref[...] > 0.0, one_ref[...] + other_ref[...], 0.0)
    weight = jnp.broadcast_to(weight_ref[...], (16, weight_ref.shape[1]))
    out_ref[...] = jnp.concatenate([total, weight], axis=0).astype(out_ref.dtype)


def add_to_payload(one, other, weight):
    rows, tok = one.shape
    return pl.pallas_call(
        payload_kernel,
        out_shape=jax.ShapeDtypeStruct((rows + 16, tok), jnp.bfloat16),
        compiler_params=params(40),
    )(one, other, weight)


def stack_kernel(_, __, *refs):
    parts, (out_ref, factors_ref) = refs[:-2], refs[-2:]
    for k, ref in enumerate(parts):
        out_ref[k] = ref[...]
        factors_ref[k] = ref[: factors_ref.shape[1]]


def stack(parts, rank, after):
    rows, tok = parts[0].shape
    whole = pl.BlockSpec(memory_space=pltpu.VMEM)
    return pl.pallas_call(
        stack_kernel,
        in_specs=[pl.BlockSpec(memory_space=pl.ANY)] * 2 + [whole] * len(parts),
        out_shape=[
            jax.ShapeDtypeStruct((len(parts), rows, tok), parts[0].dtype),
            jax.ShapeDtypeStruct((len(parts), rank, tok), parts[0].dtype),
        ],
        compiler_params=params(26),
    )(*after, *parts)


def lay_out_factors(blocks, factors, weights):
    rank = factors.shape[0] // 2
    here = pl.multiple_of(lax.rem(lax.axis_index("query"), 2) * rank, rank)
    there = pl.multiple_of(rank - here, rank)
    for k, (mine, other) in enumerate(blocks):
        span = slice(k * mine.shape[1], (k + 1) * mine.shape[1])
        factors[pl.ds(here, rank), span] = mine[:rank].astype(jnp.float32)
        factors[pl.ds(there, rank), span] = other[:rank].astype(jnp.float32)
        weights[:, span] = mine[rank:].astype(jnp.float32)[:1]


def block_pairs(mine, other):
    return [(mine.at[k], other.at[k]) for k in reversed(range(mine.shape[0]))]


def weigh_rows(first_row, end_row, row_count, factors, weights, weighted):
    rank = factors.shape[0] // 2
    act, weight = factors[:rank, :], weights[...]
    first = rank + lax.axis_index("dp") * row_count
    for i in range(first_row // rank, end_row // rank):
        left = (factors[pl.ds(first + i, 1), :] * act).astype(jnp.bfloat16)
        left = (weight * left.astype(jnp.float32)).astype(jnp.bfloat16)
        weighted[i * rank : (i + 1) * rank, :] = left


def range_scale(values):
    top = jnp.max(jnp.abs(values), keepdims=True)
    scale = jnp.ones_like(top)
    for low in (16, 48, 80, 112):
        scale = jnp.where(top > 2.0**low, 2.0 ** -min(low + 16, 126), scale)
        scale = jnp.where(top < 2.0**-low, 2.0 ** min(low + 16, 126), scale)
    return scale


def project_queries(row_count, factors, features, query_ref):
    rank = factors.shape[0] // 2
    act = factors[:rank, :]
    for near in range(2):
        first = rank + (lax.axis_index("dp") ^ near) * row_count
        for i in range(row_count):
            row = factors[pl.ds(first + i, 1), :]
            start = (near * row_count + i) * rank
            features[start : start + rank, :] = (row * act).astype(jnp.bfloat16)
    return jnp.dot(query_ref[...], features[...], preferred_element_type=jnp.float32)


def turn_kernel(row_count, query, near_query, own, own_other, *refs):
    out_ref, plain_ref, factors, weights, features = refs
    rows = query.shape[0]
    out_ref[:, :rows] = query[...].T
    out_ref[:, rows:] = near_query[...].T
    lay_out_factors([(own, own_other)], factors, weights)
    plain_ref[...] = project_queries(row_count, factors, features, out_ref)


def turn_queries(queries, near_queries, own, own_other, rank, row_count):
    rows, count = queries.shape
    tok = own.shape[1]
    out = jax.ShapeDtypeStruct((count, 2 * rows), queries.dtype)
    return pl.pallas_call(
        functools.partial(turn_kernel, row_count),
        out_shape=[out, jax.ShapeDtypeStruct((count, tok), jnp.float32)],
        scratch_shapes=[
            pltpu.VMEM((2 * rank, tok), jnp.float32),
            pltpu.VMEM((1, tok), jnp.float32),
            pltpu.VMEM((2 * rows, tok), jnp.bfloat16),
        ],
        compiler_params=params(26),
    )(queries, near_queries, own, own_other)


def scaled(values):
    scale = range_scale(values)
    return values * scale, scale


def half_kernel(own, mine, gram_ref, norm_ref, scale_ref, values):
    rank, tok = values.shape[0], own.shape[1]
    for k, part in enumerate([own] + [mine.at[k] for k in reversed(range(mine.shape[0]))]):
        values[:, k * tok : (k + 1) * tok] = part[:rank].astype(jnp.float32)
    factor, scale = scaled(values[...])
    scale_ref[...] = jnp.broadcast_to(scale, scale_ref.shape)
    norm = jnp.sum(factor * factor, axis=0, keepdims=True)
    norm_ref[...] = jnp.broadcast_to(norm, norm_ref.shape)
    factor_b, factor_rows = factor.astype(jnp.bfloat16), factor.T.astype(jnp.bfloat16)
    for n in range(gram_ref.shape[0]):
        block = slice(2 * n * tok, (2 * n + 1) * tok)
        for row in range(0, values.shape[1], TILE // 2):
            here = slice(row, row + TILE // 2)
            gram_ref[n, here, :] = jnp.dot(
                factor_rows[here], factor_b[:, block], preferred_element_type=jnp.float32
            )


def half_gram(own, mine, rank):
    blocks, tok = mine.shape[0] + 1, own.shape[1]
    tokens = blocks * tok
    return pl.pallas_call(
        half_kernel,
        out_shape=[
            jax.ShapeDtypeStruct((blocks // 2, tokens, tok), jnp.float32),
            jax.ShapeDtypeStruct((8, tokens), jnp.float32),
            jax.ShapeDtypeStruct((8, 128), jnp.float32),
        ],
        scratch_shapes=[pltpu.VMEM((rank, tokens), jnp.float32)],
        compiler_params=params(26),
    )(own, mine)


def share_kernel(row_count, own, own_other, mine, other, query_ref, own_plain_ref, *refs):
    half_gram_ref, half_norm_ref, half_scale_ref = refs[:3]
    refs = refs[3:]
    factors, weights, features, gram = refs[-4:]
    out_refs = refs[:-4]
    lay_out_factors([(own, own_other)] + block_pairs(mine, other), factors, weights)
    rank = factors.shape[0] // 2
    tokens = factors.shape[1]
    tok = own.shape[1]
    plain = project_queries(row_count, factors.at[:, tok:], features, query_ref)
    plain = jnp.concatenate([own_plain_ref[...], plain], axis=1)
    there = pl.multiple_of(rank - lax.rem(lax.axis_index("query"), 2) * rank, rank)
    factor, scale = scaled(factors[pl.ds(there, rank), :])
    weight = weights[...]
    norms = half_norm_ref[:1, :] * jnp.sum(factor * factor, axis=0, keepdims=True)
    level = jnp.sum(weight * norms, axis=1, keepdims=True) / (tokens * rank * rank)
    step = 1.1 * level
    factor_b, factor_rows = factor.astype(jnp.bfloat16), factor.T.astype(jnp.bfloat16)
    weighted = (plain * (weight * (1.0 / (tokens * step)))).astype(jnp.bfloat16)
    scale = scale * half_scale_ref[:1, :1]
    for n, out_ref in enumerate(out_refs):
        block = slice(2 * n * tok, (2 * n + 1) * tok)
        for row in range(0, tokens, TILE // 2):
            here = slice(row, row + TILE // 2)
            tile = jnp.dot(factor_rows[here], factor_b[:, block], preferred_element_type=jnp.float32)
            gram[n, here, :] = (tile * half_gram_ref[n, here, :]).astype(jnp.bfloat16)
        image = jnp.dot(weighted, gram[n], preferred_element_type=jnp.float32)
        share = ((2.0 - 0.1 / 1.1) * plain[:, block] - image) * scale * (scale / step)
        out_ref[...] = share.astype(out_ref.dtype)


def score_shares(own, own_other, mine, other, queries_t, own_plain, half, rank, row_count):
    blocks, tok = mine.shape[0] + 1, mine.shape[2]
    count, depth = queries_t.shape
    return pl.pallas_call(
        functools.partial(share_kernel, row_count),
        out_shape=[
            jax.ShapeDtypeStruct((count, tok), jnp.bfloat16 if k else jnp.float32)
            for k in range(0, blocks, 2)
        ],
        scratch_shapes=[
            pltpu.VMEM((2 * rank, tok * blocks), jnp.float32),
            pltpu.VMEM((1, tok * blocks), jnp.float32),
            pltpu.VMEM((depth, tok * (blocks - 1)), jnp.bfloat16),
            pltpu.VMEM((blocks // 2, tok * blocks, tok), jnp.bfloat16),
        ],
        compiler_params=params(26),
    )(own, own_other, mine, other, queries_t, own_plain, *half)


def build_columns(first, act, factors, right):
    rank = act.shape[0]
    for i in range(right.shape[0] // rank):
        row = rank + first + i
        right[i * rank : (i + 1) * rank, :] = (factors[row : row + 1, :] * act).astype(jnp.bfloat16)


def own_kernel(row_count, col_count, own, own_other, out, factors, weights, weighted, *rights):
    rank = factors.shape[0] // 2
    cols = col_count * rank
    lay_out_factors([(own, own_other)], factors, weights)
    weigh_rows(0, weighted.shape[0], row_count, factors, weights, weighted)
    act = factors[:rank, :]
    build_columns(0, act, factors, rights[0])
    for step in range(rank // col_count):
        if (step + 1) * col_count < rank:
            build_columns((step + 1) * col_count, act, factors, rights[(step + 1) % 2])
        out[:, step * cols : (step + 1) * cols] = lax.dot_general(
            weighted[...], rights[step % 2][...], NT, preferred_element_type=jnp.float32
        )


def own_tokens_sum(own, own_other, rank, row_count, col_count=8):
    tok = own.shape[1]
    rows, cols = row_count * rank, col_count * rank
    return pl.pallas_call(
        functools.partial(own_kernel, row_count, col_count),
        out_shape=jax.ShapeDtypeStruct((rows, rank * rank), jnp.float32),
        scratch_shapes=[
            pltpu.VMEM((2 * rank, tok), jnp.float32),
            pltpu.VMEM((1, tok), jnp.float32),
            pltpu.VMEM((rows, tok), jnp.bfloat16),
            pltpu.VMEM((cols, tok), jnp.bfloat16),
            pltpu.VMEM((cols, tok), jnp.bfloat16),
        ],
        compiler_params=params(16),
    )(own, own_other)


def hessian_kernel(row_count, col_count, mine, other, own_sum, out, *scratch):
    factors, weights, weighted, rights = *scratch[:3], scratch[3:5]
    result, sems = scratch[5:]
    rank = factors.shape[0] // 2
    blocks = mine.shape[0]
    tokens = factors.shape[1] // blocks * (blocks + 1)
    rows, cols = row_count * rank, col_count * rank
    lay_out_factors(block_pairs(mine, other), factors, weights)
    act = factors[:rank, :]
    copies = []
    build_columns(0, act, factors, rights[0])
    for step in range(rank // col_count):
        if (step + 1) * col_count < rank:
            build_columns((step + 1) * col_count, act, factors, rights[(step + 1) % 2])
        for row in range(0, rows, TILE):
            if step == 0:
                weigh_rows(row, row + TILE, row_count, factors, weights, weighted)
            here = pl.ds(row, TILE), pl.ds(step * cols, cols)
            tile = lax.dot_general(
                weighted[row : row + TILE, :],
                rights[step % 2][...],
                NT,
                preferred_element_type=jnp.float32,
            )
            result[here] = (own_sum[here] + tile) * (1.0 / tokens)
            copy = pltpu.make_async_copy(result.at[here], out.at[here], sems.at[len(copies)])
            copy.start()
            copies.append(copy)
    for copy in copies:
        copy.wait()


def hessian_rows(mine, other, own_sum, rank, row_count, col_count=8):
    blocks, _, tok = mine.shape
    feat = rank * rank
    rows, cols = row_count * rank, col_count * rank
    return pl.pallas_call(
        functools.partial(hessian_kernel, row_count, col_count),
        out_specs=pl.BlockSpec(memory_space=pl.ANY),
        out_shape=jax.ShapeDtypeStruct((rows, feat), jnp.float32),
        scratch_shapes=[
            pltpu.VMEM((2 * rank, tok * blocks), jnp.float32),
            pltpu.VMEM((1, tok * blocks), jnp.float32),
            pltpu.VMEM((rows, tok * blocks), jnp.bfloat16),
            pltpu.VMEM((cols, tok * blocks), jnp.bfloat16),
            pltpu.VMEM((cols, tok * blocks), jnp.bfloat16),
            pltpu.VMEM((rows, feat), jnp.float32),
            pltpu.SemaphoreType.DMA((feat // cols * (rows // TILE),)),
        ],
        compiler_params=params(26),
    )(mine, other, own_sum)


def finish_kernel(payload_ref, *refs):
    shares, out_ref = refs[:-1], refs[-1]
    total = shares[0][...]
    for ref in shares[1:]:
        total = total + ref[...].astype(jnp.float32)
    weight = payload_ref[...].astype(jnp.float32)[-1:]
    out_ref[...] = jnp.where(weight > 0.0, total, 0.0).T.astype(out_ref.dtype)


def finish_scores(payload, shares):
    count, tok = shares[0].shape
    return pl.pallas_call(
        finish_kernel,
        out_shape=jax.ShapeDtypeStruct((tok, count), jnp.bfloat16),
        compiler_params=params(40),
    )(payload, *shares)


def swapped(array, axis, distance):
    return lax.ppermute(array, axis, [(i, i ^ distance) for i in range(lax.axis_size(axis))])


def few_tokens(activations, out_grads, proj_in, proj_out, queries, lengths, credit):
    dp_count = lax.axis_size("dp")
    query_count = lax.axis_size("query")
    rank = proj_in.shape[1]
    row_count = rank // dp_count
    seq_len = activations.shape[0] // lengths.shape[0]
    live = jnp.arange(seq_len, dtype=jnp.int32)[None, :] < lengths[:, None]
    weight = jnp.where(live, credit[:, None], 0).astype(jnp.float32).reshape(1, -1)
    near_queries = swapped(queries, "dp", 1)
    keep, send = project(activations, out_grads, proj_in.T, proj_out.T)
    other = swapped(send, "query", 1)
    distance = 2
    while distance < query_count:
        keep = add(keep, other)
        other = swapped(keep, "query", distance)
        distance *= 2
    own = add_to_payload(keep, other, weight)
    own_other = swapped(own, "query", 1)
    others = [swapped(own, "dp", k) for k in reversed(range(1, dp_count))]
    own_sum = own_tokens_sum(own, own_other, rank, row_count)
    queries_t, own_plain = turn_queries(
        queries, near_queries, own, own_other, rank, row_count
    )
    mine, factors = stack(others, rank, (own_sum, queries_t))
    other = swapped(factors, "query", 1)
    half = half_gram(own, mine, rank)
    shares = score_shares(
        own, own_other, mine, other, queries_t, own_plain, half, rank, row_count
    )
    arrived = [swapped(share, "dp", 2 * n) for n, share in enumerate(shares) if n]
    hessian = hessian_rows(mine, other, own_sum, rank, row_count)
    return hessian, finish_scores(own, [shares[0]] + arrived)


def power_of_two(count):
    return count & (count - 1) == 0


def per_device(activations, *others):
    rank = others[1].shape[1]
    dp_count, query_count = lax.axis_size("dp"), lax.axis_size("query")
    pairs = min(dp_count, query_count) > 1 and power_of_two(dp_count) and power_of_two(query_count)
    if pairs and activations.shape[0] * dp_count <= rank * rank:
        return few_tokens(activations, *others)
    return many_tokens(activations, *others)


def solution(mesh):
    placed = (
        P(("groups", "dp"), "query"),
        P(("groups", "dp"), "query"),
        P("query", None),
        P("query", None),
        P(("groups", "dp"), "query"),
        P(("groups", "dp")),
        P(("groups", "dp")),
    )
    return jax.shard_map(
        per_device,
        mesh=mesh,
        in_specs=placed,
        out_specs=(P(("groups", "dp"), None), P(("groups", "dp"), "query")),
        check_vma=False,
    )
```
